32 devices in a mesh: fsdp: 4 (over y, x), ctx: 8 (over z, core).
Axes of the slice: x: 2, y: 2, z: 4, core: 2. Of those that a mesh axis runs over, the one named last changes fastest.
Arguments:
- tokens: bfloat16 [12288, 768], P(('fsdp', 'ctx')), may hold values from -6 to 6
- cotangent: bfloat16 [12288, 768], P(('fsdp', 'ctx')), may hold values from -6 to 6
- w_qkv: bfloat16 [768, 2304], P('fsdp'), may hold values from -0.21875 to 0.21875
- b_query: bfloat16 [768], P('fsdp'), may hold values from -1.75 to 1.75
- b_value: bfloat16 [768], P('fsdp'), may hold values from -1.75 to 1.75
- w_out: bfloat16 [768, 768], P('fsdp'), may hold values from -3.5 to 3.5
- b_out: bfloat16 [768], P('fsdp'), may hold values from -1.75 to 1.75
- w_fc: bfloat16 [768, 3072], P('fsdp'), may hold values from -0.21875 to 0.21875
- b_fc: bfloat16 [3072], P('fsdp'), may hold values from -1.75 to 1.75
- w_proj: bfloat16 [3072, 768], P('fsdp'), may hold values from -0.109375 to 0.109375
- b_proj: bfloat16 [768], P('fsdp'), may hold values from -1.75 to 1.75
- gain1: bfloat16 [768], P('fsdp'), may hold values from 0.5 to 1.5
- shift1: bfloat16 [768], P('fsdp'), may hold values from -1.75 to 1.75
- gain2: bfloat16 [768], P('fsdp'), may hold values from 0.5 to 1.5
- shift2: bfloat16 [768], P('fsdp'), may hold values from -1.75 to 1.75
- counts: int32 [4, 8], P('fsdp'), may hold values from 192 to 384, as said below
- seq_lengths: int32 [4, 3], P('fsdp'), may hold values from 1 to 3070, as said below
Outputs:
- block_out: bfloat16 [12288, 768], P(('fsdp', 'ctx'))
- d_tokens: float32 [12288, 768], P(('fsdp', 'ctx'))
- d_w_qkv: float32 [768, 2304], P('fsdp')
- d_b_query: float32 [768], P('fsdp')
- d_b_value: float32 [768], P('fsdp')
- d_w_out: float32 [768, 768], P('fsdp')
- d_b_out: float32 [768], P('fsdp')
- d_w_fc: float32 [768, 3072], P('fsdp')
- d_b_fc: float32 [3072], P('fsdp')
- d_w_proj: float32 [3072, 768], P('fsdp')
- d_b_proj: float32 [768], P('fsdp')
- d_gain1: float32 [768], P('fsdp')
- d_shift1: float32 [768], P('fsdp')
- d_gain2: float32 [768], P('fsdp')
- d_shift2: float32 [768], P('fsdp')
The draws below stay inside these ranges and needn't reach their ends.
Inputs may be any that keep to these rules, and one draw needn't show every extreme that they name: `counts`: each device holds between 192 and 384 live slots, its first ones; in every group some device holds exactly 384. `seq_lengths`: the lengths of a group sum to its live slots; in every group one sequence, at a position that varies, holds a slot of the first device and of the last device of the group; the other two have fewer than 96 tokens each.
All inputs are finite; a program needn't handle non-finite values.
Results may differ from the reference program's by a relative error of at most 0.018.
Values may be sent and summed in bfloat16 or wider, within the bound.
No kernel may reach another device: no remote copies, remote signals or barrier semaphores. Data moves between devices by JAX's collectives and lax.ppermute only.
A program may use at most 192 MiB of HBM per device.

```python
import jax
import jax.numpy as jnp
from jax import lax

D = 768
HEADS = 12
FF = 3072
HEAD_DIM = 64
CAP = 384
TOKENS = 12288
N_FSDP = 4
N_CTX = 8


def spread_total(key, total, pieces, limit):
    rows = total.shape[0]
    index = jnp.arange(pieces, dtype=jnp.int32)[None, :]
    base = total // pieces
    remain = total - base * pieces
    values = (base + (index < remain).astype(jnp.int32)).astype(jnp.int32)
    pairs = pieces // 2
    if pairs == 0:
        return values
    first = values[:, 0:2 * pairs:2]
    second = values[:, 1:2 * pairs:2]
    low_move = jnp.maximum(-first, second - limit)
    high_move = jnp.minimum(limit - first, second)
    moved = jax.random.randint(key, first.shape, low_move, high_move + 1).astype(jnp.int32)
    joined = jnp.stack([first + moved, second - moved], axis=2).reshape(rows, 2 * pairs)
    return jnp.concatenate([joined, values[:, 2 * pairs:]], axis=1).astype(jnp.int32)


def group_layout(key):
    key_total, key_short, key_spot, key_full, key_counts = jax.random.split(key, 5)
    key_whole = jax.random.fold_in(key_total, 7)
    half = CAP // 2
    lowest = CAP + (N_CTX - 1) * half
    highest = N_CTX * CAP
    group_rows = jnp.arange(N_FSDP, dtype=jnp.int32)[:, None]
    whole_group = jax.random.randint(key_whole, (), 0, N_FSDP).astype(jnp.int32)
    is_whole = group_rows == whole_group
    group_total = jax.random.randint(key_total, (N_FSDP, 1), lowest, highest + 1).astype(jnp.int32)
    group_total = jnp.where(is_whole, highest, group_total).astype(jnp.int32)
    others = half + spread_total(key_counts, group_total - CAP - (N_CTX - 1) * half, N_CTX - 1, CAP - half)
    busiest = jax.random.randint(key_full, (N_FSDP, 1), 0, N_CTX)
    columns = jnp.arange(N_CTX, dtype=jnp.int32)[None, :]
    source = jnp.clip(columns - (columns > busiest).astype(jnp.int32), 0, N_CTX - 2)
    picked = jnp.take_along_axis(others, jnp.broadcast_to(source, (N_FSDP, N_CTX)), axis=1)
    counts = jnp.where(columns == busiest, CAP, picked).astype(jnp.int32)
    shorts = jax.random.randint(key_short, (N_FSDP, 2), 1, CAP // 4).astype(jnp.int32)
    shorts = jnp.where(is_whole, 1, shorts).astype(jnp.int32)
    longest = group_total[:, 0] - shorts[:, 0] - shorts[:, 1]
    spot = jax.random.randint(key_spot, (N_FSDP,), 0, 3)
    first = jnp.where(spot == 0, longest, shorts[:, 0])
    second = jnp.where(spot == 1, longest, jnp.where(spot == 0, shorts[:, 0], shorts[:, 1]))
    third = jnp.where(spot == 2, longest, shorts[:, 1])
    lengths = jnp.stack([first, second, third], axis=1)
    return (counts, lengths.astype(jnp.int32))


def draw_counts(key, part):
    return group_layout(key)[0]


def draw_seq_lengths(key, part):
    return group_layout(key)[1]


def levels(own_key, extent, shards, smallest, high):
    factor_of, own = 1.0, jax.random.fold_in(own_key, 6)
    for axis_at, blocks in shards:
        heights = jnp.exp(jax.random.uniform(jax.random.fold_in(own, axis_at), (blocks,), jnp.float32, smallest / len(shards), high / len(shards)))
        factor_of = factor_of * jnp.repeat(heights, extent[axis_at] // blocks).reshape([-1 if axis == axis_at else 1 for axis in range(len(extent))])
    return factor_of


def centred(own_key, extent, width, most, shards=(), kind=jnp.bfloat16):
    array = width * jax.random.normal(own_key, extent, jnp.float32)
    if shards:
        array = array * levels(own_key, extent, shards, -0.22, 0.18)
    return jnp.clip(array, -most, most).astype(kind)


def setup_inputs(seed: int = 0) -> dict:
    keys = jax.random.split(jax.random.key(seed), 18)
    return {
        "tokens": centred(keys[0], (TOKENS, D), 1.0, 6.0, ((0, 32),)),
        "cotangent": centred(keys[1], (TOKENS, D), 1.0, 6.0, ((0, 32),)),
        "w_qkv": centred(keys[2], (D, 3 * D), D ** -0.5, 0.21875, ((0, 4),)),
        "b_query": centred(keys[3], (D,), 0.3, 1.75, ((0, 4),)),
        "b_value": centred(keys[4], (D,), 0.3, 1.75, ((0, 4),)),
        "w_out": centred(keys[5], (D, D), 3 ** -0.5, 3.5, ((0, 4),)),
        "b_out": centred(keys[6], (D,), 0.3, 1.75, ((0, 4),)),
        "w_fc": centred(keys[7], (D, FF), D ** -0.5, 0.21875, ((0, 4),)),
        "b_fc": centred(keys[8], (FF,), 0.3, 1.75, ((0, 4),)),
        "w_proj": centred(keys[9], (FF, D), FF ** -0.5, 0.109375, ((0, 4),)),
        "b_proj": centred(keys[10], (D,), 0.3, 1.75, ((0, 4),)),
        "gain1": jnp.clip(1.0 + 0.1 * jax.random.normal(keys[11], (D,), jnp.float32), 0.5, 1.5).astype(jnp.bfloat16),
        "shift1": centred(keys[12], (D,), 0.3, 1.75, ((0, 4),)),
        "gain2": jnp.clip(1.0 + 0.1 * jax.random.normal(keys[13], (D,), jnp.float32), 0.5, 1.5).astype(jnp.bfloat16),
        "shift2": centred(keys[14], (D,), 0.3, 1.75, ((0, 4),)),
        "counts": draw_counts(jax.random.fold_in(keys[17], 71), 0),
        "seq_lengths": draw_seq_lengths(jax.random.fold_in(keys[17], 71), 0),
    }


EPS = 1e-05
HIGH = lax.Precision.HIGHEST

@jax.custom_vjp
def low(v):
    return lax.optimization_barrier(v.astype(jnp.bfloat16)).astype(jnp.float32)

@jax.custom_vjp
def low_back(v):
    return v

def low_keep(v):
    return (low(v), None)

def low_pass(kept, grad):
    return (grad,)

def back_keep(v):
    return (v, None)

def back_low(kept, grad):
    return (low(grad),)
low.defvjp(low_keep, low_pass)
low_back.defvjp(back_keep, back_low)

def layer_norm(values, gain_row, shift_row):
    centre = values - lax.optimization_barrier(jnp.mean(values, axis=1, keepdims=True))
    variance = lax.optimization_barrier(jnp.mean(centre * centre, axis=1, keepdims=True))
    return centre * lax.rsqrt(variance + EPS) * gain_row + shift_row

def slot_table(count_row, length_row):
    offsets = (jnp.cumsum(count_row) - count_row).astype(jnp.int32)
    seq_ends = jnp.cumsum(length_row).astype(jnp.int32)
    slot_ids = jnp.arange(N_CTX * CAP, dtype=jnp.int32)
    device = slot_ids // CAP
    within = slot_ids - device * CAP
    live_mask = within < count_row[device]
    places = offsets[device] + within
    segment = lax.optimization_barrier(jnp.sum((places[:, None] >= seq_ends[None, :]).astype(jnp.int32), axis=1))
    return (live_mask, places, segment)

def attend_group(group_data):
    queries, keys_all, values_all, live_mask, places, segment = group_data
    slot_ids = jnp.arange(N_CTX * CAP, dtype=jnp.int32)

    def one_block(block_data):
        query_rows, q_live, q_place, q_segment, q_slot = block_data
        scores = jnp.einsum('qhd,khd->hqk', query_rows, keys_all, precision=HIGH) * HEAD_DIM ** (-0.5)
        scores = low_back(scores)
        permitted = q_live[:, None] & live_mask[None, :] & (q_segment[:, None] == segment[None, :]) & (places[None, :] <= q_place[:, None]) | (q_slot[:, None] == slot_ids[None, :])
        scores = jnp.where(permitted[None], scores, -jnp.inf)
        highest = lax.optimization_barrier(jnp.max(scores, axis=2, keepdims=True))
        weights = jnp.exp(scores - highest)
        totals = lax.optimization_barrier(jnp.sum(weights, axis=2))
        mixed_values = jnp.einsum('hqk,khd->qhd', low(weights), values_all, precision=HIGH)
        return mixed_values / jnp.transpose(totals)[:, :, None]
    blocks = (queries.reshape(N_CTX, CAP, HEADS, HEAD_DIM), live_mask.reshape(N_CTX, CAP), places.reshape(N_CTX, CAP), segment.reshape(N_CTX, CAP), slot_ids.reshape(N_CTX, CAP))
    return lax.map(jax.checkpoint(one_block), blocks).reshape(N_CTX * CAP, HEADS, HEAD_DIM)

def forward(tokens, w_qkv, b_query, b_value, w_out, b_out, w_fc, b_fc, w_proj, b_proj, gain1, shift1, gain2, shift2, tables):
    live_mask, places, segment = tables
    normed_one = low(layer_norm(tokens, gain1, shift1))
    bias_row = jnp.concatenate([b_query, jnp.zeros_like(b_query), b_value])
    packed = jnp.dot(normed_one, w_qkv, precision=HIGH) + bias_row
    packed = low(low_back(packed))
    head_shape = (N_FSDP, N_CTX * CAP, HEADS, HEAD_DIM)
    queries = packed[:, :D].reshape(head_shape)
    keys_all = packed[:, D:2 * D].reshape(head_shape)
    values_all = packed[:, 2 * D:].reshape(head_shape)
    attended = lax.map(attend_group, (queries, keys_all, values_all, live_mask, places, segment))
    attended = low(low_back(attended.reshape(TOKENS, D)))
    branch = low_back(jnp.dot(attended, w_out, precision=HIGH) + b_out)
    middle = tokens + branch
    normed_two = low(layer_norm(middle, gain2, shift2))
    hidden = low_back(jnp.dot(normed_two, w_fc, precision=HIGH) + b_fc)
    activated = low(jax.nn.gelu(hidden, approximate=True))
    return middle + jnp.dot(activated, w_proj, precision=HIGH) + b_proj

def reference(tokens, cotangent, w_qkv, b_query, b_value, w_out, b_out, w_fc, b_fc, w_proj, b_proj, gain1, shift1, gain2, shift2, counts, seq_lengths):
    live_mask, places, segment = jax.vmap(slot_table)(counts, seq_lengths)
    tables = (live_mask, places, segment)
    parameters = tuple((parameter.astype(jnp.float32) for parameter in (w_qkv, b_query, b_value, w_out, b_out, w_fc, b_fc, w_proj, b_proj, gain1, shift1, gain2, shift2)))

    def wrapped(*inputs):
        return forward(*inputs, tables)
    output, pull_back = jax.vjp(wrapped, tokens.astype(jnp.float32), *parameters)
    seed_grad = cotangent.astype(jnp.float32) * live_mask.reshape(TOKENS, 1).astype(jnp.float32)
    gradients = pull_back(seed_grad)
    return (output.astype(jnp.bfloat16), gradients[0], gradients[1], gradients[2], gradients[3], gradients[4], gradients[5], gradients[6], gradients[7], gradients[8], gradients[9], gradients[10], gradients[11], gradients[12], gradients[13])
```

```python
import functools

import jax
import jax.numpy as jnp
from jax import lax
from jax.experimental import pallas as pl
from jax.experimental.pallas import tpu as pltpu
from jax.sharding import PartitionSpec as P

HEADS = 12


EPS = 1e-05


def layer_norm(values, gain_row, shift_row):
    centre = values - jnp.mean(values, axis=1, keepdims=True)
    inverse = lax.rsqrt(jnp.mean(centre * centre, axis=1, keepdims=True) + EPS)
    normed = centre * inverse
    return (normed * gain_row + shift_row, normed, inverse)


def norm_back(grad_in, normed, inverse, gain_row):
    scaled = grad_in * gain_row
    inner_grad = inverse * (
        scaled
        - jnp.mean(scaled, axis=1, keepdims=True)
        - normed * jnp.mean(scaled * normed, axis=1, keepdims=True)
    )
    return (inner_grad, jnp.sum(grad_in * normed, axis=0), jnp.sum(grad_in, axis=0))


def contract_rows(left_side, right_side):
    return lax.dot_general(
        left_side, right_side, (((0,), (0,)), ((), ())), preferred_element_type=jnp.float32
    )


def times_transpose(left_side, right_side):
    return lax.dot_general(
        left_side, right_side, (((1,), (1,)), ((), ())), preferred_element_type=jnp.float32
    )


def gelu_tanh(values):
    return jax.nn.gelu(values, approximate=True)


def describe(slot_ids, row_count, count_row, offsets, seq_ends):
    peer_count = count_row.shape[0]
    device = slot_ids // row_count
    within = slot_ids - device * row_count
    matches = device[:, None] == jnp.arange(peer_count, dtype=jnp.int32)[None, :]
    live_count = jnp.sum(jnp.where(matches, count_row[None, :], 0), axis=1)
    first_place = jnp.sum(jnp.where(matches, offsets[None, :], 0), axis=1)
    places = first_place + within
    segment = jnp.sum((places[:, None] >= seq_ends[None, :]).astype(jnp.int32), axis=1)
    return (within < live_count, places, segment, slot_ids)


def allowed(query_info, key_info):
    q_live, q_place, q_seg, q_slot = query_info
    k_live, k_place, k_seg, k_slot = key_info
    same_seq = (
        q_live[:, None]
        & k_live[None, :]
        & (q_seg[:, None] == k_seg[None, :])
        & (k_place[None, :] <= q_place[:, None])
    )
    return same_seq | (q_slot[:, None] == k_slot[None, :])


def over_blocks(step_fn, status, pieces, row_count):
    total_rows = pieces[0].shape[0]
    block_total = total_rows // row_count
    stacked = tuple((piece.reshape((block_total, row_count) + piece.shape[1:]) for piece in pieces))

    def scan_body(state_now, scan_item):
        block_index, block_parts = scan_item
        return (step_fn(state_now, block_parts, block_index * row_count), None)

    status, unused = lax.scan(
        scan_body, status, (jnp.arange(block_total, dtype=jnp.int32), stacked)
    )
    return status


def score_grads(
    query_heads, key_heads, value_heads, grad_heads, lse_rows, delta_rows, permitted, scaling
):
    scores = (
        jnp.einsum("qhd,khd->hqk", query_heads, key_heads, preferred_element_type=jnp.float32)
        * scaling
    )
    probabilities = jnp.where(permitted[None], jnp.exp(scores - lse_rows[:, :, None]), 0.0)
    grad_probs = jnp.einsum(
        "qhd,khd->hqk", grad_heads, value_heads, preferred_element_type=jnp.float32
    )
    grad_scores = (probabilities * (grad_probs - delta_rows[:, :, None])).astype(jnp.bfloat16)
    return (probabilities.astype(jnp.bfloat16), grad_scores)


def general_body(
    tokens,
    cotangent,
    w_qkv,
    b_query,
    b_value,
    w_out,
    b_out,
    w_fc,
    b_fc,
    w_proj,
    b_proj,
    gain1,
    shift1,
    gain2,
    shift2,
    counts,
    seq_lengths,
):
    row_count, feature_count = tokens.shape
    peer_count = lax.axis_size("ctx")
    my_index = lax.axis_index("ctx")
    head_count = HEADS
    head_width = feature_count // head_count
    scaling = head_width ** (-0.5)
    count_row = counts[0]
    offsets = jnp.cumsum(count_row) - count_row
    seq_ends = jnp.cumsum(seq_lengths[0])

    def locate(first_slot, length):
        return describe(
            first_slot + jnp.arange(length, dtype=jnp.int32),
            row_count,
            count_row,
            offsets,
            seq_ends,
        )

    own_rows = locate(my_index * row_count, row_count)
    fp32 = jnp.float32
    bf16 = jnp.bfloat16
    (
        qkv_full,
        query_bias,
        value_bias,
        out_full,
        out_bias,
        fc_full,
        fc_bias,
        proj_full,
        proj_bias,
        gain_one,
        shift_one,
        gain_two,
        shift_two,
    ) = (
        lax.all_gather(w_qkv, "fsdp", axis=0, tiled=True),
        lax.all_gather(b_query, "fsdp", axis=0, tiled=True),
        lax.all_gather(b_value, "fsdp", axis=0, tiled=True),
        lax.all_gather(w_out, "fsdp", axis=0, tiled=True),
        lax.all_gather(b_out, "fsdp", axis=0, tiled=True),
        lax.all_gather(w_fc, "fsdp", axis=0, tiled=True),
        lax.all_gather(b_fc, "fsdp", axis=0, tiled=True),
        lax.all_gather(w_proj, "fsdp", axis=0, tiled=True),
        lax.all_gather(b_proj, "fsdp", axis=0, tiled=True),
        lax.all_gather(gain1, "fsdp", axis=0, tiled=True),
        lax.all_gather(shift1, "fsdp", axis=0, tiled=True),
        lax.all_gather(gain2, "fsdp", axis=0, tiled=True),
        lax.all_gather(shift2, "fsdp", axis=0, tiled=True),
    )
    inputs = tokens.astype(fp32)
    normed_one, unit_one, inverse_one = layer_norm(
        inputs, gain_one.astype(fp32), shift_one.astype(fp32)
    )
    normed_low = normed_one.astype(bf16)
    bias_row = jnp.concatenate([query_bias, jnp.zeros_like(query_bias), value_bias]).astype(fp32)
    packed = (jnp.dot(normed_low, qkv_full, preferred_element_type=fp32) + bias_row).astype(bf16)
    query_rows = packed[:, :feature_count]
    key_rows = packed[:, feature_count : 2 * feature_count]
    value_rows = packed[:, 2 * feature_count :]
    query_heads = query_rows.reshape(row_count, head_count, head_width)

    def forward_step(status, pieces, first_row):
        running_max, running_sum, running_acc = status
        key_piece, value_piece = pieces
        length = key_piece.shape[0]
        key_heads = key_piece.reshape(length, head_count, head_width)
        value_heads = value_piece.reshape(length, head_count, head_width)
        scores = (
            jnp.einsum("qhd,khd->hqk", query_heads, key_heads, preferred_element_type=fp32)
            * scaling
        )
        permitted = allowed(own_rows, locate(first_row, length))
        scores = jnp.where(permitted[None], scores, -jnp.inf)
        new_max = jnp.maximum(running_max, jnp.max(scores, axis=2))
        fading = jnp.exp(running_max - new_max)
        weights = jnp.exp(scores - new_max[:, :, None])
        running_sum = running_sum * fading + jnp.sum(weights, axis=2)
        update = jnp.einsum(
            "hqk,khd->qhd", weights.astype(bf16), value_heads, preferred_element_type=fp32
        )
        running_acc = running_acc * jnp.transpose(fading)[:, :, None] + update
        return (new_max, running_sum, running_acc)

    start_state = (
        jnp.full((head_count, row_count), -1e30, fp32),
        jnp.zeros((head_count, row_count), fp32),
        jnp.zeros((row_count, head_count, head_width), fp32),
    )
    final_max, final_sum, final_acc = over_blocks(
        forward_step,
        start_state,
        (
            lax.all_gather(key_rows, "ctx", axis=0, tiled=True),
            lax.all_gather(value_rows, "ctx", axis=0, tiled=True),
        ),
        row_count,
    )
    attended_heads = final_acc / jnp.transpose(final_sum)[:, :, None]
    attended = attended_heads.reshape(row_count, feature_count)
    log_total = final_max + jnp.log(final_sum)
    attended_low = attended.astype(bf16)
    middle = (
        inputs
        + jnp.dot(attended_low, out_full, preferred_element_type=fp32)
        + out_bias.astype(fp32)
    )
    normed_two, unit_two, inverse_two = layer_norm(
        middle, gain_two.astype(fp32), shift_two.astype(fp32)
    )
    normed_two_low = normed_two.astype(bf16)
    hidden = jnp.dot(normed_two_low, fc_full, preferred_element_type=fp32) + fc_bias.astype(fp32)
    activated = gelu_tanh(hidden).astype(bf16)
    output = (
        middle + jnp.dot(activated, proj_full, preferred_element_type=fp32) + proj_bias.astype(fp32)
    )
    output_low = output.astype(bf16)
    qkv_full, out_full, fc_full, proj_full, gain_one, gain_two = (
        lax.all_gather(w_qkv, "fsdp", axis=0, tiled=True),
        lax.all_gather(w_out, "fsdp", axis=0, tiled=True),
        lax.all_gather(w_fc, "fsdp", axis=0, tiled=True),
        lax.all_gather(w_proj, "fsdp", axis=0, tiled=True),
        lax.all_gather(gain1, "fsdp", axis=0, tiled=True),
        lax.all_gather(gain2, "fsdp", axis=0, tiled=True),
    )
    live_rows = own_rows[0].astype(fp32)[:, None]
    grad_out = cotangent.astype(fp32) * live_rows
    grad_out_low = grad_out.astype(bf16)
    grad_proj = contract_rows(activated, grad_out_low)
    grad_proj_bias = jnp.sum(grad_out, axis=0)
    grad_act = times_transpose(grad_out_low, proj_full)
    grad_hidden = jax.vjp(gelu_tanh, hidden)[1](grad_act)[0]
    grad_hidden_low = grad_hidden.astype(bf16)
    grad_fc = contract_rows(normed_two_low, grad_hidden_low)
    grad_fc_bias = jnp.sum(grad_hidden_low.astype(fp32), axis=0)
    grad_normed_two = times_transpose(grad_hidden_low, fc_full)
    grad_mid_norm, grad_gain_two, grad_shift_two = norm_back(
        grad_normed_two, unit_two, inverse_two, gain_two.astype(fp32)
    )
    grad_middle = grad_out + grad_mid_norm
    grad_middle_low = grad_middle.astype(bf16)
    grad_out_proj = contract_rows(attended_low, grad_middle_low)
    grad_out_bias = jnp.sum(grad_middle_low.astype(fp32), axis=0)
    grad_attended = times_transpose(grad_middle_low, out_full).astype(bf16)
    grad_heads = grad_attended.reshape(row_count, head_count, head_width)
    delta_rows = jnp.transpose(jnp.sum(grad_heads.astype(fp32) * attended_heads, axis=2))

    def back_step(status, pieces, first_row):
        grad_query, grad_keys = status
        key_piece, value_piece = pieces
        length = key_piece.shape[0]
        key_heads = key_piece.reshape(length, head_count, head_width)
        value_heads = value_piece.reshape(length, head_count, head_width)
        permitted = allowed(own_rows, locate(first_row, length))
        probs_low, grad_scores = score_grads(
            query_heads,
            key_heads,
            value_heads,
            grad_heads,
            log_total,
            delta_rows,
            permitted,
            scaling,
        )
        grad_query = (
            grad_query
            + jnp.einsum("hqk,khd->qhd", grad_scores, key_heads, preferred_element_type=fp32)
            * scaling
        )
        grad_key_part = (
            jnp.einsum("hqk,qhd->khd", grad_scores, query_heads, preferred_element_type=fp32)
            * scaling
        )
        grad_value_part = jnp.einsum(
            "hqk,qhd->khd", probs_low, grad_heads, preferred_element_type=fp32
        )
        joined = jnp.concatenate(
            [
                grad_key_part.reshape(length, feature_count),
                grad_value_part.reshape(length, feature_count),
            ],
            axis=1,
        )
        current = lax.dynamic_slice_in_dim(grad_keys, first_row, length, 0)
        grad_keys = lax.dynamic_update_slice_in_dim(grad_keys, current + joined, first_row, 0)
        return (grad_query, grad_keys)

    keys_start = jnp.zeros((peer_count * row_count, 2 * feature_count), fp32)
    grad_query, grad_keys = over_blocks(
        back_step,
        (jnp.zeros((row_count, head_count, head_width), fp32), keys_start),
        (
            lax.all_gather(key_rows, "ctx", axis=0, tiled=True),
            lax.all_gather(value_rows, "ctx", axis=0, tiled=True),
        ),
        row_count,
    )
    grad_kv = lax.psum_scatter(
        grad_keys.astype(jnp.bfloat16), "ctx", scatter_dimension=0, tiled=True
    ).astype(jnp.float32)
    grad_packed = jnp.concatenate(
        [grad_query.reshape(row_count, feature_count), grad_kv], axis=1
    ).astype(bf16)
    grad_packed_wide = grad_packed.astype(fp32)
    grad_query_bias = jnp.sum(grad_packed_wide[:, :feature_count], axis=0)
    grad_value_bias = jnp.sum(grad_packed_wide[:, 2 * feature_count :], axis=0)
    grad_qkv = contract_rows(normed_low, grad_packed)
    grad_normed_one = times_transpose(grad_packed, qkv_full)
    grad_in_norm, grad_gain_one, grad_shift_one = norm_back(
        grad_normed_one, unit_one, inverse_one, gain_one.astype(fp32)
    )
    grad_tokens = grad_middle + grad_in_norm
    (
        sum_qkv,
        sum_qbias,
        sum_vbias,
        sum_out,
        sum_obias,
        sum_fc,
        sum_fbias,
        sum_proj,
        sum_pbias,
        sum_gain_one,
        sum_shift_one,
        sum_gain_two,
        sum_shift_two,
    ) = (
        lax.psum_scatter(
            grad_qkv.astype(jnp.bfloat16), "fsdp", scatter_dimension=0, tiled=True
        ).astype(jnp.float32),
        lax.psum_scatter(
            grad_query_bias.astype(jnp.bfloat16), "fsdp", scatter_dimension=0, tiled=True
        ).astype(jnp.float32),
        lax.psum_scatter(
            grad_value_bias.astype(jnp.bfloat16), "fsdp", scatter_dimension=0, tiled=True
        ).astype(jnp.float32),
        lax.psum_scatter(
            grad_out_proj.astype(jnp.bfloat16), "fsdp", scatter_dimension=0, tiled=True
        ).astype(jnp.float32),
        lax.psum_scatter(
            grad_out_bias.astype(jnp.bfloat16), "fsdp", scatter_dimension=0, tiled=True
        ).astype(jnp.float32),
        lax.psum_scatter(
            grad_fc.astype(jnp.bfloat16), "fsdp", scatter_dimension=0, tiled=True
        ).astype(jnp.float32),
        lax.psum_scatter(
            grad_fc_bias.astype(jnp.bfloat16), "fsdp", scatter_dimension=0, tiled=True
        ).astype(jnp.float32),
        lax.psum_scatter(
            grad_proj.astype(jnp.bfloat16), "fsdp", scatter_dimension=0, tiled=True
        ).astype(jnp.float32),
        lax.psum_scatter(
            grad_proj_bias.astype(jnp.bfloat16), "fsdp", scatter_dimension=0, tiled=True
        ).astype(jnp.float32),
        lax.psum_scatter(
            grad_gain_one.astype(jnp.bfloat16), "fsdp", scatter_dimension=0, tiled=True
        ).astype(jnp.float32),
        lax.psum_scatter(
            grad_shift_one.astype(jnp.bfloat16), "fsdp", scatter_dimension=0, tiled=True
        ).astype(jnp.float32),
        lax.psum_scatter(
            grad_gain_two.astype(jnp.bfloat16), "fsdp", scatter_dimension=0, tiled=True
        ).astype(jnp.float32),
        lax.psum_scatter(
            grad_shift_two.astype(jnp.bfloat16), "fsdp", scatter_dimension=0, tiled=True
        ).astype(jnp.float32),
    )
    totals = (
        lax.psum(sum_qkv.astype(jnp.bfloat16), "ctx").astype(jnp.float32),
        lax.psum(sum_qbias.astype(jnp.bfloat16), "ctx").astype(jnp.float32),
        lax.psum(sum_vbias.astype(jnp.bfloat16), "ctx").astype(jnp.float32),
        lax.psum(sum_out.astype(jnp.bfloat16), "ctx").astype(jnp.float32),
        lax.psum(sum_obias.astype(jnp.bfloat16), "ctx").astype(jnp.float32),
        lax.psum(sum_fc.astype(jnp.bfloat16), "ctx").astype(jnp.float32),
        lax.psum(sum_fbias.astype(jnp.bfloat16), "ctx").astype(jnp.float32),
        lax.psum(sum_proj.astype(jnp.bfloat16), "ctx").astype(jnp.float32),
        lax.psum(sum_pbias.astype(jnp.bfloat16), "ctx").astype(jnp.float32),
        lax.psum(sum_gain_one.astype(jnp.bfloat16), "ctx").astype(jnp.float32),
        lax.psum(sum_shift_one.astype(jnp.bfloat16), "ctx").astype(jnp.float32),
        lax.psum(sum_gain_two.astype(jnp.bfloat16), "ctx").astype(jnp.float32),
        lax.psum(sum_shift_two.astype(jnp.bfloat16), "ctx").astype(jnp.float32),
    )
    return (
        output_low,
        grad_tokens,
        totals[0],
        totals[1],
        totals[2],
        totals[3],
        totals[4],
        totals[5],
        totals[6],
        totals[7],
        totals[8],
        totals[9],
        totals[10],
        totals[11],
        totals[12],
    )


FP32 = jnp.float32
BF16 = jnp.bfloat16
FLOOR = -1e30
NEVER = 1 << 30


def dot_nt(left_side, right_side):
    return lax.dot_general(
        left_side, right_side, (((1,), (1,)), ((), ())), preferred_element_type=FP32
    )


def dot_nn(left_side, right_side):
    return lax.dot_general(
        left_side, right_side, (((1,), (0,)), ((), ())), preferred_element_type=FP32
    )


def spread(column_tile, width):
    return jnp.concatenate([column_tile] * (width // column_tile.shape[1]), axis=1)


def masked_scores(scores, key_ids, first_row, last_row):
    permitted = key_ids >= first_row
    if last_row is not None:
        permitted = permitted & (key_ids <= last_row)
    return jnp.where(permitted, scores, -jnp.inf)


def attend_kernel(
    parity, q_ref, k_ref, vt_ref, key_ref, low_ref, high_ref, far_ref, o_ref, ot_ref, lse_ref, acc_ref
):
    blocks, rows, width = q_ref.shape
    heads = width // 64

    def query_block(index, unused):
        queries = [q_ref[index, :, 64 * h : 64 * h + 64] for h in range(heads)]
        acc_ref[...] = jnp.zeros_like(acc_ref)

        def key_step(key_block, carry, first_row, last_row):
            ids = spread(key_ref[key_block], rows)
            result = []
            for h in range(heads):
                span = slice(64 * h, 64 * h + 64)
                top, total = carry[h]
                scores = dot_nt(k_ref[key_block, :, span], queries[h])
                scores = masked_scores(scores, ids, first_row, last_row)
                new_top = jnp.maximum(top, jnp.max(scores, axis=0, keepdims=True))
                fade = jnp.exp(top - new_top)
                weights = jnp.exp(scores - new_top)
                total = total * fade + jnp.sum(weights, axis=0, keepdims=True)
                acc_ref[span, :] = acc_ref[span, :] * fade + dot_nn(
                    vt_ref[key_block, span, :], weights.astype(BF16)
                )
                result.append((new_top, total))
            return tuple(result)

        start = tuple(
            (jnp.full((1, rows), FLOOR, FP32), jnp.zeros((1, rows), FP32)) for h in range(heads)
        )
        own = 2 * index + parity[0]
        far_row = far_ref[index]
        carry = lax.fori_loop(
            0, own, lambda j, c: key_step(j, c, far_row, None), start
        )
        carry = key_step(own, carry, low_ref[index], high_ref[index])
        for h in range(heads):
            span = slice(64 * h, 64 * h + 64)
            top, total = carry[h]
            attended = acc_ref[span, :] / total
            ot_ref[index, span, :] = attended
            o_ref[index, :, span] = attended.T.astype(BF16)
            lse_ref[index, h : h + 1, :] = top + jnp.log(total)
        return unused

    lax.fori_loop(0, blocks, query_block, 0)


def attend_back_kernel(
    parity,
    q_ref,
    k_ref,
    kt_ref,
    v_ref,
    da_ref,
    key_ref,
    low_ref,
    high_ref,
    far_ref,
    ot_ref,
    lse_ref,
    dq_ref,
    keep_ref,
    send_ref,
    acc_ref,
    dk_ref,
    dv_ref,
):
    blocks, rows, width = q_ref.shape
    heads = width // 64
    dk_ref[...] = jnp.zeros_like(dk_ref)
    dv_ref[...] = jnp.zeros_like(dv_ref)

    def query_block(index, unused):
        queries = [q_ref[index, :, 64 * h : 64 * h + 64] for h in range(heads)]
        grads = [da_ref[index, :, 64 * h : 64 * h + 64] for h in range(heads)]
        deltas = [
            jnp.sum(
                grads[h].astype(FP32).T * ot_ref[index, 64 * h : 64 * h + 64, :],
                axis=0,
                keepdims=True,
            )
            for h in range(heads)
        ]
        logs = [lse_ref[index, h : h + 1, :] for h in range(heads)]
        acc_ref[...] = jnp.zeros_like(acc_ref)

        def key_step(key_block, first_row, last_row):
            ids = spread(key_ref[key_block], rows)
            for h in range(heads):
                span = slice(64 * h, 64 * h + 64)
                scores = dot_nt(k_ref[key_block, :, span], queries[h])
                scores = masked_scores(scores, ids, first_row, last_row)
                weights = jnp.exp(scores - logs[h])
                slopes = dot_nt(v_ref[key_block, :, span], grads[h])
                dscores = (weights * (slopes - deltas[h])).astype(BF16)
                dv_ref[h, key_block] += dot_nn(weights.astype(BF16), grads[h])
                dk_ref[h, key_block] += dot_nn(dscores, queries[h])
                acc_ref[span, :] += dot_nn(kt_ref[key_block, span, :], dscores)

        own = 2 * index + parity[0]
        far_row = far_ref[index]

        def far_step(key_block, state):
            key_step(key_block, far_row, None)
            return state

        lax.fori_loop(0, own, far_step, 0)
        key_step(own, low_ref[index], high_ref[index])
        for h in range(heads):
            span = slice(64 * h, 64 * h + 64)
            dq_ref[index, :, span] = (acc_ref[span, :] * 0.125).T.astype(BF16)
        return unused

    lax.fori_loop(0, blocks, query_block, 0)

    def write_block(index, unused):
        mine = 2 * index + parity[0]
        theirs = 2 * index + 1 - parity[0]
        for h in range(heads):
            left = slice(64 * h, 64 * h + 64)
            right = slice(width + 64 * h, width + 64 * h + 64)
            keep_ref[index, :, left] = dk_ref[h, mine]
            keep_ref[index, :, right] = dv_ref[h, mine]
            send_ref[index, :, left] = dk_ref[h, theirs].astype(BF16)
            send_ref[index, :, right] = dv_ref[h, theirs].astype(BF16)
        return unused

    lax.fori_loop(0, blocks, write_block, 0)


def kernel_call(kernel, outputs, scratch, operands, flops):
    in_specs = [pl.BlockSpec(memory_space=pltpu.SMEM)] + [
        pl.BlockSpec(memory_space=pltpu.VMEM) for unused in operands[1:]
    ]
    moved = sum(v.size * v.dtype.itemsize for v in list(operands) + list(outputs))
    return pl.pallas_call(
        kernel,
        out_shape=outputs,
        in_specs=in_specs,
        out_specs=[pl.BlockSpec(memory_space=pltpu.VMEM) for unused in outputs],
        scratch_shapes=scratch,
        compiler_params=pltpu.CompilerParams(vmem_limit_bytes=56 * 1024 * 1024),
        cost_estimate=pl.CostEstimate(flops=flops, bytes_accessed=moved, transcendentals=flops // 256),
    )(*operands)


def fast_body(
    tokens,
    cotangent,
    w_qkv,
    b_query,
    b_value,
    w_out,
    b_out,
    w_fc,
    b_fc,
    w_proj,
    b_proj,
    gain1,
    shift1,
    gain2,
    shift2,
    counts,
    seq_lengths,
):
    rows, features = tokens.shape
    ctx = lax.axis_size("ctx")
    fsdp = lax.axis_size("fsdp")
    chips = ctx // 2
    group_heads = HEADS // chips
    width = features // chips
    shard = features // fsdp
    hidden_width = w_fc.shape[1]
    place = lax.axis_index("ctx")
    chip = place // 2
    core = place % 2
    part = lax.axis_index("fsdp")
    near = 1 + core
    across = 2 - core

    def exchange(value, partner):
        pairs = [
            (f * ctx + c, g * ctx + d)
            for f in range(fsdp)
            for c in range(ctx)
            for g, d in [partner(f, c)]
        ]
        return jax.tree.map(lambda leaf: lax.ppermute(leaf, ("fsdp", "ctx"), pairs), value)

    def to_near(value):
        return exchange(value, lambda f, c: (f ^ (1 + c % 2), c))

    def to_across(value):
        return exchange(value, lambda f, c: (f ^ (2 - c % 2), c))

    def to_part(value, step):
        return exchange(value, lambda f, c: (f ^ step, c))

    def to_core(value):
        return exchange(value, lambda f, c: (f, c ^ 1))

    def to_chip(value, step):
        return exchange(value, lambda f, c: (f, c ^ (2 * step)))

    def pick(array, index, axis=0):
        return lax.dynamic_index_in_dim(array, index, axis, keepdims=False)

    def place_all(shape, dtype, items):
        buffer = jnp.zeros(shape, dtype)
        for index, value in items:
            full = value.reshape((1,) * (len(shape) - value.ndim) + value.shape)
            starts = tuple(index) + (0,) * (len(shape) - len(index))
            buffer = lax.dynamic_update_slice(buffer, full.astype(dtype), starts)
        return buffer

    def gather_weight(weight):
        half = weight.shape[0] // 2
        mine = lax.dynamic_slice_in_dim(weight, core * half, half, 0)
        from_near = to_near(mine)
        from_across = to_across(mine)
        from_far = to_across(from_near)
        other_near = to_core(from_across)
        other_across = to_core(from_near)
        other_far = to_core(from_far)
        items = [
            ((part ^ near, core), from_near),
            ((part ^ across, core), from_across),
            ((part ^ 3, core), from_far),
            ((part ^ near, 1 - core), other_near),
            ((part ^ across, 1 - core), other_across),
            ((part ^ 3, 1 - core), other_far),
            ((part, 0), weight.reshape(2, half, -1)),
        ]
        full = place_all((fsdp, 2, half, weight.shape[1]), weight.dtype, items)
        return full.reshape(fsdp * weight.shape[0], weight.shape[1])

    count_row = counts[0]
    offsets = jnp.cumsum(count_row) - count_row
    seq_ends = jnp.cumsum(seq_lengths[0])
    within = jnp.arange(rows, dtype=jnp.int32)
    slot = jnp.arange(ctx, dtype=jnp.int32)[:, None] * rows + within[None, :]
    live = within[None, :] < count_row[:, None]
    places = offsets[:, None] + within[None, :]
    starts = jnp.max(
        jnp.where(places[:, :, None] >= seq_ends[None, None, :], seq_ends[None, None, :], 0), axis=2
    )
    dead_id = -1 - slot
    key_ids = jnp.where(live, places, dead_id)
    lows = jnp.where(live, starts, dead_id)
    highs = key_ids
    fars = jnp.where(live, starts, NEVER)
    key_tile = jnp.broadcast_to(key_ids[:, :, None], (ctx, rows, 128))

    def own_parity(array):
        return pick(array.reshape((chips, 2) + array.shape[1:]), core, 1)

    low_rows = own_parity(lows)[:, None, :]
    high_rows = own_parity(highs)[:, None, :]
    far_rows = own_parity(fars)[:, None, :]
    live_rows = (within < pick(count_row, place)).astype(FP32)[:, None]

    smalls = jnp.concatenate(
        [b_query, b_value, b_out, b_proj, gain1, shift1, gain2, shift2, b_fc]
    ).reshape(-1, 128)
    small_all = place_all(
        (fsdp,) + smalls.shape,
        BF16,
        [((part,), smalls)] + [((part ^ s,), to_part(smalls, s)) for s in (1, 2, 3)],
    )
    small_all = small_all.reshape(fsdp, -1).astype(FP32)
    vectors = [small_all[:, n * shard : (n + 1) * shard].reshape(-1) for n in range(8)]
    bias_q, bias_v, bias_out, bias_proj, gain_one, shift_one, gain_two, shift_two = vectors
    bias_fc = small_all[:, 8 * shard :].reshape(-1)

    from_chips = [to_chip(tokens, s) for s in (1, 2, 3)]
    beside = [to_core(tokens)] + [to_core(v) for v in from_chips]
    tokens_all = place_all(
        (chips, 2, rows, features),
        BF16,
        [((chip, core), tokens), ((chip, 1 - core), beside[0])]
        + [((chip ^ s, core), from_chips[s - 1]) for s in (1, 2, 3)]
        + [((chip ^ s, 1 - core), beside[s]) for s in (1, 2, 3)],
    ).reshape(ctx, rows, features)

    qkv_full = gather_weight(w_qkv)
    out_full = gather_weight(w_out)
    fc_full = gather_weight(w_fc)
    proj_full = gather_weight(w_proj)
    qkv_parts = jnp.transpose(
        qkv_full.reshape(features, 3, chips, width), (2, 0, 1, 3)
    ).reshape(chips, features, 3 * width)

    wide_all = tokens_all.reshape(ctx * rows, features).astype(FP32)
    normed_all = layer_norm(wide_all, gain_one, shift_one)[0].astype(BF16)
    own_weight = pick(qkv_parts, chip)
    own_bias_q = lax.dynamic_slice_in_dim(bias_q, chip * width, width, 0)
    own_bias_v = lax.dynamic_slice_in_dim(bias_v, chip * width, width, 0)
    weight_q, weight_k, weight_v = (own_weight[:, n * width : (n + 1) * width] for n in range(3))
    normed_blocks = normed_all.reshape(ctx, rows, features)
    normed_mine = own_parity(normed_blocks)
    queries = dot_nn(normed_mine.reshape(chips * rows, features), weight_q) + own_bias_q
    queries = (queries.astype(BF16) * jnp.asarray(0.125, BF16)).reshape(chips, rows, width)
    keys = dot_nn(normed_all, weight_k).astype(BF16).reshape(ctx, rows, width)
    values = (dot_nn(normed_all, weight_v) + own_bias_v).astype(BF16).reshape(ctx, rows, width)
    keys_t = jnp.transpose(keys, (0, 2, 1))
    values_t = jnp.transpose(values, (0, 2, 1))
    parity = core.astype(jnp.int32).reshape(1)

    pair_count = group_heads * rows * rows * (chips * (chips + 1))
    attended_out, attended_t, logs = kernel_call(
        attend_kernel,
        [
            jax.ShapeDtypeStruct((chips, rows, width), BF16),
            jax.ShapeDtypeStruct((chips, width, rows), FP32),
            jax.ShapeDtypeStruct((chips, 8, rows), FP32),
        ],
        [pltpu.VMEM((width, rows), FP32)],
        (parity, queries, keys, values_t, key_tile, low_rows, high_rows, far_rows),
        pair_count * 256,
    )

    def scatter_chips(blocks):
        arrived = [(chip, pick(blocks, chip))]
        for s in (1, 2, 3):
            arrived.append((chip ^ s, to_chip(pick(blocks, chip ^ s), s)))
        return arrived

    attended_low = place_all(
        (chips, rows, width), BF16, [((n,), v) for n, v in scatter_chips(attended_out)]
    )
    attended_low = jnp.transpose(attended_low, (1, 0, 2)).reshape(rows, features)

    inputs = tokens.astype(FP32)
    middle = inputs + dot_nn(attended_low, out_full) + bias_out
    normed_two, unit_two, inverse_two = layer_norm(middle, gain_two, shift_two)
    normed_two_low = normed_two.astype(BF16)
    hidden = dot_nn(normed_two_low, fc_full) + bias_fc
    activated = gelu_tanh(hidden).astype(BF16)
    output_low = (middle + dot_nn(activated, proj_full) + bias_proj).astype(BF16)

    grad_out = cotangent.astype(FP32) * live_rows
    grad_out_low = grad_out.astype(BF16)
    grad_act = times_transpose(grad_out_low, proj_full)
    grad_hidden = jax.vjp(gelu_tanh, hidden)[1](grad_act)[0]
    grad_hidden_low = grad_hidden.astype(BF16)
    grad_normed_two = times_transpose(grad_hidden_low, fc_full)
    grad_mid_norm, grad_gain_two, grad_shift_two = norm_back(
        grad_normed_two, unit_two, inverse_two, gain_two
    )
    grad_middle = grad_out + grad_mid_norm
    grad_middle_low = grad_middle.astype(BF16)
    grad_attended = times_transpose(grad_middle_low, out_full).astype(BF16)
    grad_heads = jnp.transpose(grad_attended.reshape(rows, chips, width), (1, 0, 2))
    grad_blocks = place_all(
        (chips, rows, width), BF16, [((n,), v) for n, v in scatter_chips(grad_heads)]
    )

    grad_query, grad_keep, grad_send = kernel_call(
        attend_back_kernel,
        [
            jax.ShapeDtypeStruct((chips, rows, width), BF16),
            jax.ShapeDtypeStruct((chips, rows, 2 * width), FP32),
            jax.ShapeDtypeStruct((chips, rows, 2 * width), BF16),
        ],
        [
            pltpu.VMEM((width, rows), FP32),
            pltpu.VMEM((group_heads, ctx, rows, 64), FP32),
            pltpu.VMEM((group_heads, ctx, rows, 64), FP32),
        ],
        (
            parity,
            queries,
            keys,
            keys_t,
            values,
            grad_blocks,
            key_tile,
            low_rows,
            high_rows,
            far_rows,
            attended_t,
            logs,
        ),
        pair_count * 640,
    )
    grad_kv = (grad_keep + to_core(grad_send).astype(FP32)).astype(BF16)
    grad_packed = jnp.concatenate([grad_query, grad_kv], axis=2)

    grad_normed_one = jnp.zeros((rows, features), FP32)
    for source, piece in scatter_chips(grad_packed):
        grad_normed_one = grad_normed_one + times_transpose(piece, pick(qkv_parts, source))
    normed_one, unit_one, inverse_one = layer_norm(inputs, gain_one, shift_one)
    grad_in_norm = norm_back(grad_normed_one, unit_one, inverse_one, gain_one)[0]
    grad_tokens = grad_middle + grad_in_norm

    def add_up(left_side, right_side):
        return left_side.astype(FP32) + right_side.astype(FP32)

    def scatter_parts(blocks):
        theirs = to_near(pick(blocks, part ^ near).astype(BF16))
        theirs_far = to_near(pick(blocks, part ^ 3).astype(BF16))
        relay = add_up(pick(blocks, part ^ across), theirs_far).astype(BF16)
        last = to_across(relay)
        return pick(blocks, part).astype(FP32) + theirs.astype(FP32) + last.astype(FP32)

    def sum_chips(block):
        quarter = block.shape[0] // chips
        quarters = block.astype(BF16).reshape((chips, quarter) + block.shape[1:])
        total = pick(block.reshape((chips, quarter) + block.shape[1:]), chip).astype(FP32)
        for s in (1, 2, 3):
            total = total + to_chip(pick(quarters, chip ^ s), s).astype(FP32)
        total = total.astype(BF16)
        full = place_all(
            quarters.shape,
            BF16,
            [((chip,), total)] + [((chip ^ s,), to_chip(total, s)) for s in (1, 2, 3)],
        )
        return full.reshape(block.shape)

    other_grad_out = to_core(grad_out_low)
    other_normed_two = to_core(normed_two_low)
    other_attended = to_core(attended_low)
    split_act = activated.reshape(rows, fsdp, 2, hidden_width // (2 * fsdp))
    split_hidden = grad_hidden_low.reshape(rows, 2, hidden_width // 2)
    split_middle = grad_middle_low.reshape(rows, 2, features // 2)
    other_act = to_core(pick(split_act, 1 - core, 2).reshape(rows, -1))
    other_hidden = to_core(pick(split_hidden, 1 - core, 1))
    other_middle = to_core(pick(split_middle, 1 - core, 1))

    def both(mine, other, mine_grad, other_grad):
        return contract_rows(mine, mine_grad) + contract_rows(other, other_grad)

    grad_proj = both(
        pick(split_act, core, 2).reshape(rows, -1), other_act, grad_out_low, other_grad_out
    ).reshape(fsdp, -1, features)
    grad_fc = both(
        normed_two_low, other_normed_two, pick(split_hidden, core, 1), other_hidden
    ).reshape(fsdp, shard, -1)
    grad_out_proj = both(
        attended_low, other_attended, pick(split_middle, core, 1), other_middle
    ).reshape(fsdp, shard, -1)
    sums = [
        jnp.sum(grad_middle_low.astype(FP32), axis=0),
        jnp.sum(grad_out, axis=0),
        grad_gain_two,
        grad_shift_two,
        jnp.sum(grad_hidden_low.astype(FP32), axis=0),
    ]
    sum_rows = jnp.concatenate([v.reshape(fsdp, -1) for v in sums], axis=1)
    sum_rows = sum_rows.reshape(fsdp, -1, features // 2)
    pad_rows = shard // 3 - sum_rows.shape[1]
    grad_out_proj = jnp.concatenate(
        [grad_out_proj, jnp.pad(sum_rows, ((0, 0), (0, pad_rows), (0, 0)))], axis=1
    )
    proj_half = sum_chips(scatter_parts(grad_proj))
    fc_half = sum_chips(scatter_parts(grad_fc))
    out_half = sum_chips(scatter_parts(grad_out_proj))
    proj_other, fc_other, out_other = to_core(proj_half), to_core(fc_half), to_core(out_half)

    def by_core(mine, other, axis):
        first = jnp.where(core == 0, mine, other)
        second = jnp.where(core == 0, other, mine)
        return jnp.concatenate([first, second], axis=axis).astype(FP32)

    d_proj = by_core(proj_half, proj_other, 0)
    d_fc = by_core(fc_half, fc_other, 1)
    d_out = by_core(out_half[:shard], out_other[:shard], 1)
    small_sums = add_up(out_half[shard:], out_other[shard:]).reshape(-1)
    d_bias_out, d_bias_proj, d_gain_two, d_shift_two = (
        small_sums[n * shard : (n + 1) * shard] for n in range(4)
    )
    d_bias_fc = small_sums[4 * shard : 4 * shard + hidden_width // fsdp]

    grad_qkv = contract_rows(
        normed_mine.reshape(chips * rows, features), grad_packed.reshape(chips * rows, -1)
    )
    column_sums = jnp.sum(grad_packed.astype(FP32), axis=(0, 1))
    own_wide = own_weight.astype(FP32)
    grad_shift_one = jnp.sum(own_wide * column_sums[None, :], axis=1)
    grad_gain_one = (jnp.sum(own_wide * grad_qkv, axis=1) - shift_one * grad_shift_one) / gain_one
    half = shard // 2
    split_qkv = grad_qkv.reshape(fsdp, 2, half, -1)
    other_qkv = to_core(pick(split_qkv, 1 - core, 1).astype(BF16))
    qkv_blocks = add_up(pick(split_qkv, core, 1), other_qkv)
    norm_rows = jnp.concatenate(
        [
            grad_gain_one.reshape(fsdp, shard),
            grad_shift_one.reshape(fsdp, shard),
            jnp.zeros((fsdp, 3 * width - 2 * shard), FP32),
        ],
        axis=1,
    )
    extra = jnp.stack([jnp.broadcast_to(column_sums, (fsdp, 3 * width)), norm_rows], axis=1)
    qkv_blocks = jnp.concatenate([qkv_blocks, jnp.pad(extra, ((0, 0), (0, 14), (0, 0)))], axis=1)
    qkv_half = scatter_parts(qkv_blocks).astype(BF16)
    qkv_pieces = [((chip, core), qkv_half)]
    qkv_pieces += [((chip ^ s, core), to_chip(qkv_half, s)) for s in (1, 2, 3)]
    qkv_pieces += [((index[0], 1 - core), to_core(v)) for index, v in qkv_pieces]
    qkv_total = place_all((chips, 2) + qkv_half.shape, BF16, qkv_pieces)
    d_qkv = jnp.transpose(
        qkv_total[:, :, :half].reshape(chips, 2, half, 3, width), (1, 2, 3, 0, 4)
    )
    d_qkv = d_qkv.reshape(shard, 3 * features).astype(FP32)
    extra_total = jnp.sum(qkv_total[:, :, half : half + 2].astype(FP32), axis=1)
    bias_total = extra_total[:, 0].reshape(chips, 3, width)
    bias_total = jnp.transpose(bias_total, (1, 0, 2)).reshape(3, features)
    d_bias_q = lax.dynamic_slice_in_dim(bias_total[0], part * shard, shard, 0)
    d_bias_v = lax.dynamic_slice_in_dim(bias_total[2], part * shard, shard, 0)
    norm_total = jnp.sum(extra_total[:, 1], axis=0)
    d_gain_one = norm_total[:shard]
    d_shift_one = norm_total[shard : 2 * shard]

    return (
        output_low,
        grad_tokens,
        d_qkv,
        d_bias_q,
        d_bias_v,
        d_out,
        d_bias_out,
        d_fc,
        d_bias_fc,
        d_proj,
        d_bias_proj,
        d_gain_one,
        d_shift_one,
        d_gain_two,
        d_shift_two,
    )


def solution(mesh):
    in_specs = (
        P(("fsdp", "ctx"), None),
        P(("fsdp", "ctx"), None),
        P("fsdp", None),
        P("fsdp"),
        P("fsdp"),
        P("fsdp", None),
        P("fsdp"),
        P("fsdp", None),
        P("fsdp"),
        P("fsdp", None),
        P("fsdp"),
        P("fsdp"),
        P("fsdp"),
        P("fsdp"),
        P("fsdp"),
        P("fsdp", None),
        P("fsdp", None),
    )
    out_specs = (
        P(("fsdp", "ctx"), None),
        P(("fsdp", "ctx"), None),
        P("fsdp", None),
        P("fsdp"),
        P("fsdp"),
        P("fsdp", None),
        P("fsdp"),
        P("fsdp", None),
        P("fsdp"),
        P("fsdp", None),
        P("fsdp"),
        P("fsdp"),
        P("fsdp"),
        P("fsdp"),
        P("fsdp"),
    )
    ctx = mesh.shape["ctx"]
    four_by_four = mesh.shape["fsdp"] == 4 and ctx == 8 and HEADS % (ctx // 2) == 0
    body = fast_body if four_by_four else general_body
    return jax.shard_map(body, mesh=mesh, in_specs=in_specs, out_specs=out_specs, check_vma=False)
```

```python
import functools

import jax
import jax.numpy as jnp
from jax import lax
from jax.experimental import pallas as pl
from jax.experimental.pallas import tpu as pltpu
from jax.sharding import PartitionSpec as P

HEADS = 12


EPS = 1e-05


def layer_norm(values, gain_row, shift_row):
    centre = values - jnp.mean(values, axis=1, keepdims=True)
    inverse = lax.rsqrt(jnp.mean(centre * centre, axis=1, keepdims=True) + EPS)
    normed = centre * inverse
    return (normed * gain_row + shift_row, normed, inverse)


def norm_back(grad_in, normed, inverse, gain_row):
    scaled = grad_in * gain_row
    inner_grad = inverse * (
        scaled
        - jnp.mean(scaled, axis=1, keepdims=True)
        - normed * jnp.mean(scaled * normed, axis=1, keepdims=True)
    )
    return (inner_grad, jnp.sum(grad_in * normed, axis=0), jnp.sum(grad_in, axis=0))


def contract_rows(left_side, right_side):
    return lax.dot_general(
        left_side, right_side, (((0,), (0,)), ((), ())), preferred_element_type=jnp.float32
    )


def times_transpose(left_side, right_side):
    return lax.dot_general(
        left_side, right_side, (((1,), (1,)), ((), ())), preferred_element_type=jnp.float32
    )


def gelu_tanh(values):
    return jax.nn.gelu(values, approximate=True)


def describe(slot_ids, row_count, count_row, offsets, seq_ends):
    peer_count = count_row.shape[0]
    device = slot_ids // row_count
    within = slot_ids - device * row_count
    matches = device[:, None] == jnp.arange(peer_count, dtype=jnp.int32)[None, :]
    live_count = jnp.sum(jnp.where(matches, count_row[None, :], 0), axis=1)
    first_place = jnp.sum(jnp.where(matches, offsets[None, :], 0), axis=1)
    places = first_place + within
    segment = jnp.sum((places[:, None] >= seq_ends[None, :]).astype(jnp.int32), axis=1)
    return (within < live_count, places, segment, slot_ids)


def allowed(query_info, key_info):
    q_live, q_place, q_seg, q_slot = query_info
    k_live, k_place, k_seg, k_slot = key_info
    same_seq = (
        q_live[:, None]
        & k_live[None, :]
        & (q_seg[:, None] == k_seg[None, :])
        & (k_place[None, :] <= q_place[:, None])
    )
    return same_seq | (q_slot[:, None] == k_slot[None, :])


def over_blocks(step_fn, status, pieces, row_count):
    total_rows = pieces[0].shape[0]
    block_total = total_rows // row_count
    stacked = tuple((piece.reshape((block_total, row_count) + piece.shape[1:]) for piece in pieces))

    def scan_body(state_now, scan_item):
        block_index, block_parts = scan_item
        return (step_fn(state_now, block_parts, block_index * row_count), None)

    status, unused = lax.scan(
        scan_body, status, (jnp.arange(block_total, dtype=jnp.int32), stacked)
    )
    return status


def score_grads(
    query_heads, key_heads, value_heads, grad_heads, lse_rows, delta_rows, permitted, scaling
):
    scores = (
        jnp.einsum("qhd,khd->hqk", query_heads, key_heads, preferred_element_type=jnp.float32)
        * scaling
    )
    probabilities = jnp.where(permitted[None], jnp.exp(scores - lse_rows[:, :, None]), 0.0)
    grad_probs = jnp.einsum(
        "qhd,khd->hqk", grad_heads, value_heads, preferred_element_type=jnp.float32
    )
    grad_scores = (probabilities * (grad_probs - delta_rows[:, :, None])).astype(jnp.bfloat16)
    return (probabilities.astype(jnp.bfloat16), grad_scores)


def general_body(
    tokens,
    cotangent,
    w_qkv,
    b_query,
    b_value,
    w_out,
    b_out,
    w_fc,
    b_fc,
    w_proj,
    b_proj,
    gain1,
    shift1,
    gain2,
    shift2,
    counts,
    seq_lengths,
):
    row_count, feature_count = tokens.shape
    peer_count = lax.axis_size("ctx")
    my_index = lax.axis_index("ctx")
    head_count = HEADS
    head_width = feature_count // head_count
    scaling = head_width ** (-0.5)
    count_row = counts[0]
    offsets = jnp.cumsum(count_row) - count_row
    seq_ends = jnp.cumsum(seq_lengths[0])

    def locate(first_slot, length):
        return describe(
            first_slot + jnp.arange(length, dtype=jnp.int32),
            row_count,
            count_row,
            offsets,
            seq_ends,
        )

    own_rows = locate(my_index * row_count, row_count)
    fp32 = jnp.float32
    bf16 = jnp.bfloat16
    (
        qkv_full,
        query_bias,
        value_bias,
        out_full,
        out_bias,
        fc_full,
        fc_bias,
        proj_full,
        proj_bias,
        gain_one,
        shift_one,
        gain_two,
        shift_two,
    ) = (
        lax.all_gather(w_qkv, "fsdp", axis=0, tiled=True),
        lax.all_gather(b_query, "fsdp", axis=0, tiled=True),
        lax.all_gather(b_value, "fsdp", axis=0, tiled=True),
        lax.all_gather(w_out, "fsdp", axis=0, tiled=True),
        lax.all_gather(b_out, "fsdp", axis=0, tiled=True),
        lax.all_gather(w_fc, "fsdp", axis=0, tiled=True),
        lax.all_gather(b_fc, "fsdp", axis=0, tiled=True),
        lax.all_gather(w_proj, "fsdp", axis=0, tiled=True),
        lax.all_gather(b_proj, "fsdp", axis=0, tiled=True),
        lax.all_gather(gain1, "fsdp", axis=0, tiled=True),
        lax.all_gather(shift1, "fsdp", axis=0, tiled=True),
        lax.all_gather(gain2, "fsdp", axis=0, tiled=True),
        lax.all_gather(shift2, "fsdp", axis=0, tiled=True),
    )
    inputs = tokens.astype(fp32)
    normed_one, unit_one, inverse_one = layer_norm(
        inputs, gain_one.astype(fp32), shift_one.astype(fp32)
    )
    normed_low = normed_one.astype(bf16)
    bias_row = jnp.concatenate([query_bias, jnp.zeros_like(query_bias), value_bias]).astype(fp32)
    packed = (jnp.dot(normed_low, qkv_full, preferred_element_type=fp32) + bias_row).astype(bf16)
    query_rows = packed[:, :feature_count]
    key_rows = packed[:, feature_count : 2 * feature_count]
    value_rows = packed[:, 2 * feature_count :]
    query_heads = query_rows.reshape(row_count, head_count, head_width)

    def forward_step(status, pieces, first_row):
        running_max, running_sum, running_acc = status
        key_piece, value_piece = pieces
        length = key_piece.shape[0]
        key_heads = key_piece.reshape(length, head_count, head_width)
        value_heads = value_piece.reshape(length, head_count, head_width)
        scores = (
            jnp.einsum("qhd,khd->hqk", query_heads, key_heads, preferred_element_type=fp32)
            * scaling
        )
        permitted = allowed(own_rows, locate(first_row, length))
        scores = jnp.where(permitted[None], scores, -jnp.inf)
        new_max = jnp.maximum(running_max, jnp.max(scores, axis=2))
        fading = jnp.exp(running_max - new_max)
        weights = jnp.exp(scores - new_max[:, :, None])
        running_sum = running_sum * fading + jnp.sum(weights, axis=2)
        update = jnp.einsum(
            "hqk,khd->qhd", weights.astype(bf16), value_heads, preferred_element_type=fp32
        )
        running_acc = running_acc * jnp.transpose(fading)[:, :, None] + update
        return (new_max, running_sum, running_acc)

    start_state = (
        jnp.full((head_count, row_count), -1e30, fp32),
        jnp.zeros((head_count, row_count), fp32),
        jnp.zeros((row_count, head_count, head_width), fp32),
    )
    final_max, final_sum, final_acc = over_blocks(
        forward_step,
        start_state,
        (
            lax.all_gather(key_rows, "ctx", axis=0, tiled=True),
            lax.all_gather(value_rows, "ctx", axis=0, tiled=True),
        ),
        row_count,
    )
    attended_heads = final_acc / jnp.transpose(final_sum)[:, :, None]
    attended = attended_heads.reshape(row_count, feature_count)
    log_total = final_max + jnp.log(final_sum)
    attended_low = attended.astype(bf16)
    middle = (
        inputs
        + jnp.dot(attended_low, out_full, preferred_element_type=fp32)
        + out_bias.astype(fp32)
    )
    normed_two, unit_two, inverse_two = layer_norm(
        middle, gain_two.astype(fp32), shift_two.astype(fp32)
    )
    normed_two_low = normed_two.astype(bf16)
    hidden = jnp.dot(normed_two_low, fc_full, preferred_element_type=fp32) + fc_bias.astype(fp32)
    activated = gelu_tanh(hidden).astype(bf16)
    output = (
        middle + jnp.dot(activated, proj_full, preferred_element_type=fp32) + proj_bias.astype(fp32)
    )
    output_low = output.astype(bf16)
    qkv_full, out_full, fc_full, proj_full, gain_one, gain_two = (
        lax.all_gather(w_qkv, "fsdp", axis=0, tiled=True),
        lax.all_gather(w_out, "fsdp", axis=0, tiled=True),
        lax.all_gather(w_fc, "fsdp", axis=0, tiled=True),
        lax.all_gather(w_proj, "fsdp", axis=0, tiled=True),
        lax.all_gather(gain1, "fsdp", axis=0, tiled=True),
        lax.all_gather(gain2, "fsdp", axis=0, tiled=True),
    )
    live_rows = own_rows[0].astype(fp32)[:, None]
    grad_out = cotangent.astype(fp32) * live_rows
    grad_out_low = grad_out.astype(bf16)
    grad_proj = contract_rows(activated, grad_out_low)
    grad_proj_bias = jnp.sum(grad_out, axis=0)
    grad_act = times_transpose(grad_out_low, proj_full)
    grad_hidden = jax.vjp(gelu_tanh, hidden)[1](grad_act)[0]
    grad_hidden_low = grad_hidden.astype(bf16)
    grad_fc = contract_rows(normed_two_low, grad_hidden_low)
    grad_fc_bias = jnp.sum(grad_hidden_low.astype(fp32), axis=0)
    grad_normed_two = times_transpose(grad_hidden_low, fc_full)
    grad_mid_norm, grad_gain_two, grad_shift_two = norm_back(
        grad_normed_two, unit_two, inverse_two, gain_two.astype(fp32)
    )
    grad_middle = grad_out + grad_mid_norm
    grad_middle_low = grad_middle.astype(bf16)
    grad_out_proj = contract_rows(attended_low, grad_middle_low)
    grad_out_bias = jnp.sum(grad_middle_low.astype(fp32), axis=0)
    grad_attended = times_transpose(grad_middle_low, out_full).astype(bf16)
    grad_heads = grad_attended.reshape(row_count, head_count, head_width)
    delta_rows = jnp.transpose(jnp.sum(grad_heads.astype(fp32) * attended_heads, axis=2))

    def back_step(status, pieces, first_row):
        grad_query, grad_keys = status
        key_piece, value_piece = pieces
        length = key_piece.shape[0]
        key_heads = key_piece.reshape(length, head_count, head_width)
        value_heads = value_piece.reshape(length, head_count, head_width)
        permitted = allowed(own_rows, locate(first_row, length))
        probs_low, grad_scores = score_grads(
            query_heads,
            key_heads,
            value_heads,
            grad_heads,
            log_total,
            delta_rows,
            permitted,
            scaling,
        )
        grad_query = (
            grad_query
            + jnp.einsum("hqk,khd->qhd", grad_scores, key_heads, preferred_element_type=fp32)
            * scaling
        )
        grad_key_part = (
            jnp.einsum("hqk,qhd->khd", grad_scores, query_heads, preferred_element_type=fp32)
            * scaling
        )
        grad_value_part = jnp.einsum(
            "hqk,qhd->khd", probs_low, grad_heads, preferred_element_type=fp32
        )
        joined = jnp.concatenate(
            [
                grad_key_part.reshape(length, feature_count),
                grad_value_part.reshape(length, feature_count),
            ],
            axis=1,
        )
        current = lax.dynamic_slice_in_dim(grad_keys, first_row, length, 0)
        grad_keys = lax.dynamic_update_slice_in_dim(grad_keys, current + joined, first_row, 0)
        return (grad_query, grad_keys)

    keys_start = jnp.zeros((peer_count * row_count, 2 * feature_count), fp32)
    grad_query, grad_keys = over_blocks(
        back_step,
        (jnp.zeros((row_count, head_count, head_width), fp32), keys_start),
        (
            lax.all_gather(key_rows, "ctx", axis=0, tiled=True),
            lax.all_gather(value_rows, "ctx", axis=0, tiled=True),
        ),
        row_count,
    )
    grad_kv = lax.psum_scatter(
        grad_keys.astype(jnp.bfloat16), "ctx", scatter_dimension=0, tiled=True
    ).astype(jnp.float32)
    grad_packed = jnp.concatenate(
        [grad_query.reshape(row_count, feature_count), grad_kv], axis=1
    ).astype(bf16)
    grad_packed_wide = grad_packed.astype(fp32)
    grad_query_bias = jnp.sum(grad_packed_wide[:, :feature_count], axis=0)
    grad_value_bias = jnp.sum(grad_packed_wide[:, 2 * feature_count :], axis=0)
    grad_qkv = contract_rows(normed_low, grad_packed)
    grad_normed_one = times_transpose(grad_packed, qkv_full)
    grad_in_norm, grad_gain_one, grad_shift_one = norm_back(
        grad_normed_one, unit_one, inverse_one, gain_one.astype(fp32)
    )
    grad_tokens = grad_middle + grad_in_norm
    (
        sum_qkv,
        sum_qbias,
        sum_vbias,
        sum_out,
        sum_obias,
        sum_fc,
        sum_fbias,
        sum_proj,
        sum_pbias,
        sum_gain_one,
        sum_shift_one,
        sum_gain_two,
        sum_shift_two,
    ) = (
        lax.psum_scatter(
            grad_qkv.astype(jnp.bfloat16), "fsdp", scatter_dimension=0, tiled=True
        ).astype(jnp.float32),
        lax.psum_scatter(
            grad_query_bias.astype(jnp.bfloat16), "fsdp", scatter_dimension=0, tiled=True
        ).astype(jnp.float32),
        lax.psum_scatter(
            grad_value_bias.astype(jnp.bfloat16), "fsdp", scatter_dimension=0, tiled=True
        ).astype(jnp.float32),
        lax.psum_scatter(
            grad_out_proj.astype(jnp.bfloat16), "fsdp", scatter_dimension=0, tiled=True
        ).astype(jnp.float32),
        lax.psum_scatter(
            grad_out_bias.astype(jnp.bfloat16), "fsdp", scatter_dimension=0, tiled=True
        ).astype(jnp.float32),
        lax.psum_scatter(
            grad_fc.astype(jnp.bfloat16), "fsdp", scatter_dimension=0, tiled=True
        ).astype(jnp.float32),
        lax.psum_scatter(
            grad_fc_bias.astype(jnp.bfloat16), "fsdp", scatter_dimension=0, tiled=True
        ).astype(jnp.float32),
        lax.psum_scatter(
            grad_proj.astype(jnp.bfloat16), "fsdp", scatter_dimension=0, tiled=True
        ).astype(jnp.float32),
        lax.psum_scatter(
            grad_proj_bias.astype(jnp.bfloat16), "fsdp", scatter_dimension=0, tiled=True
        ).astype(jnp.float32),
        lax.psum_scatter(
            grad_gain_one.astype(jnp.bfloat16), "fsdp", scatter_dimension=0, tiled=True
        ).astype(jnp.float32),
        lax.psum_scatter(
            grad_shift_one.astype(jnp.bfloat16), "fsdp", scatter_dimension=0, tiled=True
        ).astype(jnp.float32),
        lax.psum_scatter(
            grad_gain_two.astype(jnp.bfloat16), "fsdp", scatter_dimension=0, tiled=True
        ).astype(jnp.float32),
        lax.psum_scatter(
            grad_shift_two.astype(jnp.bfloat16), "fsdp", scatter_dimension=0, tiled=True
        ).astype(jnp.float32),
    )
    totals = (
        lax.psum(sum_qkv.astype(jnp.bfloat16), "ctx").astype(jnp.float32),
        lax.psum(sum_qbias.astype(jnp.bfloat16), "ctx").astype(jnp.float32),
        lax.psum(sum_vbias.astype(jnp.bfloat16), "ctx").astype(jnp.float32),
        lax.psum(sum_out.astype(jnp.bfloat16), "ctx").astype(jnp.float32),
        lax.psum(sum_obias.astype(jnp.bfloat16), "ctx").astype(jnp.float32),
        lax.psum(sum_fc.astype(jnp.bfloat16), "ctx").astype(jnp.float32),
        lax.psum(sum_fbias.astype(jnp.bfloat16), "ctx").astype(jnp.float32),
        lax.psum(sum_proj.astype(jnp.bfloat16), "ctx").astype(jnp.float32),
        lax.psum(sum_pbias.astype(jnp.bfloat16), "ctx").astype(jnp.float32),
        lax.psum(sum_gain_one.astype(jnp.bfloat16), "ctx").astype(jnp.float32),
        lax.psum(sum_shift_one.astype(jnp.bfloat16), "ctx").astype(jnp.float32),
        lax.psum(sum_gain_two.astype(jnp.bfloat16), "ctx").astype(jnp.float32),
        lax.psum(sum_shift_two.astype(jnp.bfloat16), "ctx").astype(jnp.float32),
    )
    return (
        output_low,
        grad_tokens,
        totals[0],
        totals[1],
        totals[2],
        totals[3],
        totals[4],
        totals[5],
        totals[6],
        totals[7],
        totals[8],
        totals[9],
        totals[10],
        totals[11],
        totals[12],
    )


FP32 = jnp.float32
BF16 = jnp.bfloat16
FLOOR = -1e30
NEVER = 1 << 30


def dot_nt(left_side, right_side):
    return lax.dot_general(
        left_side, right_side, (((1,), (1,)), ((), ())), preferred_element_type=FP32
    )


def dot_nn(left_side, right_side):
    return lax.dot_general(
        left_side, right_side, (((1,), (0,)), ((), ())), preferred_element_type=FP32
    )


def spread(column_tile, width):
    return jnp.concatenate([column_tile] * (width // column_tile.shape[1]), axis=1)


def masked_scores(scores, key_ids, first_row, last_row):
    permitted = key_ids >= first_row
    if last_row is not None:
        permitted = permitted & (key_ids <= last_row)
    return jnp.where(permitted, scores, -jnp.inf)


def attend_kernel(
    parity,
    tokens_ref,
    wq_ref,
    wk_ref,
    wv_ref,
    bq_ref,
    bv_ref,
    gain_ref,
    shift_ref,
    key_ref,
    low_ref,
    high_ref,
    far_ref,
    q_ref,
    k_ref,
    kt_ref,
    v_ref,
    normed_ref,
    o_ref,
    ot_ref,
    lse_ref,
    vt_ref,
    acc_ref,
):
    blocks, rows, width = q_ref.shape
    heads = width // 64

    def project(index, unused):
        normed = layer_norm(tokens_ref[index].astype(FP32), gain_ref[...], shift_ref[...])[0]
        normed = normed.astype(BF16)
        keys = dot_nn(normed, wk_ref[...])
        values = dot_nn(normed, wv_ref[...]) + bv_ref[...]
        k_ref[index] = keys.astype(BF16)
        v_ref[index] = values.astype(BF16)
        kt_ref[index] = keys.T.astype(BF16)
        vt_ref[index] = values.T.astype(BF16)

        @pl.when(lax.rem(index, 2) == parity[0])
        def own_block():
            queries = (dot_nn(normed, wq_ref[...]) + bq_ref[...]).astype(BF16)
            q_ref[index // 2] = (queries.astype(FP32) * 0.125).astype(BF16)
            normed_ref[index // 2] = normed

        return unused

    lax.fori_loop(0, 2 * blocks, project, 0)

    def query_block(index, unused):
        queries = [q_ref[index, :, 64 * h : 64 * h + 64] for h in range(heads)]
        acc_ref[...] = jnp.zeros_like(acc_ref)

        def key_step(key_block, carry, first_row, last_row):
            ids = spread(key_ref[key_block], rows)
            result = []
            for h in range(heads):
                span = slice(64 * h, 64 * h + 64)
                top, total = carry[h]
                scores = dot_nt(k_ref[key_block, :, span], queries[h])
                scores = masked_scores(scores, ids, first_row, last_row)
                new_top = jnp.maximum(top, jnp.max(scores, axis=0, keepdims=True))
                fade = jnp.exp(top - new_top)
                weights = jnp.exp(scores - new_top)
                total = total * fade + jnp.sum(weights, axis=0, keepdims=True)
                acc_ref[span, :] = acc_ref[span, :] * fade + dot_nn(
                    vt_ref[key_block, span, :], weights.astype(BF16)
                )
                result.append((new_top, total))
            return tuple(result)

        start = tuple(
            (jnp.full((1, rows), FLOOR, FP32), jnp.zeros((1, rows), FP32)) for h in range(heads)
        )
        own = 2 * index + parity[0]
        far_row = far_ref[index]
        carry = lax.fori_loop(0, own, lambda j, c: key_step(j, c, far_row, None), start)
        carry = key_step(own, carry, low_ref[index], high_ref[index])
        for h in range(heads):
            span = slice(64 * h, 64 * h + 64)
            top, total = carry[h]
            attended = acc_ref[span, :] / total
            ot_ref[index, span, :] = attended
            o_ref[index, :, span] = attended.T.astype(BF16)
            lse_ref[index, h : h + 1, :] = top + jnp.log(total)
        return unused

    lax.fori_loop(0, blocks, query_block, 0)


def attend_back_kernel(
    parity,
    q_ref,
    k_ref,
    kt_ref,
    v_ref,
    da_ref,
    key_ref,
    low_ref,
    high_ref,
    far_ref,
    ot_ref,
    lse_ref,
    dq_ref,
    keep_ref,
    send_ref,
    acc_ref,
    dk_ref,
    dv_ref,
):
    blocks, rows, width = q_ref.shape
    heads = width // 64
    dk_ref[...] = jnp.zeros_like(dk_ref)
    dv_ref[...] = jnp.zeros_like(dv_ref)

    def query_block(index, unused):
        queries = [q_ref[index, :, 64 * h : 64 * h + 64] for h in range(heads)]
        grads = [da_ref[index, :, 64 * h : 64 * h + 64] for h in range(heads)]
        deltas = [
            jnp.sum(
                grads[h].astype(FP32).T * ot_ref[index, 64 * h : 64 * h + 64, :],
                axis=0,
                keepdims=True,
            )
            for h in range(heads)
        ]
        logs = [lse_ref[index, h : h + 1, :] for h in range(heads)]
        acc_ref[...] = jnp.zeros_like(acc_ref)

        def key_step(key_block, first_row, last_row):
            ids = spread(key_ref[key_block], rows)
            for h in range(heads):
                span = slice(64 * h, 64 * h + 64)
                scores = dot_nt(k_ref[key_block, :, span], queries[h])
                scores = masked_scores(scores, ids, first_row, last_row)
                weights = jnp.exp(scores - logs[h])
                slopes = dot_nt(v_ref[key_block, :, span], grads[h])
                dscores = (weights * (slopes - deltas[h])).astype(BF16)
                dv_ref[h, key_block] += dot_nn(weights.astype(BF16), grads[h])
                dk_ref[h, key_block] += dot_nn(dscores, queries[h])
                acc_ref[span, :] += dot_nn(kt_ref[key_block, span, :], dscores)

        own = 2 * index + parity[0]
        far_row = far_ref[index]

        def far_step(key_block, state):
            key_step(key_block, far_row, None)
            return state

        lax.fori_loop(0, own, far_step, 0)
        key_step(own, low_ref[index], high_ref[index])
        for h in range(heads):
            span = slice(64 * h, 64 * h + 64)
            dq_ref[index, :, span] = (acc_ref[span, :] * 0.125).T.astype(BF16)
        return unused

    lax.fori_loop(0, blocks, query_block, 0)

    def write_block(index, unused):
        mine = 2 * index + parity[0]
        theirs = 2 * index + 1 - parity[0]
        for h in range(heads):
            left = slice(64 * h, 64 * h + 64)
            right = slice(width + 64 * h, width + 64 * h + 64)
            keep_ref[index, :, left] = dk_ref[h, mine]
            keep_ref[index, :, right] = dv_ref[h, mine]
            send_ref[index, :, left] = dk_ref[h, theirs].astype(BF16)
            send_ref[index, :, right] = dv_ref[h, theirs].astype(BF16)
        return unused

    lax.fori_loop(0, blocks, write_block, 0)


def kernel_call(kernel, outputs, scratch, operands, flops, special={}):
    whole = pl.BlockSpec(memory_space=pltpu.VMEM)
    in_specs = [pl.BlockSpec(memory_space=pltpu.SMEM)]
    in_specs += [special.get(n, whole) for n in range(1, len(operands))]
    moved = sum(v.size * v.dtype.itemsize for v in list(operands) + list(outputs))
    return pl.pallas_call(
        kernel,
        out_shape=outputs,
        in_specs=in_specs,
        out_specs=[pl.BlockSpec(memory_space=pltpu.VMEM) for unused in outputs],
        scratch_shapes=scratch,
        compiler_params=pltpu.CompilerParams(vmem_limit_bytes=56 * 1024 * 1024),
        cost_estimate=pl.CostEstimate(flops=flops, bytes_accessed=moved, transcendentals=flops // 256),
    )(*operands)


def middle_kernel(
    where,
    a0_ref,
    a1_ref,
    a2_ref,
    a3_ref,
    tokens_ref,
    cotangent_ref,
    live_ref,
    bias_out_ref,
    gain_ref,
    shift_ref,
    bias_fc_ref,
    bias_proj_ref,
    out_shard,
    fc_shard,
    proj_shard,
    piece0,
    piece1,
    piece2,
    piece3,
    piece4,
    piece5,
    block_ref,
    dx_ref,
    da_ref,
    mine_ref,
    send_ref,
    sums_ref,
    wo_ref,
    wf_ref,
    wp_ref,
    g_ref,
    dz_ref,
    sems,
):
    rows, features = tokens_ref.shape
    shard, hidden_width = fc_shard.shape
    parts = features // shard
    columns = hidden_width // parts
    half, half_columns = shard // 2, columns // 2
    part, core, chip = where[0], where[1], where[2]
    near, across = 1 + core, 2 - core

    starts = {"proj": [], "out": [], "fc": []}

    def fetch(kind, source, target):
        number = sum(len(v) for v in starts.values())
        starts[kind].append(pltpu.make_async_copy(source, target, sems.at[number]))

    def rows_at(owner, which, size):
        return pl.ds(pl.multiple_of(owner * 2 * size + which * size, 16), size)

    pieces = [
        (piece0, part ^ near, core),
        (piece1, part ^ across, core),
        (piece2, part ^ 3, core),
        (piece3, part ^ across, 1 - core),
        (piece4, part ^ near, 1 - core),
        (piece5, part ^ 3, 1 - core),
    ]
    own = pl.ds(pl.multiple_of(part * shard, 16), shard)
    fetch("out", out_shard, wo_ref.at[own, :])
    for piece, owner, which in pieces:
        fetch("out", piece.at[half_columns : half_columns + half, :], wo_ref.at[rows_at(owner, which, half), :])
    for j in range(parts):
        fetch("fc", fc_shard.at[:, columns * j : columns * (j + 1)], wf_ref.at[j, own, :])
    for piece, owner, which in pieces:
        for j in range(parts):
            first = half_columns + half * (j + 1)
            fetch("fc", piece.at[first : first + half, :], wf_ref.at[j, rows_at(owner, which, half), :])
    fetch("proj", proj_shard, wp_ref.at[pl.ds(pl.multiple_of(part * columns, 16), columns), :])
    for piece, owner, which in pieces:
        fetch("proj", piece.at[0:half_columns, :], wp_ref.at[rows_at(owner, which, half_columns), :])
    for kind in ("out", "fc", "proj"):
        for copy in starts[kind]:
            copy.start()
    for copy in starts["out"]:
        copy.wait()

    attended = [a0_ref, a1_ref, a2_ref, a3_ref]
    middle = tokens_ref[...].astype(FP32) + bias_out_ref[...]
    a_start = 2 * parts * half_columns + features
    for s in range(parts):
        span = pl.ds(pl.multiple_of((chip ^ s) * shard, 16), shard)
        middle = middle + dot_nn(attended[s][...], wo_ref[span, :])
        mine_ref[:, a_start + shard * s : a_start + shard * (s + 1)] = attended[s][...]
        send_ref[:, a_start + shard * s : a_start + shard * (s + 1)] = attended[s][...]
    normed, unit, inverse = layer_norm(middle, gain_ref[...], shift_ref[...])
    normed_low = normed.astype(BF16)
    h_start = 2 * parts * half_columns
    mine_ref[:, h_start : h_start + features] = normed_low
    send_ref[:, h_start : h_start + features] = normed_low
    grad_out = cotangent_ref[...].astype(FP32) * live_ref[...]
    grad_out_low = grad_out.astype(BF16)
    y_start = a_start + features
    mine_ref[:, y_start : y_start + features] = grad_out_low
    send_ref[:, y_start : y_start + features] = grad_out_low
    for copy in starts["fc"] + starts["proj"]:
        copy.wait()

    sums_ref[...] = jnp.zeros_like(sums_ref)
    output = middle + bias_proj_ref[...]
    grad_normed = jnp.zeros((rows, features), FP32)
    scale, cubic = 0.7978845608028654, 0.044715
    for j in range(parts):
        span = slice(columns * j, columns * (j + 1))
        hidden = dot_nn(normed_low, wf_ref[j]) + bias_fc_ref[:, span]
        square = hidden * hidden
        bent = jnp.tanh(scale * hidden * (1.0 + cubic * square))
        active = 0.5 * hidden * (1.0 + bent)
        slope = 0.5 * (1.0 + bent) + 0.5 * hidden * (1.0 - bent * bent) * (
            scale * (1.0 + 3.0 * cubic * square)
        )
        g_ref[...] = active.astype(BF16)
        grad_hidden = (dot_nt(grad_out_low, wp_ref[span, :]) * slope).astype(BF16)
        output = output + dot_nn(g_ref[...], wp_ref[span, :])
        grad_normed = grad_normed + dot_nt(grad_hidden, wf_ref[j])
        sums_ref[0:1, span] = jnp.sum(grad_hidden.astype(FP32), axis=0, keepdims=True)
        g_span = slice(half_columns * j, half_columns * (j + 1))
        mine_ref[:, g_span] = g_ref[:, pl.ds(pl.multiple_of(core * half_columns, 128), half_columns)]
        send_ref[:, g_span] = g_ref[
            :, pl.ds(pl.multiple_of((1 - core) * half_columns, 128), half_columns)
        ]
        first = parts * half_columns + columns * (j % 2)

        @pl.when(core == j // 2)
        def keep_hidden():
            mine_ref[:, first : first + columns] = grad_hidden

        @pl.when(core != j // 2)
        def give_hidden():
            send_ref[:, first : first + columns] = grad_hidden

    block_ref[...] = output.astype(BF16)
    inner, gain_sum, shift_sum = norm_back(grad_normed, unit, inverse, gain_ref[...])
    grad_middle = grad_out + inner
    dx_ref[...] = grad_middle
    dz_ref[...] = grad_middle.astype(BF16)
    z_start = y_start + features
    part_width = features // 2
    mine_ref[:, z_start : z_start + part_width] = dz_ref[
        :, pl.ds(pl.multiple_of(core * part_width, 128), part_width)
    ]
    send_ref[:, z_start : z_start + part_width] = dz_ref[
        :, pl.ds(pl.multiple_of((1 - core) * part_width, 128), part_width)
    ]
    for z in range(parts):
        da_ref[z] = dot_nt(dz_ref[...], wo_ref[shard * z : shard * (z + 1), :]).astype(BF16)
    sums_ref[1:2, 0:features] = jnp.sum(dz_ref[...].astype(FP32), axis=0, keepdims=True)
    sums_ref[2:3, 0:features] = jnp.sum(grad_out, axis=0, keepdims=True)
    sums_ref[3:4, 0:features] = gain_sum[None, :]
    sums_ref[4:5, 0:features] = shift_sum[None, :]


def weight_grad_kernel(where, mine_ref, other_ref, small_ref, keep_ref, send_ref, fc_ref):
    rows = mine_ref.shape[0]
    features = keep_ref.shape[2]
    part, core, chip = where[0], where[1], where[2]
    near, across = 1 + core, 2 - core
    parts = 4
    shard, half_columns = features // parts, features // 2
    h_start = 2 * parts * half_columns
    a_start = h_start + features
    y_start = a_start + features
    z_start = y_start + features

    def product(left, right):
        return contract_rows(mine_ref[:, left], mine_ref[:, right]) + contract_rows(
            other_ref[:, left], other_ref[:, right]
        )

    targets = [(keep_ref, 0, part), (keep_ref, 1, part ^ across)]
    targets += [(send_ref, 0, part ^ near), (send_ref, 1, part ^ 3)]
    fc_base = parts * half_columns
    for j in range(2):
        fc_ref[j] = product(
            pl.ds(h_start, features), pl.ds(fc_base + features * j, features)
        ).astype(BF16)
    out_base = half_columns + 2 * shard
    small_base = out_base + shard // 2
    for ref, slot, owner in targets:
        g_span = pl.ds(pl.multiple_of(owner * half_columns, 128), half_columns)
        ref[slot, 0:half_columns, :] = product(g_span, pl.ds(y_start, features)).astype(BF16)
        for j in range(2):
            first = half_columns + shard * j
            ref[slot, first : first + shard, :] = fc_ref[
                j, pl.ds(pl.multiple_of(owner * shard, 16), shard), :
            ]
        ref[slot, small_base : small_base + 16, :] = small_ref[owner].astype(BF16)
        ref[slot, small_base + 16 :, :] = jnp.zeros_like(ref[slot, small_base + 16 :, :])
    for s in range(parts):
        block = product(
            pl.ds(a_start + shard * s, shard), pl.ds(z_start, half_columns)
        ).astype(BF16)
        owner = chip ^ s
        for ref, slot, wanted in targets:

            @pl.when(owner == wanted)
            def store_block():
                ref[slot, out_base:small_base, 0:half_columns] = block[: shard // 2]
                ref[slot, out_base:small_base, half_columns:] = block[shard // 2 :]


def qkv_grad_kernel(
    where, normed_ref, dq_ref, dkv_ref, w_ref, gain_ref, shift_ref, keep_ref, send_ref, total_ref
):
    blocks, rows, features = normed_ref.shape
    width = dq_ref.shape[2]
    part, core = where[0], where[1]
    near, across = 1 + core, 2 - core
    parts = 4
    shard = features // parts
    half = shard // 2
    column_sums = [jnp.zeros((1, width), FP32) for n in range(3)]
    for n in range(3):
        total = jnp.zeros((features, width), FP32)
        for b in range(blocks):
            grads = dq_ref[b] if n == 0 else dkv_ref[b, :, width * (n - 1) : width * n]
            total = total + contract_rows(normed_ref[b], grads)
            column_sums[n] = column_sums[n] + jnp.sum(grads.astype(FP32), axis=0, keepdims=True)
        total_ref[:, width * n : width * (n + 1)] = total
    sums = jnp.concatenate(column_sums, axis=1)
    wide = w_ref[...].astype(FP32)
    shift_grad = jnp.sum(wide * sums, axis=1, keepdims=True)
    gain_grad = (
        jnp.sum(wide * total_ref[...], axis=1, keepdims=True) - shift_ref[...] * shift_grad
    ) / gain_ref[...]
    columns = jnp.concatenate(
        [gain_grad, shift_grad, jnp.zeros((features, 126), FP32)], axis=1
    )
    norm_rows = columns.T[0:8]
    order = [part, part ^ across, part ^ near, part ^ 3]
    other_order = [part, part ^ near, part ^ across, part ^ 3]
    for ref, which, owners in ((keep_ref, core, order), (send_ref, 1 - core, other_order)):
        for slot in range(parts):
            owner = owners[slot]
            first = pl.multiple_of(owner * shard + which * half, 16)
            ref[slot, 0:half, :] = total_ref[pl.ds(first, half), :].astype(ref.dtype)
            picked = jnp.zeros((8, shard), FP32)
            for f in range(parts):
                picked = jnp.where(owner == f, norm_rows[:, shard * f : shard * (f + 1)], picked)
            row = lax.broadcasted_iota(jnp.int32, (8, 3 * width), 0)
            packed = jnp.concatenate([picked, jnp.zeros((8, 3 * width - shard), FP32)], axis=1)
            tail = jnp.where(row < 2, packed, jnp.where(row == 2, sums, 0.0))
            tail = jnp.concatenate([tail, jnp.zeros_like(tail)], axis=0)
            ref[slot, half : half + 16, :] = tail.astype(ref.dtype)


def input_grad_kernel(where, p0, p1, p2, p3, w_ref, tokens_ref, dx_ref, gain_ref, shift_ref, out_ref):
    chip = where[2]
    total = jnp.zeros(out_ref.shape, FP32)
    for s, piece in enumerate((p0, p1, p2, p3)):
        total = total + dot_nt(piece[...], w_ref[chip ^ s])
    unit, inverse = layer_norm(tokens_ref[...].astype(FP32), gain_ref[...], shift_ref[...])[1:]
    out_ref[...] = dx_ref[...] + norm_back(total, unit, inverse, gain_ref[...])[0]


def fast_body(
    tokens,
    cotangent,
    w_qkv,
    b_query,
    b_value,
    w_out,
    b_out,
    w_fc,
    b_fc,
    w_proj,
    b_proj,
    gain1,
    shift1,
    gain2,
    shift2,
    counts,
    seq_lengths,
):
    rows, features = tokens.shape
    ctx = lax.axis_size("ctx")
    fsdp = lax.axis_size("fsdp")
    chips = ctx // 2
    group_heads = HEADS // chips
    width = features // chips
    shard = features // fsdp
    hidden_width = w_fc.shape[1]
    columns = hidden_width // fsdp
    place = lax.axis_index("ctx")
    chip = place // 2
    core = place % 2
    part = lax.axis_index("fsdp")
    near = 1 + core
    across = 2 - core
    where = jnp.stack([part, core, chip]).astype(jnp.int32)
    same_core = [[2 * z + k for z in range(chips)] for k in range(2)]

    def exchange(value, partner):
        pairs = [
            (f * ctx + c, g * ctx + d)
            for f in range(fsdp)
            for c in range(ctx)
            for g, d in [partner(f, c)]
        ]
        return lax.ppermute(value, ("fsdp", "ctx"), pairs)

    def to_near(value):
        return exchange(value, lambda f, c: (f ^ (1 + c % 2), c))

    def to_across(value):
        return exchange(value, lambda f, c: (f ^ (2 - c % 2), c))

    def to_part(value, step):
        return exchange(value, lambda f, c: (f ^ step, c))

    def to_core(value):
        return exchange(value, lambda f, c: (f, c ^ 1))

    def to_chip(value, step):
        return exchange(value, lambda f, c: (f, c ^ (2 * step)))

    def pick(array, index, axis=0):
        return lax.dynamic_index_in_dim(array, index, axis, keepdims=False)

    def place_all(shape, dtype, items):
        buffer = jnp.zeros(shape, dtype)
        for index, value in items:
            full = value.reshape((1,) * (len(shape) - value.ndim) + value.shape)
            starts = tuple(index) + (0,) * (len(shape) - len(index))
            buffer = lax.dynamic_update_slice(buffer, full.astype(dtype), starts)
        return buffer

    def gather_pieces(mine):
        from_near = to_near(mine)
        from_across = to_across(mine)
        from_far = to_across(from_near)
        return [
            from_near,
            from_across,
            from_far,
            to_core(from_near),
            to_core(from_across),
            to_core(from_far),
        ]

    tokens_all = lax.all_gather(tokens, "ctx", axis=0)

    count_row = counts[0]
    offsets = jnp.cumsum(count_row) - count_row
    seq_ends = jnp.cumsum(seq_lengths[0])
    within = jnp.arange(rows, dtype=jnp.int32)
    slot = jnp.arange(ctx, dtype=jnp.int32)[:, None] * rows + within[None, :]
    live = within[None, :] < count_row[:, None]
    places = offsets[:, None] + within[None, :]
    starts = jnp.max(
        jnp.where(places[:, :, None] >= seq_ends[None, None, :], seq_ends[None, None, :], 0), axis=2
    )
    dead_id = -1 - slot
    key_ids = jnp.where(live, places, dead_id)
    lows = jnp.where(live, starts, dead_id)
    fars = jnp.where(live, starts, NEVER)
    key_tile = jnp.broadcast_to(key_ids[:, :, None], (ctx, rows, 128))

    def own_parity(array):
        return pick(array.reshape((chips, 2) + array.shape[1:]), core, 1)

    low_rows = own_parity(lows)[:, None, :]
    high_rows = own_parity(key_ids)[:, None, :]
    far_rows = own_parity(fars)[:, None, :]
    live_rows = (within < pick(count_row, place)).astype(FP32)[:, None]

    smalls = jnp.concatenate(
        [b_query, b_value, b_out, b_proj, gain1, shift1, gain2, shift2, b_fc]
    ).reshape(-1, 128)
    small_all = place_all(
        (fsdp,) + smalls.shape,
        BF16,
        [((part,), smalls)] + [((part ^ s,), to_part(smalls, s)) for s in (1, 2, 3)],
    )
    small_all = small_all.reshape(fsdp, -1).astype(FP32)
    vectors = [small_all[:, n * shard : (n + 1) * shard].reshape(1, -1) for n in range(8)]
    bias_q, bias_v, bias_out, bias_proj, gain_one, shift_one, gain_two, shift_two = vectors
    bias_fc = small_all[:, 8 * shard :].reshape(1, -1)

    half = shard // 2
    mine = lax.dynamic_slice_in_dim(w_qkv, core * half, half, 0)
    arrived = gather_pieces(mine)
    owners = [part ^ near, part ^ across, part ^ 3, part ^ across, part ^ near, part ^ 3]
    items = [((owners[n], core if n < 3 else 1 - core), arrived[n]) for n in range(6)]
    items.append(((part, 0), w_qkv.reshape(2, half, -1)))
    qkv_full = place_all((fsdp, 2, half, 3 * features), BF16, items).reshape(features, 3 * features)
    qkv_parts = jnp.transpose(
        qkv_full.reshape(features, 3, chips, width), (2, 0, 1, 3)
    ).reshape(chips, features, 3 * width)
    own_weight = pick(qkv_parts, chip)

    fc_half = lax.dynamic_slice_in_dim(w_fc, core * half, half, 0)
    bundle = jnp.concatenate(
        [
            lax.dynamic_slice_in_dim(w_proj, core * (columns // 2), columns // 2, 0),
            lax.dynamic_slice_in_dim(w_out, core * half, half, 0),
        ]
        + [fc_half[:, columns * j : columns * (j + 1)] for j in range(fsdp)],
        axis=0,
    )
    pieces = gather_pieces(bundle)

    own_bias_q = lax.dynamic_slice_in_dim(bias_q, chip * width, width, 1)
    own_bias_v = lax.dynamic_slice_in_dim(bias_v, chip * width, width, 1)
    pair_count = group_heads * rows * rows * (chips * (chips + 1))
    queries, keys, keys_t, values, normed_mine, attended_out, attended_t, logs = kernel_call(
        attend_kernel,
        [
            jax.ShapeDtypeStruct((chips, rows, width), BF16),
            jax.ShapeDtypeStruct((ctx, rows, width), BF16),
            jax.ShapeDtypeStruct((ctx, width, rows), BF16),
            jax.ShapeDtypeStruct((ctx, rows, width), BF16),
            jax.ShapeDtypeStruct((chips, rows, features), BF16),
            jax.ShapeDtypeStruct((chips, rows, width), BF16),
            jax.ShapeDtypeStruct((chips, width, rows), FP32),
            jax.ShapeDtypeStruct((chips, 8, rows), FP32),
        ],
        [pltpu.VMEM((ctx, width, rows), BF16), pltpu.VMEM((width, rows), FP32)],
        (
            where[1:2],
            tokens_all,
            own_weight[:, :width],
            own_weight[:, width : 2 * width],
            own_weight[:, 2 * width :],
            own_bias_q,
            own_bias_v,
            gain_one,
            shift_one,
            key_tile,
            low_rows,
            high_rows,
            far_rows,
        ),
        pair_count * 256 + 2 * ctx * rows * features * 3 * width,
    )

    def scatter_chips(blocks):
        arrived = [(chip, pick(blocks, chip))]
        for s in (1, 2, 3):
            arrived.append((chip ^ s, to_chip(pick(blocks, chip ^ s), s)))
        return arrived

    attended = [v for unused, v in scatter_chips(attended_out)]
    bundle_width = 2 * hidden_width // 2 + 3 * features + features // 2
    hbm = pl.BlockSpec(memory_space=pl.ANY)
    block_out, grad_middle, grad_heads, bundle_mine, bundle_send, sums = kernel_call(
        middle_kernel,
        [
            jax.ShapeDtypeStruct((rows, features), BF16),
            jax.ShapeDtypeStruct((rows, features), FP32),
            jax.ShapeDtypeStruct((chips, rows, width), BF16),
            jax.ShapeDtypeStruct((rows, bundle_width), BF16),
            jax.ShapeDtypeStruct((rows, bundle_width), BF16),
            jax.ShapeDtypeStruct((8, hidden_width), FP32),
        ],
        [
            pltpu.VMEM((features, features), BF16),
            pltpu.VMEM((fsdp, features, columns), BF16),
            pltpu.VMEM((hidden_width, features), BF16),
            pltpu.VMEM((rows, columns), BF16),
            pltpu.VMEM((rows, features), BF16),
            pltpu.SemaphoreType.DMA((9 + 6 * 6 - 3,)),
        ],
        tuple([where] + attended)
        + (
            tokens,
            cotangent,
            live_rows,
            bias_out,
            gain_two,
            shift_two,
            bias_fc,
            bias_proj,
            w_out,
            w_fc,
            w_proj,
        )
        + tuple(pieces),
        4 * rows * features * (2 * hidden_width + features),
        special={n: hbm for n in range(13, 22)},
    )

    grad_blocks = place_all(
        (chips, rows, width), BF16, [((n,), v) for n, v in scatter_chips(grad_heads)]
    )

    bundle_other = to_core(bundle_send)
    small_rows = jnp.concatenate(
        [sums[n, :features].reshape(fsdp, shard) for n in range(1, 5)]
        + [sums[0].reshape(fsdp, columns)],
        axis=1,
    ).reshape(fsdp, 2, features)
    small_rows = jnp.pad(small_rows, ((0, 0), (0, 14), (0, 0)))
    out_rows = columns // 2 + 2 * shard
    small_at = out_rows + half
    block_rows = small_at + 32
    pair_shape = jax.ShapeDtypeStruct((2, block_rows, features), BF16)
    grads_keep, grads_send = kernel_call(
        weight_grad_kernel,
        [pair_shape, pair_shape],
        [pltpu.VMEM((2, features, features), BF16)],
        (where, bundle_mine, bundle_other, small_rows),
        4 * rows * features * (hidden_width + features // 2),
    )

    grad_query, grad_keep, grad_send = kernel_call(
        attend_back_kernel,
        [
            jax.ShapeDtypeStruct((chips, rows, width), BF16),
            jax.ShapeDtypeStruct((chips, rows, 2 * width), FP32),
            jax.ShapeDtypeStruct((chips, rows, 2 * width), BF16),
        ],
        [
            pltpu.VMEM((width, rows), FP32),
            pltpu.VMEM((group_heads, ctx, rows, 64), FP32),
            pltpu.VMEM((group_heads, ctx, rows, 64), FP32),
        ],
        (
            where[1:2],
            queries,
            keys,
            keys_t,
            values,
            grad_blocks,
            key_tile,
            low_rows,
            high_rows,
            far_rows,
            attended_t,
            logs,
        ),
        pair_count * 640,
    )
    grad_kv = (grad_keep + to_core(grad_send).astype(FP32)).astype(BF16)
    grad_packed = jnp.concatenate([grad_query, grad_kv], axis=2)

    packed = [v for unused, v in scatter_chips(grad_packed)]
    (grad_tokens,) = kernel_call(
        input_grad_kernel,
        [jax.ShapeDtypeStruct((rows, features), FP32)],
        [],
        tuple([where] + packed) + (qkv_parts, tokens, grad_middle, gain_one, shift_one),
        6 * rows * features * features,
    )

    def add_up(left_side, right_side):
        return left_side.astype(FP32) + right_side.astype(FP32)

    def scatter_parts(keep, send):
        theirs = to_near(send)
        last = to_across(add_up(keep[1], theirs[1]).astype(BF16))
        return (add_up(keep[0], theirs[0]) + last.astype(FP32)).astype(BF16)

    grads_half = scatter_parts(grads_keep, grads_send)
    grads_half = lax.psum(grads_half, "ctx", axis_index_groups=same_core)
    grads_other = to_core(grads_half)

    def by_core(mine, other, axis):
        first = jnp.where(core == 0, mine, other)
        second = jnp.where(core == 0, other, mine)
        return jnp.concatenate([first, second], axis=axis).astype(FP32)

    mid = columns // 2
    d_proj = by_core(grads_half[:mid], grads_other[:mid], 0)

    def fc_columns(block):
        return jnp.concatenate([block[mid : mid + shard], block[mid + shard : out_rows]], axis=1)

    def out_columns(block):
        packed_out = block[out_rows:small_at]
        return jnp.concatenate([packed_out[:, : features // 2], packed_out[:, features // 2 :]], axis=0)

    d_fc = by_core(fc_columns(grads_half), fc_columns(grads_other), 1)
    d_out = by_core(out_columns(grads_half), out_columns(grads_other), 1)
    small_sums = add_up(grads_half[small_at : small_at + 2], grads_other[small_at : small_at + 2])
    d_bias_out, d_bias_proj, d_gain_two, d_shift_two = (
        small_sums[0, n * shard : (n + 1) * shard] for n in range(4)
    )
    d_bias_fc = small_sums[1]

    block_shape = (fsdp, half + 16, 3 * width)
    qkv_keep, qkv_send = kernel_call(
        qkv_grad_kernel,
        [jax.ShapeDtypeStruct(block_shape, FP32), jax.ShapeDtypeStruct(block_shape, BF16)],
        [pltpu.VMEM((features, 3 * width), FP32)],
        (
            where,
            normed_mine,
            grad_query,
            grad_kv,
            own_weight,
            gain_one.reshape(-1, 1),
            shift_one.reshape(-1, 1),
        ),
        2 * chips * rows * features * 3 * width,
    )
    qkv_blocks = add_up(qkv_keep, to_core(qkv_send)).astype(BF16)
    qkv_half = scatter_parts(qkv_blocks[:2], qkv_blocks[2:])
    qkv_total = lax.all_gather(qkv_half, "ctx", axis=0).reshape((chips, 2) + qkv_half.shape)
    d_qkv = jnp.transpose(
        qkv_total[:, :, :half].reshape(chips, 2, half, 3, width), (1, 2, 3, 0, 4)
    )
    d_qkv = d_qkv.reshape(shard, 3 * features).astype(FP32)
    extra = qkv_total[:, 0, half : half + 3].astype(FP32)
    owner_extra = pick(extra, part)
    d_bias_q = owner_extra[2, :width]
    d_bias_v = owner_extra[2, 2 * width :]
    norm_total = jnp.sum(extra[:, :2, :shard], axis=0)
    d_gain_one = norm_total[0]
    d_shift_one = norm_total[1]

    return (
        block_out,
        grad_tokens,
        d_qkv,
        d_bias_q,
        d_bias_v,
        d_out,
        d_bias_out,
        d_fc,
        d_bias_fc,
        d_proj,
        d_bias_proj,
        d_gain_one,
        d_shift_one,
        d_gain_two,
        d_shift_two,
    )


def solution(mesh):
    in_specs = (
        P(("fsdp", "ctx"), None),
        P(("fsdp", "ctx"), None),
        P("fsdp", None),
        P("fsdp"),
        P("fsdp"),
        P("fsdp", None),
        P("fsdp"),
        P("fsdp", None),
        P("fsdp"),
        P("fsdp", None),
        P("fsdp"),
        P("fsdp"),
        P("fsdp"),
        P("fsdp"),
        P("fsdp"),
        P("fsdp", None),
        P("fsdp", None),
    )
    out_specs = (
        P(("fsdp", "ctx"), None),
        P(("fsdp", "ctx"), None),
        P("fsdp", None),
        P("fsdp"),
        P("fsdp"),
        P("fsdp", None),
        P("fsdp"),
        P("fsdp", None),
        P("fsdp"),
        P("fsdp", None),
        P("fsdp"),
        P("fsdp"),
        P("fsdp"),
        P("fsdp"),
        P("fsdp"),
    )
    ctx = mesh.shape["ctx"]
    four_by_four = mesh.shape["fsdp"] == 4 and ctx == 8 and HEADS % (ctx // 2) == 0
    body = fast_body if four_by_four else general_body
    return jax.shard_map(body, mesh=mesh, in_specs=in_specs, out_specs=out_specs, check_vma=False)
```

```python
import functools

import jax
import jax.numpy as jnp
from jax import lax
from jax.experimental import pallas as pl
from jax.experimental.pallas import tpu as pltpu
from jax.sharding import PartitionSpec as P

HEADS = 12


EPS = 1e-05


def layer_norm(values, gain_row, shift_row):
    centre = values - jnp.mean(values, axis=1, keepdims=True)
    inverse = lax.rsqrt(jnp.mean(centre * centre, axis=1, keepdims=True) + EPS)
    normed = centre * inverse
    return (normed * gain_row + shift_row, normed, inverse)


def norm_back(grad_in, normed, inverse, gain_row):
    scaled = grad_in * gain_row
    inner_grad = inverse * (
        scaled
        - jnp.mean(scaled, axis=1, keepdims=True)
        - normed * jnp.mean(scaled * normed, axis=1, keepdims=True)
    )
    return (inner_grad, jnp.sum(grad_in * normed, axis=0), jnp.sum(grad_in, axis=0))


def contract_rows(left_side, right_side):
    return lax.dot_general(
        left_side, right_side, (((0,), (0,)), ((), ())), preferred_element_type=jnp.float32
    )


def times_transpose(left_side, right_side):
    return lax.dot_general(
        left_side, right_side, (((1,), (1,)), ((), ())), preferred_element_type=jnp.float32
    )


def gelu_tanh(values):
    return jax.nn.gelu(values, approximate=True)


def describe(slot_ids, row_count, count_row, offsets, seq_ends):
    peer_count = count_row.shape[0]
    device = slot_ids // row_count
    within = slot_ids - device * row_count
    matches = device[:, None] == jnp.arange(peer_count, dtype=jnp.int32)[None, :]
    live_count = jnp.sum(jnp.where(matches, count_row[None, :], 0), axis=1)
    first_place = jnp.sum(jnp.where(matches, offsets[None, :], 0), axis=1)
    places = first_place + within
    segment = jnp.sum((places[:, None] >= seq_ends[None, :]).astype(jnp.int32), axis=1)
    return (within < live_count, places, segment, slot_ids)


def allowed(query_info, key_info):
    q_live, q_place, q_seg, q_slot = query_info
    k_live, k_place, k_seg, k_slot = key_info
    same_seq = (
        q_live[:, None]
        & k_live[None, :]
        & (q_seg[:, None] == k_seg[None, :])
        & (k_place[None, :] <= q_place[:, None])
    )
    return same_seq | (q_slot[:, None] == k_slot[None, :])


def over_blocks(step_fn, status, pieces, row_count):
    total_rows = pieces[0].shape[0]
    block_total = total_rows // row_count
    stacked = tuple((piece.reshape((block_total, row_count) + piece.shape[1:]) for piece in pieces))

    def scan_body(state_now, scan_item):
        block_index, block_parts = scan_item
        return (step_fn(state_now, block_parts, block_index * row_count), None)

    status, unused = lax.scan(
        scan_body, status, (jnp.arange(block_total, dtype=jnp.int32), stacked)
    )
    return status


def score_grads(
    query_heads, key_heads, value_heads, grad_heads, lse_rows, delta_rows, permitted, scaling
):
    scores = (
        jnp.einsum("qhd,khd->hqk", query_heads, key_heads, preferred_element_type=jnp.float32)
        * scaling
    )
    probabilities = jnp.where(permitted[None], jnp.exp(scores - lse_rows[:, :, None]), 0.0)
    grad_probs = jnp.einsum(
        "qhd,khd->hqk", grad_heads, value_heads, preferred_element_type=jnp.float32
    )
    grad_scores = (probabilities * (grad_probs - delta_rows[:, :, None])).astype(jnp.bfloat16)
    return (probabilities.astype(jnp.bfloat16), grad_scores)


def general_body(
    tokens,
    cotangent,
    w_qkv,
    b_query,
    b_value,
    w_out,
    b_out,
    w_fc,
    b_fc,
    w_proj,
    b_proj,
    gain1,
    shift1,
    gain2,
    shift2,
    counts,
    seq_lengths,
):
    row_count, feature_count = tokens.shape
    peer_count = lax.axis_size("ctx")
    my_index = lax.axis_index("ctx")
    head_count = HEADS
    head_width = feature_count // head_count
    scaling = head_width ** (-0.5)
    count_row = counts[0]
    offsets = jnp.cumsum(count_row) - count_row
    seq_ends = jnp.cumsum(seq_lengths[0])

    def locate(first_slot, length):
        return describe(
            first_slot + jnp.arange(length, dtype=jnp.int32),
            row_count,
            count_row,
            offsets,
            seq_ends,
        )

    own_rows = locate(my_index * row_count, row_count)
    fp32 = jnp.float32
    bf16 = jnp.bfloat16
    (
        qkv_full,
        query_bias,
        value_bias,
        out_full,
        out_bias,
        fc_full,
        fc_bias,
        proj_full,
        proj_bias,
        gain_one,
        shift_one,
        gain_two,
        shift_two,
    ) = (
        lax.all_gather(w_qkv, "fsdp", axis=0, tiled=True),
        lax.all_gather(b_query, "fsdp", axis=0, tiled=True),
        lax.all_gather(b_value, "fsdp", axis=0, tiled=True),
        lax.all_gather(w_out, "fsdp", axis=0, tiled=True),
        lax.all_gather(b_out, "fsdp", axis=0, tiled=True),
        lax.all_gather(w_fc, "fsdp", axis=0, tiled=True),
        lax.all_gather(b_fc, "fsdp", axis=0, tiled=True),
        lax.all_gather(w_proj, "fsdp", axis=0, tiled=True),
        lax.all_gather(b_proj, "fsdp", axis=0, tiled=True),
        lax.all_gather(gain1, "fsdp", axis=0, tiled=True),
        lax.all_gather(shift1, "fsdp", axis=0, tiled=True),
        lax.all_gather(gain2, "fsdp", axis=0, tiled=True),
        lax.all_gather(shift2, "fsdp", axis=0, tiled=True),
    )
    inputs = tokens.astype(fp32)
    normed_one, unit_one, inverse_one = layer_norm(
        inputs, gain_one.astype(fp32), shift_one.astype(fp32)
    )
    normed_low = normed_one.astype(bf16)
    bias_row = jnp.concatenate([query_bias, jnp.zeros_like(query_bias), value_bias]).astype(fp32)
    packed = (jnp.dot(normed_low, qkv_full, preferred_element_type=fp32) + bias_row).astype(bf16)
    query_rows = packed[:, :feature_count]
    key_rows = packed[:, feature_count : 2 * feature_count]
    value_rows = packed[:, 2 * feature_count :]
    query_heads = query_rows.reshape(row_count, head_count, head_width)

    def forward_step(status, pieces, first_row):
        running_max, running_sum, running_acc = status
        key_piece, value_piece = pieces
        length = key_piece.shape[0]
        key_heads = key_piece.reshape(length, head_count, head_width)
        value_heads = value_piece.reshape(length, head_count, head_width)
        scores = (
            jnp.einsum("qhd,khd->hqk", query_heads, key_heads, preferred_element_type=fp32)
            * scaling
        )
        permitted = allowed(own_rows, locate(first_row, length))
        scores = jnp.where(permitted[None], scores, -jnp.inf)
        new_max = jnp.maximum(running_max, jnp.max(scores, axis=2))
        fading = jnp.exp(running_max - new_max)
        weights = jnp.exp(scores - new_max[:, :, None])
        running_sum = running_sum * fading + jnp.sum(weights, axis=2)
        update = jnp.einsum(
            "hqk,khd->qhd", weights.astype(bf16), value_heads, preferred_element_type=fp32
        )
        running_acc = running_acc * jnp.transpose(fading)[:, :, None] + update
        return (new_max, running_sum, running_acc)

    start_state = (
        jnp.full((head_count, row_count), -1e30, fp32),
        jnp.zeros((head_count, row_count), fp32),
        jnp.zeros((row_count, head_count, head_width), fp32),
    )
    final_max, final_sum, final_acc = over_blocks(
        forward_step,
        start_state,
        (
            lax.all_gather(key_rows, "ctx", axis=0, tiled=True),
            lax.all_gather(value_rows, "ctx", axis=0, tiled=True),
        ),
        row_count,
    )
    attended_heads = final_acc / jnp.transpose(final_sum)[:, :, None]
    attended = attended_heads.reshape(row_count, feature_count)
    log_total = final_max + jnp.log(final_sum)
    attended_low = attended.astype(bf16)
    middle = (
        inputs
        + jnp.dot(attended_low, out_full, preferred_element_type=fp32)
        + out_bias.astype(fp32)
    )
    normed_two, unit_two, inverse_two = layer_norm(
        middle, gain_two.astype(fp32), shift_two.astype(fp32)
    )
    normed_two_low = normed_two.astype(bf16)
    hidden = jnp.dot(normed_two_low, fc_full, preferred_element_type=fp32) + fc_bias.astype(fp32)
    activated = gelu_tanh(hidden).astype(bf16)
    output = (
        middle + jnp.dot(activated, proj_full, preferred_element_type=fp32) + proj_bias.astype(fp32)
    )
    output_low = output.astype(bf16)
    qkv_full, out_full, fc_full, proj_full, gain_one, gain_two = (
        lax.all_gather(w_qkv, "fsdp", axis=0, tiled=True),
        lax.all_gather(w_out, "fsdp", axis=0, tiled=True),
        lax.all_gather(w_fc, "fsdp", axis=0, tiled=True),
        lax.all_gather(w_proj, "fsdp", axis=0, tiled=True),
        lax.all_gather(gain1, "fsdp", axis=0, tiled=True),
        lax.all_gather(gain2, "fsdp", axis=0, tiled=True),
    )
    live_rows = own_rows[0].astype(fp32)[:, None]
    grad_out = cotangent.astype(fp32) * live_rows
    grad_out_low = grad_out.astype(bf16)
    grad_proj = contract_rows(activated, grad_out_low)
    grad_proj_bias = jnp.sum(grad_out, axis=0)
    grad_act = times_transpose(grad_out_low, proj_full)
    grad_hidden = jax.vjp(gelu_tanh, hidden)[1](grad_act)[0]
    grad_hidden_low = grad_hidden.astype(bf16)
    grad_fc = contract_rows(normed_two_low, grad_hidden_low)
    grad_fc_bias = jnp.sum(grad_hidden_low.astype(fp32), axis=0)
    grad_normed_two = times_transpose(grad_hidden_low, fc_full)
    grad_mid_norm, grad_gain_two, grad_shift_two = norm_back(
        grad_normed_two, unit_two, inverse_two, gain_two.astype(fp32)
    )
    grad_middle = grad_out + grad_mid_norm
    grad_middle_low = grad_middle.astype(bf16)
    grad_out_proj = contract_rows(attended_low, grad_middle_low)
    grad_out_bias = jnp.sum(grad_middle_low.astype(fp32), axis=0)
    grad_attended = times_transpose(grad_middle_low, out_full).astype(bf16)
    grad_heads = grad_attended.reshape(row_count, head_count, head_width)
    delta_rows = jnp.transpose(jnp.sum(grad_heads.astype(fp32) * attended_heads, axis=2))

    def back_step(status, pieces, first_row):
        grad_query, grad_keys = status
        key_piece, value_piece = pieces
        length = key_piece.shape[0]
        key_heads = key_piece.reshape(length, head_count, head_width)
        value_heads = value_piece.reshape(length, head_count, head_width)
        permitted = allowed(own_rows, locate(first_row, length))
        probs_low, grad_scores = score_grads(
            query_heads,
            key_heads,
            value_heads,
            grad_heads,
            log_total,
            delta_rows,
            permitted,
            scaling,
        )
        grad_query = (
            grad_query
            + jnp.einsum("hqk,khd->qhd", grad_scores, key_heads, preferred_element_type=fp32)
            * scaling
        )
        grad_key_part = (
            jnp.einsum("hqk,qhd->khd", grad_scores, query_heads, preferred_element_type=fp32)
            * scaling
        )
        grad_value_part = jnp.einsum(
            "hqk,qhd->khd", probs_low, grad_heads, preferred_element_type=fp32
        )
        joined = jnp.concatenate(
            [
                grad_key_part.reshape(length, feature_count),
                grad_value_part.reshape(length, feature_count),
            ],
            axis=1,
        )
        current = lax.dynamic_slice_in_dim(grad_keys, first_row, length, 0)
        grad_keys = lax.dynamic_update_slice_in_dim(grad_keys, current + joined, first_row, 0)
        return (grad_query, grad_keys)

    keys_start = jnp.zeros((peer_count * row_count, 2 * feature_count), fp32)
    grad_query, grad_keys = over_blocks(
        back_step,
        (jnp.zeros((row_count, head_count, head_width), fp32), keys_start),
        (
            lax.all_gather(key_rows, "ctx", axis=0, tiled=True),
            lax.all_gather(value_rows, "ctx", axis=0, tiled=True),
        ),
        row_count,
    )
    grad_kv = lax.psum_scatter(
        grad_keys.astype(jnp.bfloat16), "ctx", scatter_dimension=0, tiled=True
    ).astype(jnp.float32)
    grad_packed = jnp.concatenate(
        [grad_query.reshape(row_count, feature_count), grad_kv], axis=1
    ).astype(bf16)
    grad_packed_wide = grad_packed.astype(fp32)
    grad_query_bias = jnp.sum(grad_packed_wide[:, :feature_count], axis=0)
    grad_value_bias = jnp.sum(grad_packed_wide[:, 2 * feature_count :], axis=0)
    grad_qkv = contract_rows(normed_low, grad_packed)
    grad_normed_one = times_transpose(grad_packed, qkv_full)
    grad_in_norm, grad_gain_one, grad_shift_one = norm_back(
        grad_normed_one, unit_one, inverse_one, gain_one.astype(fp32)
    )
    grad_tokens = grad_middle + grad_in_norm
    (
        sum_qkv,
        sum_qbias,
        sum_vbias,
        sum_out,
        sum_obias,
        sum_fc,
        sum_fbias,
        sum_proj,
        sum_pbias,
        sum_gain_one,
        sum_shift_one,
        sum_gain_two,
        sum_shift_two,
    ) = (
        lax.psum_scatter(
            grad_qkv.astype(jnp.bfloat16), "fsdp", scatter_dimension=0, tiled=True
        ).astype(jnp.float32),
        lax.psum_scatter(
            grad_query_bias.astype(jnp.bfloat16), "fsdp", scatter_dimension=0, tiled=True
        ).astype(jnp.float32),
        lax.psum_scatter(
            grad_value_bias.astype(jnp.bfloat16), "fsdp", scatter_dimension=0, tiled=True
        ).astype(jnp.float32),
        lax.psum_scatter(
            grad_out_proj.astype(jnp.bfloat16), "fsdp", scatter_dimension=0, tiled=True
        ).astype(jnp.float32),
        lax.psum_scatter(
            grad_out_bias.astype(jnp.bfloat16), "fsdp", scatter_dimension=0, tiled=True
        ).astype(jnp.float32),
        lax.psum_scatter(
            grad_fc.astype(jnp.bfloat16), "fsdp", scatter_dimension=0, tiled=True
        ).astype(jnp.float32),
        lax.psum_scatter(
            grad_fc_bias.astype(jnp.bfloat16), "fsdp", scatter_dimension=0, tiled=True
        ).astype(jnp.float32),
        lax.psum_scatter(
            grad_proj.astype(jnp.bfloat16), "fsdp", scatter_dimension=0, tiled=True
        ).astype(jnp.float32),
        lax.psum_scatter(
            grad_proj_bias.astype(jnp.bfloat16), "fsdp", scatter_dimension=0, tiled=True
        ).astype(jnp.float32),
        lax.psum_scatter(
            grad_gain_one.astype(jnp.bfloat16), "fsdp", scatter_dimension=0, tiled=True
        ).astype(jnp.float32),
        lax.psum_scatter(
            grad_shift_one.astype(jnp.bfloat16), "fsdp", scatter_dimension=0, tiled=True
        ).astype(jnp.float32),
        lax.psum_scatter(
            grad_gain_two.astype(jnp.bfloat16), "fsdp", scatter_dimension=0, tiled=True
        ).astype(jnp.float32),
        lax.psum_scatter(
            grad_shift_two.astype(jnp.bfloat16), "fsdp", scatter_dimension=0, tiled=True
        ).astype(jnp.float32),
    )
    totals = (
        lax.psum(sum_qkv.astype(jnp.bfloat16), "ctx").astype(jnp.float32),
        lax.psum(sum_qbias.astype(jnp.bfloat16), "ctx").astype(jnp.float32),
        lax.psum(sum_vbias.astype(jnp.bfloat16), "ctx").astype(jnp.float32),
        lax.psum(sum_out.astype(jnp.bfloat16), "ctx").astype(jnp.float32),
        lax.psum(sum_obias.astype(jnp.bfloat16), "ctx").astype(jnp.float32),
        lax.psum(sum_fc.astype(jnp.bfloat16), "ctx").astype(jnp.float32),
        lax.psum(sum_fbias.astype(jnp.bfloat16), "ctx").astype(jnp.float32),
        lax.psum(sum_proj.astype(jnp.bfloat16), "ctx").astype(jnp.float32),
        lax.psum(sum_pbias.astype(jnp.bfloat16), "ctx").astype(jnp.float32),
        lax.psum(sum_gain_one.astype(jnp.bfloat16), "ctx").astype(jnp.float32),
        lax.psum(sum_shift_one.astype(jnp.bfloat16), "ctx").astype(jnp.float32),
        lax.psum(sum_gain_two.astype(jnp.bfloat16), "ctx").astype(jnp.float32),
        lax.psum(sum_shift_two.astype(jnp.bfloat16), "ctx").astype(jnp.float32),
    )
    return (
        output_low,
        grad_tokens,
        totals[0],
        totals[1],
        totals[2],
        totals[3],
        totals[4],
        totals[5],
        totals[6],
        totals[7],
        totals[8],
        totals[9],
        totals[10],
        totals[11],
        totals[12],
    )


FP32 = jnp.float32
BF16 = jnp.bfloat16
FLOOR = -1e30
NEVER = 1 << 30


def dot_nt(left_side, right_side):
    return lax.dot_general(
        left_side, right_side, (((1,), (1,)), ((), ())), preferred_element_type=FP32
    )


def dot_nn(left_side, right_side):
    return lax.dot_general(
        left_side, right_side, (((1,), (0,)), ((), ())), preferred_element_type=FP32
    )


def spread(column_tile, width):
    return jnp.concatenate([column_tile] * (width // column_tile.shape[1]), axis=1)


def masked_scores(scores, key_ids, first_row, last_row):
    permitted = key_ids >= first_row
    if last_row is not None:
        permitted = permitted & (key_ids <= last_row)
    return jnp.where(permitted, scores, -jnp.inf)


def project_block(
    tokens_ref, wq_ref, wk_ref, wv_ref, bq_ref, bv_ref, gain_ref, shift_ref, stores, position, wanted
):
    q_ref, k_ref, kt_ref, v_ref, vt_ref, normed_ref = stores
    normed = layer_norm(tokens_ref[...].astype(FP32), gain_ref[...], shift_ref[...])[0]
    normed = normed.astype(BF16)
    keys = dot_nn(normed, wk_ref[...])
    values = dot_nn(normed, wv_ref[...]) + bv_ref[...]
    k_ref[position] = keys.astype(BF16)
    v_ref[position] = values.astype(BF16)
    kt_ref[position] = keys.T.astype(BF16)
    vt_ref[position] = values.T.astype(BF16)
    if wanted:
        queries = (dot_nn(normed, wq_ref[...]) + bq_ref[...]).astype(BF16)
        q_ref[position // 2] = (queries.astype(FP32) * 0.125).astype(BF16)
        normed_ref[position // 2] = normed


def project_kernel(where, t0, t1, t2, t3, wq, wk, wv, bq, bv, gain, shift, q, k, kt, v, vt, normed):
    core, chip = where[1], where[2]
    stores = (q, k, kt, v, vt, normed)
    for n, block in enumerate((t0, t1, t2, t3)):
        owner = (chip ^ (n // 2)) % 2
        position = 2 * owner + (core if n % 2 == 0 else 1 - core)
        project_block(block, wq, wk, wv, bq, bv, gain, shift, stores, position, n % 2 == 0)


def attend_kernel(
    where,
    t0,
    t1,
    t2,
    t3,
    wq_ref,
    wk_ref,
    wv_ref,
    bq_ref,
    bv_ref,
    gain_ref,
    shift_ref,
    q_half,
    k_half,
    kt_half,
    v_half,
    vt_half,
    normed_half,
    key_ref,
    low_ref,
    high_ref,
    far_ref,
    q_ref,
    k_ref,
    kt_ref,
    v_ref,
    normed_ref,
    o0_ref,
    o1_ref,
    o2_ref,
    o3_ref,
    ot_ref,
    lse_ref,
    zero_ref,
    vt_ref,
    acc_ref,
    o_ref,
):
    blocks, rows, width = q_ref.shape
    heads = width // 64
    core, chip = where[1], where[2]
    side = chip // 2
    zero_ref[...] = jnp.zeros_like(zero_ref)
    stores = (q_ref, k_ref, kt_ref, v_ref, vt_ref, normed_ref)
    for n, block in enumerate((t0, t1, t2, t3)):
        owner = chip ^ (2 + n // 2)
        position = 2 * owner + (core if n % 2 == 0 else 1 - core)
        project_block(
            block,
            wq_ref,
            wk_ref,
            wv_ref,
            bq_ref,
            bv_ref,
            gain_ref,
            shift_ref,
            stores,
            position,
            n % 2 == 0,
        )
    for n in range(blocks):
        for source, target in ((k_half, k_ref), (kt_half, kt_ref), (v_half, v_ref), (vt_half, vt_ref)):
            target[side * blocks + n] = source[n]
    for n in range(blocks // 2):
        q_ref[side * (blocks // 2) + n] = q_half[n]
        normed_ref[side * (blocks // 2) + n] = normed_half[n]

    def query_block(index, unused):
        queries = [q_ref[index, :, 64 * h : 64 * h + 64] for h in range(heads)]
        acc_ref[...] = jnp.zeros_like(acc_ref)

        def key_step(key_block, carry, first_row, last_row):
            ids = spread(key_ref[key_block], rows)
            result = []
            for h in range(heads):
                span = slice(64 * h, 64 * h + 64)
                top, total = carry[h]
                scores = dot_nt(k_ref[key_block, :, span], queries[h])
                scores = masked_scores(scores, ids, first_row, last_row)
                new_top = jnp.maximum(top, jnp.max(scores, axis=0, keepdims=True))
                fade = jnp.exp(top - new_top)
                weights = jnp.exp(scores - new_top)
                total = total * fade + jnp.sum(weights, axis=0, keepdims=True)
                acc_ref[span, :] = acc_ref[span, :] * fade + dot_nn(
                    vt_ref[key_block, span, :], weights.astype(BF16)
                )
                result.append((new_top, total))
            return tuple(result)

        start = tuple(
            (jnp.full((1, rows), FLOOR, FP32), jnp.zeros((1, rows), FP32)) for h in range(heads)
        )
        own = 2 * index + core
        far_row = far_ref[index]
        carry = lax.fori_loop(0, own, lambda j, c: key_step(j, c, far_row, None), start)
        carry = key_step(own, carry, low_ref[index], high_ref[index])
        for h in range(heads):
            span = slice(64 * h, 64 * h + 64)
            top, total = carry[h]
            attended = acc_ref[span, :] / total
            ot_ref[index, span, :] = attended
            o_ref[index, :, span] = attended.T.astype(BF16)
            lse_ref[index, h : h + 1, :] = top + jnp.log(total)
        return unused

    lax.fori_loop(0, blocks, query_block, 0)
    for s, ref in enumerate((o0_ref, o1_ref, o2_ref, o3_ref)):
        ref[...] = o_ref[chip ^ s]


def attend_back_kernel(
    where,
    q_ref,
    k_ref,
    kt_ref,
    v_ref,
    d0_ref,
    d1_ref,
    d2_ref,
    d3_ref,
    key_ref,
    low_ref,
    high_ref,
    far_ref,
    ot_ref,
    lse_ref,
    dq_ref,
    keep_ref,
    send_ref,
    acc_ref,
    dk_ref,
    dv_ref,
    da_ref,
):
    blocks, rows, width = q_ref.shape
    heads = width // 64
    core, chip = where[1], where[2]
    for s, ref in enumerate((d0_ref, d1_ref, d2_ref, d3_ref)):
        da_ref[chip ^ s] = ref[...]
    dk_ref[...] = jnp.zeros_like(dk_ref)
    dv_ref[...] = jnp.zeros_like(dv_ref)

    def query_block(index, unused):
        queries = [q_ref[index, :, 64 * h : 64 * h + 64] for h in range(heads)]
        grads = [da_ref[index, :, 64 * h : 64 * h + 64] for h in range(heads)]
        deltas = [
            jnp.sum(
                grads[h].astype(FP32).T * ot_ref[index, 64 * h : 64 * h + 64, :],
                axis=0,
                keepdims=True,
            )
            for h in range(heads)
        ]
        logs = [lse_ref[index, h : h + 1, :] for h in range(heads)]
        acc_ref[...] = jnp.zeros_like(acc_ref)

        def key_step(key_block, first_row, last_row):
            ids = spread(key_ref[key_block], rows)
            for h in range(heads):
                span = slice(64 * h, 64 * h + 64)
                scores = dot_nt(k_ref[key_block, :, span], queries[h])
                scores = masked_scores(scores, ids, first_row, last_row)
                weights = jnp.exp(scores - logs[h])
                slopes = dot_nt(v_ref[key_block, :, span], grads[h])
                dscores = (weights * (slopes - deltas[h])).astype(BF16)
                dv_ref[h, key_block] += dot_nn(weights.astype(BF16), grads[h])
                dk_ref[h, key_block] += dot_nn(dscores, queries[h])
                acc_ref[span, :] += dot_nn(kt_ref[key_block, span, :], dscores)

        own = 2 * index + core
        far_row = far_ref[index]

        def far_step(key_block, state):
            key_step(key_block, far_row, None)
            return state

        lax.fori_loop(0, own, far_step, 0)
        key_step(own, low_ref[index], high_ref[index])
        for h in range(heads):
            span = slice(64 * h, 64 * h + 64)
            dq_ref[index, :, span] = (acc_ref[span, :] * 0.125).T.astype(BF16)
        return unused

    lax.fori_loop(0, blocks, query_block, 0)

    def write_block(index, unused):
        mine = 2 * index + core
        theirs = 2 * index + 1 - core
        for h in range(heads):
            left = slice(64 * h, 64 * h + 64)
            right = slice(width + 64 * h, width + 64 * h + 64)
            keep_ref[index, :, left] = dk_ref[h, mine]
            keep_ref[index, :, right] = dv_ref[h, mine]
            send_ref[index, :, left] = dk_ref[h, theirs].astype(BF16)
            send_ref[index, :, right] = dv_ref[h, theirs].astype(BF16)
        return unused

    lax.fori_loop(0, blocks, write_block, 0)


def kernel_call(kernel, outputs, scratch, operands, cost, special={}, after=()):
    whole = pl.BlockSpec(memory_space=pltpu.VMEM)
    in_specs = [pl.BlockSpec(memory_space=pltpu.SMEM)]
    in_specs += [special.get(n, whole) for n in range(1, len(operands))]
    in_specs += [pl.BlockSpec(memory_space=pl.ANY) for unused in after]
    count = len(operands)

    def ordered(*refs):
        return kernel(*refs[:count], *refs[count + len(after) :])

    moved = sum(v.size * v.dtype.itemsize for v in list(operands) + list(outputs))
    return pl.pallas_call(
        ordered,
        out_shape=outputs,
        in_specs=in_specs,
        out_specs=[pl.BlockSpec(memory_space=pltpu.VMEM) for unused in outputs],
        scratch_shapes=scratch,
        compiler_params=pltpu.CompilerParams(vmem_limit_bytes=56 * 1024 * 1024),
        cost_estimate=pl.CostEstimate(
            flops=cost * 1153 * 10**6, bytes_accessed=moved, transcendentals=0
        ),
    )(*operands, *after)


def pack_kernel(where, dq_ref, keep_ref, arrived_ref, p0, p1, p2, p3):
    chip = where[2]
    width = dq_ref.shape[2]
    for s, ref in enumerate((p0, p1, p2, p3)):
        owner = chip ^ s
        ref[:, 0:width] = dq_ref[owner]
        ref[:, width:] = (keep_ref[owner] + arrived_ref[owner].astype(FP32)).astype(BF16)


def middle_kernel(
    where,
    a0_ref,
    a1_ref,
    a2_ref,
    a3_ref,
    tokens_ref,
    cotangent_ref,
    live_ref,
    bias_out_ref,
    gain_ref,
    shift_ref,
    bias_fc_ref,
    bias_proj_ref,
    bundle_own,
    bundle_other,
    block_ref,
    dx_ref,
    d0_ref,
    d1_ref,
    d2_ref,
    d3_ref,
    mine_ref,
    send_ref,
    sums_ref,
    wo_ref,
    wf_ref,
    wp_ref,
    g_ref,
    dz_ref,
    sems,
):
    rows, features = tokens_ref.shape
    parts = wf_ref.shape[0]
    shard, hidden_width = features // parts, wp_ref.shape[0]
    columns = hidden_width // parts
    half, half_columns = shard // 2, columns // 2
    core, chip = where[1], where[2]

    starts = {"proj": [], "out": [], "fc": []}

    def fetch(kind, source, target):
        number = sum(len(v) for v in starts.values())
        starts[kind].append(pltpu.make_async_copy(source, target, sems.at[number]))

    def rows_at(owner, which, size):
        return pl.ds(pl.multiple_of(owner * 2 * size + which * size, 16), size)

    pieces = []
    for owner in range(parts):
        pieces.append((bundle_own.at[owner], owner, core))
        pieces.append((bundle_other.at[owner], owner, 1 - core))
    for piece, owner, which in pieces:
        fetch("out", piece.at[half_columns : half_columns + half, :], wo_ref.at[rows_at(owner, which, half), :])
    for piece, owner, which in pieces:
        for j in range(parts):
            first = half_columns + half * (j + 1)
            fetch("fc", piece.at[first : first + half, :], wf_ref.at[j, rows_at(owner, which, half), :])
    for piece, owner, which in pieces:
        fetch("proj", piece.at[0:half_columns, :], wp_ref.at[rows_at(owner, which, half_columns), :])
    for kind in ("out", "fc", "proj"):
        for copy in starts[kind]:
            copy.start()
    for copy in starts["out"]:
        copy.wait()

    attended = [a0_ref, a1_ref, a2_ref, a3_ref]
    middle = tokens_ref[...].astype(FP32) + bias_out_ref[...]
    a_start = 2 * parts * half_columns + features
    for s in range(parts):
        span = pl.ds(pl.multiple_of((chip ^ s) * shard, 16), shard)
        middle = middle + dot_nn(attended[s][...], wo_ref[span, :])
        mine_ref[:, a_start + shard * s : a_start + shard * (s + 1)] = attended[s][...]
        send_ref[:, a_start + shard * s : a_start + shard * (s + 1)] = attended[s][...]
    normed, unit, inverse = layer_norm(middle, gain_ref[...], shift_ref[...])
    normed_low = normed.astype(BF16)
    h_start = 2 * parts * half_columns
    mine_ref[:, h_start : h_start + features] = normed_low
    send_ref[:, h_start : h_start + features] = normed_low
    grad_out = cotangent_ref[...].astype(FP32) * live_ref[...]
    grad_out_low = grad_out.astype(BF16)
    y_start = a_start + features
    mine_ref[:, y_start : y_start + features] = grad_out_low
    send_ref[:, y_start : y_start + features] = grad_out_low
    for copy in starts["fc"] + starts["proj"]:
        copy.wait()

    sums_ref[...] = jnp.zeros_like(sums_ref)
    output = middle + bias_proj_ref[...]
    grad_normed = jnp.zeros((rows, features), FP32)
    scale, cubic = 0.7978845608028654, 0.044715
    for j in range(parts):
        span = slice(columns * j, columns * (j + 1))
        hidden = dot_nn(normed_low, wf_ref[j]) + bias_fc_ref[:, span]
        square = hidden * hidden
        bent = jnp.tanh(scale * hidden * (1.0 + cubic * square))
        active = 0.5 * hidden * (1.0 + bent)
        slope = 0.5 * (1.0 + bent) + 0.5 * hidden * (1.0 - bent * bent) * (
            scale * (1.0 + 3.0 * cubic * square)
        )
        g_ref[...] = active.astype(BF16)
        grad_hidden = (dot_nt(grad_out_low, wp_ref[span, :]) * slope).astype(BF16)
        output = output + dot_nn(g_ref[...], wp_ref[span, :])
        grad_normed = grad_normed + dot_nt(grad_hidden, wf_ref[j])
        sums_ref[j, 1:2, :] = jnp.sum(grad_hidden.astype(FP32), axis=0, keepdims=True)
        g_span = slice(half_columns * j, half_columns * (j + 1))
        mine_ref[:, g_span] = g_ref[:, pl.ds(pl.multiple_of(core * half_columns, 128), half_columns)]
        send_ref[:, g_span] = g_ref[
            :, pl.ds(pl.multiple_of((1 - core) * half_columns, 128), half_columns)
        ]
        first = parts * half_columns + columns * (j % 2)

        @pl.when(core == j // 2)
        def keep_hidden():
            mine_ref[:, first : first + columns] = grad_hidden

        @pl.when(core != j // 2)
        def give_hidden():
            send_ref[:, first : first + columns] = grad_hidden

    block_ref[...] = output.astype(BF16)
    inner, gain_sum, shift_sum = norm_back(grad_normed, unit, inverse, gain_ref[...])
    grad_middle = grad_out + inner
    dx_ref[...] = grad_middle
    dz_ref[...] = grad_middle.astype(BF16)
    z_start = y_start + features
    part_width = features // 2
    mine_ref[:, z_start : z_start + part_width] = dz_ref[
        :, pl.ds(pl.multiple_of(core * part_width, 128), part_width)
    ]
    send_ref[:, z_start : z_start + part_width] = dz_ref[
        :, pl.ds(pl.multiple_of((1 - core) * part_width, 128), part_width)
    ]
    for s, ref in enumerate((d0_ref, d1_ref, d2_ref, d3_ref)):
        span = pl.ds(pl.multiple_of((chip ^ s) * shard, 16), shard)
        ref[...] = dot_nt(dz_ref[...], wo_ref[span, :]).astype(BF16)
    rows_of_sums = (
        jnp.sum(dz_ref[...].astype(FP32), axis=0, keepdims=True),
        jnp.sum(grad_out, axis=0, keepdims=True),
        gain_sum[None, :],
        shift_sum[None, :],
    )
    for n, row in enumerate(rows_of_sums):
        for f in range(parts):
            sums_ref[f, 0:1, shard * n : shard * (n + 1)] = row[:, shard * f : shard * (f + 1)]


def weight_grad_kernel(where, mine_ref, other_ref, small_ref, keep_ref, send_ref, fc_ref):
    rows = mine_ref.shape[0]
    features = keep_ref.shape[2]
    part, core, chip = where[0], where[1], where[2]
    near, across = 1 + core, 2 - core
    parts = 4
    shard, half_columns = features // parts, features // 2
    h_start = 2 * parts * half_columns
    a_start = h_start + features
    y_start = a_start + features
    z_start = y_start + features

    def product(left, right):
        return contract_rows(mine_ref[:, left], mine_ref[:, right]) + contract_rows(
            other_ref[:, left], other_ref[:, right]
        )

    targets = [(keep_ref, 0, part), (keep_ref, 1, part ^ across)]
    targets += [(send_ref, 0, part ^ near), (send_ref, 1, part ^ 3)]
    fc_base = parts * half_columns
    for j in range(2):
        fc_ref[j] = product(
            pl.ds(h_start, features), pl.ds(fc_base + features * j, features)
        ).astype(BF16)
    out_base = half_columns + 2 * shard
    small_base = out_base + shard // 2
    for ref, slot, owner in targets:
        g_span = pl.ds(pl.multiple_of(owner * half_columns, 128), half_columns)
        ref[slot, 0:half_columns, :] = product(g_span, pl.ds(y_start, features)).astype(BF16)
        for j in range(2):
            first = half_columns + shard * j
            ref[slot, first : first + shard, :] = fc_ref[
                j, pl.ds(pl.multiple_of(owner * shard, 16), shard), :
            ]
        ref[slot, small_base : small_base + 16, :] = small_ref[owner].astype(BF16)
        ref[slot, small_base + 16 :, :] = jnp.zeros_like(ref[slot, small_base + 16 :, :])
    for s in range(parts):
        block = product(
            pl.ds(a_start + shard * s, shard), pl.ds(z_start, half_columns)
        ).astype(BF16)
        owner = chip ^ s
        for ref, slot, wanted in targets:

            @pl.when(owner == wanted)
            def store_block():
                ref[slot, out_base:small_base, 0:half_columns] = block[: shard // 2]
                ref[slot, out_base:small_base, half_columns:] = block[shard // 2 :]


def qkv_grad_kernel(
    where,
    normed_ref,
    p0,
    p1,
    p2,
    p3,
    wq_ref,
    wk_ref,
    wv_ref,
    gain_ref,
    shift_ref,
    keep_ref,
    send_ref,
    total_ref,
):
    blocks, rows, features = normed_ref.shape
    width = wq_ref.shape[1]
    part, core, chip = where[0], where[1], where[2]
    near, across = 1 + core, 2 - core
    parts = 4
    shard = features // parts
    half = shard // 2
    column_sums = [jnp.zeros((1, width), FP32) for n in range(3)]
    for n in range(3):
        total = jnp.zeros((features, width), FP32)
        for b in range(blocks):
            grads = (p0, p1, p2, p3)[b][:, width * n : width * (n + 1)]
            total = total + contract_rows(normed_ref[chip ^ b], grads)
            column_sums[n] = column_sums[n] + jnp.sum(grads.astype(FP32), axis=0, keepdims=True)
        total_ref[:, width * n : width * (n + 1)] = total
    sums = jnp.concatenate(column_sums, axis=1)
    shift_grad = jnp.zeros((features, 1), FP32)
    gain_grad = jnp.zeros((features, 1), FP32)
    for n, ref in enumerate((wq_ref, wk_ref, wv_ref)):
        wide = ref[...].astype(FP32)
        shift_grad = shift_grad + jnp.sum(wide * column_sums[n], axis=1, keepdims=True)
        gain_grad = gain_grad + jnp.sum(
            wide * total_ref[:, width * n : width * (n + 1)], axis=1, keepdims=True
        )
    gain_grad = (gain_grad - shift_ref[...] * shift_grad) / gain_ref[...]
    columns = jnp.concatenate(
        [gain_grad, shift_grad, jnp.zeros((features, 126), FP32)], axis=1
    )
    norm_rows = columns.T[0:8]
    order = [part, part ^ across, part ^ near, part ^ 3]
    other_order = [part, part ^ near, part ^ across, part ^ 3]
    for ref, which, owners in ((keep_ref, core, order), (send_ref, 1 - core, other_order)):
        for slot in range(parts):
            owner = owners[slot]
            first = pl.multiple_of(owner * shard + which * half, 16)
            ref[slot, 0:half, :] = total_ref[pl.ds(first, half), :].astype(ref.dtype)
            picked = jnp.zeros((8, shard), FP32)
            for f in range(parts):
                picked = jnp.where(owner == f, norm_rows[:, shard * f : shard * (f + 1)], picked)
            row = lax.broadcasted_iota(jnp.int32, (8, 3 * width), 0)
            packed = jnp.concatenate([picked, jnp.zeros((8, 3 * width - shard), FP32)], axis=1)
            tail = jnp.where(row < 2, packed, jnp.where(row == 2, sums, 0.0))
            tail = jnp.concatenate([tail, jnp.zeros_like(tail)], axis=0)
            ref[slot, half : half + 16, :] = tail.astype(ref.dtype)


def relay_kernel(where, keep_ref, theirs_ref, relay_ref):
    relay_ref[...] = (keep_ref[1].astype(FP32) + theirs_ref[1].astype(FP32)).astype(BF16)


def pair_kernel(where, keep_ref, theirs_ref, last_ref, stay_ref, give_ref):
    low = where[2] % 2
    count = stay_ref.shape[0]
    for ref, which in ((stay_ref, low), (give_ref, 1 - low)):
        span = pl.ds(pl.multiple_of(which * count, 16), count)
        total = keep_ref[0, span, :].astype(FP32) + theirs_ref[0, span, :].astype(FP32)
        ref[...] = (total + last_ref[span, :].astype(FP32)).astype(ref.dtype)


def quad_kernel(where, stay_ref, arrived_ref, keep_ref, give_ref):
    high = where[2] // 2
    count = keep_ref.shape[0]
    for ref, which in ((keep_ref, high), (give_ref, 1 - high)):
        span = pl.ds(pl.multiple_of(which * count, 16), count)
        total = stay_ref[span, :] + arrived_ref[span, :].astype(FP32)
        ref[...] = total.astype(ref.dtype)


def total_kernel(where, keep_ref, arrived_ref, out_ref):
    out_ref[...] = (keep_ref[...] + arrived_ref[...].astype(FP32)).astype(BF16)


def join_kernel(where, mine_ref, arrived_ref, out_ref):
    high = where[2] // 2
    count = mine_ref.shape[0]
    out_ref[pl.ds(pl.multiple_of(high * count, 16), count), :] = mine_ref[...]
    out_ref[pl.ds(pl.multiple_of((1 - high) * count, 16), count), :] = arrived_ref[...]


def input_grad_kernel(
    where, p0, p1, p2, p3, w_ref, tokens_ref, dx_ref, gain_ref, shift_ref, out_ref, packed_ref
):
    chip = where[2]
    features = w_ref.shape[0]
    width = p0.shape[1] // 3
    for z in range(4):
        for s, piece in enumerate((p0, p1, p2, p3)):

            @pl.when(chip == z ^ s)
            def place_piece():
                for n in range(3):
                    first = features * n + width * z
                    packed_ref[:, first : first + width] = piece[:, width * n : width * (n + 1)]

    total = dot_nt(packed_ref[...], w_ref[...])
    unit, inverse = layer_norm(tokens_ref[...].astype(FP32), gain_ref[...], shift_ref[...])[1:]
    out_ref[...] = dx_ref[...] + norm_back(total, unit, inverse, gain_ref[...])[0]


def output_kernel(
    where, m0, m1, t0, t1, proj_ref, fc_ref, out_ref, sums_ref, mine_ref, other_ref
):
    core, low = where[1], where[2] % 2
    count = m0.shape[0]
    for n, (mine, other) in enumerate(((m0, t0), (m1, t1))):
        span = pl.ds(pl.multiple_of((low if n == 0 else 1 - low) * count, 16), count)
        mine_ref[span, :] = mine[...]
        other_ref[span, :] = other[...]
    half_columns = proj_ref.shape[0] // 2
    shard, features = out_ref.shape
    out_rows = half_columns + 2 * shard
    small_at = out_rows + shard // 2
    sums_ref[...] = mine_ref[small_at : small_at + 16, :].astype(FP32) + other_ref[
        small_at : small_at + 16, :
    ].astype(FP32)

    def place(ref, which):
        proj_ref[which * half_columns : (which + 1) * half_columns, :] = ref[
            0:half_columns, :
        ].astype(FP32)
        for j in range(2):
            first = half_columns + shard * j
            column = features * (2 * which + j)
            fc_ref[:, column : column + features] = ref[first : first + shard, :].astype(FP32)
        span = slice(features // 2 * which, features // 2 * (which + 1))
        middle = out_rows + shard // 2
        out_ref[0 : shard // 2, span] = ref[out_rows:middle, 0 : features // 2].astype(FP32)
        out_ref[shard // 2 :, span] = ref[out_rows:middle, features // 2 :].astype(FP32)

    @pl.when(core == 0)
    def first_core():
        place(mine_ref, 0)
        place(other_ref, 1)

    @pl.when(core == 1)
    def second_core():
        place(mine_ref, 1)
        place(other_ref, 0)


def qkv_output_kernel(where, h0, h1, h2, h3, out_ref, extra_ref):
    core, chip = where[1], where[2]
    shard, wide = out_ref.shape
    features = wide // 3
    half = shard // 2
    width = h0.shape[2] // 3
    for s, ref in enumerate((h0, h1, h2, h3)):
        extra_ref[chip ^ s] = jnp.where(
            core == 0, ref[0, half : half + 16, :], ref[1, half : half + 16, :]
        ).astype(FP32)
        for z in range(4):

            @pl.when(chip == z ^ s)
            def place_piece():
                for n in range(3):
                    first = features * n + width * z
                    for slot, which in ((0, core), (1, 1 - core)):
                        rows = pl.ds(pl.multiple_of(which * half, 8), half)
                        out_ref[rows, first : first + width] = ref[
                            slot, 0:half, width * n : width * (n + 1)
                        ].astype(FP32)


def fast_body(
    tokens,
    cotangent,
    w_qkv,
    b_query,
    b_value,
    w_out,
    b_out,
    w_fc,
    b_fc,
    w_proj,
    b_proj,
    gain1,
    shift1,
    gain2,
    shift2,
    counts,
    seq_lengths,
):
    rows, features = tokens.shape
    ctx = lax.axis_size("ctx")
    fsdp = lax.axis_size("fsdp")
    chips = ctx // 2
    group_heads = HEADS // chips
    width = features // chips
    shard = features // fsdp
    hidden_width = w_fc.shape[1]
    columns = hidden_width // fsdp
    place = lax.axis_index("ctx")
    chip = place // 2
    core = place % 2
    part = lax.axis_index("fsdp")
    near = 1 + core
    across = 2 - core
    where = jnp.stack([part, core, chip]).astype(jnp.int32)

    def exchange(value, partner):
        pairs = [
            (f * ctx + c, g * ctx + d)
            for f in range(fsdp)
            for c in range(ctx)
            for g, d in [partner(f, c)]
        ]
        return lax.ppermute(value, ("fsdp", "ctx"), pairs)

    def to_near(value):
        return exchange(value, lambda f, c: (f ^ (1 + c % 2), c))

    def to_across(value):
        return exchange(value, lambda f, c: (f ^ (2 - c % 2), c))

    def to_core(value):
        return exchange(value, lambda f, c: (f, c ^ 1))

    def to_chip(value, step):
        return exchange(value, lambda f, c: (f, c ^ (2 * step)))

    def pick(array, index, axis=0):
        return lax.dynamic_index_in_dim(array, index, axis, keepdims=False)

    def place_all(shape, dtype, items):
        buffer = jnp.zeros(shape, dtype)
        for index, value in items:
            full = value.reshape((1,) * (len(shape) - value.ndim) + value.shape)
            starts = tuple(index) + (0,) * (len(shape) - len(index))
            buffer = lax.dynamic_update_slice(buffer, full.astype(dtype), starts)
        return buffer

    half = shard // 2
    fc_half = lax.dynamic_slice_in_dim(w_fc, core * half, half, 0)
    bundle = jnp.concatenate(
        [
            lax.dynamic_slice_in_dim(w_proj, core * (columns // 2), columns // 2, 0),
            lax.dynamic_slice_in_dim(w_out, core * half, half, 0),
        ]
        + [fc_half[:, columns * j : columns * (j + 1)] for j in range(fsdp)],
        axis=0,
    )

    blocks = [tokens] + [to_chip(tokens, s) for s in (1, 2, 3)]
    near_pair = to_core(jnp.stack(blocks[:2]))
    far_pair = to_core(jnp.stack(blocks[2:]))
    beside = [near_pair[0], near_pair[1], far_pair[0], far_pair[1]]
    bundles = lax.all_gather(bundle, "fsdp", axis=0)

    count_row = counts[0]
    offsets = jnp.cumsum(count_row) - count_row
    seq_ends = jnp.cumsum(seq_lengths[0])
    within = jnp.arange(rows, dtype=jnp.int32)
    slot = jnp.arange(ctx, dtype=jnp.int32)[:, None] * rows + within[None, :]
    live = within[None, :] < count_row[:, None]
    places = offsets[:, None] + within[None, :]
    starts = jnp.max(
        jnp.where(places[:, :, None] >= seq_ends[None, None, :], seq_ends[None, None, :], 0), axis=2
    )
    dead_id = -1 - slot
    key_ids = jnp.where(live, places, dead_id)
    lows = jnp.where(live, starts, dead_id)
    fars = jnp.where(live, starts, NEVER)
    key_tile = jnp.broadcast_to(key_ids[:, :, None], (ctx, rows, 128))

    def own_parity(array):
        return pick(array.reshape((chips, 2) + array.shape[1:]), core, 1)

    low_rows = own_parity(lows)[:, None, :]
    high_rows = own_parity(key_ids)[:, None, :]
    far_rows = own_parity(fars)[:, None, :]
    live_rows = (within < pick(count_row, place)).astype(FP32)[:, None]

    smalls = jnp.concatenate(
        [b_query, b_value, b_out, b_proj, gain1, shift1, gain2, shift2, b_fc]
    ).reshape(1, -1)
    mine = jnp.concatenate(
        [
            lax.dynamic_slice_in_dim(w_qkv, core * half, half, 0),
            jnp.pad(smalls, ((0, 15), (0, 0))),
        ],
        axis=0,
    )
    from_near, from_across = to_near(mine), to_across(mine)
    from_far = to_across(from_near)
    swapped = to_core(jnp.stack([from_near, from_across, from_far])[:, :half])
    qkv_full = place_all(
        (fsdp, 2, half, 3 * features),
        BF16,
        [
            ((part, 0), w_qkv.reshape(2, half, -1)),
            ((part ^ near, core), from_near[:half]),
            ((part ^ across, core), from_across[:half]),
            ((part ^ 3, core), from_far[:half]),
            ((part ^ across, 1 - core), swapped[0]),
            ((part ^ near, 1 - core), swapped[1]),
            ((part ^ 3, 1 - core), swapped[2]),
        ],
    ).reshape(features, 3 * features)
    own_weights = tuple(
        lax.dynamic_slice(qkv_full, (0, features * n + width * chip), (features, width))
        for n in range(3)
    )
    small_all = place_all(
        (fsdp, smalls.shape[1]),
        BF16,
        [
            ((part,), smalls[0]),
            ((part ^ near,), from_near[half]),
            ((part ^ across,), from_across[half]),
            ((part ^ 3,), from_far[half]),
        ],
    ).astype(FP32)
    vectors = [small_all[:, n * shard : (n + 1) * shard].reshape(1, -1) for n in range(8)]
    bias_q, bias_v, bias_out, bias_proj, gain_one, shift_one, gain_two, shift_two = vectors
    bias_fc = small_all[:, 8 * shard :].reshape(1, -1)

    own_bias_q = lax.dynamic_slice_in_dim(bias_q, chip * width, width, 1)
    own_bias_v = lax.dynamic_slice_in_dim(bias_v, chip * width, width, 1)
    normal = own_weights + (own_bias_q, own_bias_v, gain_one, shift_one)
    half_stores = kernel_call(
        project_kernel,
        [
            jax.ShapeDtypeStruct((chips // 2, rows, width), BF16),
            jax.ShapeDtypeStruct((chips, rows, width), BF16),
            jax.ShapeDtypeStruct((chips, width, rows), BF16),
            jax.ShapeDtypeStruct((chips, rows, width), BF16),
            jax.ShapeDtypeStruct((chips, width, rows), BF16),
            jax.ShapeDtypeStruct((chips // 2, rows, features), BF16),
        ],
        [],
        (where, blocks[0], beside[0], blocks[1], beside[1]) + normal,
        5,
    )
    queries, keys, keys_t, values, normed_mine, *rest = kernel_call(
        attend_kernel,
        [
            jax.ShapeDtypeStruct((chips, rows, width), BF16),
            jax.ShapeDtypeStruct((ctx, rows, width), BF16),
            jax.ShapeDtypeStruct((ctx, width, rows), BF16),
            jax.ShapeDtypeStruct((ctx, rows, width), BF16),
            jax.ShapeDtypeStruct((chips, rows, features), BF16),
        ]
        + [jax.ShapeDtypeStruct((rows, width), BF16)] * 4
        + [
            jax.ShapeDtypeStruct((chips, width, rows), FP32),
            jax.ShapeDtypeStruct((chips, 8, rows), FP32),
            jax.ShapeDtypeStruct((16, 128), BF16),
        ],
        [
            pltpu.VMEM((ctx, width, rows), BF16),
            pltpu.VMEM((width, rows), FP32),
            pltpu.VMEM((chips, rows, width), BF16),
        ],
        (where, blocks[2], beside[2], blocks[3], beside[3])
        + normal
        + tuple(half_stores)
        + (key_tile, low_rows, high_rows, far_rows),
        30,
    )
    attended_t, logs, zeros = rest[4:]

    def swap_chips(pieces):
        return [pieces[0]] + [to_chip(pieces[s], s) for s in (1, 2, 3)]

    bundles = lax.dynamic_update_slice(bundles, (bundles[0, :16, :128] + zeros)[None], (0, 0, 0))
    bundles_other = to_core(bundles)
    attended = swap_chips(rest[:4])
    bundle_width = 2 * hidden_width // 2 + 3 * features + features // 2
    hbm = pl.BlockSpec(memory_space=pl.ANY)
    block_out, grad_middle, d0, d1, d2, d3, bundle_mine, bundle_send, small_rows = kernel_call(
        middle_kernel,
        [
            jax.ShapeDtypeStruct((rows, features), BF16),
            jax.ShapeDtypeStruct((rows, features), FP32),
        ]
        + [jax.ShapeDtypeStruct((rows, width), BF16)] * 4
        + [
            jax.ShapeDtypeStruct((rows, bundle_width), BF16),
            jax.ShapeDtypeStruct((rows, bundle_width), BF16),
            jax.ShapeDtypeStruct((fsdp, 16, features), FP32),
        ],
        [
            pltpu.VMEM((features, features), BF16),
            pltpu.VMEM((fsdp, features, columns), BF16),
            pltpu.VMEM((hidden_width, features), BF16),
            pltpu.VMEM((rows, columns), BF16),
            pltpu.VMEM((rows, features), BF16),
            pltpu.SemaphoreType.DMA((8 * 6,)),
        ],
        tuple([where] + attended)
        + (
            tokens,
            cotangent,
            live_rows,
            bias_out,
            gain_two,
            shift_two,
            bias_fc,
            bias_proj,
            bundles,
            bundles_other,
        ),
        21,
        special={13: hbm, 14: hbm},
    )

    grad_blocks = swap_chips([d0, d1, d2, d3])

    bundle_other = to_core(bundle_send)
    out_rows = columns // 2 + 2 * shard
    small_at = out_rows + half
    block_rows = small_at + 32
    pair_shape = jax.ShapeDtypeStruct((2, block_rows, features), BF16)
    grads_keep, grads_send = kernel_call(
        weight_grad_kernel,
        [pair_shape, pair_shape],
        [pltpu.VMEM((2, features, features), BF16)],
        (where, bundle_mine, bundle_other, small_rows),
        14,
        after=(grad_blocks[1],),
    )

    grad_query, grad_keep, grad_send = kernel_call(
        attend_back_kernel,
        [
            jax.ShapeDtypeStruct((chips, rows, width), BF16),
            jax.ShapeDtypeStruct((chips, rows, 2 * width), FP32),
            jax.ShapeDtypeStruct((chips, rows, 2 * width), BF16),
        ],
        [
            pltpu.VMEM((width, rows), FP32),
            pltpu.VMEM((group_heads, ctx, rows, 64), FP32),
            pltpu.VMEM((group_heads, ctx, rows, 64), FP32),
            pltpu.VMEM((chips, rows, width), BF16),
        ],
        (
            where,
            queries,
            keys,
            keys_t,
            values,
            *grad_blocks,
            key_tile,
            low_rows,
            high_rows,
            far_rows,
            attended_t,
            logs,
        ),
        30,
    )
    packed = kernel_call(
        pack_kernel,
        [jax.ShapeDtypeStruct((rows, 3 * width), BF16)] * 4,
        [],
        (where, grad_query, grad_keep, to_core(grad_send)),
        2,
    )

    arrived = swap_chips(packed)
    (grad_tokens,) = kernel_call(
        input_grad_kernel,
        [jax.ShapeDtypeStruct((rows, features), FP32)],
        [pltpu.VMEM((rows, 3 * features), BF16)],
        tuple([where] + arrived) + (qkv_full, tokens, grad_middle, gain_one, shift_one),
        5,
    )

    def add_up(left_side, right_side):
        return left_side.astype(FP32) + right_side.astype(FP32)

    def scatter_parts(keep, send):
        theirs = to_near(send)
        last = to_across(add_up(keep[1], theirs[1]).astype(BF16))
        return (add_up(keep[0], theirs[0]) + last.astype(FP32)).astype(BF16)

    theirs = to_near(grads_send)
    block = jax.ShapeDtypeStruct((block_rows, features), BF16)

    def shaped(count, dtype):
        return jax.ShapeDtypeStruct((count, features), dtype)

    (relay,) = kernel_call(
        relay_kernel, [block], [], (where, grads_keep, theirs), 1, after=(grad_query,)
    )
    stay, give = kernel_call(
        pair_kernel,
        [shaped(block_rows // 2, FP32), shaped(block_rows // 2, BF16)],
        [],
        (where, grads_keep, theirs, to_across(relay)),
        2,
    )
    stay, give = kernel_call(
        quad_kernel,
        [shaped(block_rows // 4, FP32), shaped(block_rows // 4, BF16)],
        [],
        (where, stay, to_chip(give, 1)),
        2,
    )
    (quad,) = kernel_call(
        total_kernel, [shaped(block_rows // 4, BF16)], [], (where, stay, to_chip(give, 2)), 1
    )
    (joined,) = kernel_call(
        join_kernel, [shaped(block_rows // 2, BF16)], [], (where, quad, to_chip(quad, 2)), 1
    )
    joined_next = to_chip(joined, 1)
    d_proj, d_fc, d_out, small_sums = kernel_call(
        output_kernel,
        [
            jax.ShapeDtypeStruct((columns, features), FP32),
            jax.ShapeDtypeStruct((shard, hidden_width), FP32),
            jax.ShapeDtypeStruct((shard, features), FP32),
            jax.ShapeDtypeStruct((16, features), FP32),
        ],
        [pltpu.VMEM((block_rows, features), BF16), pltpu.VMEM((block_rows, features), BF16)],
        (where, joined, joined_next, to_core(joined), to_core(joined_next)),
        2,
    )
    d_bias_out, d_bias_proj, d_gain_two, d_shift_two = (
        small_sums[0, n * shard : (n + 1) * shard] for n in range(4)
    )
    d_bias_fc = small_sums[1]

    block_shape = (fsdp, half + 16, 3 * width)
    qkv_keep, qkv_send = kernel_call(
        qkv_grad_kernel,
        [jax.ShapeDtypeStruct(block_shape, FP32), jax.ShapeDtypeStruct(block_shape, BF16)],
        [pltpu.VMEM((features, 3 * width), FP32)],
        (
            where,
            normed_mine,
            *packed,
            *own_weights,
            gain_one.reshape(-1, 1),
            shift_one.reshape(-1, 1),
        ),
        8,
        after=tuple(arrived[1:]),
    )
    qkv_blocks = add_up(qkv_keep, to_core(qkv_send)).astype(BF16)
    qkv_half = scatter_parts(qkv_blocks[:2], qkv_blocks[2:])
    halves = swap_chips([jnp.stack([qkv_half, to_core(qkv_half)])] * 4)
    d_qkv, extra = kernel_call(
        qkv_output_kernel,
        [
            jax.ShapeDtypeStruct((shard, 3 * features), FP32),
            jax.ShapeDtypeStruct((chips, 16, 3 * width), FP32),
        ],
        [],
        tuple([where] + halves),
        2,
    )
    owner_extra = pick(extra, part)
    d_bias_q = owner_extra[2, :width]
    d_bias_v = owner_extra[2, 2 * width :]
    norm_total = jnp.sum(extra[:, :2, :shard], axis=0)
    d_gain_one = norm_total[0]
    d_shift_one = norm_total[1]

    return (
        block_out,
        grad_tokens,
        d_qkv,
        d_bias_q,
        d_bias_v,
        d_out,
        d_bias_out,
        d_fc,
        d_bias_fc,
        d_proj,
        d_bias_proj,
        d_gain_one,
        d_shift_one,
        d_gain_two,
        d_shift_two,
    )


def solution(mesh):
    in_specs = (
        P(("fsdp", "ctx"), None),
        P(("fsdp", "ctx"), None),
        P("fsdp", None),
        P("fsdp"),
        P("fsdp"),
        P("fsdp", None),
        P("fsdp"),
        P("fsdp", None),
        P("fsdp"),
        P("fsdp", None),
        P("fsdp"),
        P("fsdp"),
        P("fsdp"),
        P("fsdp"),
        P("fsdp"),
        P("fsdp", None),
        P("fsdp", None),
    )
    out_specs = (
        P(("fsdp", "ctx"), None),
        P(("fsdp", "ctx"), None),
        P("fsdp", None),
        P("fsdp"),
        P("fsdp"),
        P("fsdp", None),
        P("fsdp"),
        P("fsdp", None),
        P("fsdp"),
        P("fsdp", None),
        P("fsdp"),
        P("fsdp"),
        P("fsdp"),
        P("fsdp"),
        P("fsdp"),
    )
    ctx = mesh.shape["ctx"]
    four_by_four = mesh.shape["fsdp"] == 4 and ctx == 8 and HEADS % (ctx // 2) == 0
    body = fast_body if four_by_four else general_body
    return jax.shard_map(body, mesh=mesh, in_specs=in_specs, out_specs=out_specs, check_vma=False)
```

```python
import functools

import jax
import jax.numpy as jnp
from jax import lax
from jax.experimental import pallas as pl
from jax.experimental.pallas import tpu as pltpu
from jax.sharding import PartitionSpec as P

HEADS = 12


EPS = 1e-05


def layer_norm(values, gain_row, shift_row):
    centre = values - jnp.mean(values, axis=1, keepdims=True)
    inverse = lax.rsqrt(jnp.mean(centre * centre, axis=1, keepdims=True) + EPS)
    normed = centre * inverse
    return (normed * gain_row + shift_row, normed, inverse)


def norm_back(grad_in, normed, inverse, gain_row):
    scaled = grad_in * gain_row
    inner_grad = inverse * (
        scaled
        - jnp.mean(scaled, axis=1, keepdims=True)
        - normed * jnp.mean(scaled * normed, axis=1, keepdims=True)
    )
    return (inner_grad, jnp.sum(grad_in * normed, axis=0), jnp.sum(grad_in, axis=0))


def contract_rows(left_side, right_side):
    return lax.dot_general(
        left_side, right_side, (((0,), (0,)), ((), ())), preferred_element_type=jnp.float32
    )


def times_transpose(left_side, right_side):
    return lax.dot_general(
        left_side, right_side, (((1,), (1,)), ((), ())), preferred_element_type=jnp.float32
    )


def gelu_tanh(values):
    return jax.nn.gelu(values, approximate=True)


def describe(slot_ids, row_count, count_row, offsets, seq_ends):
    peer_count = count_row.shape[0]
    device = slot_ids // row_count
    within = slot_ids - device * row_count
    matches = device[:, None] == jnp.arange(peer_count, dtype=jnp.int32)[None, :]
    live_count = jnp.sum(jnp.where(matches, count_row[None, :], 0), axis=1)
    first_place = jnp.sum(jnp.where(matches, offsets[None, :], 0), axis=1)
    places = first_place + within
    segment = jnp.sum((places[:, None] >= seq_ends[None, :]).astype(jnp.int32), axis=1)
    return (within < live_count, places, segment, slot_ids)


def allowed(query_info, key_info):
    q_live, q_place, q_seg, q_slot = query_info
    k_live, k_place, k_seg, k_slot = key_info
    same_seq = (
        q_live[:, None]
        & k_live[None, :]
        & (q_seg[:, None] == k_seg[None, :])
        & (k_place[None, :] <= q_place[:, None])
    )
    return same_seq | (q_slot[:, None] == k_slot[None, :])


def over_blocks(step_fn, status, pieces, row_count):
    total_rows = pieces[0].shape[0]
    block_total = total_rows // row_count
    stacked = tuple((piece.reshape((block_total, row_count) + piece.shape[1:]) for piece in pieces))

    def scan_body(state_now, scan_item):
        block_index, block_parts = scan_item
        return (step_fn(state_now, block_parts, block_index * row_count), None)

    status, unused = lax.scan(
        scan_body, status, (jnp.arange(block_total, dtype=jnp.int32), stacked)
    )
    return status


def score_grads(
    query_heads, key_heads, value_heads, grad_heads, lse_rows, delta_rows, permitted, scaling
):
    scores = (
        jnp.einsum("qhd,khd->hqk", query_heads, key_heads, preferred_element_type=jnp.float32)
        * scaling
    )
    probabilities = jnp.where(permitted[None], jnp.exp(scores - lse_rows[:, :, None]), 0.0)
    grad_probs = jnp.einsum(
        "qhd,khd->hqk", grad_heads, value_heads, preferred_element_type=jnp.float32
    )
    grad_scores = (probabilities * (grad_probs - delta_rows[:, :, None])).astype(jnp.bfloat16)
    return (probabilities.astype(jnp.bfloat16), grad_scores)


def general_body(
    tokens,
    cotangent,
    w_qkv,
    b_query,
    b_value,
    w_out,
    b_out,
    w_fc,
    b_fc,
    w_proj,
    b_proj,
    gain1,
    shift1,
    gain2,
    shift2,
    counts,
    seq_lengths,
):
    row_count, feature_count = tokens.shape
    peer_count = lax.axis_size("ctx")
    my_index = lax.axis_index("ctx")
    head_count = HEADS
    head_width = feature_count // head_count
    scaling = head_width ** (-0.5)
    count_row = counts[0]
    offsets = jnp.cumsum(count_row) - count_row
    seq_ends = jnp.cumsum(seq_lengths[0])

    def locate(first_slot, length):
        return describe(
            first_slot + jnp.arange(length, dtype=jnp.int32),
            row_count,
            count_row,
            offsets,
            seq_ends,
        )

    own_rows = locate(my_index * row_count, row_count)
    fp32 = jnp.float32
    bf16 = jnp.bfloat16
    (
        qkv_full,
        query_bias,
        value_bias,
        out_full,
        out_bias,
        fc_full,
        fc_bias,
        proj_full,
        proj_bias,
        gain_one,
        shift_one,
        gain_two,
        shift_two,
    ) = (
        lax.all_gather(w_qkv, "fsdp", axis=0, tiled=True),
        lax.all_gather(b_query, "fsdp", axis=0, tiled=True),
        lax.all_gather(b_value, "fsdp", axis=0, tiled=True),
        lax.all_gather(w_out, "fsdp", axis=0, tiled=True),
        lax.all_gather(b_out, "fsdp", axis=0, tiled=True),
        lax.all_gather(w_fc, "fsdp", axis=0, tiled=True),
        lax.all_gather(b_fc, "fsdp", axis=0, tiled=True),
        lax.all_gather(w_proj, "fsdp", axis=0, tiled=True),
        lax.all_gather(b_proj, "fsdp", axis=0, tiled=True),
        lax.all_gather(gain1, "fsdp", axis=0, tiled=True),
        lax.all_gather(shift1, "fsdp", axis=0, tiled=True),
        lax.all_gather(gain2, "fsdp", axis=0, tiled=True),
        lax.all_gather(shift2, "fsdp", axis=0, tiled=True),
    )
    inputs = tokens.astype(fp32)
    normed_one, unit_one, inverse_one = layer_norm(
        inputs, gain_one.astype(fp32), shift_one.astype(fp32)
    )
    normed_low = normed_one.astype(bf16)
    bias_row = jnp.concatenate([query_bias, jnp.zeros_like(query_bias), value_bias]).astype(fp32)
    packed = (jnp.dot(normed_low, qkv_full, preferred_element_type=fp32) + bias_row).astype(bf16)
    query_rows = packed[:, :feature_count]
    key_rows = packed[:, feature_count : 2 * feature_count]
    value_rows = packed[:, 2 * feature_count :]
    query_heads = query_rows.reshape(row_count, head_count, head_width)

    def forward_step(status, pieces, first_row):
        running_max, running_sum, running_acc = status
        key_piece, value_piece = pieces
        length = key_piece.shape[0]
        key_heads = key_piece.reshape(length, head_count, head_width)
        value_heads = value_piece.reshape(length, head_count, head_width)
        scores = (
            jnp.einsum("qhd,khd->hqk", query_heads, key_heads, preferred_element_type=fp32)
            * scaling
        )
        permitted = allowed(own_rows, locate(first_row, length))
        scores = jnp.where(permitted[None], scores, -jnp.inf)
        new_max = jnp.maximum(running_max, jnp.max(scores, axis=2))
        fading = jnp.exp(running_max - new_max)
        weights = jnp.exp(scores - new_max[:, :, None])
        running_sum = running_sum * fading + jnp.sum(weights, axis=2)
        update = jnp.einsum(
            "hqk,khd->qhd", weights.astype(bf16), value_heads, preferred_element_type=fp32
        )
        running_acc = running_acc * jnp.transpose(fading)[:, :, None] + update
        return (new_max, running_sum, running_acc)

    start_state = (
        jnp.full((head_count, row_count), -1e30, fp32),
        jnp.zeros((head_count, row_count), fp32),
        jnp.zeros((row_count, head_count, head_width), fp32),
    )
    final_max, final_sum, final_acc = over_blocks(
        forward_step,
        start_state,
        (
            lax.all_gather(key_rows, "ctx", axis=0, tiled=True),
            lax.all_gather(value_rows, "ctx", axis=0, tiled=True),
        ),
        row_count,
    )
    attended_heads = final_acc / jnp.transpose(final_sum)[:, :, None]
    attended = attended_heads.reshape(row_count, feature_count)
    log_total = final_max + jnp.log(final_sum)
    attended_low = attended.astype(bf16)
    middle = (
        inputs
        + jnp.dot(attended_low, out_full, preferred_element_type=fp32)
        + out_bias.astype(fp32)
    )
    normed_two, unit_two, inverse_two = layer_norm(
        middle, gain_two.astype(fp32), shift_two.astype(fp32)
    )
    normed_two_low = normed_two.astype(bf16)
    hidden = jnp.dot(normed_two_low, fc_full, preferred_element_type=fp32) + fc_bias.astype(fp32)
    activated = gelu_tanh(hidden).astype(bf16)
    output = (
        middle + jnp.dot(activated, proj_full, preferred_element_type=fp32) + proj_bias.astype(fp32)
    )
    output_low = output.astype(bf16)
    qkv_full, out_full, fc_full, proj_full, gain_one, gain_two = (
        lax.all_gather(w_qkv, "fsdp", axis=0, tiled=True),
        lax.all_gather(w_out, "fsdp", axis=0, tiled=True),
        lax.all_gather(w_fc, "fsdp", axis=0, tiled=True),
        lax.all_gather(w_proj, "fsdp", axis=0, tiled=True),
        lax.all_gather(gain1, "fsdp", axis=0, tiled=True),
        lax.all_gather(gain2, "fsdp", axis=0, tiled=True),
    )
    live_rows = own_rows[0].astype(fp32)[:, None]
    grad_out = cotangent.astype(fp32) * live_rows
    grad_out_low = grad_out.astype(bf16)
    grad_proj = contract_rows(activated, grad_out_low)
    grad_proj_bias = jnp.sum(grad_out, axis=0)
    grad_act = times_transpose(grad_out_low, proj_full)
    grad_hidden = jax.vjp(gelu_tanh, hidden)[1](grad_act)[0]
    grad_hidden_low = grad_hidden.astype(bf16)
    grad_fc = contract_rows(normed_two_low, grad_hidden_low)
    grad_fc_bias = jnp.sum(grad_hidden_low.astype(fp32), axis=0)
    grad_normed_two = times_transpose(grad_hidden_low, fc_full)
    grad_mid_norm, grad_gain_two, grad_shift_two = norm_back(
        grad_normed_two, unit_two, inverse_two, gain_two.astype(fp32)
    )
    grad_middle = grad_out + grad_mid_norm
    grad_middle_low = grad_middle.astype(bf16)
    grad_out_proj = contract_rows(attended_low, grad_middle_low)
    grad_out_bias = jnp.sum(grad_middle_low.astype(fp32), axis=0)
    grad_attended = times_transpose(grad_middle_low, out_full).astype(bf16)
    grad_heads = grad_attended.reshape(row_count, head_count, head_width)
    delta_rows = jnp.transpose(jnp.sum(grad_heads.astype(fp32) * attended_heads, axis=2))

    def back_step(status, pieces, first_row):
        grad_query, grad_keys = status
        key_piece, value_piece = pieces
        length = key_piece.shape[0]
        key_heads = key_piece.reshape(length, head_count, head_width)
        value_heads = value_piece.reshape(length, head_count, head_width)
        permitted = allowed(own_rows, locate(first_row, length))
        probs_low, grad_scores = score_grads(
            query_heads,
            key_heads,
            value_heads,
            grad_heads,
            log_total,
            delta_rows,
            permitted,
            scaling,
        )
        grad_query = (
            grad_query
            + jnp.einsum("hqk,khd->qhd", grad_scores, key_heads, preferred_element_type=fp32)
            * scaling
        )
        grad_key_part = (
            jnp.einsum("hqk,qhd->khd", grad_scores, query_heads, preferred_element_type=fp32)
            * scaling
        )
        grad_value_part = jnp.einsum(
            "hqk,qhd->khd", probs_low, grad_heads, preferred_element_type=fp32
        )
        joined = jnp.concatenate(
            [
                grad_key_part.reshape(length, feature_count),
                grad_value_part.reshape(length, feature_count),
            ],
            axis=1,
        )
        current = lax.dynamic_slice_in_dim(grad_keys, first_row, length, 0)
        grad_keys = lax.dynamic_update_slice_in_dim(grad_keys, current + joined, first_row, 0)
        return (grad_query, grad_keys)

    keys_start = jnp.zeros((peer_count * row_count, 2 * feature_count), fp32)
    grad_query, grad_keys = over_blocks(
        back_step,
        (jnp.zeros((row_count, head_count, head_width), fp32), keys_start),
        (
            lax.all_gather(key_rows, "ctx", axis=0, tiled=True),
            lax.all_gather(value_rows, "ctx", axis=0, tiled=True),
        ),
        row_count,
    )
    grad_kv = lax.psum_scatter(
        grad_keys.astype(jnp.bfloat16), "ctx", scatter_dimension=0, tiled=True
    ).astype(jnp.float32)
    grad_packed = jnp.concatenate(
        [grad_query.reshape(row_count, feature_count), grad_kv], axis=1
    ).astype(bf16)
    grad_packed_wide = grad_packed.astype(fp32)
    grad_query_bias = jnp.sum(grad_packed_wide[:, :feature_count], axis=0)
    grad_value_bias = jnp.sum(grad_packed_wide[:, 2 * feature_count :], axis=0)
    grad_qkv = contract_rows(normed_low, grad_packed)
    grad_normed_one = times_transpose(grad_packed, qkv_full)
    grad_in_norm, grad_gain_one, grad_shift_one = norm_back(
        grad_normed_one, unit_one, inverse_one, gain_one.astype(fp32)
    )
    grad_tokens = grad_middle + grad_in_norm
    (
        sum_qkv,
        sum_qbias,
        sum_vbias,
        sum_out,
        sum_obias,
        sum_fc,
        sum_fbias,
        sum_proj,
        sum_pbias,
        sum_gain_one,
        sum_shift_one,
        sum_gain_two,
        sum_shift_two,
    ) = (
        lax.psum_scatter(
            grad_qkv.astype(jnp.bfloat16), "fsdp", scatter_dimension=0, tiled=True
        ).astype(jnp.float32),
        lax.psum_scatter(
            grad_query_bias.astype(jnp.bfloat16), "fsdp", scatter_dimension=0, tiled=True
        ).astype(jnp.float32),
        lax.psum_scatter(
            grad_value_bias.astype(jnp.bfloat16), "fsdp", scatter_dimension=0, tiled=True
        ).astype(jnp.float32),
        lax.psum_scatter(
            grad_out_proj.astype(jnp.bfloat16), "fsdp", scatter_dimension=0, tiled=True
        ).astype(jnp.float32),
        lax.psum_scatter(
            grad_out_bias.astype(jnp.bfloat16), "fsdp", scatter_dimension=0, tiled=True
        ).astype(jnp.float32),
        lax.psum_scatter(
            grad_fc.astype(jnp.bfloat16), "fsdp", scatter_dimension=0, tiled=True
        ).astype(jnp.float32),
        lax.psum_scatter(
            grad_fc_bias.astype(jnp.bfloat16), "fsdp", scatter_dimension=0, tiled=True
        ).astype(jnp.float32),
        lax.psum_scatter(
            grad_proj.astype(jnp.bfloat16), "fsdp", scatter_dimension=0, tiled=True
        ).astype(jnp.float32),
        lax.psum_scatter(
            grad_proj_bias.astype(jnp.bfloat16), "fsdp", scatter_dimension=0, tiled=True
        ).astype(jnp.float32),
        lax.psum_scatter(
            grad_gain_one.astype(jnp.bfloat16), "fsdp", scatter_dimension=0, tiled=True
        ).astype(jnp.float32),
        lax.psum_scatter(
            grad_shift_one.astype(jnp.bfloat16), "fsdp", scatter_dimension=0, tiled=True
        ).astype(jnp.float32),
        lax.psum_scatter(
            grad_gain_two.astype(jnp.bfloat16), "fsdp", scatter_dimension=0, tiled=True
        ).astype(jnp.float32),
        lax.psum_scatter(
            grad_shift_two.astype(jnp.bfloat16), "fsdp", scatter_dimension=0, tiled=True
        ).astype(jnp.float32),
    )
    totals = (
        lax.psum(sum_qkv.astype(jnp.bfloat16), "ctx").astype(jnp.float32),
        lax.psum(sum_qbias.astype(jnp.bfloat16), "ctx").astype(jnp.float32),
        lax.psum(sum_vbias.astype(jnp.bfloat16), "ctx").astype(jnp.float32),
        lax.psum(sum_out.astype(jnp.bfloat16), "ctx").astype(jnp.float32),
        lax.psum(sum_obias.astype(jnp.bfloat16), "ctx").astype(jnp.float32),
        lax.psum(sum_fc.astype(jnp.bfloat16), "ctx").astype(jnp.float32),
        lax.psum(sum_fbias.astype(jnp.bfloat16), "ctx").astype(jnp.float32),
        lax.psum(sum_proj.astype(jnp.bfloat16), "ctx").astype(jnp.float32),
        lax.psum(sum_pbias.astype(jnp.bfloat16), "ctx").astype(jnp.float32),
        lax.psum(sum_gain_one.astype(jnp.bfloat16), "ctx").astype(jnp.float32),
        lax.psum(sum_shift_one.astype(jnp.bfloat16), "ctx").astype(jnp.float32),
        lax.psum(sum_gain_two.astype(jnp.bfloat16), "ctx").astype(jnp.float32),
        lax.psum(sum_shift_two.astype(jnp.bfloat16), "ctx").astype(jnp.float32),
    )
    return (
        output_low,
        grad_tokens,
        totals[0],
        totals[1],
        totals[2],
        totals[3],
        totals[4],
        totals[5],
        totals[6],
        totals[7],
        totals[8],
        totals[9],
        totals[10],
        totals[11],
        totals[12],
    )


FP32 = jnp.float32
BF16 = jnp.bfloat16
FLOOR = -1e30
NEVER = 1 << 30


def dot_nt(left_side, right_side):
    return lax.dot_general(
        left_side, right_side, (((1,), (1,)), ((), ())), preferred_element_type=FP32
    )


def dot_nn(left_side, right_side):
    return lax.dot_general(
        left_side, right_side, (((1,), (0,)), ((), ())), preferred_element_type=FP32
    )


def spread(column_tile, width):
    return jnp.concatenate([column_tile] * (width // column_tile.shape[1]), axis=1)


def masked_scores(scores, key_ids, first_row, last_row):
    permitted = key_ids >= first_row
    if last_row is not None:
        permitted = permitted & (key_ids <= last_row)
    return jnp.where(permitted, scores, -jnp.inf)


def whole_vector(small_ref, number):
    parts = [small_ref[f, number : number + 1, :] for f in range(small_ref.shape[0])]
    return jnp.concatenate(parts, axis=1)


def project_block(
    tokens_ref, wq_ref, wk_ref, wv_ref, small_ref, chip, stores, position, wanted
):
    q_ref, k_ref, kt_ref, v_ref, vt_ref, normed_ref = stores
    gain, shift = whole_vector(small_ref, 4), whole_vector(small_ref, 5)
    normed = layer_norm(tokens_ref[...].astype(FP32), gain, shift)[0]
    normed = normed.astype(BF16)
    keys = dot_nn(normed, wk_ref[...])
    values = dot_nn(normed, wv_ref[...]) + small_ref[chip, 1:2, :]
    k_ref[position] = keys.astype(BF16)
    v_ref[position] = values.astype(BF16)
    kt_ref[position] = keys.T.astype(BF16)
    vt_ref[position] = values.T.astype(BF16)
    if wanted:
        queries = (dot_nn(normed, wq_ref[...]) + small_ref[chip, 0:1, :]).astype(BF16)
        q_ref[position // 2] = (queries.astype(FP32) * 0.125).astype(BF16)
        normed_ref[position // 2] = normed


def project_kernel(
    where,
    t0,
    t1,
    t2,
    t3,
    w_ref,
    smalls_ref,
    near_ref,
    across_ref,
    far_ref,
    near_other,
    across_other,
    far_other,
    q,
    k,
    kt,
    v,
    vt,
    normed,
    full_ref,
    wq,
    wk,
    wv,
    small_ref,
):
    part, core, chip = where[0], where[1], where[2]
    near, across = 1 + core, 2 - core
    shard, wide = w_ref.shape
    features, half, width = wide // 3, shard // 2, wq.shape[1]
    full_ref[pl.ds(pl.multiple_of(part * shard, 16), shard), :] = w_ref[...]
    small_ref[part] = smalls_ref[...].astype(FP32)
    for ref, owner in ((near_ref, part ^ near), (across_ref, part ^ across), (far_ref, part ^ 3)):
        first = pl.multiple_of(owner * shard + core * half, 16)
        full_ref[pl.ds(first, half), :] = ref[0:half, :]
        small_ref[owner] = ref[half:, 0:width].astype(FP32)
    for ref, owner in (
        (near_other, part ^ across),
        (across_other, part ^ near),
        (far_other, part ^ 3),
    ):
        first = pl.multiple_of(owner * shard + (1 - core) * half, 16)
        full_ref[pl.ds(first, half), :] = ref[0:half, :]
    for z in range(features // width):

        @pl.when(chip == z)
        def own_columns():
            for n, ref in enumerate((wq, wk, wv)):
                first = features * n + width * z
                ref[...] = full_ref[:, first : first + width]

    stores = (q, k, kt, v, vt, normed)
    for n, block in enumerate((t0, t1, t2, t3)):
        owner = (chip ^ (n // 2)) % 2
        position = 2 * owner + (core if n % 2 == 0 else 1 - core)
        project_block(block, wq, wk, wv, small_ref, chip, stores, position, n % 2 == 0)


def attend_kernel(
    where,
    t0,
    t1,
    t2,
    t3,
    wq_ref,
    wk_ref,
    wv_ref,
    small_ref,
    q_half,
    k_half,
    kt_half,
    v_half,
    vt_half,
    normed_half,
    key_ref,
    low_ref,
    high_ref,
    far_ref,
    q_ref,
    k_ref,
    kt_ref,
    v_ref,
    normed_ref,
    o0_ref,
    o1_ref,
    o2_ref,
    o3_ref,
    ot_ref,
    lse_ref,
    zero_ref,
    vt_ref,
    acc_ref,
    o_ref,
):
    blocks, rows, width = q_ref.shape
    heads = width // 64
    core, chip = where[1], where[2]
    side = chip // 2
    zero_ref[...] = jnp.zeros_like(zero_ref)
    stores = (q_ref, k_ref, kt_ref, v_ref, vt_ref, normed_ref)
    for n, block in enumerate((t0, t1, t2, t3)):
        owner = chip ^ (2 + n // 2)
        position = 2 * owner + (core if n % 2 == 0 else 1 - core)
        project_block(
            block,
            wq_ref,
            wk_ref,
            wv_ref,
            small_ref,
            chip,
            stores,
            position,
            n % 2 == 0,
        )
    for n in range(blocks):
        for source, target in ((k_half, k_ref), (kt_half, kt_ref), (v_half, v_ref), (vt_half, vt_ref)):
            target[side * blocks + n] = source[n]
    for n in range(blocks // 2):
        q_ref[side * (blocks // 2) + n] = q_half[n]
        normed_ref[side * (blocks // 2) + n] = normed_half[n]

    def query_block(index, unused):
        queries = [q_ref[index, :, 64 * h : 64 * h + 64] for h in range(heads)]
        acc_ref[...] = jnp.zeros_like(acc_ref)

        def key_step(key_block, carry, first_row, last_row):
            ids = spread(key_ref[key_block], rows)
            result = []
            for h in range(heads):
                span = slice(64 * h, 64 * h + 64)
                top, total = carry[h]
                scores = dot_nt(k_ref[key_block, :, span], queries[h])
                scores = masked_scores(scores, ids, first_row, last_row)
                new_top = jnp.maximum(top, jnp.max(scores, axis=0, keepdims=True))
                fade = jnp.exp(top - new_top)
                weights = jnp.exp(scores - new_top)
                total = total * fade + jnp.sum(weights, axis=0, keepdims=True)
                acc_ref[span, :] = acc_ref[span, :] * fade + dot_nn(
                    vt_ref[key_block, span, :], weights.astype(BF16)
                )
                result.append((new_top, total))
            return tuple(result)

        start = tuple(
            (jnp.full((1, rows), FLOOR, FP32), jnp.zeros((1, rows), FP32)) for h in range(heads)
        )
        own = 2 * index + core
        far_row = far_ref[index]
        carry = lax.fori_loop(0, own, lambda j, c: key_step(j, c, far_row, None), start)
        carry = key_step(own, carry, low_ref[index], high_ref[index])
        for h in range(heads):
            span = slice(64 * h, 64 * h + 64)
            top, total = carry[h]
            attended = acc_ref[span, :] / total
            ot_ref[index, span, :] = attended
            o_ref[index, :, span] = attended.T.astype(BF16)
            lse_ref[index, h : h + 1, :] = top + jnp.log(total)
        return unused

    lax.fori_loop(0, blocks, query_block, 0)
    for s, ref in enumerate((o0_ref, o1_ref, o2_ref, o3_ref)):
        ref[...] = o_ref[chip ^ s]


def attend_back_kernel(
    where,
    q_ref,
    k_ref,
    kt_ref,
    v_ref,
    d0_ref,
    d1_ref,
    d2_ref,
    d3_ref,
    key_ref,
    low_ref,
    high_ref,
    far_ref,
    ot_ref,
    lse_ref,
    dq_ref,
    keep_ref,
    send_ref,
    acc_ref,
    dk_ref,
    dv_ref,
    da_ref,
):
    blocks, rows, width = q_ref.shape
    heads = width // 64
    core, chip = where[1], where[2]
    for s, ref in enumerate((d0_ref, d1_ref, d2_ref, d3_ref)):
        da_ref[chip ^ s] = ref[...]
    dk_ref[...] = jnp.zeros_like(dk_ref)
    dv_ref[...] = jnp.zeros_like(dv_ref)

    def query_block(index, unused):
        queries = [q_ref[index, :, 64 * h : 64 * h + 64] for h in range(heads)]
        grads = [da_ref[index, :, 64 * h : 64 * h + 64] for h in range(heads)]
        deltas = [
            jnp.sum(
                grads[h].astype(FP32).T * ot_ref[index, 64 * h : 64 * h + 64, :],
                axis=0,
                keepdims=True,
            )
            for h in range(heads)
        ]
        logs = [lse_ref[index, h : h + 1, :] for h in range(heads)]
        acc_ref[...] = jnp.zeros_like(acc_ref)

        def key_step(key_block, first_row, last_row):
            ids = spread(key_ref[key_block], rows)
            for h in range(heads):
                span = slice(64 * h, 64 * h + 64)
                scores = dot_nt(k_ref[key_block, :, span], queries[h])
                scores = masked_scores(scores, ids, first_row, last_row)
                weights = jnp.exp(scores - logs[h])
                slopes = dot_nt(v_ref[key_block, :, span], grads[h])
                dscores = (weights * (slopes - deltas[h])).astype(BF16)
                dv_ref[h, key_block] += dot_nn(weights.astype(BF16), grads[h])
                dk_ref[h, key_block] += dot_nn(dscores, queries[h])
                acc_ref[span, :] += dot_nn(kt_ref[key_block, span, :], dscores)

        own = 2 * index + core
        far_row = far_ref[index]

        def far_step(key_block, state):
            key_step(key_block, far_row, None)
            return state

        lax.fori_loop(0, own, far_step, 0)
        key_step(own, low_ref[index], high_ref[index])
        for h in range(heads):
            span = slice(64 * h, 64 * h + 64)
            dq_ref[index, :, span] = (acc_ref[span, :] * 0.125).T.astype(BF16)
        return unused

    lax.fori_loop(0, blocks, query_block, 0)

    def write_block(index, unused):
        mine = 2 * index + core
        theirs = 2 * index + 1 - core
        for h in range(heads):
            left = slice(64 * h, 64 * h + 64)
            right = slice(width + 64 * h, width + 64 * h + 64)
            keep_ref[index, :, left] = dk_ref[h, mine]
            keep_ref[index, :, right] = dv_ref[h, mine]
            send_ref[index, :, left] = dk_ref[h, theirs].astype(BF16)
            send_ref[index, :, right] = dv_ref[h, theirs].astype(BF16)
        return unused

    lax.fori_loop(0, blocks, write_block, 0)


def kernel_call(kernel, outputs, scratch, operands, cost, special={}, after=()):
    whole = pl.BlockSpec(memory_space=pltpu.VMEM)
    in_specs = [pl.BlockSpec(memory_space=pltpu.SMEM)]
    in_specs += [special.get(n, whole) for n in range(1, len(operands))]
    in_specs += [pl.BlockSpec(memory_space=pl.ANY) for unused in after]
    count = len(operands)

    def ordered(*refs):
        return kernel(*refs[:count], *refs[count + len(after) :])

    moved = sum(v.size * v.dtype.itemsize for v in list(operands) + list(outputs))
    return pl.pallas_call(
        ordered,
        out_shape=outputs,
        in_specs=in_specs,
        out_specs=[pl.BlockSpec(memory_space=pltpu.VMEM) for unused in outputs],
        scratch_shapes=scratch,
        compiler_params=pltpu.CompilerParams(vmem_limit_bytes=56 * 1024 * 1024),
        cost_estimate=pl.CostEstimate(
            flops=cost * 1153 * 10**6, bytes_accessed=moved, transcendentals=0
        ),
    )(*operands, *after)


def pack_kernel(where, dq_ref, keep_ref, arrived_ref, p0, p1, p2, p3):
    chip = where[2]
    width = dq_ref.shape[2]
    for s, ref in enumerate((p0, p1, p2, p3)):
        owner = chip ^ s
        ref[:, 0:width] = dq_ref[owner]
        ref[:, width:] = (keep_ref[owner] + arrived_ref[owner].astype(FP32)).astype(BF16)


def middle_kernel(
    where,
    a0_ref,
    a1_ref,
    a2_ref,
    a3_ref,
    tokens_ref,
    cotangent_ref,
    live_ref,
    small_ref,
    bundle_own,
    bundle_other,
    block_ref,
    dx_ref,
    d0_ref,
    d1_ref,
    d2_ref,
    d3_ref,
    mine_ref,
    send_ref,
    sums_ref,
    wo_ref,
    wf_ref,
    wp_ref,
    g_ref,
    dz_ref,
    sems,
):
    rows, features = tokens_ref.shape
    parts = wf_ref.shape[0]
    shard, hidden_width = features // parts, wp_ref.shape[0]
    columns = hidden_width // parts
    half, half_columns = shard // 2, columns // 2
    core, chip = where[1], where[2]

    starts = {"proj": [], "out": [], "fc": []}

    def fetch(kind, source, target):
        number = sum(len(v) for v in starts.values())
        starts[kind].append(pltpu.make_async_copy(source, target, sems.at[number]))

    def rows_at(owner, which, size):
        return pl.ds(pl.multiple_of(owner * 2 * size + which * size, 16), size)

    pieces = []
    for owner in range(parts):
        pieces.append((bundle_own.at[owner], owner, core))
        pieces.append((bundle_other.at[owner], owner, 1 - core))
    for piece, owner, which in pieces:
        fetch("out", piece.at[half_columns : half_columns + half, :], wo_ref.at[rows_at(owner, which, half), :])
    for piece, owner, which in pieces:
        for j in range(parts):
            first = half_columns + half * (j + 1)
            fetch("fc", piece.at[first : first + half, :], wf_ref.at[j, rows_at(owner, which, half), :])
    for piece, owner, which in pieces:
        fetch("proj", piece.at[0:half_columns, :], wp_ref.at[rows_at(owner, which, half_columns), :])
    for kind in ("out", "fc", "proj"):
        for copy in starts[kind]:
            copy.start()
    for copy in starts["out"]:
        copy.wait()

    attended = [a0_ref, a1_ref, a2_ref, a3_ref]
    middle = tokens_ref[...].astype(FP32) + whole_vector(small_ref, 2)
    a_start = 2 * parts * half_columns + features
    for s in range(parts):
        span = pl.ds(pl.multiple_of((chip ^ s) * shard, 16), shard)
        middle = middle + dot_nn(attended[s][...], wo_ref[span, :])
        mine_ref[:, a_start + shard * s : a_start + shard * (s + 1)] = attended[s][...]
        send_ref[:, a_start + shard * s : a_start + shard * (s + 1)] = attended[s][...]
    normed, unit, inverse = layer_norm(
        middle, whole_vector(small_ref, 6), whole_vector(small_ref, 7)
    )
    normed_low = normed.astype(BF16)
    h_start = 2 * parts * half_columns
    mine_ref[:, h_start : h_start + features] = normed_low
    send_ref[:, h_start : h_start + features] = normed_low
    grad_out = cotangent_ref[...].astype(FP32) * live_ref[...]
    grad_out_low = grad_out.astype(BF16)
    y_start = a_start + features
    mine_ref[:, y_start : y_start + features] = grad_out_low
    send_ref[:, y_start : y_start + features] = grad_out_low
    for copy in starts["fc"] + starts["proj"]:
        copy.wait()

    sums_ref[...] = jnp.zeros_like(sums_ref)
    output = middle + whole_vector(small_ref, 3)
    grad_normed = jnp.zeros((rows, features), FP32)
    scale, cubic = 0.7978845608028654, 0.044715
    for j in range(parts):
        span = slice(columns * j, columns * (j + 1))
        bias_fc = jnp.concatenate([small_ref[j, 8 + n : 9 + n, :] for n in range(parts)], axis=1)
        hidden = dot_nn(normed_low, wf_ref[j]) + bias_fc
        square = hidden * hidden
        bent = jnp.tanh(scale * hidden * (1.0 + cubic * square))
        active = 0.5 * hidden * (1.0 + bent)
        slope = 0.5 * (1.0 + bent) + 0.5 * hidden * (1.0 - bent * bent) * (
            scale * (1.0 + 3.0 * cubic * square)
        )
        g_ref[...] = active.astype(BF16)
        grad_hidden = (dot_nt(grad_out_low, wp_ref[span, :]) * slope).astype(BF16)
        output = output + dot_nn(g_ref[...], wp_ref[span, :])
        grad_normed = grad_normed + dot_nt(grad_hidden, wf_ref[j])
        sums_ref[j, 1:2, :] = jnp.sum(grad_hidden.astype(FP32), axis=0, keepdims=True)
        g_span = slice(half_columns * j, half_columns * (j + 1))
        mine_ref[:, g_span] = g_ref[:, pl.ds(pl.multiple_of(core * half_columns, 128), half_columns)]
        send_ref[:, g_span] = g_ref[
            :, pl.ds(pl.multiple_of((1 - core) * half_columns, 128), half_columns)
        ]
        first = parts * half_columns + columns * (j % 2)

        @pl.when(core == j // 2)
        def keep_hidden():
            mine_ref[:, first : first + columns] = grad_hidden

        @pl.when(core != j // 2)
        def give_hidden():
            send_ref[:, first : first + columns] = grad_hidden

    block_ref[...] = output.astype(BF16)
    inner, gain_sum, shift_sum = norm_back(
        grad_normed, unit, inverse, whole_vector(small_ref, 6)
    )
    grad_middle = grad_out + inner
    dx_ref[...] = grad_middle
    dz_ref[...] = grad_middle.astype(BF16)
    z_start = y_start + features
    part_width = features // 2
    mine_ref[:, z_start : z_start + part_width] = dz_ref[
        :, pl.ds(pl.multiple_of(core * part_width, 128), part_width)
    ]
    send_ref[:, z_start : z_start + part_width] = dz_ref[
        :, pl.ds(pl.multiple_of((1 - core) * part_width, 128), part_width)
    ]
    for s, ref in enumerate((d0_ref, d1_ref, d2_ref, d3_ref)):
        span = pl.ds(pl.multiple_of((chip ^ s) * shard, 16), shard)
        ref[...] = dot_nt(dz_ref[...], wo_ref[span, :]).astype(BF16)
    rows_of_sums = (
        jnp.sum(dz_ref[...].astype(FP32), axis=0, keepdims=True),
        jnp.sum(grad_out, axis=0, keepdims=True),
        gain_sum[None, :],
        shift_sum[None, :],
    )
    for n, row in enumerate(rows_of_sums):
        for f in range(parts):
            sums_ref[f, 0:1, shard * n : shard * (n + 1)] = row[:, shard * f : shard * (f + 1)]


def weight_grad_kernel(where, mine_ref, other_ref, small_ref, keep_ref, send_ref, fc_ref):
    rows = mine_ref.shape[0]
    features = keep_ref.shape[2]
    part, core, chip = where[0], where[1], where[2]
    near, across = 1 + core, 2 - core
    parts = 4
    shard, half_columns = features // parts, features // 2
    h_start = 2 * parts * half_columns
    a_start = h_start + features
    y_start = a_start + features
    z_start = y_start + features

    def product(left, right):
        return contract_rows(mine_ref[:, left], mine_ref[:, right]) + contract_rows(
            other_ref[:, left], other_ref[:, right]
        )

    targets = [(keep_ref, 0, part), (keep_ref, 1, part ^ across)]
    targets += [(send_ref, 0, part ^ near), (send_ref, 1, part ^ 3)]
    fc_base = parts * half_columns
    for j in range(2):
        fc_ref[j] = product(
            pl.ds(h_start, features), pl.ds(fc_base + features * j, features)
        ).astype(BF16)
    out_base = half_columns + 2 * shard
    small_base = out_base + shard // 2
    for ref, slot, owner in targets:
        g_span = pl.ds(pl.multiple_of(owner * half_columns, 128), half_columns)
        ref[slot, 0:half_columns, :] = product(g_span, pl.ds(y_start, features)).astype(BF16)
        for j in range(2):
            first = half_columns + shard * j
            ref[slot, first : first + shard, :] = fc_ref[
                j, pl.ds(pl.multiple_of(owner * shard, 16), shard), :
            ]
        ref[slot, small_base : small_base + 16, :] = small_ref[owner].astype(BF16)
        ref[slot, small_base + 16 :, :] = jnp.zeros_like(ref[slot, small_base + 16 :, :])
    for s in range(parts):
        block = product(
            pl.ds(a_start + shard * s, shard), pl.ds(z_start, half_columns)
        ).astype(BF16)
        owner = chip ^ s
        for ref, slot, wanted in targets:

            @pl.when(owner == wanted)
            def store_block():
                ref[slot, out_base:small_base, 0:half_columns] = block[: shard // 2]
                ref[slot, out_base:small_base, half_columns:] = block[shard // 2 :]


def qkv_grad_kernel(
    where,
    normed_ref,
    p0,
    p1,
    p2,
    p3,
    wq_ref,
    wk_ref,
    wv_ref,
    small_ref,
    keep_ref,
    send_ref,
    total_ref,
):
    blocks, rows, features = normed_ref.shape
    width = wq_ref.shape[1]
    part, core, chip = where[0], where[1], where[2]
    near, across = 1 + core, 2 - core
    parts = 4
    shard = features // parts
    half = shard // 2
    column_sums = [jnp.zeros((1, width), FP32) for n in range(3)]
    for n in range(3):
        total = jnp.zeros((features, width), FP32)
        for b in range(blocks):
            grads = (p0, p1, p2, p3)[b][:, width * n : width * (n + 1)]
            total = total + contract_rows(normed_ref[chip ^ b], grads)
            column_sums[n] = column_sums[n] + jnp.sum(grads.astype(FP32), axis=0, keepdims=True)
        total_ref[:, width * n : width * (n + 1)] = total
    sums = jnp.concatenate(column_sums, axis=1)
    shift_grad = jnp.zeros((features, 1), FP32)
    gain_grad = jnp.zeros((features, 1), FP32)
    for n, ref in enumerate((wq_ref, wk_ref, wv_ref)):
        wide = ref[...].astype(FP32)
        shift_grad = shift_grad + jnp.sum(wide * column_sums[n], axis=1, keepdims=True)
        gain_grad = gain_grad + jnp.sum(
            wide * total_ref[:, width * n : width * (n + 1)], axis=1, keepdims=True
        )
    columns = jnp.concatenate(
        [gain_grad, shift_grad, jnp.zeros((features, 126), FP32)], axis=1
    )
    norm_rows = columns.T[0:8]
    gain, shift = whole_vector(small_ref, 4), whole_vector(small_ref, 5)
    gain_row = (norm_rows[0:1] - shift * norm_rows[1:2]) / gain
    norm_rows = jnp.concatenate([gain_row, norm_rows[1:]], axis=0)
    order = [part, part ^ across, part ^ near, part ^ 3]
    other_order = [part, part ^ near, part ^ across, part ^ 3]
    for ref, which, owners in ((keep_ref, core, order), (send_ref, 1 - core, other_order)):
        for slot in range(parts):
            owner = owners[slot]
            first = pl.multiple_of(owner * shard + which * half, 16)
            ref[slot, 0:half, :] = total_ref[pl.ds(first, half), :].astype(ref.dtype)
            picked = jnp.zeros((8, shard), FP32)
            for f in range(parts):
                picked = jnp.where(owner == f, norm_rows[:, shard * f : shard * (f + 1)], picked)
            row = lax.broadcasted_iota(jnp.int32, (8, 3 * width), 0)
            packed = jnp.concatenate([picked, jnp.zeros((8, 3 * width - shard), FP32)], axis=1)
            tail = jnp.where(row < 2, packed, jnp.where(row == 2, sums, 0.0))
            tail = jnp.concatenate([tail, jnp.zeros_like(tail)], axis=0)
            ref[slot, half : half + 16, :] = tail.astype(ref.dtype)


def first_bit(core, chip):
    return jnp.where(core == 0, chip % 2, chip // 2)


def relay_kernel(where, keep_ref, theirs_ref, relay_ref):
    relay_ref[...] = (keep_ref[1].astype(FP32) + theirs_ref[1].astype(FP32)).astype(BF16)


def pair_kernel(where, keep_ref, theirs_ref, last_ref, stay_ref, give_ref):
    low = first_bit(where[1], where[2])
    count = stay_ref.shape[0]
    for ref, which in ((stay_ref, low), (give_ref, 1 - low)):
        span = pl.ds(pl.multiple_of(which * count, 16), count)
        total = keep_ref[0, span, :].astype(FP32) + theirs_ref[0, span, :].astype(FP32)
        ref[...] = (total + last_ref[span, :].astype(FP32)).astype(ref.dtype)


def quad_kernel(where, stay_ref, arrived_ref, keep_ref, give_ref):
    high = first_bit(1 - where[1], where[2])
    count = keep_ref.shape[0]
    for ref, which in ((keep_ref, high), (give_ref, 1 - high)):
        span = pl.ds(pl.multiple_of(which * count, 16), count)
        total = stay_ref[span, :] + arrived_ref[span, :].astype(FP32)
        ref[...] = total.astype(ref.dtype)


def total_kernel(where, keep_ref, arrived_ref, out_ref):
    out_ref[...] = (keep_ref[...] + arrived_ref[...].astype(FP32)).astype(BF16)


def join_kernel(where, mine_ref, arrived_ref, out_ref):
    high = first_bit(1 - where[1], where[2])
    count = mine_ref.shape[0]
    out_ref[pl.ds(pl.multiple_of(high * count, 16), count), :] = mine_ref[...]
    out_ref[pl.ds(pl.multiple_of((1 - high) * count, 16), count), :] = arrived_ref[...]


def input_grad_kernel(
    where, p0, p1, p2, p3, w_ref, tokens_ref, dx_ref, small_ref, out_ref, packed_ref
):
    chip = where[2]
    features = w_ref.shape[0]
    width = p0.shape[1] // 3
    for z in range(4):
        for s, piece in enumerate((p0, p1, p2, p3)):

            @pl.when(chip == z ^ s)
            def place_piece():
                for n in range(3):
                    first = features * n + width * z
                    packed_ref[:, first : first + width] = piece[:, width * n : width * (n + 1)]

    total = dot_nt(packed_ref[...], w_ref[...])
    unit, inverse = layer_norm(
        tokens_ref[...].astype(FP32), whole_vector(small_ref, 4), whole_vector(small_ref, 5)
    )[1:]
    out_ref[...] = dx_ref[...] + norm_back(total, unit, inverse, whole_vector(small_ref, 4))[0]


def output_kernel(
    where, m0, m1, t0, t1, proj_ref, fc_ref, out_ref, sums_ref, mine_ref, other_ref
):
    core = where[1]
    count = m0.shape[0]
    own_bit, other_bit = first_bit(core, where[2]), first_bit(1 - core, where[2])
    for n, (mine, other) in enumerate(((m0, t0), (m1, t1))):
        for bit, source, target in ((own_bit, mine, mine_ref), (other_bit, other, other_ref)):
            first = pl.multiple_of((bit if n == 0 else 1 - bit) * count, 16)
            target[pl.ds(first, count), :] = source[...]
    half_columns = proj_ref.shape[0] // 2
    shard, features = out_ref.shape
    out_rows = half_columns + 2 * shard
    small_at = out_rows + shard // 2
    sums_ref[...] = mine_ref[small_at : small_at + 16, :].astype(FP32) + other_ref[
        small_at : small_at + 16, :
    ].astype(FP32)

    def place(ref, which):
        proj_ref[which * half_columns : (which + 1) * half_columns, :] = ref[
            0:half_columns, :
        ].astype(FP32)
        for j in range(2):
            first = half_columns + shard * j
            column = features * (2 * which + j)
            fc_ref[:, column : column + features] = ref[first : first + shard, :].astype(FP32)
        span = slice(features // 2 * which, features // 2 * (which + 1))
        middle = out_rows + shard // 2
        out_ref[0 : shard // 2, span] = ref[out_rows:middle, 0 : features // 2].astype(FP32)
        out_ref[shard // 2 :, span] = ref[out_rows:middle, features // 2 :].astype(FP32)

    @pl.when(core == 0)
    def first_core():
        place(mine_ref, 0)
        place(other_ref, 1)

    @pl.when(core == 1)
    def second_core():
        place(mine_ref, 1)
        place(other_ref, 0)


def qkv_output_kernel(where, h0, h1, h2, h3, out_ref, extra_ref):
    core, chip = where[1], where[2]
    shard, wide = out_ref.shape
    features = wide // 3
    half = shard // 2
    width = h0.shape[2] // 3
    for s, ref in enumerate((h0, h1, h2, h3)):
        extra_ref[chip ^ s] = jnp.where(
            core == 0, ref[0, half : half + 16, :], ref[1, half : half + 16, :]
        ).astype(FP32)
        for z in range(4):

            @pl.when(chip == z ^ s)
            def place_piece():
                for n in range(3):
                    first = features * n + width * z
                    for slot, which in ((0, core), (1, 1 - core)):
                        rows = pl.ds(pl.multiple_of(which * half, 8), half)
                        out_ref[rows, first : first + width] = ref[
                            slot, 0:half, width * n : width * (n + 1)
                        ].astype(FP32)


def fast_body(
    tokens,
    cotangent,
    w_qkv,
    b_query,
    b_value,
    w_out,
    b_out,
    w_fc,
    b_fc,
    w_proj,
    b_proj,
    gain1,
    shift1,
    gain2,
    shift2,
    counts,
    seq_lengths,
):
    rows, features = tokens.shape
    ctx = lax.axis_size("ctx")
    fsdp = lax.axis_size("fsdp")
    chips = ctx // 2
    group_heads = HEADS // chips
    width = features // chips
    shard = features // fsdp
    hidden_width = w_fc.shape[1]
    columns = hidden_width // fsdp
    place = lax.axis_index("ctx")
    chip = place // 2
    core = place % 2
    part = lax.axis_index("fsdp")
    near = 1 + core
    across = 2 - core
    where = jnp.stack([part, core, chip]).astype(jnp.int32)

    def exchange(value, partner):
        pairs = [
            (f * ctx + c, g * ctx + d)
            for f in range(fsdp)
            for c in range(ctx)
            for g, d in [partner(f, c)]
        ]
        return lax.ppermute(value, ("fsdp", "ctx"), pairs)

    def to_near(value):
        return exchange(value, lambda f, c: (f ^ (1 + c % 2), c))

    def to_across(value):
        return exchange(value, lambda f, c: (f ^ (2 - c % 2), c))

    def to_core(value):
        return exchange(value, lambda f, c: (f, c ^ 1))

    def to_chip(value, step):
        return exchange(value, lambda f, c: (f, c ^ (2 * step)))

    def to_first(value):
        return exchange(value, lambda f, c: (f, c ^ (2 + 2 * (c % 2))))

    def to_second(value):
        return exchange(value, lambda f, c: (f, c ^ (4 - 2 * (c % 2))))

    def pick(array, index, axis=0):
        return lax.dynamic_index_in_dim(array, index, axis, keepdims=False)

    def place_all(shape, dtype, items):
        buffer = jnp.zeros(shape, dtype)
        for index, value in items:
            full = value.reshape((1,) * (len(shape) - value.ndim) + value.shape)
            starts = tuple(index) + (0,) * (len(shape) - len(index))
            buffer = lax.dynamic_update_slice(buffer, full.astype(dtype), starts)
        return buffer

    half = shard // 2
    fc_half = lax.dynamic_slice_in_dim(w_fc, core * half, half, 0)
    bundle = jnp.concatenate(
        [
            lax.dynamic_slice_in_dim(w_proj, core * (columns // 2), columns // 2, 0),
            lax.dynamic_slice_in_dim(w_out, core * half, half, 0),
        ]
        + [fc_half[:, columns * j : columns * (j + 1)] for j in range(fsdp)],
        axis=0,
    )

    blocks = [tokens] + [to_chip(tokens, s) for s in (1, 2, 3)]
    beside = [to_core(v) for v in blocks]
    bundles = lax.all_gather(bundle, "fsdp", axis=0)

    count_row = counts[0]
    offsets = jnp.cumsum(count_row) - count_row
    seq_ends = jnp.cumsum(seq_lengths[0])
    within = jnp.arange(rows, dtype=jnp.int32)
    slot = jnp.arange(ctx, dtype=jnp.int32)[:, None] * rows + within[None, :]
    live = within[None, :] < count_row[:, None]
    places = offsets[:, None] + within[None, :]
    starts = jnp.max(
        jnp.where(places[:, :, None] >= seq_ends[None, None, :], seq_ends[None, None, :], 0), axis=2
    )
    dead_id = -1 - slot
    key_ids = jnp.where(live, places, dead_id)
    lows = jnp.where(live, starts, dead_id)
    fars = jnp.where(live, starts, NEVER)
    key_tile = jnp.broadcast_to(key_ids[:, :, None], (ctx, rows, 128))

    def own_parity(array):
        return pick(array.reshape((chips, 2) + array.shape[1:]), core, 1)

    low_rows = own_parity(lows)[:, None, :]
    high_rows = own_parity(key_ids)[:, None, :]
    far_rows = own_parity(fars)[:, None, :]
    live_rows = (within < pick(count_row, place)).astype(FP32)[:, None]

    vectors = [b_query, b_value, b_out, b_proj, gain1, shift1, gain2, shift2]
    vectors += [b_fc[shard * n : shard * (n + 1)] for n in range(fsdp)]
    row = lax.broadcasted_iota(jnp.int32, (16, shard), 0)
    smalls = jnp.zeros((16, shard), BF16)
    for n, vector in enumerate(vectors):
        smalls = jnp.where(row == n, vector[None, :], smalls)
    mine = jnp.concatenate(
        [
            lax.dynamic_slice_in_dim(w_qkv, core * half, half, 0),
            jnp.pad(smalls, ((0, 0), (0, 3 * features - shard))),
        ],
        axis=0,
    )
    from_near, from_across = to_near(mine), to_across(mine)
    from_far = to_across(from_near)
    gathered = (from_near, from_across, from_far)
    gathered += tuple(to_core(v) for v in gathered)
    *half_stores, qkv_full, weight_q, weight_k, weight_v, small_all = kernel_call(
        project_kernel,
        [
            jax.ShapeDtypeStruct((chips // 2, rows, width), BF16),
            jax.ShapeDtypeStruct((chips, rows, width), BF16),
            jax.ShapeDtypeStruct((chips, width, rows), BF16),
            jax.ShapeDtypeStruct((chips, rows, width), BF16),
            jax.ShapeDtypeStruct((chips, width, rows), BF16),
            jax.ShapeDtypeStruct((chips // 2, rows, features), BF16),
            jax.ShapeDtypeStruct((features, 3 * features), BF16),
            jax.ShapeDtypeStruct((features, width), BF16),
            jax.ShapeDtypeStruct((features, width), BF16),
            jax.ShapeDtypeStruct((features, width), BF16),
            jax.ShapeDtypeStruct((fsdp, 16, width), FP32),
        ],
        [],
        (where, blocks[0], beside[0], blocks[1], beside[1], w_qkv, smalls) + gathered,
        9,
    )
    queries, keys, keys_t, values, normed_mine, *rest = kernel_call(
        attend_kernel,
        [
            jax.ShapeDtypeStruct((chips, rows, width), BF16),
            jax.ShapeDtypeStruct((ctx, rows, width), BF16),
            jax.ShapeDtypeStruct((ctx, width, rows), BF16),
            jax.ShapeDtypeStruct((ctx, rows, width), BF16),
            jax.ShapeDtypeStruct((chips, rows, features), BF16),
        ]
        + [jax.ShapeDtypeStruct((rows, width), BF16)] * 4
        + [
            jax.ShapeDtypeStruct((chips, width, rows), FP32),
            jax.ShapeDtypeStruct((chips, 8, rows), FP32),
            jax.ShapeDtypeStruct((16, 128), BF16),
        ],
        [
            pltpu.VMEM((ctx, width, rows), BF16),
            pltpu.VMEM((width, rows), FP32),
            pltpu.VMEM((chips, rows, width), BF16),
        ],
        (where, blocks[2], beside[2], blocks[3], beside[3])
        + (weight_q, weight_k, weight_v, small_all)
        + tuple(half_stores)
        + (key_tile, low_rows, high_rows, far_rows),
        30,
    )
    attended_t, logs, zeros = rest[4:]

    def swap_chips(pieces):
        return [pieces[0]] + [to_chip(pieces[s], s) for s in (1, 2, 3)]

    bundles = lax.dynamic_update_slice(bundles, (bundles[0, :16, :128] + zeros)[None], (0, 0, 0))
    bundles_other = to_core(bundles)
    attended = swap_chips(rest[:4])
    bundle_width = 2 * hidden_width // 2 + 3 * features + features // 2
    hbm = pl.BlockSpec(memory_space=pl.ANY)
    block_out, grad_middle, d0, d1, d2, d3, bundle_mine, bundle_send, small_rows = kernel_call(
        middle_kernel,
        [
            jax.ShapeDtypeStruct((rows, features), BF16),
            jax.ShapeDtypeStruct((rows, features), FP32),
        ]
        + [jax.ShapeDtypeStruct((rows, width), BF16)] * 4
        + [
            jax.ShapeDtypeStruct((rows, bundle_width), BF16),
            jax.ShapeDtypeStruct((rows, bundle_width), BF16),
            jax.ShapeDtypeStruct((fsdp, 16, features), FP32),
        ],
        [
            pltpu.VMEM((features, features), BF16),
            pltpu.VMEM((fsdp, features, columns), BF16),
            pltpu.VMEM((hidden_width, features), BF16),
            pltpu.VMEM((rows, columns), BF16),
            pltpu.VMEM((rows, features), BF16),
            pltpu.SemaphoreType.DMA((8 * 6,)),
        ],
        tuple([where] + attended)
        + (
            tokens,
            cotangent,
            live_rows,
            small_all,
            bundles,
            bundles_other,
        ),
        21,
        special={9: hbm, 10: hbm},
    )

    grad_blocks = swap_chips([d0, d1, d2, d3])

    bundle_other = to_core(bundle_send)
    out_rows = columns // 2 + 2 * shard
    small_at = out_rows + half
    block_rows = small_at + 32
    pair_shape = jax.ShapeDtypeStruct((2, block_rows, features), BF16)
    grads_keep, grads_send = kernel_call(
        weight_grad_kernel,
        [pair_shape, pair_shape],
        [pltpu.VMEM((2, features, features), BF16)],
        (where, bundle_mine, bundle_other, small_rows),
        14,
        after=(grad_blocks[1],),
    )

    grad_query, grad_keep, grad_send = kernel_call(
        attend_back_kernel,
        [
            jax.ShapeDtypeStruct((chips, rows, width), BF16),
            jax.ShapeDtypeStruct((chips, rows, 2 * width), FP32),
            jax.ShapeDtypeStruct((chips, rows, 2 * width), BF16),
        ],
        [
            pltpu.VMEM((width, rows), FP32),
            pltpu.VMEM((group_heads, ctx, rows, 64), FP32),
            pltpu.VMEM((group_heads, ctx, rows, 64), FP32),
            pltpu.VMEM((chips, rows, width), BF16),
        ],
        (
            where,
            queries,
            keys,
            keys_t,
            values,
            *grad_blocks,
            key_tile,
            low_rows,
            high_rows,
            far_rows,
            attended_t,
            logs,
        ),
        30,
    )
    packed = kernel_call(
        pack_kernel,
        [jax.ShapeDtypeStruct((rows, 3 * width), BF16)] * 4,
        [],
        (where, grad_query, grad_keep, to_core(grad_send)),
        2,
    )

    def add_up(left_side, right_side):
        return left_side.astype(FP32) + right_side.astype(FP32)

    def scatter_parts(keep, send):
        theirs = to_near(send)
        last = to_across(add_up(keep[1], theirs[1]).astype(BF16))
        return (add_up(keep[0], theirs[0]) + last.astype(FP32)).astype(BF16)

    arrived = swap_chips(packed)
    theirs = to_near(grads_send)
    block = jax.ShapeDtypeStruct((block_rows, features), BF16)

    def shaped(count, dtype):
        return jax.ShapeDtypeStruct((count, features), dtype)

    (relay,) = kernel_call(
        relay_kernel, [block], [], (where, grads_keep, theirs), 1, after=(packed[0],)
    )
    stay, give = kernel_call(
        pair_kernel,
        [shaped(block_rows // 2, FP32), shaped(block_rows // 2, BF16)],
        [],
        (where, grads_keep, theirs, to_across(relay)),
        2,
        after=tuple(arrived[1:]),
    )
    stay, give = kernel_call(
        quad_kernel,
        [shaped(block_rows // 4, FP32), shaped(block_rows // 4, BF16)],
        [],
        (where, stay, to_first(give)),
        2,
    )
    (grad_tokens,) = kernel_call(
        input_grad_kernel,
        [jax.ShapeDtypeStruct((rows, features), FP32)],
        [pltpu.VMEM((rows, 3 * features), BF16)],
        tuple([where] + arrived) + (qkv_full, tokens, grad_middle, small_all),
        5,
        after=(give,),
    )

    (quad,) = kernel_call(
        total_kernel, [shaped(block_rows // 4, BF16)], [], (where, stay, to_second(give)), 1
    )
    (joined,) = kernel_call(
        join_kernel, [shaped(block_rows // 2, BF16)], [], (where, quad, to_second(quad)), 1
    )
    joined_next = to_first(joined)
    d_proj, d_fc, d_out, small_sums = kernel_call(
        output_kernel,
        [
            jax.ShapeDtypeStruct((columns, features), FP32),
            jax.ShapeDtypeStruct((shard, hidden_width), FP32),
            jax.ShapeDtypeStruct((shard, features), FP32),
            jax.ShapeDtypeStruct((16, features), FP32),
        ],
        [pltpu.VMEM((block_rows, features), BF16), pltpu.VMEM((block_rows, features), BF16)],
        (where, joined, joined_next, to_core(joined), to_core(joined_next)),
        2,
    )
    d_bias_out, d_bias_proj, d_gain_two, d_shift_two = (
        small_sums[0, n * shard : (n + 1) * shard] for n in range(4)
    )
    d_bias_fc = small_sums[1]

    block_shape = (fsdp, half + 16, 3 * width)
    qkv_keep, qkv_send = kernel_call(
        qkv_grad_kernel,
        [jax.ShapeDtypeStruct(block_shape, FP32), jax.ShapeDtypeStruct(block_shape, BF16)],
        [pltpu.VMEM((features, 3 * width), FP32)],
        (
            where,
            normed_mine,
            *packed,
            weight_q,
            weight_k,
            weight_v,
            small_all,
        ),
        8,
        after=tuple(arrived[1:]) + (give,),
    )
    qkv_blocks = add_up(qkv_keep, to_core(qkv_send)).astype(BF16)
    qkv_half = scatter_parts(qkv_blocks[:2], qkv_blocks[2:])
    halves = swap_chips([jnp.stack([qkv_half, to_core(qkv_half)])] * 4)
    d_qkv, extra = kernel_call(
        qkv_output_kernel,
        [
            jax.ShapeDtypeStruct((shard, 3 * features), FP32),
            jax.ShapeDtypeStruct((chips, 16, 3 * width), FP32),
        ],
        [],
        tuple([where] + halves),
        2,
    )
    owner_extra = pick(extra, part)
    d_bias_q = owner_extra[2, :width]
    d_bias_v = owner_extra[2, 2 * width :]
    norm_total = jnp.sum(extra[:, :2, :shard], axis=0)
    d_gain_one = norm_total[0]
    d_shift_one = norm_total[1]

    return (
        block_out,
        grad_tokens,
        d_qkv,
        d_bias_q,
        d_bias_v,
        d_out,
        d_bias_out,
        d_fc,
        d_bias_fc,
        d_proj,
        d_bias_proj,
        d_gain_one,
        d_shift_one,
        d_gain_two,
        d_shift_two,
    )


def solution(mesh):
    in_specs = (
        P(("fsdp", "ctx"), None),
        P(("fsdp", "ctx"), None),
        P("fsdp", None),
        P("fsdp"),
        P("fsdp"),
        P("fsdp", None),
        P("fsdp"),
        P("fsdp", None),
        P("fsdp"),
        P("fsdp", None),
        P("fsdp"),
        P("fsdp"),
        P("fsdp"),
        P("fsdp"),
        P("fsdp"),
        P("fsdp", None),
        P("fsdp", None),
    )
    out_specs = (
        P(("fsdp", "ctx"), None),
        P(("fsdp", "ctx"), None),
        P("fsdp", None),
        P("fsdp"),
        P("fsdp"),
        P("fsdp", None),
        P("fsdp"),
        P("fsdp", None),
        P("fsdp"),
        P("fsdp", None),
        P("fsdp"),
        P("fsdp"),
        P("fsdp"),
        P("fsdp"),
        P("fsdp"),
    )
    ctx = mesh.shape["ctx"]
    four_by_four = mesh.shape["fsdp"] == 4 and ctx == 8 and HEADS % (ctx // 2) == 0
    body = fast_body if four_by_four else general_body
    return jax.shard_map(body, mesh=mesh, in_specs=in_specs, out_specs=out_specs, check_vma=False)
```

```python
import functools

import jax
import jax.numpy as jnp
from jax import lax
from jax.experimental import pallas as pl
from jax.experimental.pallas import tpu as pltpu
from jax.sharding import PartitionSpec as P

HEADS = 12


EPS = 1e-05


def layer_norm(values, gain_row, shift_row):
    centre = values - jnp.mean(values, axis=1, keepdims=True)
    inverse = lax.rsqrt(jnp.mean(centre * centre, axis=1, keepdims=True) + EPS)
    normed = centre * inverse
    return (normed * gain_row + shift_row, normed, inverse)


def norm_back(grad_in, normed, inverse, gain_row):
    scaled = grad_in * gain_row
    inner_grad = inverse * (
        scaled
        - jnp.mean(scaled, axis=1, keepdims=True)
        - normed * jnp.mean(scaled * normed, axis=1, keepdims=True)
    )
    return (inner_grad, jnp.sum(grad_in * normed, axis=0), jnp.sum(grad_in, axis=0))


def contract_rows(left_side, right_side):
    return lax.dot_general(
        left_side, right_side, (((0,), (0,)), ((), ())), preferred_element_type=jnp.float32
    )


def times_transpose(left_side, right_side):
    return lax.dot_general(
        left_side, right_side, (((1,), (1,)), ((), ())), preferred_element_type=jnp.float32
    )


def gelu_tanh(values):
    return jax.nn.gelu(values, approximate=True)


def describe(slot_ids, row_count, count_row, offsets, seq_ends):
    peer_count = count_row.shape[0]
    device = slot_ids // row_count
    within = slot_ids - device * row_count
    matches = device[:, None] == jnp.arange(peer_count, dtype=jnp.int32)[None, :]
    live_count = jnp.sum(jnp.where(matches, count_row[None, :], 0), axis=1)
    first_place = jnp.sum(jnp.where(matches, offsets[None, :], 0), axis=1)
    places = first_place + within
    segment = jnp.sum((places[:, None] >= seq_ends[None, :]).astype(jnp.int32), axis=1)
    return (within < live_count, places, segment, slot_ids)


def allowed(query_info, key_info):
    q_live, q_place, q_seg, q_slot = query_info
    k_live, k_place, k_seg, k_slot = key_info
    same_seq = (
        q_live[:, None]
        & k_live[None, :]
        & (q_seg[:, None] == k_seg[None, :])
        & (k_place[None, :] <= q_place[:, None])
    )
    return same_seq | (q_slot[:, None] == k_slot[None, :])


def over_blocks(step_fn, status, pieces, row_count):
    total_rows = pieces[0].shape[0]
    block_total = total_rows // row_count
    stacked = tuple((piece.reshape((block_total, row_count) + piece.shape[1:]) for piece in pieces))

    def scan_body(state_now, scan_item):
        block_index, block_parts = scan_item
        return (step_fn(state_now, block_parts, block_index * row_count), None)

    status, unused = lax.scan(
        scan_body, status, (jnp.arange(block_total, dtype=jnp.int32), stacked)
    )
    return status


def score_grads(
    query_heads, key_heads, value_heads, grad_heads, lse_rows, delta_rows, permitted, scaling
):
    scores = (
        jnp.einsum("qhd,khd->hqk", query_heads, key_heads, preferred_element_type=jnp.float32)
        * scaling
    )
    probabilities = jnp.where(permitted[None], jnp.exp(scores - lse_rows[:, :, None]), 0.0)
    grad_probs = jnp.einsum(
        "qhd,khd->hqk", grad_heads, value_heads, preferred_element_type=jnp.float32
    )
    grad_scores = (probabilities * (grad_probs - delta_rows[:, :, None])).astype(jnp.bfloat16)
    return (probabilities.astype(jnp.bfloat16), grad_scores)


def general_body(
    tokens,
    cotangent,
    w_qkv,
    b_query,
    b_value,
    w_out,
    b_out,
    w_fc,
    b_fc,
    w_proj,
    b_proj,
    gain1,
    shift1,
    gain2,
    shift2,
    counts,
    seq_lengths,
):
    row_count, feature_count = tokens.shape
    peer_count = lax.axis_size("ctx")
    my_index = lax.axis_index("ctx")
    head_count = HEADS
    head_width = feature_count // head_count
    scaling = head_width ** (-0.5)
    count_row = counts[0]
    offsets = jnp.cumsum(count_row) - count_row
    seq_ends = jnp.cumsum(seq_lengths[0])

    def locate(first_slot, length):
        return describe(
            first_slot + jnp.arange(length, dtype=jnp.int32),
            row_count,
            count_row,
            offsets,
            seq_ends,
        )

    own_rows = locate(my_index * row_count, row_count)
    fp32 = jnp.float32
    bf16 = jnp.bfloat16
    (
        qkv_full,
        query_bias,
        value_bias,
        out_full,
        out_bias,
        fc_full,
        fc_bias,
        proj_full,
        proj_bias,
        gain_one,
        shift_one,
        gain_two,
        shift_two,
    ) = (
        lax.all_gather(w_qkv, "fsdp", axis=0, tiled=True),
        lax.all_gather(b_query, "fsdp", axis=0, tiled=True),
        lax.all_gather(b_value, "fsdp", axis=0, tiled=True),
        lax.all_gather(w_out, "fsdp", axis=0, tiled=True),
        lax.all_gather(b_out, "fsdp", axis=0, tiled=True),
        lax.all_gather(w_fc, "fsdp", axis=0, tiled=True),
        lax.all_gather(b_fc, "fsdp", axis=0, tiled=True),
        lax.all_gather(w_proj, "fsdp", axis=0, tiled=True),
        lax.all_gather(b_proj, "fsdp", axis=0, tiled=True),
        lax.all_gather(gain1, "fsdp", axis=0, tiled=True),
        lax.all_gather(shift1, "fsdp", axis=0, tiled=True),
        lax.all_gather(gain2, "fsdp", axis=0, tiled=True),
        lax.all_gather(shift2, "fsdp", axis=0, tiled=True),
    )
    inputs = tokens.astype(fp32)
    normed_one, unit_one, inverse_one = layer_norm(
        inputs, gain_one.astype(fp32), shift_one.astype(fp32)
    )
    normed_low = normed_one.astype(bf16)
    bias_row = jnp.concatenate([query_bias, jnp.zeros_like(query_bias), value_bias]).astype(fp32)
    packed = (jnp.dot(normed_low, qkv_full, preferred_element_type=fp32) + bias_row).astype(bf16)
    query_rows = packed[:, :feature_count]
    key_rows = packed[:, feature_count : 2 * feature_count]
    value_rows = packed[:, 2 * feature_count :]
    query_heads = query_rows.reshape(row_count, head_count, head_width)

    def forward_step(status, pieces, first_row):
        running_max, running_sum, running_acc = status
        key_piece, value_piece = pieces
        length = key_piece.shape[0]
        key_heads = key_piece.reshape(length, head_count, head_width)
        value_heads = value_piece.reshape(length, head_count, head_width)
        scores = (
            jnp.einsum("qhd,khd->hqk", query_heads, key_heads, preferred_element_type=fp32)
            * scaling
        )
        permitted = allowed(own_rows, locate(first_row, length))
        scores = jnp.where(permitted[None], scores, -jnp.inf)
        new_max = jnp.maximum(running_max, jnp.max(scores, axis=2))
        fading = jnp.exp(running_max - new_max)
        weights = jnp.exp(scores - new_max[:, :, None])
        running_sum = running_sum * fading + jnp.sum(weights, axis=2)
        update = jnp.einsum(
            "hqk,khd->qhd", weights.astype(bf16), value_heads, preferred_element_type=fp32
        )
        running_acc = running_acc * jnp.transpose(fading)[:, :, None] + update
        return (new_max, running_sum, running_acc)

    start_state = (
        jnp.full((head_count, row_count), -1e30, fp32),
        jnp.zeros((head_count, row_count), fp32),
        jnp.zeros((row_count, head_count, head_width), fp32),
    )
    final_max, final_sum, final_acc = over_blocks(
        forward_step,
        start_state,
        (
            lax.all_gather(key_rows, "ctx", axis=0, tiled=True),
            lax.all_gather(value_rows, "ctx", axis=0, tiled=True),
        ),
        row_count,
    )
    attended_heads = final_acc / jnp.transpose(final_sum)[:, :, None]
    attended = attended_heads.reshape(row_count, feature_count)
    log_total = final_max + jnp.log(final_sum)
    attended_low = attended.astype(bf16)
    middle = (
        inputs
        + jnp.dot(attended_low, out_full, preferred_element_type=fp32)
        + out_bias.astype(fp32)
    )
    normed_two, unit_two, inverse_two = layer_norm(
        middle, gain_two.astype(fp32), shift_two.astype(fp32)
    )
    normed_two_low = normed_two.astype(bf16)
    hidden = jnp.dot(normed_two_low, fc_full, preferred_element_type=fp32) + fc_bias.astype(fp32)
    activated = gelu_tanh(hidden).astype(bf16)
    output = (
        middle + jnp.dot(activated, proj_full, preferred_element_type=fp32) + proj_bias.astype(fp32)
    )
    output_low = output.astype(bf16)
    qkv_full, out_full, fc_full, proj_full, gain_one, gain_two = (
        lax.all_gather(w_qkv, "fsdp", axis=0, tiled=True),
        lax.all_gather(w_out, "fsdp", axis=0, tiled=True),
        lax.all_gather(w_fc, "fsdp", axis=0, tiled=True),
        lax.all_gather(w_proj, "fsdp", axis=0, tiled=True),
        lax.all_gather(gain1, "fsdp", axis=0, tiled=True),
        lax.all_gather(gain2, "fsdp", axis=0, tiled=True),
    )
    live_rows = own_rows[0].astype(fp32)[:, None]
    grad_out = cotangent.astype(fp32) * live_rows
    grad_out_low = grad_out.astype(bf16)
    grad_proj = contract_rows(activated, grad_out_low)
    grad_proj_bias = jnp.sum(grad_out, axis=0)
    grad_act = times_transpose(grad_out_low, proj_full)
    grad_hidden = jax.vjp(gelu_tanh, hidden)[1](grad_act)[0]
    grad_hidden_low = grad_hidden.astype(bf16)
    grad_fc = contract_rows(normed_two_low, grad_hidden_low)
    grad_fc_bias = jnp.sum(grad_hidden_low.astype(fp32), axis=0)
    grad_normed_two = times_transpose(grad_hidden_low, fc_full)
    grad_mid_norm, grad_gain_two, grad_shift_two = norm_back(
        grad_normed_two, unit_two, inverse_two, gain_two.astype(fp32)
    )
    grad_middle = grad_out + grad_mid_norm
    grad_middle_low = grad_middle.astype(bf16)
    grad_out_proj = contract_rows(attended_low, grad_middle_low)
    grad_out_bias = jnp.sum(grad_middle_low.astype(fp32), axis=0)
    grad_attended = times_transpose(grad_middle_low, out_full).astype(bf16)
    grad_heads = grad_attended.reshape(row_count, head_count, head_width)
    delta_rows = jnp.transpose(jnp.sum(grad_heads.astype(fp32) * attended_heads, axis=2))

    def back_step(status, pieces, first_row):
        grad_query, grad_keys = status
        key_piece, value_piece = pieces
        length = key_piece.shape[0]
        key_heads = key_piece.reshape(length, head_count, head_width)
        value_heads = value_piece.reshape(length, head_count, head_width)
        permitted = allowed(own_rows, locate(first_row, length))
        probs_low, grad_scores = score_grads(
            query_heads,
            key_heads,
            value_heads,
            grad_heads,
            log_total,
            delta_rows,
            permitted,
            scaling,
        )
        grad_query = (
            grad_query
            + jnp.einsum("hqk,khd->qhd", grad_scores, key_heads, preferred_element_type=fp32)
            * scaling
        )
        grad_key_part = (
            jnp.einsum("hqk,qhd->khd", grad_scores, query_heads, preferred_element_type=fp32)
            * scaling
        )
        grad_value_part = jnp.einsum(
            "hqk,qhd->khd", probs_low, grad_heads, preferred_element_type=fp32
        )
        joined = jnp.concatenate(
            [
                grad_key_part.reshape(length, feature_count),
                grad_value_part.reshape(length, feature_count),
            ],
            axis=1,
        )
        current = lax.dynamic_slice_in_dim(grad_keys, first_row, length, 0)
        grad_keys = lax.dynamic_update_slice_in_dim(grad_keys, current + joined, first_row, 0)
        return (grad_query, grad_keys)

    keys_start = jnp.zeros((peer_count * row_count, 2 * feature_count), fp32)
    grad_query, grad_keys = over_blocks(
        back_step,
        (jnp.zeros((row_count, head_count, head_width), fp32), keys_start),
        (
            lax.all_gather(key_rows, "ctx", axis=0, tiled=True),
            lax.all_gather(value_rows, "ctx", axis=0, tiled=True),
        ),
        row_count,
    )
    grad_kv = lax.psum_scatter(
        grad_keys.astype(jnp.bfloat16), "ctx", scatter_dimension=0, tiled=True
    ).astype(jnp.float32)
    grad_packed = jnp.concatenate(
        [grad_query.reshape(row_count, feature_count), grad_kv], axis=1
    ).astype(bf16)
    grad_packed_wide = grad_packed.astype(fp32)
    grad_query_bias = jnp.sum(grad_packed_wide[:, :feature_count], axis=0)
    grad_value_bias = jnp.sum(grad_packed_wide[:, 2 * feature_count :], axis=0)
    grad_qkv = contract_rows(normed_low, grad_packed)
    grad_normed_one = times_transpose(grad_packed, qkv_full)
    grad_in_norm, grad_gain_one, grad_shift_one = norm_back(
        grad_normed_one, unit_one, inverse_one, gain_one.astype(fp32)
    )
    grad_tokens = grad_middle + grad_in_norm
    (
        sum_qkv,
        sum_qbias,
        sum_vbias,
        sum_out,
        sum_obias,
        sum_fc,
        sum_fbias,
        sum_proj,
        sum_pbias,
        sum_gain_one,
        sum_shift_one,
        sum_gain_two,
        sum_shift_two,
    ) = (
        lax.psum_scatter(
            grad_qkv.astype(jnp.bfloat16), "fsdp", scatter_dimension=0, tiled=True
        ).astype(jnp.float32),
        lax.psum_scatter(
            grad_query_bias.astype(jnp.bfloat16), "fsdp", scatter_dimension=0, tiled=True
        ).astype(jnp.float32),
        lax.psum_scatter(
            grad_value_bias.astype(jnp.bfloat16), "fsdp", scatter_dimension=0, tiled=True
        ).astype(jnp.float32),
        lax.psum_scatter(
            grad_out_proj.astype(jnp.bfloat16), "fsdp", scatter_dimension=0, tiled=True
        ).astype(jnp.float32),
        lax.psum_scatter(
            grad_out_bias.astype(jnp.bfloat16), "fsdp", scatter_dimension=0, tiled=True
        ).astype(jnp.float32),
        lax.psum_scatter(
            grad_fc.astype(jnp.bfloat16), "fsdp", scatter_dimension=0, tiled=True
        ).astype(jnp.float32),
        lax.psum_scatter(
            grad_fc_bias.astype(jnp.bfloat16), "fsdp", scatter_dimension=0, tiled=True
        ).astype(jnp.float32),
        lax.psum_scatter(
            grad_proj.astype(jnp.bfloat16), "fsdp", scatter_dimension=0, tiled=True
        ).astype(jnp.float32),
        lax.psum_scatter(
            grad_proj_bias.astype(jnp.bfloat16), "fsdp", scatter_dimension=0, tiled=True
        ).astype(jnp.float32),
        lax.psum_scatter(
            grad_gain_one.astype(jnp.bfloat16), "fsdp", scatter_dimension=0, tiled=True
        ).astype(jnp.float32),
        lax.psum_scatter(
            grad_shift_one.astype(jnp.bfloat16), "fsdp", scatter_dimension=0, tiled=True
        ).astype(jnp.float32),
        lax.psum_scatter(
            grad_gain_two.astype(jnp.bfloat16), "fsdp", scatter_dimension=0, tiled=True
        ).astype(jnp.float32),
        lax.psum_scatter(
            grad_shift_two.astype(jnp.bfloat16), "fsdp", scatter_dimension=0, tiled=True
        ).astype(jnp.float32),
    )
    totals = (
        lax.psum(sum_qkv.astype(jnp.bfloat16), "ctx").astype(jnp.float32),
        lax.psum(sum_qbias.astype(jnp.bfloat16), "ctx").astype(jnp.float32),
        lax.psum(sum_vbias.astype(jnp.bfloat16), "ctx").astype(jnp.float32),
        lax.psum(sum_out.astype(jnp.bfloat16), "ctx").astype(jnp.float32),
        lax.psum(sum_obias.astype(jnp.bfloat16), "ctx").astype(jnp.float32),
        lax.psum(sum_fc.astype(jnp.bfloat16), "ctx").astype(jnp.float32),
        lax.psum(sum_fbias.astype(jnp.bfloat16), "ctx").astype(jnp.float32),
        lax.psum(sum_proj.astype(jnp.bfloat16), "ctx").astype(jnp.float32),
        lax.psum(sum_pbias.astype(jnp.bfloat16), "ctx").astype(jnp.float32),
        lax.psum(sum_gain_one.astype(jnp.bfloat16), "ctx").astype(jnp.float32),
        lax.psum(sum_shift_one.astype(jnp.bfloat16), "ctx").astype(jnp.float32),
        lax.psum(sum_gain_two.astype(jnp.bfloat16), "ctx").astype(jnp.float32),
        lax.psum(sum_shift_two.astype(jnp.bfloat16), "ctx").astype(jnp.float32),
    )
    return (
        output_low,
        grad_tokens,
        totals[0],
        totals[1],
        totals[2],
        totals[3],
        totals[4],
        totals[5],
        totals[6],
        totals[7],
        totals[8],
        totals[9],
        totals[10],
        totals[11],
        totals[12],
    )


FP32 = jnp.float32
BF16 = jnp.bfloat16
FLOOR = -1e30
NEVER = 1 << 30


def dot_nt(left_side, right_side):
    return lax.dot_general(
        left_side, right_side, (((1,), (1,)), ((), ())), preferred_element_type=FP32
    )


def dot_nn(left_side, right_side):
    return lax.dot_general(
        left_side, right_side, (((1,), (0,)), ((), ())), preferred_element_type=FP32
    )


def spread(column_tile, width):
    return jnp.concatenate([column_tile] * (width // column_tile.shape[1]), axis=1)


def masked_scores(scores, key_ids, first_row, last_row):
    permitted = key_ids >= first_row
    if last_row is not None:
        permitted = permitted & (key_ids <= last_row)
    return jnp.where(permitted, scores, -jnp.inf)


def whole_vector(small_ref, number):
    parts = [small_ref[f, number : number + 1, :] for f in range(small_ref.shape[0])]
    return jnp.concatenate(parts, axis=1)


def project_block(
    tokens_ref, wq_ref, wk_ref, wv_ref, small_ref, chip, stores, position, wanted
):
    q_ref, k_ref, kt_ref, v_ref, vt_ref, normed_ref = stores
    gain, shift = whole_vector(small_ref, 4), whole_vector(small_ref, 5)
    normed = layer_norm(tokens_ref[...].astype(FP32), gain, shift)[0]
    normed = normed.astype(BF16)
    keys = dot_nn(normed, wk_ref[...])
    values = dot_nn(normed, wv_ref[...]) + small_ref[chip, 1:2, :]
    k_ref[position] = keys.astype(BF16)
    v_ref[position] = values.astype(BF16)
    kt_ref[position] = keys.T.astype(BF16)
    vt_ref[position] = values.T.astype(BF16)
    if wanted:
        queries = (dot_nn(normed, wq_ref[...]) + small_ref[chip, 0:1, :]).astype(BF16)
        q_ref[position // 2] = (queries.astype(FP32) * 0.125).astype(BF16)
        normed_ref[position // 2] = normed


def project_kernel(
    where,
    t0,
    t1,
    t2,
    t3,
    w_ref,
    smalls_ref,
    near_ref,
    across_ref,
    near_other,
    across_other,
    q,
    k,
    kt,
    v,
    vt,
    normed,
    full_ref,
    wq,
    wk,
    wv,
    small_ref,
):
    part, core, chip = where[0], where[1], where[2]
    near, across = 1 + core, 2 - core
    shard, wide = w_ref.shape
    features, half, width = wide // 3, shard // 2, wq.shape[1]
    full_ref[pl.ds(pl.multiple_of(part * shard, 16), shard), :] = w_ref[...]
    small_ref[part] = smalls_ref[...].astype(FP32)
    step = half + 16
    pieces = (
        (near_ref, 0, part ^ near, core),
        (across_ref, 0, part ^ across, core),
        (across_ref, step, part ^ 3, core),
        (near_other, 0, part ^ across, 1 - core),
        (across_other, 0, part ^ near, 1 - core),
        (across_other, step, part ^ 3, 1 - core),
    )
    for ref, at, owner, which in pieces:
        first = pl.multiple_of(owner * shard + which * half, 16)
        full_ref[pl.ds(first, half), :] = ref[at : at + half, :]
        small_ref[owner] = ref[at + half : at + step, 0:width].astype(FP32)
    for z in range(features // width):

        @pl.when(chip == z)
        def own_columns():
            for n, ref in enumerate((wq, wk, wv)):
                first = features * n + width * z
                ref[...] = full_ref[:, first : first + width]

    stores = (q, k, kt, v, vt, normed)
    for n, block in enumerate((t0, t1, t2, t3)):
        owner = (chip ^ (n // 2)) % 2
        position = 2 * owner + (core if n % 2 == 0 else 1 - core)
        project_block(block, wq, wk, wv, small_ref, chip, stores, position, n % 2 == 0)


def attend_kernel(
    where,
    t0,
    t1,
    t2,
    t3,
    wq_ref,
    wk_ref,
    wv_ref,
    small_ref,
    q_half,
    k_half,
    kt_half,
    v_half,
    vt_half,
    normed_half,
    key_ref,
    low_ref,
    high_ref,
    far_ref,
    q_ref,
    k_ref,
    kt_ref,
    v_ref,
    normed_ref,
    o0_ref,
    o1_ref,
    o2_ref,
    o3_ref,
    ot_ref,
    lse_ref,
    zero_ref,
    vt_ref,
    acc_ref,
    o_ref,
):
    blocks, rows, width = q_ref.shape
    heads = width // 64
    core, chip = where[1], where[2]
    side = chip // 2
    zero_ref[...] = jnp.zeros_like(zero_ref)
    stores = (q_ref, k_ref, kt_ref, v_ref, vt_ref, normed_ref)
    for n, block in enumerate((t0, t1, t2, t3)):
        owner = chip ^ (2 + n // 2)
        position = 2 * owner + (core if n % 2 == 0 else 1 - core)
        project_block(
            block,
            wq_ref,
            wk_ref,
            wv_ref,
            small_ref,
            chip,
            stores,
            position,
            n % 2 == 0,
        )
    for n in range(blocks):
        for source, target in ((k_half, k_ref), (kt_half, kt_ref), (v_half, v_ref), (vt_half, vt_ref)):
            target[side * blocks + n] = source[n]
    for n in range(blocks // 2):
        q_ref[side * (blocks // 2) + n] = q_half[n]
        normed_ref[side * (blocks // 2) + n] = normed_half[n]

    def query_block(index, unused):
        queries = [q_ref[index, :, 64 * h : 64 * h + 64] for h in range(heads)]
        acc_ref[...] = jnp.zeros_like(acc_ref)

        def key_step(key_block, carry, first_row, last_row):
            ids = spread(key_ref[key_block], rows)
            result = []
            for h in range(heads):
                span = slice(64 * h, 64 * h + 64)
                top, total = carry[h]
                scores = dot_nt(k_ref[key_block, :, span], queries[h])
                scores = masked_scores(scores, ids, first_row, last_row)
                new_top = jnp.maximum(top, jnp.max(scores, axis=0, keepdims=True))
                fade = jnp.exp(top - new_top)
                weights = jnp.exp(scores - new_top)
                total = total * fade + jnp.sum(weights, axis=0, keepdims=True)
                acc_ref[span, :] = acc_ref[span, :] * fade + dot_nn(
                    vt_ref[key_block, span, :], weights.astype(BF16)
                )
                result.append((new_top, total))
            return tuple(result)

        start = tuple(
            (jnp.full((1, rows), FLOOR, FP32), jnp.zeros((1, rows), FP32)) for h in range(heads)
        )
        own = 2 * index + core
        far_row = far_ref[index]
        carry = lax.fori_loop(0, own, lambda j, c: key_step(j, c, far_row, None), start)
        carry = key_step(own, carry, low_ref[index], high_ref[index])
        for h in range(heads):
            span = slice(64 * h, 64 * h + 64)
            top, total = carry[h]
            attended = acc_ref[span, :] / total
            ot_ref[index, span, :] = attended
            o_ref[index, :, span] = attended.T.astype(BF16)
            lse_ref[index, h : h + 1, :] = top + jnp.log(total)
        return unused

    lax.fori_loop(0, blocks, query_block, 0)
    for s, ref in enumerate((o0_ref, o1_ref, o2_ref, o3_ref)):
        ref[...] = o_ref[chip ^ s]


def attend_back_kernel(
    where,
    q_ref,
    k_ref,
    kt_ref,
    v_ref,
    d0_ref,
    d1_ref,
    d2_ref,
    d3_ref,
    key_ref,
    low_ref,
    high_ref,
    far_ref,
    ot_ref,
    lse_ref,
    dq_ref,
    keep_ref,
    send_ref,
    acc_ref,
    dk_ref,
    dv_ref,
    da_ref,
):
    blocks, rows, width = q_ref.shape
    heads = width // 64
    core, chip = where[1], where[2]
    for s, ref in enumerate((d0_ref, d1_ref, d2_ref, d3_ref)):
        da_ref[chip ^ s] = ref[...]
    dk_ref[...] = jnp.zeros_like(dk_ref)
    dv_ref[...] = jnp.zeros_like(dv_ref)

    def query_block(index, unused):
        queries = [q_ref[index, :, 64 * h : 64 * h + 64] for h in range(heads)]
        grads = [da_ref[index, :, 64 * h : 64 * h + 64] for h in range(heads)]
        deltas = [
            jnp.sum(
                grads[h].astype(FP32).T * ot_ref[index, 64 * h : 64 * h + 64, :],
                axis=0,
                keepdims=True,
            )
            for h in range(heads)
        ]
        logs = [lse_ref[index, h : h + 1, :] for h in range(heads)]
        acc_ref[...] = jnp.zeros_like(acc_ref)

        def key_step(key_block, first_row, last_row):
            ids = spread(key_ref[key_block], rows)
            for h in range(heads):
                span = slice(64 * h, 64 * h + 64)
                scores = dot_nt(k_ref[key_block, :, span], queries[h])
                scores = masked_scores(scores, ids, first_row, last_row)
                weights = jnp.exp(scores - logs[h])
                slopes = dot_nt(v_ref[key_block, :, span], grads[h])
                dscores = (weights * (slopes - deltas[h])).astype(BF16)
                dv_ref[h, key_block] += dot_nn(weights.astype(BF16), grads[h])
                dk_ref[h, key_block] += dot_nn(dscores, queries[h])
                acc_ref[span, :] += dot_nn(kt_ref[key_block, span, :], dscores)

        own = 2 * index + core
        far_row = far_ref[index]

        def far_step(key_block, state):
            key_step(key_block, far_row, None)
            return state

        lax.fori_loop(0, own, far_step, 0)
        key_step(own, low_ref[index], high_ref[index])
        for h in range(heads):
            span = slice(64 * h, 64 * h + 64)
            dq_ref[index, :, span] = (acc_ref[span, :] * 0.125).T.astype(BF16)
        return unused

    lax.fori_loop(0, blocks, query_block, 0)

    def write_block(index, unused):
        mine = 2 * index + core
        theirs = 2 * index + 1 - core
        for h in range(heads):
            left = slice(64 * h, 64 * h + 64)
            right = slice(width + 64 * h, width + 64 * h + 64)
            keep_ref[index, :, left] = dk_ref[h, mine]
            keep_ref[index, :, right] = dv_ref[h, mine]
            send_ref[index, :, left] = dk_ref[h, theirs].astype(BF16)
            send_ref[index, :, right] = dv_ref[h, theirs].astype(BF16)
        return unused

    lax.fori_loop(0, blocks, write_block, 0)


def kernel_call(kernel, outputs, scratch, operands, cost, special={}, after=()):
    whole = pl.BlockSpec(memory_space=pltpu.VMEM)
    in_specs = [pl.BlockSpec(memory_space=pltpu.SMEM)]
    in_specs += [special.get(n, whole) for n in range(1, len(operands))]
    in_specs += [pl.BlockSpec(memory_space=pl.ANY) for unused in after]
    count = len(operands)

    def ordered(*refs):
        return kernel(*refs[:count], *refs[count + len(after) :])

    moved = sum(v.size * v.dtype.itemsize for v in list(operands) + list(outputs))
    return pl.pallas_call(
        ordered,
        out_shape=outputs,
        in_specs=in_specs,
        out_specs=[pl.BlockSpec(memory_space=pltpu.VMEM) for unused in outputs],
        scratch_shapes=scratch,
        compiler_params=pltpu.CompilerParams(vmem_limit_bytes=56 * 1024 * 1024),
        cost_estimate=pl.CostEstimate(
            flops=cost * 1153 * 10**6, bytes_accessed=moved, transcendentals=0
        ),
    )(*operands, *after)


def pack_kernel(where, dq_ref, keep_ref, arrived_ref, p0, p1, p2, p3):
    chip = where[2]
    width = dq_ref.shape[2]
    for s, ref in enumerate((p0, p1, p2, p3)):
        owner = chip ^ s
        ref[:, 0:width] = dq_ref[owner]
        ref[:, width:] = (keep_ref[owner] + arrived_ref[owner].astype(FP32)).astype(BF16)


def middle_kernel(
    where,
    a0_ref,
    a1_ref,
    a2_ref,
    a3_ref,
    tokens_ref,
    cotangent_ref,
    live_ref,
    small_ref,
    bundle_own,
    bundle_other,
    block_ref,
    dx_ref,
    d0_ref,
    d1_ref,
    d2_ref,
    d3_ref,
    mine_ref,
    send_ref,
    sums_ref,
    wo_ref,
    wf_ref,
    wp_ref,
    g_ref,
    dz_ref,
    sems,
):
    rows, features = tokens_ref.shape
    parts = wf_ref.shape[0]
    shard, hidden_width = features // parts, wp_ref.shape[0]
    columns = hidden_width // parts
    half, half_columns = shard // 2, columns // 2
    core, chip = where[1], where[2]

    starts = {"proj": [], "out": [], "fc": []}

    def fetch(kind, source, target):
        number = sum(len(v) for v in starts.values())
        starts[kind].append(pltpu.make_async_copy(source, target, sems.at[number]))

    def rows_at(owner, which, size):
        return pl.ds(pl.multiple_of(owner * 2 * size + which * size, 16), size)

    pieces = []
    for owner in range(parts):
        pieces.append((bundle_own.at[owner], owner, core))
        pieces.append((bundle_other.at[owner], owner, 1 - core))
    for piece, owner, which in pieces:
        fetch("out", piece.at[half_columns : half_columns + half, :], wo_ref.at[rows_at(owner, which, half), :])
    for piece, owner, which in pieces:
        for j in range(parts):
            first = half_columns + half * (j + 1)
            fetch("fc", piece.at[first : first + half, :], wf_ref.at[j, rows_at(owner, which, half), :])
    for piece, owner, which in pieces:
        fetch("proj", piece.at[0:half_columns, :], wp_ref.at[rows_at(owner, which, half_columns), :])
    for kind in ("out", "fc", "proj"):
        for copy in starts[kind]:
            copy.start()
    for copy in starts["out"]:
        copy.wait()

    attended = [a0_ref, a1_ref, a2_ref, a3_ref]
    middle = tokens_ref[...].astype(FP32) + whole_vector(small_ref, 2)
    a_start = 2 * parts * half_columns + features
    for s in range(parts):
        span = pl.ds(pl.multiple_of((chip ^ s) * shard, 16), shard)
        middle = middle + dot_nn(attended[s][...], wo_ref[span, :])
        mine_ref[:, a_start + shard * s : a_start + shard * (s + 1)] = attended[s][...]
        send_ref[:, a_start + shard * s : a_start + shard * (s + 1)] = attended[s][...]
    normed, unit, inverse = layer_norm(
        middle, whole_vector(small_ref, 6), whole_vector(small_ref, 7)
    )
    normed_low = normed.astype(BF16)
    h_start = 2 * parts * half_columns
    mine_ref[:, h_start : h_start + features] = normed_low
    send_ref[:, h_start : h_start + features] = normed_low
    grad_out = cotangent_ref[...].astype(FP32) * live_ref[...]
    grad_out_low = grad_out.astype(BF16)
    y_start = a_start + features
    mine_ref[:, y_start : y_start + features] = grad_out_low
    send_ref[:, y_start : y_start + features] = grad_out_low
    for copy in starts["fc"] + starts["proj"]:
        copy.wait()

    sums_ref[...] = jnp.zeros_like(sums_ref)
    output = middle + whole_vector(small_ref, 3)
    grad_normed = jnp.zeros((rows, features), FP32)
    scale, cubic = 0.7978845608028654, 0.044715
    for j in range(parts):
        span = slice(columns * j, columns * (j + 1))
        bias_fc = jnp.concatenate([small_ref[j, 8 + n : 9 + n, :] for n in range(parts)], axis=1)
        hidden = dot_nn(normed_low, wf_ref[j]) + bias_fc
        square = hidden * hidden
        bent = jnp.tanh(scale * hidden * (1.0 + cubic * square))
        active = 0.5 * hidden * (1.0 + bent)
        slope = 0.5 * (1.0 + bent) + 0.5 * hidden * (1.0 - bent * bent) * (
            scale * (1.0 + 3.0 * cubic * square)
        )
        g_ref[...] = active.astype(BF16)
        grad_hidden = (dot_nt(grad_out_low, wp_ref[span, :]) * slope).astype(BF16)
        output = output + dot_nn(g_ref[...], wp_ref[span, :])
        grad_normed = grad_normed + dot_nt(grad_hidden, wf_ref[j])
        sums_ref[j, 1:2, :] = jnp.sum(grad_hidden.astype(FP32), axis=0, keepdims=True)
        g_span = slice(half_columns * j, half_columns * (j + 1))
        mine_ref[:, g_span] = g_ref[:, pl.ds(pl.multiple_of(core * half_columns, 128), half_columns)]
        send_ref[:, g_span] = g_ref[
            :, pl.ds(pl.multiple_of((1 - core) * half_columns, 128), half_columns)
        ]
        first = parts * half_columns + columns * (j % 2)

        @pl.when(core == j // 2)
        def keep_hidden():
            mine_ref[:, first : first + columns] = grad_hidden

        @pl.when(core != j // 2)
        def give_hidden():
            send_ref[:, first : first + columns] = grad_hidden

    block_ref[...] = output.astype(BF16)
    inner, gain_sum, shift_sum = norm_back(
        grad_normed, unit, inverse, whole_vector(small_ref, 6)
    )
    grad_middle = grad_out + inner
    dx_ref[...] = grad_middle
    dz_ref[...] = grad_middle.astype(BF16)
    z_start = y_start + features
    part_width = features // 2
    mine_ref[:, z_start : z_start + part_width] = dz_ref[
        :, pl.ds(pl.multiple_of(core * part_width, 128), part_width)
    ]
    send_ref[:, z_start : z_start + part_width] = dz_ref[
        :, pl.ds(pl.multiple_of((1 - core) * part_width, 128), part_width)
    ]
    for s, ref in enumerate((d0_ref, d1_ref, d2_ref, d3_ref)):
        span = pl.ds(pl.multiple_of((chip ^ s) * shard, 16), shard)
        ref[...] = dot_nt(dz_ref[...], wo_ref[span, :]).astype(BF16)
    rows_of_sums = (
        jnp.sum(dz_ref[...].astype(FP32), axis=0, keepdims=True),
        jnp.sum(grad_out, axis=0, keepdims=True),
        gain_sum[None, :],
        shift_sum[None, :],
    )
    for n, row in enumerate(rows_of_sums):
        for f in range(parts):
            sums_ref[f, 0:1, shard * n : shard * (n + 1)] = row[:, shard * f : shard * (f + 1)]


def weight_grad_kernel(where, mine_ref, other_ref, small_ref, keep_ref, send_ref, fc_ref):
    rows = mine_ref.shape[0]
    features = keep_ref.shape[2]
    part, core, chip = where[0], where[1], where[2]
    near, across = 1 + core, 2 - core
    parts = 4
    shard, half_columns = features // parts, features // 2
    h_start = 2 * parts * half_columns
    a_start = h_start + features
    y_start = a_start + features
    z_start = y_start + features

    def product(left, right):
        return contract_rows(mine_ref[:, left], mine_ref[:, right]) + contract_rows(
            other_ref[:, left], other_ref[:, right]
        )

    targets = [(keep_ref, 0, part), (keep_ref, 1, part ^ across)]
    targets += [(send_ref, 0, part ^ near), (send_ref, 1, part ^ 3)]
    fc_base = parts * half_columns
    for j in range(2):
        fc_ref[j] = product(
            pl.ds(h_start, features), pl.ds(fc_base + features * j, features)
        ).astype(BF16)
    out_base = half_columns + 2 * shard
    small_base = out_base + shard // 2
    for ref, slot, owner in targets:
        g_span = pl.ds(pl.multiple_of(owner * half_columns, 128), half_columns)
        ref[slot, 0:half_columns, :] = product(g_span, pl.ds(y_start, features)).astype(BF16)
        for j in range(2):
            first = half_columns + shard * j
            ref[slot, first : first + shard, :] = fc_ref[
                j, pl.ds(pl.multiple_of(owner * shard, 16), shard), :
            ]
        ref[slot, small_base : small_base + 16, :] = small_ref[owner].astype(BF16)
        ref[slot, small_base + 16 :, :] = jnp.zeros_like(ref[slot, small_base + 16 :, :])
    for s in range(parts):
        block = product(
            pl.ds(a_start + shard * s, shard), pl.ds(z_start, half_columns)
        ).astype(BF16)
        owner = chip ^ s
        for ref, slot, wanted in targets:

            @pl.when(owner == wanted)
            def store_block():
                ref[slot, out_base:small_base, 0:half_columns] = block[: shard // 2]
                ref[slot, out_base:small_base, half_columns:] = block[shard // 2 :]


def qkv_grad_kernel(
    where,
    normed_ref,
    p0,
    p1,
    p2,
    p3,
    wq_ref,
    wk_ref,
    wv_ref,
    small_ref,
    keep_ref,
    send_ref,
    total_ref,
):
    blocks, rows, features = normed_ref.shape
    width = wq_ref.shape[1]
    part, core, chip = where[0], where[1], where[2]
    near, across = 1 + core, 2 - core
    parts = 4
    shard = features // parts
    half = shard // 2
    column_sums = [jnp.zeros((1, width), FP32) for n in range(3)]
    for n in range(3):
        total = jnp.zeros((features, width), FP32)
        for b in range(blocks):
            grads = (p0, p1, p2, p3)[b][:, width * n : width * (n + 1)]
            total = total + contract_rows(normed_ref[chip ^ b], grads)
            column_sums[n] = column_sums[n] + jnp.sum(grads.astype(FP32), axis=0, keepdims=True)
        total_ref[:, width * n : width * (n + 1)] = total
    sums = jnp.concatenate(column_sums, axis=1)
    shift_grad = jnp.zeros((features, 1), FP32)
    gain_grad = jnp.zeros((features, 1), FP32)
    for n, ref in enumerate((wq_ref, wk_ref, wv_ref)):
        wide = ref[...].astype(FP32)
        shift_grad = shift_grad + jnp.sum(wide * column_sums[n], axis=1, keepdims=True)
        gain_grad = gain_grad + jnp.sum(
            wide * total_ref[:, width * n : width * (n + 1)], axis=1, keepdims=True
        )
    columns = jnp.concatenate(
        [gain_grad, shift_grad, jnp.zeros((features, 126), FP32)], axis=1
    )
    norm_rows = columns.T[0:8]
    gain, shift = whole_vector(small_ref, 4), whole_vector(small_ref, 5)
    gain_row = (norm_rows[0:1] - shift * norm_rows[1:2]) / gain
    norm_rows = jnp.concatenate([gain_row, norm_rows[1:]], axis=0)
    order = [part, part ^ across, part ^ near, part ^ 3]
    other_order = [part, part ^ near, part ^ across, part ^ 3]
    for ref, which, owners in ((keep_ref, core, order), (send_ref, 1 - core, other_order)):
        for slot in range(parts):
            owner = owners[slot]
            first = pl.multiple_of(owner * shard + which * half, 16)
            ref[slot, 0:half, :] = total_ref[pl.ds(first, half), :].astype(ref.dtype)
            picked = jnp.zeros((8, shard), FP32)
            for f in range(parts):
                picked = jnp.where(owner == f, norm_rows[:, shard * f : shard * (f + 1)], picked)
            row = lax.broadcasted_iota(jnp.int32, (8, 3 * width), 0)
            packed = jnp.concatenate([picked, jnp.zeros((8, 3 * width - shard), FP32)], axis=1)
            tail = jnp.where(row < 2, packed, jnp.where(row == 2, sums, 0.0))
            tail = jnp.concatenate([tail, jnp.zeros_like(tail)], axis=0)
            ref[slot, half : half + 16, :] = tail.astype(ref.dtype)


def relay_kernel(where, keep_ref, theirs_ref, relay_ref):
    relay_ref[...] = (keep_ref[1].astype(FP32) + theirs_ref[1].astype(FP32)).astype(BF16)


def block_kernel(where, keep_ref, theirs_ref, last_ref, out_ref):
    total = keep_ref[0].astype(FP32) + theirs_ref[0].astype(FP32)
    out_ref[...] = (total + last_ref[...].astype(FP32)).astype(BF16)


def input_grad_kernel(
    where, p0, p1, p2, p3, w_ref, tokens_ref, dx_ref, small_ref, out_ref, packed_ref
):
    chip = where[2]
    features = w_ref.shape[0]
    width = p0.shape[1] // 3
    for z in range(4):
        for s, piece in enumerate((p0, p1, p2, p3)):

            @pl.when(chip == z ^ s)
            def place_piece():
                for n in range(3):
                    first = features * n + width * z
                    packed_ref[:, first : first + width] = piece[:, width * n : width * (n + 1)]

    total = dot_nt(packed_ref[...], w_ref[...])
    unit, inverse = layer_norm(
        tokens_ref[...].astype(FP32), whole_vector(small_ref, 4), whole_vector(small_ref, 5)
    )[1:]
    out_ref[...] = dx_ref[...] + norm_back(total, unit, inverse, whole_vector(small_ref, 4))[0]


def output_kernel(
    where, mine_ref, other_ref, proj_ref, fc_ref, out_ref, sums_ref
):
    core = where[1]
    half_columns = proj_ref.shape[0] // 2
    shard, features = out_ref.shape
    out_rows = half_columns + 2 * shard
    small_at = out_rows + shard // 2
    sums_ref[...] = mine_ref[small_at : small_at + 16, :].astype(FP32) + other_ref[
        small_at : small_at + 16, :
    ].astype(FP32)

    def place(ref, which):
        proj_ref[which * half_columns : (which + 1) * half_columns, :] = ref[
            0:half_columns, :
        ].astype(FP32)
        for j in range(2):
            first = half_columns + shard * j
            column = features * (2 * which + j)
            fc_ref[:, column : column + features] = ref[first : first + shard, :].astype(FP32)
        span = slice(features // 2 * which, features // 2 * (which + 1))
        middle = out_rows + shard // 2
        out_ref[0 : shard // 2, span] = ref[out_rows:middle, 0 : features // 2].astype(FP32)
        out_ref[shard // 2 :, span] = ref[out_rows:middle, features // 2 :].astype(FP32)

    @pl.when(core == 0)
    def first_core():
        place(mine_ref, 0)
        place(other_ref, 1)

    @pl.when(core == 1)
    def second_core():
        place(mine_ref, 1)
        place(other_ref, 0)


def qkv_output_kernel(where, h0, h1, h2, h3, out_ref, extra_ref, zero_ref):
    zero_ref[...] = jnp.zeros_like(zero_ref)
    core, chip = where[1], where[2]
    shard, wide = out_ref.shape
    features = wide // 3
    half = shard // 2
    width = h0.shape[2] // 3
    for s, ref in enumerate((h0, h1, h2, h3)):
        extra_ref[chip ^ s] = jnp.where(
            core == 0, ref[0, half : half + 16, :], ref[1, half : half + 16, :]
        ).astype(FP32)
        for z in range(4):

            @pl.when(chip == z ^ s)
            def place_piece():
                for n in range(3):
                    first = features * n + width * z
                    for slot, which in ((0, core), (1, 1 - core)):
                        rows = pl.ds(pl.multiple_of(which * half, 8), half)
                        out_ref[rows, first : first + width] = ref[
                            slot, 0:half, width * n : width * (n + 1)
                        ].astype(FP32)


def fast_body(
    tokens,
    cotangent,
    w_qkv,
    b_query,
    b_value,
    w_out,
    b_out,
    w_fc,
    b_fc,
    w_proj,
    b_proj,
    gain1,
    shift1,
    gain2,
    shift2,
    counts,
    seq_lengths,
):
    rows, features = tokens.shape
    ctx = lax.axis_size("ctx")
    fsdp = lax.axis_size("fsdp")
    chips = ctx // 2
    group_heads = HEADS // chips
    width = features // chips
    shard = features // fsdp
    hidden_width = w_fc.shape[1]
    columns = hidden_width // fsdp
    place = lax.axis_index("ctx")
    chip = place // 2
    core = place % 2
    part = lax.axis_index("fsdp")
    near = 1 + core
    across = 2 - core
    same_core = [[2 * z + k for z in range(chips)] for k in range(2)]
    where = jnp.stack([part, core, chip]).astype(jnp.int32)

    def exchange(value, partner):
        pairs = [
            (f * ctx + c, g * ctx + d)
            for f in range(fsdp)
            for c in range(ctx)
            for g, d in [partner(f, c)]
        ]
        return lax.ppermute(value, ("fsdp", "ctx"), pairs)

    def to_near(value):
        return exchange(value, lambda f, c: (f ^ (1 + c % 2), c))

    def to_across(value):
        return exchange(value, lambda f, c: (f ^ (2 - c % 2), c))

    def to_core(value):
        return exchange(value, lambda f, c: (f, c ^ 1))

    def to_chip(value, step):
        return exchange(value, lambda f, c: (f, c ^ (2 * step)))

    def pick(array, index, axis=0):
        return lax.dynamic_index_in_dim(array, index, axis, keepdims=False)

    def place_all(shape, dtype, items):
        buffer = jnp.zeros(shape, dtype)
        for index, value in items:
            full = value.reshape((1,) * (len(shape) - value.ndim) + value.shape)
            starts = tuple(index) + (0,) * (len(shape) - len(index))
            buffer = lax.dynamic_update_slice(buffer, full.astype(dtype), starts)
        return buffer

    half = shard // 2
    fc_half = lax.dynamic_slice_in_dim(w_fc, core * half, half, 0)
    bundle = jnp.concatenate(
        [
            lax.dynamic_slice_in_dim(w_proj, core * (columns // 2), columns // 2, 0),
            lax.dynamic_slice_in_dim(w_out, core * half, half, 0),
        ]
        + [fc_half[:, columns * j : columns * (j + 1)] for j in range(fsdp)],
        axis=0,
    )

    blocks = [tokens] + [to_chip(tokens, s) for s in (1, 2, 3)]
    bundles = lax.all_gather(bundle, "fsdp", axis=0)

    count_row = counts[0]
    offsets = jnp.cumsum(count_row) - count_row
    seq_ends = jnp.cumsum(seq_lengths[0])
    within = jnp.arange(rows, dtype=jnp.int32)
    slot = jnp.arange(ctx, dtype=jnp.int32)[:, None] * rows + within[None, :]
    live = within[None, :] < count_row[:, None]
    places = offsets[:, None] + within[None, :]
    starts = jnp.max(
        jnp.where(places[:, :, None] >= seq_ends[None, None, :], seq_ends[None, None, :], 0), axis=2
    )
    dead_id = -1 - slot
    key_ids = jnp.where(live, places, dead_id)
    lows = jnp.where(live, starts, dead_id)
    fars = jnp.where(live, starts, NEVER)
    key_tile = jnp.broadcast_to(key_ids[:, :, None], (ctx, rows, 128))

    def own_parity(array):
        return pick(array.reshape((chips, 2) + array.shape[1:]), core, 1)

    low_rows = own_parity(lows)[:, None, :]
    high_rows = own_parity(key_ids)[:, None, :]
    far_rows = own_parity(fars)[:, None, :]
    live_rows = (within < pick(count_row, place)).astype(FP32)[:, None]

    vectors = [b_query, b_value, b_out, b_proj, gain1, shift1, gain2, shift2]
    vectors += [b_fc[shard * n : shard * (n + 1)] for n in range(fsdp)]
    row = lax.broadcasted_iota(jnp.int32, (16, shard), 0)
    smalls = jnp.zeros((16, shard), BF16)
    for n, vector in enumerate(vectors):
        smalls = jnp.where(row == n, vector[None, :], smalls)
    mine = jnp.concatenate(
        [
            lax.dynamic_slice_in_dim(w_qkv, core * half, half, 0),
            jnp.pad(smalls, ((0, 0), (0, 3 * features - shard))),
        ],
        axis=0,
    )
    from_near = to_near(mine)
    from_across = to_across(jnp.concatenate([mine, from_near], axis=0))
    gathered = (from_near, from_across, to_core(from_near), to_core(from_across))
    first_tile = tokens[:16, :128] + from_near[:16, :128] * jnp.asarray(0, BF16)
    swap_tokens = lax.dynamic_update_slice(tokens, first_tile, (0, 0))
    beside = [to_core(v) for v in [swap_tokens] + blocks[1:]]
    *half_stores, qkv_full, weight_q, weight_k, weight_v, small_all = kernel_call(
        project_kernel,
        [
            jax.ShapeDtypeStruct((chips // 2, rows, width), BF16),
            jax.ShapeDtypeStruct((chips, rows, width), BF16),
            jax.ShapeDtypeStruct((chips, width, rows), BF16),
            jax.ShapeDtypeStruct((chips, rows, width), BF16),
            jax.ShapeDtypeStruct((chips, width, rows), BF16),
            jax.ShapeDtypeStruct((chips // 2, rows, features), BF16),
            jax.ShapeDtypeStruct((features, 3 * features), BF16),
            jax.ShapeDtypeStruct((features, width), BF16),
            jax.ShapeDtypeStruct((features, width), BF16),
            jax.ShapeDtypeStruct((features, width), BF16),
            jax.ShapeDtypeStruct((fsdp, 16, width), FP32),
        ],
        [],
        (where, blocks[0], beside[0], blocks[1], beside[1], w_qkv, smalls) + gathered,
        9,
    )
    queries, keys, keys_t, values, normed_mine, *rest = kernel_call(
        attend_kernel,
        [
            jax.ShapeDtypeStruct((chips, rows, width), BF16),
            jax.ShapeDtypeStruct((ctx, rows, width), BF16),
            jax.ShapeDtypeStruct((ctx, width, rows), BF16),
            jax.ShapeDtypeStruct((ctx, rows, width), BF16),
            jax.ShapeDtypeStruct((chips, rows, features), BF16),
        ]
        + [jax.ShapeDtypeStruct((rows, width), BF16)] * 4
        + [
            jax.ShapeDtypeStruct((chips, width, rows), FP32),
            jax.ShapeDtypeStruct((chips, 8, rows), FP32),
            jax.ShapeDtypeStruct((16, 128), BF16),
        ],
        [
            pltpu.VMEM((ctx, width, rows), BF16),
            pltpu.VMEM((width, rows), FP32),
            pltpu.VMEM((chips, rows, width), BF16),
        ],
        (where, blocks[2], beside[2], blocks[3], beside[3])
        + (weight_q, weight_k, weight_v, small_all)
        + tuple(half_stores)
        + (key_tile, low_rows, high_rows, far_rows),
        30,
    )
    attended_t, logs, zeros = rest[4:]

    def swap_chips(pieces):
        return [pieces[0]] + [to_chip(pieces[s], s) for s in (1, 2, 3)]

    bundles = lax.dynamic_update_slice(bundles, (bundles[0, :16, :128] + zeros)[None], (0, 0, 0))
    bundles_other = to_core(bundles)
    attended = swap_chips(rest[:4])
    bundle_width = 2 * hidden_width // 2 + 3 * features + features // 2
    hbm = pl.BlockSpec(memory_space=pl.ANY)
    block_out, grad_middle, d0, d1, d2, d3, bundle_mine, bundle_send, small_rows = kernel_call(
        middle_kernel,
        [
            jax.ShapeDtypeStruct((rows, features), BF16),
            jax.ShapeDtypeStruct((rows, features), FP32),
        ]
        + [jax.ShapeDtypeStruct((rows, width), BF16)] * 4
        + [
            jax.ShapeDtypeStruct((rows, bundle_width), BF16),
            jax.ShapeDtypeStruct((rows, bundle_width), BF16),
            jax.ShapeDtypeStruct((fsdp, 16, features), FP32),
        ],
        [
            pltpu.VMEM((features, features), BF16),
            pltpu.VMEM((fsdp, features, columns), BF16),
            pltpu.VMEM((hidden_width, features), BF16),
            pltpu.VMEM((rows, columns), BF16),
            pltpu.VMEM((rows, features), BF16),
            pltpu.SemaphoreType.DMA((8 * 6,)),
        ],
        tuple([where] + attended)
        + (
            tokens,
            cotangent,
            live_rows,
            small_all,
            bundles,
            bundles_other,
        ),
        21,
        special={9: hbm, 10: hbm},
    )

    grad_blocks = swap_chips([d0, d1, d2, d3])

    bundle_other = to_core(bundle_send)
    out_rows = columns // 2 + 2 * shard
    small_at = out_rows + half
    block_rows = small_at + 32
    pair_shape = jax.ShapeDtypeStruct((2, block_rows, features), BF16)
    grads_keep, grads_send = kernel_call(
        weight_grad_kernel,
        [pair_shape, pair_shape],
        [pltpu.VMEM((2, features, features), BF16)],
        (where, bundle_mine, bundle_other, small_rows),
        14,
        after=(grad_blocks[1],),
    )

    grad_query, grad_keep, grad_send = kernel_call(
        attend_back_kernel,
        [
            jax.ShapeDtypeStruct((chips, rows, width), BF16),
            jax.ShapeDtypeStruct((chips, rows, 2 * width), FP32),
            jax.ShapeDtypeStruct((chips, rows, 2 * width), BF16),
        ],
        [
            pltpu.VMEM((width, rows), FP32),
            pltpu.VMEM((group_heads, ctx, rows, 64), FP32),
            pltpu.VMEM((group_heads, ctx, rows, 64), FP32),
            pltpu.VMEM((chips, rows, width), BF16),
        ],
        (
            where,
            queries,
            keys,
            keys_t,
            values,
            *grad_blocks,
            key_tile,
            low_rows,
            high_rows,
            far_rows,
            attended_t,
            logs,
        ),
        30,
    )
    packed = kernel_call(
        pack_kernel,
        [jax.ShapeDtypeStruct((rows, 3 * width), BF16)] * 4,
        [],
        (where, grad_query, grad_keep, to_core(grad_send)),
        2,
    )

    def add_up(left_side, right_side):
        return left_side.astype(FP32) + right_side.astype(FP32)

    arrived = swap_chips(packed)
    theirs = to_near(grads_send)
    block = jax.ShapeDtypeStruct((block_rows, features), BF16)

    (relay,) = kernel_call(
        relay_kernel, [block], [], (where, grads_keep, theirs), 1, after=(packed[0],)
    )
    (grads_block,) = kernel_call(
        block_kernel,
        [block],
        [],
        (where, grads_keep, theirs, to_across(relay)),
        2,
        after=tuple(arrived[1:]),
    )

    grads_half = lax.psum(grads_block, "ctx", axis_index_groups=same_core)
    block_shape = (fsdp, half + 16, 3 * width)
    qkv_keep, qkv_send = kernel_call(
        qkv_grad_kernel,
        [jax.ShapeDtypeStruct(block_shape, FP32), jax.ShapeDtypeStruct(block_shape, BF16)],
        [pltpu.VMEM((features, 3 * width), FP32)],
        (
            where,
            normed_mine,
            *packed,
            weight_q,
            weight_k,
            weight_v,
            small_all,
        ),
        8,
        after=tuple(arrived[1:]) + (grads_block,),
    )
    qkv_blocks = add_up(qkv_keep, to_core(qkv_send)).astype(BF16)
    theirs_qkv = to_near(qkv_blocks[2:])
    last_qkv = to_across(add_up(qkv_blocks[1], theirs_qkv[1]).astype(BF16))
    qkv_half = (add_up(qkv_blocks[0], theirs_qkv[0]) + last_qkv.astype(FP32)).astype(BF16)
    (grad_tokens,) = kernel_call(
        input_grad_kernel,
        [jax.ShapeDtypeStruct((rows, features), FP32)],
        [pltpu.VMEM((rows, 3 * features), BF16)],
        tuple([where] + arrived) + (qkv_full, tokens, grad_middle, small_all),
        5,
        after=(theirs_qkv,),
    )

    halves = swap_chips([jnp.stack([qkv_half, to_core(qkv_half)])] * 4)
    d_qkv, extra, zeros = kernel_call(
        qkv_output_kernel,
        [
            jax.ShapeDtypeStruct((shard, 3 * features), FP32),
            jax.ShapeDtypeStruct((chips, 16, 3 * width), FP32),
            jax.ShapeDtypeStruct((16, 128), BF16),
        ],
        [],
        tuple([where] + halves),
        2,
        after=(grad_tokens,),
    )
    grads_half = lax.dynamic_update_slice(grads_half, grads_half[:16, :128] + zeros, (0, 0))
    d_proj, d_fc, d_out, small_sums = kernel_call(
        output_kernel,
        [
            jax.ShapeDtypeStruct((columns, features), FP32),
            jax.ShapeDtypeStruct((shard, hidden_width), FP32),
            jax.ShapeDtypeStruct((shard, features), FP32),
            jax.ShapeDtypeStruct((16, features), FP32),
        ],
        [],
        (where, grads_half, to_core(grads_half)),
        2,
    )
    d_bias_out, d_bias_proj, d_gain_two, d_shift_two = (
        small_sums[0, n * shard : (n + 1) * shard] for n in range(4)
    )
    d_bias_fc = small_sums[1]

    owner_extra = pick(extra, part)
    d_bias_q = owner_extra[2, :width]
    d_bias_v = owner_extra[2, 2 * width :]
    norm_total = jnp.sum(extra[:, :2, :shard], axis=0)
    d_gain_one = norm_total[0]
    d_shift_one = norm_total[1]

    return (
        block_out,
        grad_tokens,
        d_qkv,
        d_bias_q,
        d_bias_v,
        d_out,
        d_bias_out,
        d_fc,
        d_bias_fc,
        d_proj,
        d_bias_proj,
        d_gain_one,
        d_shift_one,
        d_gain_two,
        d_shift_two,
    )


def solution(mesh):
    in_specs = (
        P(("fsdp", "ctx"), None),
        P(("fsdp", "ctx"), None),
        P("fsdp", None),
        P("fsdp"),
        P("fsdp"),
        P("fsdp", None),
        P("fsdp"),
        P("fsdp", None),
        P("fsdp"),
        P("fsdp", None),
        P("fsdp"),
        P("fsdp"),
        P("fsdp"),
        P("fsdp"),
        P("fsdp"),
        P("fsdp", None),
        P("fsdp", None),
    )
    out_specs = (
        P(("fsdp", "ctx"), None),
        P(("fsdp", "ctx"), None),
        P("fsdp", None),
        P("fsdp"),
        P("fsdp"),
        P("fsdp", None),
        P("fsdp"),
        P("fsdp", None),
        P("fsdp"),
        P("fsdp", None),
        P("fsdp"),
        P("fsdp"),
        P("fsdp"),
        P("fsdp"),
        P("fsdp"),
    )
    ctx = mesh.shape["ctx"]
    four_by_four = mesh.shape["fsdp"] == 4 and ctx == 8 and HEADS % (ctx // 2) == 0
    body = fast_body if four_by_four else general_body
    return jax.shard_map(body, mesh=mesh, in_specs=in_specs, out_specs=out_specs, check_vma=False)
```

```python
import functools

import jax
import jax.numpy as jnp
from jax import lax
from jax.experimental import pallas as pl
from jax.experimental.pallas import tpu as pltpu
from jax.sharding import PartitionSpec as P

HEADS = 12


EPS = 1e-05


def layer_norm(values, gain_row, shift_row):
    centre = values - jnp.mean(values, axis=1, keepdims=True)
    inverse = lax.rsqrt(jnp.mean(centre * centre, axis=1, keepdims=True) + EPS)
    normed = centre * inverse
    return (normed * gain_row + shift_row, normed, inverse)


def norm_back(grad_in, normed, inverse, gain_row):
    scaled = grad_in * gain_row
    inner_grad = inverse * (
        scaled
        - jnp.mean(scaled, axis=1, keepdims=True)
        - normed * jnp.mean(scaled * normed, axis=1, keepdims=True)
    )
    return (inner_grad, jnp.sum(grad_in * normed, axis=0), jnp.sum(grad_in, axis=0))


def contract_rows(left_side, right_side):
    return lax.dot_general(
        left_side, right_side, (((0,), (0,)), ((), ())), preferred_element_type=jnp.float32
    )


def times_transpose(left_side, right_side):
    return lax.dot_general(
        left_side, right_side, (((1,), (1,)), ((), ())), preferred_element_type=jnp.float32
    )


def gelu_tanh(values):
    return jax.nn.gelu(values, approximate=True)


def describe(slot_ids, row_count, count_row, offsets, seq_ends):
    peer_count = count_row.shape[0]
    device = slot_ids // row_count
    within = slot_ids - device * row_count
    matches = device[:, None] == jnp.arange(peer_count, dtype=jnp.int32)[None, :]
    live_count = jnp.sum(jnp.where(matches, count_row[None, :], 0), axis=1)
    first_place = jnp.sum(jnp.where(matches, offsets[None, :], 0), axis=1)
    places = first_place + within
    segment = jnp.sum((places[:, None] >= seq_ends[None, :]).astype(jnp.int32), axis=1)
    return (within < live_count, places, segment, slot_ids)


def allowed(query_info, key_info):
    q_live, q_place, q_seg, q_slot = query_info
    k_live, k_place, k_seg, k_slot = key_info
    same_seq = (
        q_live[:, None]
        & k_live[None, :]
        & (q_seg[:, None] == k_seg[None, :])
        & (k_place[None, :] <= q_place[:, None])
    )
    return same_seq | (q_slot[:, None] == k_slot[None, :])


def over_blocks(step_fn, status, pieces, row_count):
    total_rows = pieces[0].shape[0]
    block_total = total_rows // row_count
    stacked = tuple((piece.reshape((block_total, row_count) + piece.shape[1:]) for piece in pieces))

    def scan_body(state_now, scan_item):
        block_index, block_parts = scan_item
        return (step_fn(state_now, block_parts, block_index * row_count), None)

    status, unused = lax.scan(
        scan_body, status, (jnp.arange(block_total, dtype=jnp.int32), stacked)
    )
    return status


def score_grads(
    query_heads, key_heads, value_heads, grad_heads, lse_rows, delta_rows, permitted, scaling
):
    scores = (
        jnp.einsum("qhd,khd->hqk", query_heads, key_heads, preferred_element_type=jnp.float32)
        * scaling
    )
    probabilities = jnp.where(permitted[None], jnp.exp(scores - lse_rows[:, :, None]), 0.0)
    grad_probs = jnp.einsum(
        "qhd,khd->hqk", grad_heads, value_heads, preferred_element_type=jnp.float32
    )
    grad_scores = (probabilities * (grad_probs - delta_rows[:, :, None])).astype(jnp.bfloat16)
    return (probabilities.astype(jnp.bfloat16), grad_scores)


def general_body(
    tokens,
    cotangent,
    w_qkv,
    b_query,
    b_value,
    w_out,
    b_out,
    w_fc,
    b_fc,
    w_proj,
    b_proj,
    gain1,
    shift1,
    gain2,
    shift2,
    counts,
    seq_lengths,
):
    row_count, feature_count = tokens.shape
    peer_count = lax.axis_size("ctx")
    my_index = lax.axis_index("ctx")
    head_count = HEADS
    head_width = feature_count // head_count
    scaling = head_width ** (-0.5)
    count_row = counts[0]
    offsets = jnp.cumsum(count_row) - count_row
    seq_ends = jnp.cumsum(seq_lengths[0])

    def locate(first_slot, length):
        return describe(
            first_slot + jnp.arange(length, dtype=jnp.int32),
            row_count,
            count_row,
            offsets,
            seq_ends,
        )

    own_rows = locate(my_index * row_count, row_count)
    fp32 = jnp.float32
    bf16 = jnp.bfloat16
    (
        qkv_full,
        query_bias,
        value_bias,
        out_full,
        out_bias,
        fc_full,
        fc_bias,
        proj_full,
        proj_bias,
        gain_one,
        shift_one,
        gain_two,
        shift_two,
    ) = (
        lax.all_gather(w_qkv, "fsdp", axis=0, tiled=True),
        lax.all_gather(b_query, "fsdp", axis=0, tiled=True),
        lax.all_gather(b_value, "fsdp", axis=0, tiled=True),
        lax.all_gather(w_out, "fsdp", axis=0, tiled=True),
        lax.all_gather(b_out, "fsdp", axis=0, tiled=True),
        lax.all_gather(w_fc, "fsdp", axis=0, tiled=True),
        lax.all_gather(b_fc, "fsdp", axis=0, tiled=True),
        lax.all_gather(w_proj, "fsdp", axis=0, tiled=True),
        lax.all_gather(b_proj, "fsdp", axis=0, tiled=True),
        lax.all_gather(gain1, "fsdp", axis=0, tiled=True),
        lax.all_gather(shift1, "fsdp", axis=0, tiled=True),
        lax.all_gather(gain2, "fsdp", axis=0, tiled=True),
        lax.all_gather(shift2, "fsdp", axis=0, tiled=True),
    )
    inputs = tokens.astype(fp32)
    normed_one, unit_one, inverse_one = layer_norm(
        inputs, gain_one.astype(fp32), shift_one.astype(fp32)
    )
    normed_low = normed_one.astype(bf16)
    bias_row = jnp.concatenate([query_bias, jnp.zeros_like(query_bias), value_bias]).astype(fp32)
    packed = (jnp.dot(normed_low, qkv_full, preferred_element_type=fp32) + bias_row).astype(bf16)
    query_rows = packed[:, :feature_count]
    key_rows = packed[:, feature_count : 2 * feature_count]
    value_rows = packed[:, 2 * feature_count :]
    query_heads = query_rows.reshape(row_count, head_count, head_width)

    def forward_step(status, pieces, first_row):
        running_max, running_sum, running_acc = status
        key_piece, value_piece = pieces
        length = key_piece.shape[0]
        key_heads = key_piece.reshape(length, head_count, head_width)
        value_heads = value_piece.reshape(length, head_count, head_width)
        scores = (
            jnp.einsum("qhd,khd->hqk", query_heads, key_heads, preferred_element_type=fp32)
            * scaling
        )
        permitted = allowed(own_rows, locate(first_row, length))
        scores = jnp.where(permitted[None], scores, -jnp.inf)
        new_max = jnp.maximum(running_max, jnp.max(scores, axis=2))
        fading = jnp.exp(running_max - new_max)
        weights = jnp.exp(scores - new_max[:, :, None])
        running_sum = running_sum * fading + jnp.sum(weights, axis=2)
        update = jnp.einsum(
            "hqk,khd->qhd", weights.astype(bf16), value_heads, preferred_element_type=fp32
        )
        running_acc = running_acc * jnp.transpose(fading)[:, :, None] + update
        return (new_max, running_sum, running_acc)

    start_state = (
        jnp.full((head_count, row_count), -1e30, fp32),
        jnp.zeros((head_count, row_count), fp32),
        jnp.zeros((row_count, head_count, head_width), fp32),
    )
    final_max, final_sum, final_acc = over_blocks(
        forward_step,
        start_state,
        (
            lax.all_gather(key_rows, "ctx", axis=0, tiled=True),
            lax.all_gather(value_rows, "ctx", axis=0, tiled=True),
        ),
        row_count,
    )
    attended_heads = final_acc / jnp.transpose(final_sum)[:, :, None]
    attended = attended_heads.reshape(row_count, feature_count)
    log_total = final_max + jnp.log(final_sum)
    attended_low = attended.astype(bf16)
    middle = (
        inputs
        + jnp.dot(attended_low, out_full, preferred_element_type=fp32)
        + out_bias.astype(fp32)
    )
    normed_two, unit_two, inverse_two = layer_norm(
        middle, gain_two.astype(fp32), shift_two.astype(fp32)
    )
    normed_two_low = normed_two.astype(bf16)
    hidden = jnp.dot(normed_two_low, fc_full, preferred_element_type=fp32) + fc_bias.astype(fp32)
    activated = gelu_tanh(hidden).astype(bf16)
    output = (
        middle + jnp.dot(activated, proj_full, preferred_element_type=fp32) + proj_bias.astype(fp32)
    )
    output_low = output.astype(bf16)
    qkv_full, out_full, fc_full, proj_full, gain_one, gain_two = (
        lax.all_gather(w_qkv, "fsdp", axis=0, tiled=True),
        lax.all_gather(w_out, "fsdp", axis=0, tiled=True),
        lax.all_gather(w_fc, "fsdp", axis=0, tiled=True),
        lax.all_gather(w_proj, "fsdp", axis=0, tiled=True),
        lax.all_gather(gain1, "fsdp", axis=0, tiled=True),
        lax.all_gather(gain2, "fsdp", axis=0, tiled=True),
    )
    live_rows = own_rows[0].astype(fp32)[:, None]
    grad_out = cotangent.astype(fp32) * live_rows
    grad_out_low = grad_out.astype(bf16)
    grad_proj = contract_rows(activated, grad_out_low)
    grad_proj_bias = jnp.sum(grad_out, axis=0)
    grad_act = times_transpose(grad_out_low, proj_full)
    grad_hidden = jax.vjp(gelu_tanh, hidden)[1](grad_act)[0]
    grad_hidden_low = grad_hidden.astype(bf16)
    grad_fc = contract_rows(normed_two_low, grad_hidden_low)
    grad_fc_bias = jnp.sum(grad_hidden_low.astype(fp32), axis=0)
    grad_normed_two = times_transpose(grad_hidden_low, fc_full)
    grad_mid_norm, grad_gain_two, grad_shift_two = norm_back(
        grad_normed_two, unit_two, inverse_two, gain_two.astype(fp32)
    )
    grad_middle = grad_out + grad_mid_norm
    grad_middle_low = grad_middle.astype(bf16)
    grad_out_proj = contract_rows(attended_low, grad_middle_low)
    grad_out_bias = jnp.sum(grad_middle_low.astype(fp32), axis=0)
    grad_attended = times_transpose(grad_middle_low, out_full).astype(bf16)
    grad_heads = grad_attended.reshape(row_count, head_count, head_width)
    delta_rows = jnp.transpose(jnp.sum(grad_heads.astype(fp32) * attended_heads, axis=2))

    def back_step(status, pieces, first_row):
        grad_query, grad_keys = status
        key_piece, value_piece = pieces
        length = key_piece.shape[0]
        key_heads = key_piece.reshape(length, head_count, head_width)
        value_heads = value_piece.reshape(length, head_count, head_width)
        permitted = allowed(own_rows, locate(first_row, length))
        probs_low, grad_scores = score_grads(
            query_heads,
            key_heads,
            value_heads,
            grad_heads,
            log_total,
            delta_rows,
            permitted,
            scaling,
        )
        grad_query = (
            grad_query
            + jnp.einsum("hqk,khd->qhd", grad_scores, key_heads, preferred_element_type=fp32)
            * scaling
        )
        grad_key_part = (
            jnp.einsum("hqk,qhd->khd", grad_scores, query_heads, preferred_element_type=fp32)
            * scaling
        )
        grad_value_part = jnp.einsum(
            "hqk,qhd->khd", probs_low, grad_heads, preferred_element_type=fp32
        )
        joined = jnp.concatenate(
            [
                grad_key_part.reshape(length, feature_count),
                grad_value_part.reshape(length, feature_count),
            ],
            axis=1,
        )
        current = lax.dynamic_slice_in_dim(grad_keys, first_row, length, 0)
        grad_keys = lax.dynamic_update_slice_in_dim(grad_keys, current + joined, first_row, 0)
        return (grad_query, grad_keys)

    keys_start = jnp.zeros((peer_count * row_count, 2 * feature_count), fp32)
    grad_query, grad_keys = over_blocks(
        back_step,
        (jnp.zeros((row_count, head_count, head_width), fp32), keys_start),
        (
            lax.all_gather(key_rows, "ctx", axis=0, tiled=True),
            lax.all_gather(value_rows, "ctx", axis=0, tiled=True),
        ),
        row_count,
    )
    grad_kv = lax.psum_scatter(
        grad_keys.astype(jnp.bfloat16), "ctx", scatter_dimension=0, tiled=True
    ).astype(jnp.float32)
    grad_packed = jnp.concatenate(
        [grad_query.reshape(row_count, feature_count), grad_kv], axis=1
    ).astype(bf16)
    grad_packed_wide = grad_packed.astype(fp32)
    grad_query_bias = jnp.sum(grad_packed_wide[:, :feature_count], axis=0)
    grad_value_bias = jnp.sum(grad_packed_wide[:, 2 * feature_count :], axis=0)
    grad_qkv = contract_rows(normed_low, grad_packed)
    grad_normed_one = times_transpose(grad_packed, qkv_full)
    grad_in_norm, grad_gain_one, grad_shift_one = norm_back(
        grad_normed_one, unit_one, inverse_one, gain_one.astype(fp32)
    )
    grad_tokens = grad_middle + grad_in_norm
    (
        sum_qkv,
        sum_qbias,
        sum_vbias,
        sum_out,
        sum_obias,
        sum_fc,
        sum_fbias,
        sum_proj,
        sum_pbias,
        sum_gain_one,
        sum_shift_one,
        sum_gain_two,
        sum_shift_two,
    ) = (
        lax.psum_scatter(
            grad_qkv.astype(jnp.bfloat16), "fsdp", scatter_dimension=0, tiled=True
        ).astype(jnp.float32),
        lax.psum_scatter(
            grad_query_bias.astype(jnp.bfloat16), "fsdp", scatter_dimension=0, tiled=True
        ).astype(jnp.float32),
        lax.psum_scatter(
            grad_value_bias.astype(jnp.bfloat16), "fsdp", scatter_dimension=0, tiled=True
        ).astype(jnp.float32),
        lax.psum_scatter(
            grad_out_proj.astype(jnp.bfloat16), "fsdp", scatter_dimension=0, tiled=True
        ).astype(jnp.float32),
        lax.psum_scatter(
            grad_out_bias.astype(jnp.bfloat16), "fsdp", scatter_dimension=0, tiled=True
        ).astype(jnp.float32),
        lax.psum_scatter(
            grad_fc.astype(jnp.bfloat16), "fsdp", scatter_dimension=0, tiled=True
        ).astype(jnp.float32),
        lax.psum_scatter(
            grad_fc_bias.astype(jnp.bfloat16), "fsdp", scatter_dimension=0, tiled=True
        ).astype(jnp.float32),
        lax.psum_scatter(
            grad_proj.astype(jnp.bfloat16), "fsdp", scatter_dimension=0, tiled=True
        ).astype(jnp.float32),
        lax.psum_scatter(
            grad_proj_bias.astype(jnp.bfloat16), "fsdp", scatter_dimension=0, tiled=True
        ).astype(jnp.float32),
        lax.psum_scatter(
            grad_gain_one.astype(jnp.bfloat16), "fsdp", scatter_dimension=0, tiled=True
        ).astype(jnp.float32),
        lax.psum_scatter(
            grad_shift_one.astype(jnp.bfloat16), "fsdp", scatter_dimension=0, tiled=True
        ).astype(jnp.float32),
        lax.psum_scatter(
            grad_gain_two.astype(jnp.bfloat16), "fsdp", scatter_dimension=0, tiled=True
        ).astype(jnp.float32),
        lax.psum_scatter(
            grad_shift_two.astype(jnp.bfloat16), "fsdp", scatter_dimension=0, tiled=True
        ).astype(jnp.float32),
    )
    totals = (
        lax.psum(sum_qkv.astype(jnp.bfloat16), "ctx").astype(jnp.float32),
        lax.psum(sum_qbias.astype(jnp.bfloat16), "ctx").astype(jnp.float32),
        lax.psum(sum_vbias.astype(jnp.bfloat16), "ctx").astype(jnp.float32),
        lax.psum(sum_out.astype(jnp.bfloat16), "ctx").astype(jnp.float32),
        lax.psum(sum_obias.astype(jnp.bfloat16), "ctx").astype(jnp.float32),
        lax.psum(sum_fc.astype(jnp.bfloat16), "ctx").astype(jnp.float32),
        lax.psum(sum_fbias.astype(jnp.bfloat16), "ctx").astype(jnp.float32),
        lax.psum(sum_proj.astype(jnp.bfloat16), "ctx").astype(jnp.float32),
        lax.psum(sum_pbias.astype(jnp.bfloat16), "ctx").astype(jnp.float32),
        lax.psum(sum_gain_one.astype(jnp.bfloat16), "ctx").astype(jnp.float32),
        lax.psum(sum_shift_one.astype(jnp.bfloat16), "ctx").astype(jnp.float32),
        lax.psum(sum_gain_two.astype(jnp.bfloat16), "ctx").astype(jnp.float32),
        lax.psum(sum_shift_two.astype(jnp.bfloat16), "ctx").astype(jnp.float32),
    )
    return (
        output_low,
        grad_tokens,
        totals[0],
        totals[1],
        totals[2],
        totals[3],
        totals[4],
        totals[5],
        totals[6],
        totals[7],
        totals[8],
        totals[9],
        totals[10],
        totals[11],
        totals[12],
    )


FP32 = jnp.float32
BF16 = jnp.bfloat16
FLOOR = -1e30
NEVER = 1 << 30


def dot_nt(left_side, right_side):
    return lax.dot_general(
        left_side, right_side, (((1,), (1,)), ((), ())), preferred_element_type=FP32
    )


def dot_nn(left_side, right_side):
    return lax.dot_general(
        left_side, right_side, (((1,), (0,)), ((), ())), preferred_element_type=FP32
    )


def spread(column_tile, width):
    return jnp.concatenate([column_tile] * (width // column_tile.shape[1]), axis=1)


def masked_scores(scores, key_ids, first_row, last_row):
    permitted = key_ids >= first_row
    if last_row is not None:
        permitted = permitted & (key_ids <= last_row)
    return jnp.where(permitted, scores, -jnp.inf)


def whole_vector(small_ref, number):
    parts = [small_ref[f, number : number + 1, :] for f in range(small_ref.shape[0])]
    return jnp.concatenate(parts, axis=1)


def project_block(
    tokens_ref, wq_ref, wk_ref, wv_ref, small_ref, chip, stores, position, wanted
):
    q_ref, k_ref, kt_ref, v_ref, vt_ref, normed_ref = stores
    gain, shift = whole_vector(small_ref, 4), whole_vector(small_ref, 5)
    normed = layer_norm(tokens_ref[...].astype(FP32), gain, shift)[0]
    normed = normed.astype(BF16)
    keys = dot_nn(normed, wk_ref[...])
    values = dot_nn(normed, wv_ref[...]) + small_ref[chip, 1:2, :]
    k_ref[position] = keys.astype(BF16)
    v_ref[position] = values.astype(BF16)
    kt_ref[position] = keys.T.astype(BF16)
    vt_ref[position] = values.T.astype(BF16)
    if wanted:
        queries = (dot_nn(normed, wq_ref[...]) + small_ref[chip, 0:1, :]).astype(BF16)
        q_ref[position // 2] = (queries.astype(FP32) * 0.125).astype(BF16)
        normed_ref[position // 2] = normed


def project_kernel(
    where,
    t0,
    t1,
    t2,
    t3,
    w_ref,
    halves_ref,
    others_ref,
    q,
    k,
    kt,
    v,
    vt,
    normed,
    full_ref,
    wq,
    wk,
    wv,
    small_ref,
):
    core, chip = where[1], where[2]
    shard, wide = w_ref.shape
    features, half, width = wide // 3, shard // 2, wq.shape[1]
    for f in range(halves_ref.shape[0]):
        for ref, which in ((halves_ref, core), (others_ref, 1 - core)):
            first = pl.multiple_of(f * shard + which * half, 16)
            full_ref[pl.ds(first, half), :] = ref[f, 0:half, :]
        small_ref[f] = halves_ref[f, half:, 0:width].astype(FP32)
    for z in range(features // width):

        @pl.when(chip == z)
        def own_columns():
            for n, ref in enumerate((wq, wk, wv)):
                first = features * n + width * z
                ref[...] = full_ref[:, first : first + width]

    stores = (q, k, kt, v, vt, normed)
    for n, block in enumerate((t0, t1, t2, t3)):
        owner = (chip ^ (n // 2)) % 2
        position = 2 * owner + (core if n % 2 == 0 else 1 - core)
        project_block(block, wq, wk, wv, small_ref, chip, stores, position, n % 2 == 0)


def attend_kernel(
    where,
    t0,
    t1,
    t2,
    t3,
    wq_ref,
    wk_ref,
    wv_ref,
    small_ref,
    q_half,
    k_half,
    kt_half,
    v_half,
    vt_half,
    normed_half,
    key_ref,
    low_ref,
    high_ref,
    far_ref,
    q_ref,
    k_ref,
    kt_ref,
    v_ref,
    normed_ref,
    o0_ref,
    o1_ref,
    o2_ref,
    o3_ref,
    ot_ref,
    lse_ref,
    zero_ref,
    vt_ref,
    acc_ref,
    o_ref,
):
    blocks, rows, width = q_ref.shape
    heads = width // 64
    core, chip = where[1], where[2]
    side = chip // 2
    zero_ref[...] = jnp.zeros_like(zero_ref)
    stores = (q_ref, k_ref, kt_ref, v_ref, vt_ref, normed_ref)
    for n, block in enumerate((t0, t1, t2, t3)):
        owner = chip ^ (2 + n // 2)
        position = 2 * owner + (core if n % 2 == 0 else 1 - core)
        project_block(
            block,
            wq_ref,
            wk_ref,
            wv_ref,
            small_ref,
            chip,
            stores,
            position,
            n % 2 == 0,
        )
    for n in range(blocks):
        for source, target in ((k_half, k_ref), (kt_half, kt_ref), (v_half, v_ref), (vt_half, vt_ref)):
            target[side * blocks + n] = source[n]
    for n in range(blocks // 2):
        q_ref[side * (blocks // 2) + n] = q_half[n]
        normed_ref[side * (blocks // 2) + n] = normed_half[n]

    def query_block(index, unused):
        queries = [q_ref[index, :, 64 * h : 64 * h + 64] for h in range(heads)]
        acc_ref[...] = jnp.zeros_like(acc_ref)

        def key_step(key_block, carry, first_row, last_row):
            ids = spread(key_ref[key_block], rows)
            result = []
            for h in range(heads):
                span = slice(64 * h, 64 * h + 64)
                top, total = carry[h]
                scores = dot_nt(k_ref[key_block, :, span], queries[h])
                scores = masked_scores(scores, ids, first_row, last_row)
                new_top = jnp.maximum(top, jnp.max(scores, axis=0, keepdims=True))
                fade = jnp.exp(top - new_top)
                weights = jnp.exp(scores - new_top)
                total = total * fade + jnp.sum(weights, axis=0, keepdims=True)
                acc_ref[span, :] = acc_ref[span, :] * fade + dot_nn(
                    vt_ref[key_block, span, :], weights.astype(BF16)
                )
                result.append((new_top, total))
            return tuple(result)

        start = tuple(
            (jnp.full((1, rows), FLOOR, FP32), jnp.zeros((1, rows), FP32)) for h in range(heads)
        )
        own = 2 * index + core
        far_row = far_ref[index]
        carry = lax.fori_loop(0, own, lambda j, c: key_step(j, c, far_row, None), start)
        carry = key_step(own, carry, low_ref[index], high_ref[index])
        for h in range(heads):
            span = slice(64 * h, 64 * h + 64)
            top, total = carry[h]
            attended = acc_ref[span, :] / total
            ot_ref[index, span, :] = attended
            o_ref[index, :, span] = attended.T.astype(BF16)
            lse_ref[index, h : h + 1, :] = top + jnp.log(total)
        return unused

    lax.fori_loop(0, blocks, query_block, 0)
    for s, ref in enumerate((o0_ref, o1_ref, o2_ref, o3_ref)):
        ref[...] = o_ref[chip ^ s]


def attend_back_kernel(
    where,
    q_ref,
    k_ref,
    kt_ref,
    v_ref,
    d0_ref,
    d1_ref,
    d2_ref,
    d3_ref,
    key_ref,
    low_ref,
    high_ref,
    far_ref,
    ot_ref,
    lse_ref,
    dq_ref,
    keep_ref,
    send_ref,
    acc_ref,
    dk_ref,
    dv_ref,
    da_ref,
):
    blocks, rows, width = q_ref.shape
    heads = width // 64
    core, chip = where[1], where[2]
    for s, ref in enumerate((d0_ref, d1_ref, d2_ref, d3_ref)):
        da_ref[chip ^ s] = ref[...]
    dk_ref[...] = jnp.zeros_like(dk_ref)
    dv_ref[...] = jnp.zeros_like(dv_ref)

    def query_block(index, unused):
        queries = [q_ref[index, :, 64 * h : 64 * h + 64] for h in range(heads)]
        grads = [da_ref[index, :, 64 * h : 64 * h + 64] for h in range(heads)]
        deltas = [
            jnp.sum(
                grads[h].astype(FP32).T * ot_ref[index, 64 * h : 64 * h + 64, :],
                axis=0,
                keepdims=True,
            )
            for h in range(heads)
        ]
        logs = [lse_ref[index, h : h + 1, :] for h in range(heads)]
        acc_ref[...] = jnp.zeros_like(acc_ref)

        def key_step(key_block, first_row, last_row):
            ids = spread(key_ref[key_block], rows)
            for h in range(heads):
                span = slice(64 * h, 64 * h + 64)
                scores = dot_nt(k_ref[key_block, :, span], queries[h])
                scores = masked_scores(scores, ids, first_row, last_row)
                weights = jnp.exp(scores - logs[h])
                slopes = dot_nt(v_ref[key_block, :, span], grads[h])
                dscores = (weights * (slopes - deltas[h])).astype(BF16)
                dv_ref[h, key_block] += dot_nn(weights.astype(BF16), grads[h])
                dk_ref[h, key_block] += dot_nn(dscores, queries[h])
                acc_ref[span, :] += dot_nn(kt_ref[key_block, span, :], dscores)

        own = 2 * index + core
        far_row = far_ref[index]

        def far_step(key_block, state):
            key_step(key_block, far_row, None)
            return state

        lax.fori_loop(0, own, far_step, 0)
        key_step(own, low_ref[index], high_ref[index])
        for h in range(heads):
            span = slice(64 * h, 64 * h + 64)
            dq_ref[index, :, span] = (acc_ref[span, :] * 0.125).T.astype(BF16)
        return unused

    lax.fori_loop(0, blocks, query_block, 0)

    def write_block(index, unused):
        mine = 2 * index + core
        theirs = 2 * index + 1 - core
        for h in range(heads):
            left = slice(64 * h, 64 * h + 64)
            right = slice(width + 64 * h, width + 64 * h + 64)
            keep_ref[index, :, left] = dk_ref[h, mine]
            keep_ref[index, :, right] = dv_ref[h, mine]
            send_ref[index, :, left] = dk_ref[h, theirs].astype(BF16)
            send_ref[index, :, right] = dv_ref[h, theirs].astype(BF16)
        return unused

    lax.fori_loop(0, blocks, write_block, 0)


def kernel_call(kernel, outputs, scratch, operands, cost, special={}, after=(), grid=()):
    whole = pl.BlockSpec(memory_space=pltpu.VMEM)
    in_specs = [pl.BlockSpec(memory_space=pltpu.SMEM)]
    in_specs += [special.get(n, whole) for n in range(1, len(operands))]
    in_specs += [pl.BlockSpec(memory_space=pl.ANY) for unused in after]
    count = len(operands)

    def ordered(*refs):
        return kernel(*refs[:count], *refs[count + len(after) :])

    moved = sum(v.size * v.dtype.itemsize for v in list(operands) + list(outputs))
    return pl.pallas_call(
        ordered,
        grid=grid,
        out_shape=outputs,
        in_specs=in_specs,
        out_specs=[pl.BlockSpec(memory_space=pltpu.VMEM) for unused in outputs],
        scratch_shapes=scratch,
        compiler_params=pltpu.CompilerParams(vmem_limit_bytes=56 * 1024 * 1024),
        cost_estimate=pl.CostEstimate(
            flops=cost * 1153 * 10**6, bytes_accessed=moved, transcendentals=0
        ),
    )(*operands, *after)


def pack_kernel(where, dq_ref, keep_ref, arrived_ref, p0, p1, p2, p3):
    chip = where[2]
    width = dq_ref.shape[2]
    for s, ref in enumerate((p0, p1, p2, p3)):
        owner = chip ^ s
        ref[:, 0:width] = dq_ref[owner]
        ref[:, width:] = (keep_ref[owner] + arrived_ref[owner].astype(FP32)).astype(BF16)


def middle_kernel(
    where,
    a0_ref,
    a1_ref,
    a2_ref,
    a3_ref,
    tokens_ref,
    cotangent_ref,
    live_ref,
    small_ref,
    bundle_own,
    bundle_other,
    block_ref,
    dx_ref,
    d0_ref,
    d1_ref,
    d2_ref,
    d3_ref,
    mine_ref,
    send_ref,
    sums_ref,
    wo_ref,
    wf_ref,
    wp_ref,
    g_ref,
    dz_ref,
    sems,
):
    rows, features = tokens_ref.shape
    parts = wf_ref.shape[0]
    shard, hidden_width = features // parts, wp_ref.shape[0]
    columns = hidden_width // parts
    half, half_columns = shard // 2, columns // 2
    core, chip = where[1], where[2]

    starts = {"proj": [], "out": [], "fc": []}

    def fetch(kind, source, target):
        number = sum(len(v) for v in starts.values())
        starts[kind].append(pltpu.make_async_copy(source, target, sems.at[number]))

    def rows_at(owner, which, size):
        return pl.ds(pl.multiple_of(owner * 2 * size + which * size, 16), size)

    pieces = []
    for owner in range(parts):
        pieces.append((bundle_own.at[owner], owner, core))
        pieces.append((bundle_other.at[owner], owner, 1 - core))
    for piece, owner, which in pieces:
        fetch("out", piece.at[half_columns : half_columns + half, :], wo_ref.at[rows_at(owner, which, half), :])
    for piece, owner, which in pieces:
        for j in range(parts):
            first = half_columns + half * (j + 1)
            fetch("fc", piece.at[first : first + half, :], wf_ref.at[j, rows_at(owner, which, half), :])
    for piece, owner, which in pieces:
        fetch("proj", piece.at[0:half_columns, :], wp_ref.at[rows_at(owner, which, half_columns), :])
    for kind in ("out", "fc", "proj"):
        for copy in starts[kind]:
            copy.start()
    for copy in starts["out"]:
        copy.wait()

    attended = [a0_ref, a1_ref, a2_ref, a3_ref]
    middle = tokens_ref[...].astype(FP32) + whole_vector(small_ref, 2)
    a_start = 2 * parts * half_columns + features
    for s in range(parts):
        span = pl.ds(pl.multiple_of((chip ^ s) * shard, 16), shard)
        middle = middle + dot_nn(attended[s][...], wo_ref[span, :])
        mine_ref[:, a_start + shard * s : a_start + shard * (s + 1)] = attended[s][...]
        send_ref[:, a_start + shard * s : a_start + shard * (s + 1)] = attended[s][...]
    normed, unit, inverse = layer_norm(
        middle, whole_vector(small_ref, 6), whole_vector(small_ref, 7)
    )
    normed_low = normed.astype(BF16)
    h_start = 2 * parts * half_columns
    mine_ref[:, h_start : h_start + features] = normed_low
    send_ref[:, h_start : h_start + features] = normed_low
    grad_out = cotangent_ref[...].astype(FP32) * live_ref[...]
    grad_out_low = grad_out.astype(BF16)
    y_start = a_start + features
    mine_ref[:, y_start : y_start + features] = grad_out_low
    send_ref[:, y_start : y_start + features] = grad_out_low
    for copy in starts["fc"] + starts["proj"]:
        copy.wait()

    sums_ref[...] = jnp.zeros_like(sums_ref)
    output = middle + whole_vector(small_ref, 3)
    grad_normed = jnp.zeros((rows, features), FP32)
    scale, cubic = 0.7978845608028654, 0.044715
    for j in range(parts):
        span = slice(columns * j, columns * (j + 1))
        bias_fc = jnp.concatenate([small_ref[j, 8 + n : 9 + n, :] for n in range(parts)], axis=1)
        hidden = dot_nn(normed_low, wf_ref[j]) + bias_fc
        square = hidden * hidden
        bent = jnp.tanh(scale * hidden * (1.0 + cubic * square))
        active = 0.5 * hidden * (1.0 + bent)
        slope = 0.5 * (1.0 + bent) + 0.5 * hidden * (1.0 - bent * bent) * (
            scale * (1.0 + 3.0 * cubic * square)
        )
        g_ref[...] = active.astype(BF16)
        grad_hidden = (dot_nt(grad_out_low, wp_ref[span, :]) * slope).astype(BF16)
        output = output + dot_nn(g_ref[...], wp_ref[span, :])
        grad_normed = grad_normed + dot_nt(grad_hidden, wf_ref[j])
        sums_ref[j, 1:2, :] = jnp.sum(grad_hidden.astype(FP32), axis=0, keepdims=True)
        g_span = slice(half_columns * j, half_columns * (j + 1))
        mine_ref[:, g_span] = g_ref[:, pl.ds(pl.multiple_of(core * half_columns, 128), half_columns)]
        send_ref[:, g_span] = g_ref[
            :, pl.ds(pl.multiple_of((1 - core) * half_columns, 128), half_columns)
        ]
        first = parts * half_columns + columns * (j % 2)

        @pl.when(core == j // 2)
        def keep_hidden():
            mine_ref[:, first : first + columns] = grad_hidden

        @pl.when(core != j // 2)
        def give_hidden():
            send_ref[:, first : first + columns] = grad_hidden

    block_ref[...] = output.astype(BF16)
    inner, gain_sum, shift_sum = norm_back(
        grad_normed, unit, inverse, whole_vector(small_ref, 6)
    )
    grad_middle = grad_out + inner
    dx_ref[...] = grad_middle
    dz_ref[...] = grad_middle.astype(BF16)
    z_start = y_start + features
    part_width = features // 2
    mine_ref[:, z_start : z_start + part_width] = dz_ref[
        :, pl.ds(pl.multiple_of(core * part_width, 128), part_width)
    ]
    send_ref[:, z_start : z_start + part_width] = dz_ref[
        :, pl.ds(pl.multiple_of((1 - core) * part_width, 128), part_width)
    ]
    for s, ref in enumerate((d0_ref, d1_ref, d2_ref, d3_ref)):
        span = pl.ds(pl.multiple_of((chip ^ s) * shard, 16), shard)
        ref[...] = dot_nt(dz_ref[...], wo_ref[span, :]).astype(BF16)
    rows_of_sums = (
        jnp.sum(dz_ref[...].astype(FP32), axis=0, keepdims=True),
        jnp.sum(grad_out, axis=0, keepdims=True),
        gain_sum[None, :],
        shift_sum[None, :],
    )
    for n, row in enumerate(rows_of_sums):
        for f in range(parts):
            sums_ref[f, 0:1, shard * n : shard * (n + 1)] = row[:, shard * f : shard * (f + 1)]


def weight_grad_kernel(where, mine_ref, other_ref, small_ref, keep_ref, send_ref, fc_ref):
    rows = mine_ref.shape[0]
    features = keep_ref.shape[2]
    part, core, chip = where[0], where[1], where[2]
    near, across = 1 + core, 2 - core
    parts = 4
    shard, half_columns = features // parts, features // 2
    h_start = 2 * parts * half_columns
    a_start = h_start + features
    y_start = a_start + features
    z_start = y_start + features

    def product(left, right):
        return contract_rows(mine_ref[:, left], mine_ref[:, right]) + contract_rows(
            other_ref[:, left], other_ref[:, right]
        )

    targets = [(keep_ref, 0, part), (keep_ref, 1, part ^ across)]
    targets += [(send_ref, 0, part ^ near), (send_ref, 1, part ^ 3)]
    fc_base = parts * half_columns
    for j in range(2):
        fc_ref[j] = product(
            pl.ds(h_start, features), pl.ds(fc_base + features * j, features)
        ).astype(BF16)
    out_base = half_columns + 2 * shard
    small_base = out_base + shard // 2
    for ref, slot, owner in targets:
        g_span = pl.ds(pl.multiple_of(owner * half_columns, 128), half_columns)
        ref[slot, 0:half_columns, :] = product(g_span, pl.ds(y_start, features)).astype(BF16)
        for j in range(2):
            first = half_columns + shard * j
            ref[slot, first : first + shard, :] = fc_ref[
                j, pl.ds(pl.multiple_of(owner * shard, 16), shard), :
            ]
        ref[slot, small_base : small_base + 16, :] = small_ref[owner].astype(BF16)
        ref[slot, small_base + 16 :, :] = jnp.zeros_like(ref[slot, small_base + 16 :, :])
    for s in range(parts):
        block = product(
            pl.ds(a_start + shard * s, shard), pl.ds(z_start, half_columns)
        ).astype(BF16)
        owner = chip ^ s
        for ref, slot, wanted in targets:

            @pl.when(owner == wanted)
            def store_block():
                ref[slot, out_base:small_base, 0:half_columns] = block[: shard // 2]
                ref[slot, out_base:small_base, half_columns:] = block[shard // 2 :]


def qkv_grad_kernel(
    where,
    normed_ref,
    p0,
    p1,
    p2,
    p3,
    wq_ref,
    wk_ref,
    wv_ref,
    small_ref,
    keep_ref,
    send_ref,
    total_ref,
):
    blocks, rows, features = normed_ref.shape
    width = wq_ref.shape[1]
    part, core, chip = where[0], where[1], where[2]
    near, across = 1 + core, 2 - core
    parts = 4
    shard = features // parts
    half = shard // 2
    column_sums = [jnp.zeros((1, width), FP32) for n in range(3)]
    for n in range(3):
        total = jnp.zeros((features, width), FP32)
        for b in range(blocks):
            grads = (p0, p1, p2, p3)[b][:, width * n : width * (n + 1)]
            total = total + contract_rows(normed_ref[chip ^ b], grads)
            column_sums[n] = column_sums[n] + jnp.sum(grads.astype(FP32), axis=0, keepdims=True)
        total_ref[:, width * n : width * (n + 1)] = total
    sums = jnp.concatenate(column_sums, axis=1)
    shift_grad = jnp.zeros((features, 1), FP32)
    gain_grad = jnp.zeros((features, 1), FP32)
    for n, ref in enumerate((wq_ref, wk_ref, wv_ref)):
        wide = ref[...].astype(FP32)
        shift_grad = shift_grad + jnp.sum(wide * column_sums[n], axis=1, keepdims=True)
        gain_grad = gain_grad + jnp.sum(
            wide * total_ref[:, width * n : width * (n + 1)], axis=1, keepdims=True
        )
    columns = jnp.concatenate(
        [gain_grad, shift_grad, jnp.zeros((features, 126), FP32)], axis=1
    )
    norm_rows = columns.T[0:8]
    gain, shift = whole_vector(small_ref, 4), whole_vector(small_ref, 5)
    gain_row = (norm_rows[0:1] - shift * norm_rows[1:2]) / gain
    norm_rows = jnp.concatenate([gain_row, norm_rows[1:]], axis=0)
    order = [part, part ^ across, part ^ near, part ^ 3]
    other_order = [part, part ^ near, part ^ across, part ^ 3]
    for ref, which, owners in ((keep_ref, core, order), (send_ref, 1 - core, other_order)):
        for slot in range(parts):
            owner = owners[slot]
            first = pl.multiple_of(owner * shard + which * half, 16)
            ref[slot, 0:half, :] = total_ref[pl.ds(first, half), :].astype(ref.dtype)
            picked = jnp.zeros((8, shard), FP32)
            for f in range(parts):
                picked = jnp.where(owner == f, norm_rows[:, shard * f : shard * (f + 1)], picked)
            row = lax.broadcasted_iota(jnp.int32, (8, 3 * width), 0)
            packed = jnp.concatenate([picked, jnp.zeros((8, 3 * width - shard), FP32)], axis=1)
            tail = jnp.where(row < 2, packed, jnp.where(row == 2, sums, 0.0))
            tail = jnp.concatenate([tail, jnp.zeros_like(tail)], axis=0)
            ref[slot, half : half + 16, :] = tail.astype(ref.dtype)


def first_bit(core, chip):
    return jnp.where(core == 0, chip % 2, chip // 2)


def relay_kernel(where, keep_ref, theirs_ref, relay_ref):
    relay_ref[...] = (keep_ref[0].astype(FP32) + theirs_ref[0].astype(FP32)).astype(BF16)


def pair_kernel(where, keep_ref, theirs_ref, last_ref, stay_ref, give_ref):
    low = first_bit(where[1], where[2])
    count = stay_ref.shape[0]
    for ref, which in ((stay_ref, low), (give_ref, 1 - low)):
        span = pl.ds(pl.multiple_of(which * count, 16), count)
        total = keep_ref[0, span, :].astype(FP32) + theirs_ref[0, span, :].astype(FP32)
        ref[...] = (total + last_ref[span, :].astype(FP32)).astype(ref.dtype)


def quad_kernel(where, stay_ref, arrived_ref, keep_ref, give_ref):
    high = first_bit(1 - where[1], where[2])
    count = keep_ref.shape[0]
    for ref, which in ((keep_ref, high), (give_ref, 1 - high)):
        span = pl.ds(pl.multiple_of(which * count, 16), count)
        total = stay_ref[span, :] + arrived_ref[span, :].astype(FP32)
        ref[...] = total.astype(ref.dtype)


def total_kernel(where, keep_ref, arrived_ref, out_ref):
    out_ref[...] = (keep_ref[...] + arrived_ref[...].astype(FP32)).astype(BF16)


def join_kernel(where, mine_ref, arrived_ref, out_ref):
    high = first_bit(1 - where[1], where[2])
    count = mine_ref.shape[0]
    out_ref[pl.ds(pl.multiple_of(high * count, 16), count), :] = mine_ref[...]
    out_ref[pl.ds(pl.multiple_of((1 - high) * count, 16), count), :] = arrived_ref[...]


def input_grad_kernel(
    where, p0, p1, p2, p3, w_ref, tokens_ref, dx_ref, small_ref, out_ref, packed_ref
):
    chip = where[2]
    features = w_ref.shape[0]
    width = p0.shape[1] // 3
    for z in range(4):
        for s, piece in enumerate((p0, p1, p2, p3)):

            @pl.when(chip == z ^ s)
            def place_piece():
                for n in range(3):
                    first = features * n + width * z
                    packed_ref[:, first : first + width] = piece[:, width * n : width * (n + 1)]

    total = dot_nt(packed_ref[...], w_ref[...])
    unit, inverse = layer_norm(
        tokens_ref[...].astype(FP32), whole_vector(small_ref, 4), whole_vector(small_ref, 5)
    )[1:]
    out_ref[...] = dx_ref[...] + norm_back(total, unit, inverse, whole_vector(small_ref, 4))[0]


def output_kernel(
    where, m0, m1, t0, t1, proj_ref, fc_ref, out_ref, sums_ref, mine_ref, other_ref
):
    core = where[1]
    count = m0.shape[0]
    own_bit, other_bit = first_bit(core, where[2]), first_bit(1 - core, where[2])
    for n, (mine, other) in enumerate(((m0, t0), (m1, t1))):
        for bit, source, target in ((own_bit, mine, mine_ref), (other_bit, other, other_ref)):
            first = pl.multiple_of((bit if n == 0 else 1 - bit) * count, 16)
            target[pl.ds(first, count), :] = source[...]
    half_columns = proj_ref.shape[0] // 2
    shard, features = out_ref.shape
    out_rows = half_columns + 2 * shard
    small_at = out_rows + shard // 2
    sums_ref[...] = mine_ref[small_at : small_at + 16, :].astype(FP32) + other_ref[
        small_at : small_at + 16, :
    ].astype(FP32)

    def place(ref, which):
        proj_ref[which * half_columns : (which + 1) * half_columns, :] = ref[
            0:half_columns, :
        ].astype(FP32)
        for j in range(2):
            first = half_columns + shard * j
            column = features * (2 * which + j)
            fc_ref[:, column : column + features] = ref[first : first + shard, :].astype(FP32)
        span = slice(features // 2 * which, features // 2 * (which + 1))
        middle = out_rows + shard // 2
        out_ref[0 : shard // 2, span] = ref[out_rows:middle, 0 : features // 2].astype(FP32)
        out_ref[shard // 2 :, span] = ref[out_rows:middle, features // 2 :].astype(FP32)

    @pl.when(core == 0)
    def first_core():
        place(mine_ref, 0)
        place(other_ref, 1)

    @pl.when(core == 1)
    def second_core():
        place(mine_ref, 1)
        place(other_ref, 0)


def qkv_output_kernel(where, h0, h1, h2, h3, out_ref, extra_ref):
    core, chip = where[1], where[2]
    shard, wide = out_ref.shape
    features = wide // 3
    half = shard // 2
    width = h0.shape[2] // 3
    for s, ref in enumerate((h0, h1, h2, h3)):
        extra_ref[chip ^ s] = jnp.where(
            core == 0, ref[0, half : half + 16, :], ref[1, half : half + 16, :]
        ).astype(FP32)
        for z in range(4):

            @pl.when(chip == z ^ s)
            def place_piece():
                for n in range(3):
                    first = features * n + width * z
                    for slot, which in ((0, core), (1, 1 - core)):
                        rows = pl.ds(pl.multiple_of(which * half, 8), half)
                        out_ref[rows, first : first + width] = ref[
                            slot, 0:half, width * n : width * (n + 1)
                        ].astype(FP32)


def fast_body(
    tokens,
    cotangent,
    w_qkv,
    b_query,
    b_value,
    w_out,
    b_out,
    w_fc,
    b_fc,
    w_proj,
    b_proj,
    gain1,
    shift1,
    gain2,
    shift2,
    counts,
    seq_lengths,
):
    rows, features = tokens.shape
    ctx = lax.axis_size("ctx")
    fsdp = lax.axis_size("fsdp")
    chips = ctx // 2
    group_heads = HEADS // chips
    width = features // chips
    shard = features // fsdp
    hidden_width = w_fc.shape[1]
    columns = hidden_width // fsdp
    place = lax.axis_index("ctx")
    chip = place // 2
    core = place % 2
    part = lax.axis_index("fsdp")
    near = 1 + core
    across = 2 - core
    same_core = [[2 * z + k for z in range(chips)] for k in range(2)]
    where = jnp.stack([part, core, chip]).astype(jnp.int32)

    def exchange(value, partner):
        pairs = [
            (f * ctx + c, g * ctx + d)
            for f in range(fsdp)
            for c in range(ctx)
            for g, d in [partner(f, c)]
        ]
        return lax.ppermute(value, ("fsdp", "ctx"), pairs)

    def to_near(value):
        return exchange(value, lambda f, c: (f ^ (1 + c % 2), c))

    def to_across(value):
        return exchange(value, lambda f, c: (f ^ (2 - c % 2), c))

    def to_core(value):
        return exchange(value, lambda f, c: (f, c ^ 1))

    def to_chip(value, step):
        return exchange(value, lambda f, c: (f, c ^ (2 * step)))

    def to_first(value):
        return exchange(value, lambda f, c: (f, c ^ (2 + 2 * (c % 2))))

    def to_second(value):
        return exchange(value, lambda f, c: (f, c ^ (4 - 2 * (c % 2))))

    def pick(array, index, axis=0):
        return lax.dynamic_index_in_dim(array, index, axis, keepdims=False)

    def place_all(shape, dtype, items):
        buffer = jnp.zeros(shape, dtype)
        for index, value in items:
            full = value.reshape((1,) * (len(shape) - value.ndim) + value.shape)
            starts = tuple(index) + (0,) * (len(shape) - len(index))
            buffer = lax.dynamic_update_slice(buffer, full.astype(dtype), starts)
        return buffer

    half = shard // 2
    fc_half = lax.dynamic_slice_in_dim(w_fc, core * half, half, 0)
    bundle = jnp.concatenate(
        [
            lax.dynamic_slice_in_dim(w_proj, core * (columns // 2), columns // 2, 0),
            lax.dynamic_slice_in_dim(w_out, core * half, half, 0),
        ]
        + [fc_half[:, columns * j : columns * (j + 1)] for j in range(fsdp)],
        axis=0,
    )

    blocks = [tokens] + [to_chip(tokens, s) for s in (1, 2, 3)]
    beside = [to_core(v) for v in blocks]
    bundles = lax.all_gather(bundle, "fsdp", axis=0)

    count_row = counts[0]
    offsets = jnp.cumsum(count_row) - count_row
    seq_ends = jnp.cumsum(seq_lengths[0])
    within = jnp.arange(rows, dtype=jnp.int32)
    slot = jnp.arange(ctx, dtype=jnp.int32)[:, None] * rows + within[None, :]
    live = within[None, :] < count_row[:, None]
    places = offsets[:, None] + within[None, :]
    starts = jnp.max(
        jnp.where(places[:, :, None] >= seq_ends[None, None, :], seq_ends[None, None, :], 0), axis=2
    )
    dead_id = -1 - slot
    key_ids = jnp.where(live, places, dead_id)
    lows = jnp.where(live, starts, dead_id)
    fars = jnp.where(live, starts, NEVER)
    key_tile = jnp.broadcast_to(key_ids[:, :, None], (ctx, rows, 128))

    def own_parity(array):
        return pick(array.reshape((chips, 2) + array.shape[1:]), core, 1)

    low_rows = own_parity(lows)[:, None, :]
    high_rows = own_parity(key_ids)[:, None, :]
    far_rows = own_parity(fars)[:, None, :]
    live_rows = (within < pick(count_row, place)).astype(FP32)[:, None]

    vectors = [b_query, b_value, b_out, b_proj, gain1, shift1, gain2, shift2]
    vectors += [b_fc[shard * n : shard * (n + 1)] for n in range(fsdp)]
    row = lax.broadcasted_iota(jnp.int32, (16, shard), 0)
    smalls = jnp.zeros((16, shard), BF16)
    for n, vector in enumerate(vectors):
        smalls = jnp.where(row == n, vector[None, :], smalls)
    mine = jnp.concatenate(
        [
            lax.dynamic_slice_in_dim(w_qkv, core * half, half, 0),
            jnp.pad(smalls, ((0, 0), (0, 3 * features - shard))),
        ],
        axis=0,
    )
    gathered = lax.all_gather(mine, "fsdp", axis=0)
    gathered = (gathered, to_core(gathered))
    *half_stores, qkv_full, weight_q, weight_k, weight_v, small_all = kernel_call(
        project_kernel,
        [
            jax.ShapeDtypeStruct((chips // 2, rows, width), BF16),
            jax.ShapeDtypeStruct((chips, rows, width), BF16),
            jax.ShapeDtypeStruct((chips, width, rows), BF16),
            jax.ShapeDtypeStruct((chips, rows, width), BF16),
            jax.ShapeDtypeStruct((chips, width, rows), BF16),
            jax.ShapeDtypeStruct((chips // 2, rows, features), BF16),
            jax.ShapeDtypeStruct((features, 3 * features), BF16),
            jax.ShapeDtypeStruct((features, width), BF16),
            jax.ShapeDtypeStruct((features, width), BF16),
            jax.ShapeDtypeStruct((features, width), BF16),
            jax.ShapeDtypeStruct((fsdp, 16, width), FP32),
        ],
        [],
        (where, blocks[0], beside[0], blocks[1], beside[1], w_qkv) + gathered,
        9,
    )
    queries, keys, keys_t, values, normed_mine, *rest = kernel_call(
        attend_kernel,
        [
            jax.ShapeDtypeStruct((chips, rows, width), BF16),
            jax.ShapeDtypeStruct((ctx, rows, width), BF16),
            jax.ShapeDtypeStruct((ctx, width, rows), BF16),
            jax.ShapeDtypeStruct((ctx, rows, width), BF16),
            jax.ShapeDtypeStruct((chips, rows, features), BF16),
        ]
        + [jax.ShapeDtypeStruct((rows, width), BF16)] * 4
        + [
            jax.ShapeDtypeStruct((chips, width, rows), FP32),
            jax.ShapeDtypeStruct((chips, 8, rows), FP32),
            jax.ShapeDtypeStruct((16, 128), BF16),
        ],
        [
            pltpu.VMEM((ctx, width, rows), BF16),
            pltpu.VMEM((width, rows), FP32),
            pltpu.VMEM((chips, rows, width), BF16),
        ],
        (where, blocks[2], beside[2], blocks[3], beside[3])
        + (weight_q, weight_k, weight_v, small_all)
        + tuple(half_stores)
        + (key_tile, low_rows, high_rows, far_rows),
        30,
    )
    attended_t, logs, zeros = rest[4:]

    def swap_chips(pieces):
        return [pieces[0]] + [to_chip(pieces[s], s) for s in (1, 2, 3)]

    bundles = lax.dynamic_update_slice(bundles, (bundles[0, :16, :128] + zeros)[None], (0, 0, 0))
    bundles_other = to_core(bundles)
    attended = swap_chips(rest[:4])
    bundle_width = 2 * hidden_width // 2 + 3 * features + features // 2
    hbm = pl.BlockSpec(memory_space=pl.ANY)
    block_out, grad_middle, d0, d1, d2, d3, bundle_mine, bundle_send, small_rows = kernel_call(
        middle_kernel,
        [
            jax.ShapeDtypeStruct((rows, features), BF16),
            jax.ShapeDtypeStruct((rows, features), FP32),
        ]
        + [jax.ShapeDtypeStruct((rows, width), BF16)] * 4
        + [
            jax.ShapeDtypeStruct((rows, bundle_width), BF16),
            jax.ShapeDtypeStruct((rows, bundle_width), BF16),
            jax.ShapeDtypeStruct((fsdp, 16, features), FP32),
        ],
        [
            pltpu.VMEM((features, features), BF16),
            pltpu.VMEM((fsdp, features, columns), BF16),
            pltpu.VMEM((hidden_width, features), BF16),
            pltpu.VMEM((rows, columns), BF16),
            pltpu.VMEM((rows, features), BF16),
            pltpu.SemaphoreType.DMA((8 * 6,)),
        ],
        tuple([where] + attended)
        + (
            tokens,
            cotangent,
            live_rows,
            small_all,
            bundles,
            bundles_other,
        ),
        21,
        special={9: hbm, 10: hbm},
    )

    grad_blocks = swap_chips([d0, d1, d2, d3])

    bundle_other = to_core(bundle_send)
    out_rows = columns // 2 + 2 * shard
    small_at = out_rows + half
    block_rows = small_at + 32
    pair_shape = jax.ShapeDtypeStruct((2, block_rows, features), BF16)
    grads_keep, grads_send = kernel_call(
        weight_grad_kernel,
        [pair_shape, pair_shape],
        [pltpu.VMEM((2, features, features), BF16)],
        (where, bundle_mine, bundle_other, small_rows),
        14,
        after=(grad_blocks[1],),
    )

    grad_query, grad_keep, grad_send = kernel_call(
        attend_back_kernel,
        [
            jax.ShapeDtypeStruct((chips, rows, width), BF16),
            jax.ShapeDtypeStruct((chips, rows, 2 * width), FP32),
            jax.ShapeDtypeStruct((chips, rows, 2 * width), BF16),
        ],
        [
            pltpu.VMEM((width, rows), FP32),
            pltpu.VMEM((group_heads, ctx, rows, 64), FP32),
            pltpu.VMEM((group_heads, ctx, rows, 64), FP32),
            pltpu.VMEM((chips, rows, width), BF16),
        ],
        (
            where,
            queries,
            keys,
            keys_t,
            values,
            *grad_blocks,
            key_tile,
            low_rows,
            high_rows,
            far_rows,
            attended_t,
            logs,
        ),
        30,
    )
    packed = kernel_call(
        pack_kernel,
        [jax.ShapeDtypeStruct((rows, 3 * width), BF16)] * 4,
        [],
        (where, grad_query, grad_keep, to_core(grad_send)),
        2,
    )

    def add_up(left_side, right_side):
        return left_side.astype(FP32) + right_side.astype(FP32)

    arrived = swap_chips(packed)
    theirs = to_near(grads_send)
    block = jax.ShapeDtypeStruct((block_rows, features), BF16)

    def one_of(slot):
        spec = pl.BlockSpec((1, block_rows, features), lambda step: (slot, 0, 0))
        return {1: spec, 2: spec}

    (relay,) = kernel_call(
        relay_kernel,
        [block],
        [],
        (where, grads_keep, theirs),
        1,
        special=one_of(1),
        grid=(1,),
        after=(packed[0],),
    )

    def shaped(count, dtype):
        return jax.ShapeDtypeStruct((count, features), dtype)

    stay, give = kernel_call(
        pair_kernel,
        [shaped(block_rows // 2, FP32), shaped(block_rows // 2, BF16)],
        [],
        (where, grads_keep, theirs, to_across(relay)),
        2,
        special=one_of(0),
        grid=(1,),
        after=tuple(arrived[1:]),
    )
    given = give
    block_shape = (fsdp, half + 16, 3 * width)
    qkv_keep, qkv_send = kernel_call(
        qkv_grad_kernel,
        [jax.ShapeDtypeStruct(block_shape, FP32), jax.ShapeDtypeStruct(block_shape, BF16)],
        [pltpu.VMEM((features, 3 * width), FP32)],
        (
            where,
            normed_mine,
            *packed,
            weight_q,
            weight_k,
            weight_v,
            small_all,
        ),
        8,
        after=tuple(arrived[1:]) + (given,),
    )
    stay, give = kernel_call(
        quad_kernel,
        [shaped(block_rows // 4, FP32), shaped(block_rows // 4, BF16)],
        [],
        (where, stay, to_first(give)),
        1,
        after=(qkv_keep,),
    )
    given = give
    qkv_blocks = add_up(qkv_keep, to_core(qkv_send)).astype(BF16)
    theirs_qkv = to_near(qkv_blocks[2:])
    last_qkv = to_across(add_up(qkv_blocks[1], theirs_qkv[1]).astype(BF16))
    qkv_half = (add_up(qkv_blocks[0], theirs_qkv[0]) + last_qkv.astype(FP32)).astype(BF16)
    (grad_tokens,) = kernel_call(
        input_grad_kernel,
        [jax.ShapeDtypeStruct((rows, features), FP32)],
        [pltpu.VMEM((rows, 3 * features), BF16)],
        tuple([where] + arrived) + (qkv_full, tokens, grad_middle, small_all),
        5,
        after=(given,),
    )

    halves = swap_chips([jnp.stack([qkv_half, to_core(qkv_half)])] * 4)
    d_qkv, extra = kernel_call(
        qkv_output_kernel,
        [
            jax.ShapeDtypeStruct((shard, 3 * features), FP32),
            jax.ShapeDtypeStruct((chips, 16, 3 * width), FP32),
        ],
        [],
        tuple([where] + halves),
        2,
    )
    (quad,) = kernel_call(
        total_kernel, [shaped(block_rows // 4, BF16)], [], (where, stay, to_second(give)), 1
    )
    (joined,) = kernel_call(
        join_kernel, [shaped(block_rows // 2, BF16)], [], (where, quad, to_second(quad)), 1
    )
    joined_next = to_first(joined)
    d_proj, d_fc, d_out, small_sums = kernel_call(
        output_kernel,
        [
            jax.ShapeDtypeStruct((columns, features), FP32),
            jax.ShapeDtypeStruct((shard, hidden_width), FP32),
            jax.ShapeDtypeStruct((shard, features), FP32),
            jax.ShapeDtypeStruct((16, features), FP32),
        ],
        [pltpu.VMEM((block_rows, features), BF16), pltpu.VMEM((block_rows, features), BF16)],
        (where, joined, joined_next, to_core(joined), to_core(joined_next)),
        2,
    )
    d_bias_out, d_bias_proj, d_gain_two, d_shift_two = (
        small_sums[0, n * shard : (n + 1) * shard] for n in range(4)
    )
    d_bias_fc = small_sums[1]

    owner_extra = pick(extra, part)
    d_bias_q = owner_extra[2, :width]
    d_bias_v = owner_extra[2, 2 * width :]
    norm_total = jnp.sum(extra[:, :2, :shard], axis=0)
    d_gain_one = norm_total[0]
    d_shift_one = norm_total[1]

    return (
        block_out,
        grad_tokens,
        d_qkv,
        d_bias_q,
        d_bias_v,
        d_out,
        d_bias_out,
        d_fc,
        d_bias_fc,
        d_proj,
        d_bias_proj,
        d_gain_one,
        d_shift_one,
        d_gain_two,
        d_shift_two,
    )


def solution(mesh):
    in_specs = (
        P(("fsdp", "ctx"), None),
        P(("fsdp", "ctx"), None),
        P("fsdp", None),
        P("fsdp"),
        P("fsdp"),
        P("fsdp", None),
        P("fsdp"),
        P("fsdp", None),
        P("fsdp"),
        P("fsdp", None),
        P("fsdp"),
        P("fsdp"),
        P("fsdp"),
        P("fsdp"),
        P("fsdp"),
        P("fsdp", None),
        P("fsdp", None),
    )
    out_specs = (
        P(("fsdp", "ctx"), None),
        P(("fsdp", "ctx"), None),
        P("fsdp", None),
        P("fsdp"),
        P("fsdp"),
        P("fsdp", None),
        P("fsdp"),
        P("fsdp", None),
        P("fsdp"),
        P("fsdp", None),
        P("fsdp"),
        P("fsdp"),
        P("fsdp"),
        P("fsdp"),
        P("fsdp"),
    )
    ctx = mesh.shape["ctx"]
    four_by_four = mesh.shape["fsdp"] == 4 and ctx == 8 and HEADS % (ctx // 2) == 0
    body = fast_body if four_by_four else general_body
    return jax.shard_map(body, mesh=mesh, in_specs=in_specs, out_specs=out_specs, check_vma=False)
```

```python
import functools

import jax
import jax.numpy as jnp
from jax import lax
from jax.experimental import pallas as pl
from jax.experimental.pallas import tpu as pltpu
from jax.sharding import PartitionSpec as P

HEADS = 12


EPS = 1e-05


def layer_norm(values, gain_row, shift_row):
    centre = values - jnp.mean(values, axis=1, keepdims=True)
    inverse = lax.rsqrt(jnp.mean(centre * centre, axis=1, keepdims=True) + EPS)
    normed = centre * inverse
    return (normed * gain_row + shift_row, normed, inverse)


def norm_back(grad_in, normed, inverse, gain_row):
    scaled = grad_in * gain_row
    inner_grad = inverse * (
        scaled
        - jnp.mean(scaled, axis=1, keepdims=True)
        - normed * jnp.mean(scaled * normed, axis=1, keepdims=True)
    )
    return (inner_grad, jnp.sum(grad_in * normed, axis=0), jnp.sum(grad_in, axis=0))


def contract_rows(left_side, right_side):
    return lax.dot_general(
        left_side, right_side, (((0,), (0,)), ((), ())), preferred_element_type=jnp.float32
    )


def times_transpose(left_side, right_side):
    return lax.dot_general(
        left_side, right_side, (((1,), (1,)), ((), ())), preferred_element_type=jnp.float32
    )


def gelu_tanh(values):
    return jax.nn.gelu(values, approximate=True)


def describe(slot_ids, row_count, count_row, offsets, seq_ends):
    peer_count = count_row.shape[0]
    device = slot_ids // row_count
    within = slot_ids - device * row_count
    matches = device[:, None] == jnp.arange(peer_count, dtype=jnp.int32)[None, :]
    live_count = jnp.sum(jnp.where(matches, count_row[None, :], 0), axis=1)
    first_place = jnp.sum(jnp.where(matches, offsets[None, :], 0), axis=1)
    places = first_place + within
    segment = jnp.sum((places[:, None] >= seq_ends[None, :]).astype(jnp.int32), axis=1)
    return (within < live_count, places, segment, slot_ids)


def allowed(query_info, key_info):
    q_live, q_place, q_seg, q_slot = query_info
    k_live, k_place, k_seg, k_slot = key_info
    same_seq = (
        q_live[:, None]
        & k_live[None, :]
        & (q_seg[:, None] == k_seg[None, :])
        & (k_place[None, :] <= q_place[:, None])
    )
    return same_seq | (q_slot[:, None] == k_slot[None, :])


def over_blocks(step_fn, status, pieces, row_count):
    total_rows = pieces[0].shape[0]
    block_total = total_rows // row_count
    stacked = tuple((piece.reshape((block_total, row_count) + piece.shape[1:]) for piece in pieces))

    def scan_body(state_now, scan_item):
        block_index, block_parts = scan_item
        return (step_fn(state_now, block_parts, block_index * row_count), None)

    status, unused = lax.scan(
        scan_body, status, (jnp.arange(block_total, dtype=jnp.int32), stacked)
    )
    return status


def score_grads(
    query_heads, key_heads, value_heads, grad_heads, lse_rows, delta_rows, permitted, scaling
):
    scores = (
        jnp.einsum("qhd,khd->hqk", query_heads, key_heads, preferred_element_type=jnp.float32)
        * scaling
    )
    probabilities = jnp.where(permitted[None], jnp.exp(scores - lse_rows[:, :, None]), 0.0)
    grad_probs = jnp.einsum(
        "qhd,khd->hqk", grad_heads, value_heads, preferred_element_type=jnp.float32
    )
    grad_scores = (probabilities * (grad_probs - delta_rows[:, :, None])).astype(jnp.bfloat16)
    return (probabilities.astype(jnp.bfloat16), grad_scores)


def general_body(
    tokens,
    cotangent,
    w_qkv,
    b_query,
    b_value,
    w_out,
    b_out,
    w_fc,
    b_fc,
    w_proj,
    b_proj,
    gain1,
    shift1,
    gain2,
    shift2,
    counts,
    seq_lengths,
):
    row_count, feature_count = tokens.shape
    peer_count = lax.axis_size("ctx")
    my_index = lax.axis_index("ctx")
    head_count = HEADS
    head_width = feature_count // head_count
    scaling = head_width ** (-0.5)
    count_row = counts[0]
    offsets = jnp.cumsum(count_row) - count_row
    seq_ends = jnp.cumsum(seq_lengths[0])

    def locate(first_slot, length):
        return describe(
            first_slot + jnp.arange(length, dtype=jnp.int32),
            row_count,
            count_row,
            offsets,
            seq_ends,
        )

    own_rows = locate(my_index * row_count, row_count)
    fp32 = jnp.float32
    bf16 = jnp.bfloat16
    (
        qkv_full,
        query_bias,
        value_bias,
        out_full,
        out_bias,
        fc_full,
        fc_bias,
        proj_full,
        proj_bias,
        gain_one,
        shift_one,
        gain_two,
        shift_two,
    ) = (
        lax.all_gather(w_qkv, "fsdp", axis=0, tiled=True),
        lax.all_gather(b_query, "fsdp", axis=0, tiled=True),
        lax.all_gather(b_value, "fsdp", axis=0, tiled=True),
        lax.all_gather(w_out, "fsdp", axis=0, tiled=True),
        lax.all_gather(b_out, "fsdp", axis=0, tiled=True),
        lax.all_gather(w_fc, "fsdp", axis=0, tiled=True),
        lax.all_gather(b_fc, "fsdp", axis=0, tiled=True),
        lax.all_gather(w_proj, "fsdp", axis=0, tiled=True),
        lax.all_gather(b_proj, "fsdp", axis=0, tiled=True),
        lax.all_gather(gain1, "fsdp", axis=0, tiled=True),
        lax.all_gather(shift1, "fsdp", axis=0, tiled=True),
        lax.all_gather(gain2, "fsdp", axis=0, tiled=True),
        lax.all_gather(shift2, "fsdp", axis=0, tiled=True),
    )
    inputs = tokens.astype(fp32)
    normed_one, unit_one, inverse_one = layer_norm(
        inputs, gain_one.astype(fp32), shift_one.astype(fp32)
    )
    normed_low = normed_one.astype(bf16)
    bias_row = jnp.concatenate([query_bias, jnp.zeros_like(query_bias), value_bias]).astype(fp32)
    packed = (jnp.dot(normed_low, qkv_full, preferred_element_type=fp32) + bias_row).astype(bf16)
    query_rows = packed[:, :feature_count]
    key_rows = packed[:, feature_count : 2 * feature_count]
    value_rows = packed[:, 2 * feature_count :]
    query_heads = query_rows.reshape(row_count, head_count, head_width)

    def forward_step(status, pieces, first_row):
        running_max, running_sum, running_acc = status
        key_piece, value_piece = pieces
        length = key_piece.shape[0]
        key_heads = key_piece.reshape(length, head_count, head_width)
        value_heads = value_piece.reshape(length, head_count, head_width)
        scores = (
            jnp.einsum("qhd,khd->hqk", query_heads, key_heads, preferred_element_type=fp32)
            * scaling
        )
        permitted = allowed(own_rows, locate(first_row, length))
        scores = jnp.where(permitted[None], scores, -jnp.inf)
        new_max = jnp.maximum(running_max, jnp.max(scores, axis=2))
        fading = jnp.exp(running_max - new_max)
        weights = jnp.exp(scores - new_max[:, :, None])
        running_sum = running_sum * fading + jnp.sum(weights, axis=2)
        update = jnp.einsum(
            "hqk,khd->qhd", weights.astype(bf16), value_heads, preferred_element_type=fp32
        )
        running_acc = running_acc * jnp.transpose(fading)[:, :, None] + update
        return (new_max, running_sum, running_acc)

    start_state = (
        jnp.full((head_count, row_count), -1e30, fp32),
        jnp.zeros((head_count, row_count), fp32),
        jnp.zeros((row_count, head_count, head_width), fp32),
    )
    final_max, final_sum, final_acc = over_blocks(
        forward_step,
        start_state,
        (
            lax.all_gather(key_rows, "ctx", axis=0, tiled=True),
            lax.all_gather(value_rows, "ctx", axis=0, tiled=True),
        ),
        row_count,
    )
    attended_heads = final_acc / jnp.transpose(final_sum)[:, :, None]
    attended = attended_heads.reshape(row_count, feature_count)
    log_total = final_max + jnp.log(final_sum)
    attended_low = attended.astype(bf16)
    middle = (
        inputs
        + jnp.dot(attended_low, out_full, preferred_element_type=fp32)
        + out_bias.astype(fp32)
    )
    normed_two, unit_two, inverse_two = layer_norm(
        middle, gain_two.astype(fp32), shift_two.astype(fp32)
    )
    normed_two_low = normed_two.astype(bf16)
    hidden = jnp.dot(normed_two_low, fc_full, preferred_element_type=fp32) + fc_bias.astype(fp32)
    activated = gelu_tanh(hidden).astype(bf16)
    output = (
        middle + jnp.dot(activated, proj_full, preferred_element_type=fp32) + proj_bias.astype(fp32)
    )
    output_low = output.astype(bf16)
    qkv_full, out_full, fc_full, proj_full, gain_one, gain_two = (
        lax.all_gather(w_qkv, "fsdp", axis=0, tiled=True),
        lax.all_gather(w_out, "fsdp", axis=0, tiled=True),
        lax.all_gather(w_fc, "fsdp", axis=0, tiled=True),
        lax.all_gather(w_proj, "fsdp", axis=0, tiled=True),
        lax.all_gather(gain1, "fsdp", axis=0, tiled=True),
        lax.all_gather(gain2, "fsdp", axis=0, tiled=True),
    )
    live_rows = own_rows[0].astype(fp32)[:, None]
    grad_out = cotangent.astype(fp32) * live_rows
    grad_out_low = grad_out.astype(bf16)
    grad_proj = contract_rows(activated, grad_out_low)
    grad_proj_bias = jnp.sum(grad_out, axis=0)
    grad_act = times_transpose(grad_out_low, proj_full)
    grad_hidden = jax.vjp(gelu_tanh, hidden)[1](grad_act)[0]
    grad_hidden_low = grad_hidden.astype(bf16)
    grad_fc = contract_rows(normed_two_low, grad_hidden_low)
    grad_fc_bias = jnp.sum(grad_hidden_low.astype(fp32), axis=0)
    grad_normed_two = times_transpose(grad_hidden_low, fc_full)
    grad_mid_norm, grad_gain_two, grad_shift_two = norm_back(
        grad_normed_two, unit_two, inverse_two, gain_two.astype(fp32)
    )
    grad_middle = grad_out + grad_mid_norm
    grad_middle_low = grad_middle.astype(bf16)
    grad_out_proj = contract_rows(attended_low, grad_middle_low)
    grad_out_bias = jnp.sum(grad_middle_low.astype(fp32), axis=0)
    grad_attended = times_transpose(grad_middle_low, out_full).astype(bf16)
    grad_heads = grad_attended.reshape(row_count, head_count, head_width)
    delta_rows = jnp.transpose(jnp.sum(grad_heads.astype(fp32) * attended_heads, axis=2))

    def back_step(status, pieces, first_row):
        grad_query, grad_keys = status
        key_piece, value_piece = pieces
        length = key_piece.shape[0]
        key_heads = key_piece.reshape(length, head_count, head_width)
        value_heads = value_piece.reshape(length, head_count, head_width)
        permitted = allowed(own_rows, locate(first_row, length))
        probs_low, grad_scores = score_grads(
            query_heads,
            key_heads,
            value_heads,
            grad_heads,
            log_total,
            delta_rows,
            permitted,
            scaling,
        )
        grad_query = (
            grad_query
            + jnp.einsum("hqk,khd->qhd", grad_scores, key_heads, preferred_element_type=fp32)
            * scaling
        )
        grad_key_part = (
            jnp.einsum("hqk,qhd->khd", grad_scores, query_heads, preferred_element_type=fp32)
            * scaling
        )
        grad_value_part = jnp.einsum(
            "hqk,qhd->khd", probs_low, grad_heads, preferred_element_type=fp32
        )
        joined = jnp.concatenate(
            [
                grad_key_part.reshape(length, feature_count),
                grad_value_part.reshape(length, feature_count),
            ],
            axis=1,
        )
        current = lax.dynamic_slice_in_dim(grad_keys, first_row, length, 0)
        grad_keys = lax.dynamic_update_slice_in_dim(grad_keys, current + joined, first_row, 0)
        return (grad_query, grad_keys)

    keys_start = jnp.zeros((peer_count * row_count, 2 * feature_count), fp32)
    grad_query, grad_keys = over_blocks(
        back_step,
        (jnp.zeros((row_count, head_count, head_width), fp32), keys_start),
        (
            lax.all_gather(key_rows, "ctx", axis=0, tiled=True),
            lax.all_gather(value_rows, "ctx", axis=0, tiled=True),
        ),
        row_count,
    )
    grad_kv = lax.psum_scatter(
        grad_keys.astype(jnp.bfloat16), "ctx", scatter_dimension=0, tiled=True
    ).astype(jnp.float32)
    grad_packed = jnp.concatenate(
        [grad_query.reshape(row_count, feature_count), grad_kv], axis=1
    ).astype(bf16)
    grad_packed_wide = grad_packed.astype(fp32)
    grad_query_bias = jnp.sum(grad_packed_wide[:, :feature_count], axis=0)
    grad_value_bias = jnp.sum(grad_packed_wide[:, 2 * feature_count :], axis=0)
    grad_qkv = contract_rows(normed_low, grad_packed)
    grad_normed_one = times_transpose(grad_packed, qkv_full)
    grad_in_norm, grad_gain_one, grad_shift_one = norm_back(
        grad_normed_one, unit_one, inverse_one, gain_one.astype(fp32)
    )
    grad_tokens = grad_middle + grad_in_norm
    (
        sum_qkv,
        sum_qbias,
        sum_vbias,
        sum_out,
        sum_obias,
        sum_fc,
        sum_fbias,
        sum_proj,
        sum_pbias,
        sum_gain_one,
        sum_shift_one,
        sum_gain_two,
        sum_shift_two,
    ) = (
        lax.psum_scatter(
            grad_qkv.astype(jnp.bfloat16), "fsdp", scatter_dimension=0, tiled=True
        ).astype(jnp.float32),
        lax.psum_scatter(
            grad_query_bias.astype(jnp.bfloat16), "fsdp", scatter_dimension=0, tiled=True
        ).astype(jnp.float32),
        lax.psum_scatter(
            grad_value_bias.astype(jnp.bfloat16), "fsdp", scatter_dimension=0, tiled=True
        ).astype(jnp.float32),
        lax.psum_scatter(
            grad_out_proj.astype(jnp.bfloat16), "fsdp", scatter_dimension=0, tiled=True
        ).astype(jnp.float32),
        lax.psum_scatter(
            grad_out_bias.astype(jnp.bfloat16), "fsdp", scatter_dimension=0, tiled=True
        ).astype(jnp.float32),
        lax.psum_scatter(
            grad_fc.astype(jnp.bfloat16), "fsdp", scatter_dimension=0, tiled=True
        ).astype(jnp.float32),
        lax.psum_scatter(
            grad_fc_bias.astype(jnp.bfloat16), "fsdp", scatter_dimension=0, tiled=True
        ).astype(jnp.float32),
        lax.psum_scatter(
            grad_proj.astype(jnp.bfloat16), "fsdp", scatter_dimension=0, tiled=True
        ).astype(jnp.float32),
        lax.psum_scatter(
            grad_proj_bias.astype(jnp.bfloat16), "fsdp", scatter_dimension=0, tiled=True
        ).astype(jnp.float32),
        lax.psum_scatter(
            grad_gain_one.astype(jnp.bfloat16), "fsdp", scatter_dimension=0, tiled=True
        ).astype(jnp.float32),
        lax.psum_scatter(
            grad_shift_one.astype(jnp.bfloat16), "fsdp", scatter_dimension=0, tiled=True
        ).astype(jnp.float32),
        lax.psum_scatter(
            grad_gain_two.astype(jnp.bfloat16), "fsdp", scatter_dimension=0, tiled=True
        ).astype(jnp.float32),
        lax.psum_scatter(
            grad_shift_two.astype(jnp.bfloat16), "fsdp", scatter_dimension=0, tiled=True
        ).astype(jnp.float32),
    )
    totals = (
        lax.psum(sum_qkv.astype(jnp.bfloat16), "ctx").astype(jnp.float32),
        lax.psum(sum_qbias.astype(jnp.bfloat16), "ctx").astype(jnp.float32),
        lax.psum(sum_vbias.astype(jnp.bfloat16), "ctx").astype(jnp.float32),
        lax.psum(sum_out.astype(jnp.bfloat16), "ctx").astype(jnp.float32),
        lax.psum(sum_obias.astype(jnp.bfloat16), "ctx").astype(jnp.float32),
        lax.psum(sum_fc.astype(jnp.bfloat16), "ctx").astype(jnp.float32),
        lax.psum(sum_fbias.astype(jnp.bfloat16), "ctx").astype(jnp.float32),
        lax.psum(sum_proj.astype(jnp.bfloat16), "ctx").astype(jnp.float32),
        lax.psum(sum_pbias.astype(jnp.bfloat16), "ctx").astype(jnp.float32),
        lax.psum(sum_gain_one.astype(jnp.bfloat16), "ctx").astype(jnp.float32),
        lax.psum(sum_shift_one.astype(jnp.bfloat16), "ctx").astype(jnp.float32),
        lax.psum(sum_gain_two.astype(jnp.bfloat16), "ctx").astype(jnp.float32),
        lax.psum(sum_shift_two.astype(jnp.bfloat16), "ctx").astype(jnp.float32),
    )
    return (
        output_low,
        grad_tokens,
        totals[0],
        totals[1],
        totals[2],
        totals[3],
        totals[4],
        totals[5],
        totals[6],
        totals[7],
        totals[8],
        totals[9],
        totals[10],
        totals[11],
        totals[12],
    )


FP32 = jnp.float32
BF16 = jnp.bfloat16
FLOOR = -1e30
NEVER = 1 << 30


def dot_nt(left_side, right_side):
    return lax.dot_general(
        left_side, right_side, (((1,), (1,)), ((), ())), preferred_element_type=FP32
    )


def dot_nn(left_side, right_side):
    return lax.dot_general(
        left_side, right_side, (((1,), (0,)), ((), ())), preferred_element_type=FP32
    )


def spread(column_tile, width):
    return jnp.concatenate([column_tile] * (width // column_tile.shape[1]), axis=1)


def masked_scores(scores, key_ids, first_row, last_row):
    permitted = key_ids >= first_row
    if last_row is not None:
        permitted = permitted & (key_ids <= last_row)
    return jnp.where(permitted, scores, -jnp.inf)


def whole_vector(small_ref, number):
    parts = [small_ref[f, number : number + 1, :] for f in range(small_ref.shape[0])]
    return jnp.concatenate(parts, axis=1)


def stats_kernel(where, *refs):
    out_ref = refs[-1]
    for n, ref in enumerate(refs[:-1]):
        wide = ref[...].astype(FP32)
        mean = jnp.mean(wide, axis=1, keepdims=True)
        centre = wide - mean
        inverse = lax.rsqrt(jnp.mean(centre * centre, axis=1, keepdims=True) + EPS)
        out_ref[n, :, 0:1] = mean
        out_ref[n, :, 1:2] = inverse


def project_block(
    tokens_ref, row_stats, wq_ref, wk_ref, wv_ref, small_ref, chip, stores, position, wanted
):
    q_ref, k_ref, kt_ref, v_ref, vt_ref, normed_ref = stores
    gain, shift = whole_vector(small_ref, 4), whole_vector(small_ref, 5)
    centre = tokens_ref[...].astype(FP32) - row_stats[:, 0:1]
    normed = centre * row_stats[:, 1:2] * gain + shift
    normed = normed.astype(BF16)
    keys = dot_nn(normed, wk_ref[...])
    values = dot_nn(normed, wv_ref[...]) + small_ref[chip, 1:2, :]
    k_ref[position] = keys.astype(BF16)
    v_ref[position] = values.astype(BF16)
    kt_ref[position] = keys.T.astype(BF16)
    vt_ref[position] = values.T.astype(BF16)
    if wanted:
        queries = (dot_nn(normed, wq_ref[...]) + small_ref[chip, 0:1, :]).astype(BF16)
        q_ref[position // 2] = (queries.astype(FP32) * 0.125).astype(BF16)
        normed_ref[position // 2] = normed


def project_kernel(
    where,
    t0,
    t1,
    t2,
    t3,
    stats_ref,
    w_ref,
    halves_ref,
    others_ref,
    q,
    k,
    kt,
    v,
    vt,
    normed,
    full_ref,
    wq,
    wk,
    wv,
    small_ref,
):
    core, chip = where[1], where[2]
    shard, wide = w_ref.shape
    features, half, width = wide // 3, shard // 2, wq.shape[1]
    for f in range(halves_ref.shape[0]):
        for ref, which in ((halves_ref, core), (others_ref, 1 - core)):
            first = pl.multiple_of(f * shard + which * half, 16)
            full_ref[pl.ds(first, half), :] = ref[f, 0:half, :]
        small_ref[f] = halves_ref[f, half:, 0:width].astype(FP32)
    for z in range(features // width):

        @pl.when(chip == z)
        def own_columns():
            for n, ref in enumerate((wq, wk, wv)):
                first = features * n + width * z
                ref[...] = full_ref[:, first : first + width]

    stores = (q, k, kt, v, vt, normed)
    for n, block in enumerate((t0, t1, t2, t3)):
        owner = (chip ^ (n // 2)) % 2
        position = 2 * owner + (core if n % 2 == 0 else 1 - core)
        project_block(block, stats_ref[n], wq, wk, wv, small_ref, chip, stores, position, n % 2 == 0)


def attend_kernel(
    where,
    t0,
    t1,
    t2,
    t3,
    stats_ref,
    wq_ref,
    wk_ref,
    wv_ref,
    small_ref,
    q_half,
    k_half,
    kt_half,
    v_half,
    vt_half,
    normed_half,
    key_ref,
    low_ref,
    high_ref,
    far_ref,
    q_ref,
    k_ref,
    kt_ref,
    v_ref,
    normed_ref,
    o0_ref,
    o1_ref,
    o2_ref,
    o3_ref,
    ot_ref,
    lse_ref,
    zero_ref,
    vt_ref,
    acc_ref,
    o_ref,
):
    blocks, rows, width = q_ref.shape
    heads = width // 64
    core, chip = where[1], where[2]
    side = chip // 2
    zero_ref[...] = jnp.zeros_like(zero_ref)
    stores = (q_ref, k_ref, kt_ref, v_ref, vt_ref, normed_ref)
    for n, block in enumerate((t0, t1, t2, t3)):
        owner = chip ^ (2 + n // 2)
        position = 2 * owner + (core if n % 2 == 0 else 1 - core)
        project_block(
            block,
            stats_ref[4 + n],
            wq_ref,
            wk_ref,
            wv_ref,
            small_ref,
            chip,
            stores,
            position,
            n % 2 == 0,
        )
    for n in range(blocks):
        for source, target in ((k_half, k_ref), (kt_half, kt_ref), (v_half, v_ref), (vt_half, vt_ref)):
            target[side * blocks + n] = source[n]
    for n in range(blocks // 2):
        q_ref[side * (blocks // 2) + n] = q_half[n]
        normed_ref[side * (blocks // 2) + n] = normed_half[n]

    def query_block(index, unused):
        queries = [q_ref[index, :, 64 * h : 64 * h + 64] for h in range(heads)]
        acc_ref[...] = jnp.zeros_like(acc_ref)

        def key_step(key_block, carry, first_row, last_row):
            ids = spread(key_ref[key_block], rows)
            result = []
            for h in range(heads):
                span = slice(64 * h, 64 * h + 64)
                top, total = carry[h]
                scores = dot_nt(k_ref[key_block, :, span], queries[h])
                scores = masked_scores(scores, ids, first_row, last_row)
                new_top = jnp.maximum(top, jnp.max(scores, axis=0, keepdims=True))
                fade = jnp.exp(top - new_top)
                weights = jnp.exp(scores - new_top)
                total = total * fade + jnp.sum(weights, axis=0, keepdims=True)
                acc_ref[span, :] = acc_ref[span, :] * fade + dot_nn(
                    vt_ref[key_block, span, :], weights.astype(BF16)
                )
                result.append((new_top, total))
            return tuple(result)

        start = tuple(
            (jnp.full((1, rows), FLOOR, FP32), jnp.zeros((1, rows), FP32)) for h in range(heads)
        )
        own = 2 * index + core
        far_row = far_ref[index]
        carry = lax.fori_loop(0, own, lambda j, c: key_step(j, c, far_row, None), start)
        carry = key_step(own, carry, low_ref[index], high_ref[index])
        for h in range(heads):
            span = slice(64 * h, 64 * h + 64)
            top, total = carry[h]
            attended = acc_ref[span, :] / total
            ot_ref[index, span, :] = attended
            o_ref[index, :, span] = attended.T.astype(BF16)
            lse_ref[index, h : h + 1, :] = top + jnp.log(total)
        return unused

    lax.fori_loop(0, blocks, query_block, 0)
    for s, ref in enumerate((o0_ref, o1_ref, o2_ref, o3_ref)):
        ref[...] = o_ref[chip ^ s]


def attend_back_kernel(
    where,
    q_ref,
    k_ref,
    kt_ref,
    v_ref,
    d0_ref,
    d1_ref,
    d2_ref,
    d3_ref,
    key_ref,
    low_ref,
    high_ref,
    far_ref,
    ot_ref,
    lse_ref,
    dq_ref,
    keep_ref,
    send_ref,
    acc_ref,
    dk_ref,
    dv_ref,
    da_ref,
):
    blocks, rows, width = q_ref.shape
    heads = width // 64
    core, chip = where[1], where[2]
    for s, ref in enumerate((d0_ref, d1_ref, d2_ref, d3_ref)):
        da_ref[chip ^ s] = ref[...]
    dk_ref[...] = jnp.zeros_like(dk_ref)
    dv_ref[...] = jnp.zeros_like(dv_ref)

    def query_block(index, unused):
        queries = [q_ref[index, :, 64 * h : 64 * h + 64] for h in range(heads)]
        grads = [da_ref[index, :, 64 * h : 64 * h + 64] for h in range(heads)]
        deltas = [
            jnp.sum(
                grads[h].astype(FP32).T * ot_ref[index, 64 * h : 64 * h + 64, :],
                axis=0,
                keepdims=True,
            )
            for h in range(heads)
        ]
        logs = [lse_ref[index, h : h + 1, :] for h in range(heads)]
        acc_ref[...] = jnp.zeros_like(acc_ref)

        def key_step(key_block, first_row, last_row):
            ids = spread(key_ref[key_block], rows)
            for h in range(heads):
                span = slice(64 * h, 64 * h + 64)
                scores = dot_nt(k_ref[key_block, :, span], queries[h])
                scores = masked_scores(scores, ids, first_row, last_row)
                weights = jnp.exp(scores - logs[h])
                slopes = dot_nt(v_ref[key_block, :, span], grads[h])
                dscores = (weights * (slopes - deltas[h])).astype(BF16)
                dv_ref[h, key_block] += dot_nn(weights.astype(BF16), grads[h])
                dk_ref[h, key_block] += dot_nn(dscores, queries[h])
                acc_ref[span, :] += dot_nn(kt_ref[key_block, span, :], dscores)

        own = 2 * index + core
        far_row = far_ref[index]

        def far_step(key_block, state):
            key_step(key_block, far_row, None)
            return state

        lax.fori_loop(0, own, far_step, 0)
        key_step(own, low_ref[index], high_ref[index])
        for h in range(heads):
            span = slice(64 * h, 64 * h + 64)
            dq_ref[index, :, span] = (acc_ref[span, :] * 0.125).T.astype(BF16)
        return unused

    lax.fori_loop(0, blocks, query_block, 0)

    def write_block(index, unused):
        mine = 2 * index + core
        theirs = 2 * index + 1 - core
        for h in range(heads):
            left = slice(64 * h, 64 * h + 64)
            right = slice(width + 64 * h, width + 64 * h + 64)
            keep_ref[index, :, left] = dk_ref[h, mine]
            keep_ref[index, :, right] = dv_ref[h, mine]
            send_ref[index, :, left] = dk_ref[h, theirs].astype(BF16)
            send_ref[index, :, right] = dv_ref[h, theirs].astype(BF16)
        return unused

    lax.fori_loop(0, blocks, write_block, 0)


def kernel_call(kernel, outputs, scratch, operands, cost, special={}, after=()):
    whole = pl.BlockSpec(memory_space=pltpu.VMEM)
    in_specs = [pl.BlockSpec(memory_space=pltpu.SMEM)]
    in_specs += [special.get(n, whole) for n in range(1, len(operands))]
    in_specs += [pl.BlockSpec(memory_space=pl.ANY) for unused in after]
    count = len(operands)

    def ordered(*refs):
        return kernel(*refs[:count], *refs[count + len(after) :])

    moved = sum(v.size * v.dtype.itemsize for v in list(operands) + list(outputs))
    return pl.pallas_call(
        ordered,
        out_shape=outputs,
        in_specs=in_specs,
        out_specs=[pl.BlockSpec(memory_space=pltpu.VMEM) for unused in outputs],
        scratch_shapes=scratch,
        compiler_params=pltpu.CompilerParams(vmem_limit_bytes=56 * 1024 * 1024),
        cost_estimate=pl.CostEstimate(
            flops=cost * 1153 * 10**6, bytes_accessed=moved, transcendentals=0
        ),
    )(*operands, *after)


def pack_kernel(where, dq_ref, keep_ref, arrived_ref, p0, p1, p2, p3):
    chip = where[2]
    width = dq_ref.shape[2]
    for s, ref in enumerate((p0, p1, p2, p3)):
        owner = chip ^ s
        ref[:, 0:width] = dq_ref[owner]
        ref[:, width:] = (keep_ref[owner] + arrived_ref[owner].astype(FP32)).astype(BF16)


def middle_kernel(
    where,
    a0_ref,
    a1_ref,
    a2_ref,
    a3_ref,
    tokens_ref,
    cotangent_ref,
    live_ref,
    small_ref,
    bundle_own,
    bundle_other,
    block_ref,
    dx_ref,
    d0_ref,
    d1_ref,
    d2_ref,
    d3_ref,
    mine_ref,
    send_ref,
    sums_ref,
    wo_ref,
    wf_ref,
    wp_ref,
    g_ref,
    dz_ref,
    sems,
):
    rows, features = tokens_ref.shape
    parts = wf_ref.shape[0]
    shard, hidden_width = features // parts, wp_ref.shape[0]
    columns = hidden_width // parts
    half, half_columns = shard // 2, columns // 2
    core, chip = where[1], where[2]

    starts = {"proj": [], "out": [], "fc": []}

    def fetch(kind, source, target):
        number = sum(len(v) for v in starts.values())
        starts[kind].append(pltpu.make_async_copy(source, target, sems.at[number]))

    def rows_at(owner, which, size):
        return pl.ds(pl.multiple_of(owner * 2 * size + which * size, 16), size)

    pieces = []
    for owner in range(parts):
        pieces.append((bundle_own.at[owner], owner, core))
        pieces.append((bundle_other.at[owner], owner, 1 - core))
    for piece, owner, which in pieces:
        fetch("out", piece.at[half_columns : half_columns + half, :], wo_ref.at[rows_at(owner, which, half), :])
    for piece, owner, which in pieces:
        for j in range(parts):
            first = half_columns + half * (j + 1)
            fetch("fc", piece.at[first : first + half, :], wf_ref.at[j, rows_at(owner, which, half), :])
    for piece, owner, which in pieces:
        fetch("proj", piece.at[0:half_columns, :], wp_ref.at[rows_at(owner, which, half_columns), :])
    for kind in ("out", "fc", "proj"):
        for copy in starts[kind]:
            copy.start()
    for copy in starts["out"]:
        copy.wait()

    attended = [a0_ref, a1_ref, a2_ref, a3_ref]
    middle = tokens_ref[...].astype(FP32) + whole_vector(small_ref, 2)
    a_start = 2 * parts * half_columns + features
    for s in range(parts):
        span = pl.ds(pl.multiple_of((chip ^ s) * shard, 16), shard)
        middle = middle + dot_nn(attended[s][...], wo_ref[span, :])
        mine_ref[:, a_start + shard * s : a_start + shard * (s + 1)] = attended[s][...]
        send_ref[:, a_start + shard * s : a_start + shard * (s + 1)] = attended[s][...]
    normed, unit, inverse = layer_norm(
        middle, whole_vector(small_ref, 6), whole_vector(small_ref, 7)
    )
    normed_low = normed.astype(BF16)
    h_start = 2 * parts * half_columns
    mine_ref[:, h_start : h_start + features] = normed_low
    send_ref[:, h_start : h_start + features] = normed_low
    grad_out = cotangent_ref[...].astype(FP32) * live_ref[...]
    grad_out_low = grad_out.astype(BF16)
    y_start = a_start + features
    mine_ref[:, y_start : y_start + features] = grad_out_low
    send_ref[:, y_start : y_start + features] = grad_out_low
    for copy in starts["fc"] + starts["proj"]:
        copy.wait()

    sums_ref[...] = jnp.zeros_like(sums_ref)
    output = middle + whole_vector(small_ref, 3)
    grad_normed = jnp.zeros((rows, features), FP32)
    scale, cubic = 0.7978845608028654, 0.044715
    for j in range(parts):
        span = slice(columns * j, columns * (j + 1))
        bias_fc = jnp.concatenate([small_ref[j, 8 + n : 9 + n, :] for n in range(parts)], axis=1)
        hidden = dot_nn(normed_low, wf_ref[j]) + bias_fc
        square = hidden * hidden
        bent = jnp.tanh(scale * hidden * (1.0 + cubic * square))
        active = 0.5 * hidden * (1.0 + bent)
        slope = 0.5 * (1.0 + bent) + 0.5 * hidden * (1.0 - bent * bent) * (
            scale * (1.0 + 3.0 * cubic * square)
        )
        g_ref[...] = active.astype(BF16)
        grad_hidden = (dot_nt(grad_out_low, wp_ref[span, :]) * slope).astype(BF16)
        output = output + dot_nn(g_ref[...], wp_ref[span, :])
        grad_normed = grad_normed + dot_nt(grad_hidden, wf_ref[j])
        sums_ref[j, 1:2, :] = jnp.sum(grad_hidden.astype(FP32), axis=0, keepdims=True)
        g_span = slice(half_columns * j, half_columns * (j + 1))
        mine_ref[:, g_span] = g_ref[:, pl.ds(pl.multiple_of(core * half_columns, 128), half_columns)]
        send_ref[:, g_span] = g_ref[
            :, pl.ds(pl.multiple_of((1 - core) * half_columns, 128), half_columns)
        ]
        first = parts * half_columns + columns * (j % 2)

        @pl.when(core == j // 2)
        def keep_hidden():
            mine_ref[:, first : first + columns] = grad_hidden

        @pl.when(core != j // 2)
        def give_hidden():
            send_ref[:, first : first + columns] = grad_hidden

    block_ref[...] = output.astype(BF16)
    inner, gain_sum, shift_sum = norm_back(
        grad_normed, unit, inverse, whole_vector(small_ref, 6)
    )
    grad_middle = grad_out + inner
    dx_ref[...] = grad_middle
    dz_ref[...] = grad_middle.astype(BF16)
    z_start = y_start + features
    part_width = features // 2
    mine_ref[:, z_start : z_start + part_width] = dz_ref[
        :, pl.ds(pl.multiple_of(core * part_width, 128), part_width)
    ]
    send_ref[:, z_start : z_start + part_width] = dz_ref[
        :, pl.ds(pl.multiple_of((1 - core) * part_width, 128), part_width)
    ]
    for s, ref in enumerate((d0_ref, d1_ref, d2_ref, d3_ref)):
        span = pl.ds(pl.multiple_of((chip ^ s) * shard, 16), shard)
        ref[...] = dot_nt(dz_ref[...], wo_ref[span, :]).astype(BF16)
    rows_of_sums = (
        jnp.sum(dz_ref[...].astype(FP32), axis=0, keepdims=True),
        jnp.sum(grad_out, axis=0, keepdims=True),
        gain_sum[None, :],
        shift_sum[None, :],
    )
    for n, row in enumerate(rows_of_sums):
        for f in range(parts):
            sums_ref[f, 0:1, shard * n : shard * (n + 1)] = row[:, shard * f : shard * (f + 1)]


def weight_grad_kernel(where, mine_ref, other_ref, small_ref, keep_ref, send_ref, fc_ref):
    rows = mine_ref.shape[0]
    features = keep_ref.shape[2]
    part, core, chip = where[0], where[1], where[2]
    near, across = 1 + core, 2 - core
    parts = 4
    shard, half_columns = features // parts, features // 2
    h_start = 2 * parts * half_columns
    a_start = h_start + features
    y_start = a_start + features
    z_start = y_start + features

    def product(left, right):
        return contract_rows(mine_ref[:, left], mine_ref[:, right]) + contract_rows(
            other_ref[:, left], other_ref[:, right]
        )

    targets = [(keep_ref, 0, part), (keep_ref, 1, part ^ across)]
    targets += [(send_ref, 0, part ^ near), (send_ref, 1, part ^ 3)]
    fc_base = parts * half_columns
    for j in range(2):
        fc_ref[j] = product(
            pl.ds(h_start, features), pl.ds(fc_base + features * j, features)
        ).astype(BF16)
    out_base = half_columns + 2 * shard
    small_base = out_base + shard // 2
    for ref, slot, owner in targets:
        g_span = pl.ds(pl.multiple_of(owner * half_columns, 128), half_columns)
        ref[slot, 0:half_columns, :] = product(g_span, pl.ds(y_start, features)).astype(BF16)
        for j in range(2):
            first = half_columns + shard * j
            ref[slot, first : first + shard, :] = fc_ref[
                j, pl.ds(pl.multiple_of(owner * shard, 16), shard), :
            ]
        ref[slot, small_base : small_base + 16, :] = small_ref[owner].astype(BF16)
        ref[slot, small_base + 16 :, :] = jnp.zeros_like(ref[slot, small_base + 16 :, :])
    for s in range(parts):
        block = product(
            pl.ds(a_start + shard * s, shard), pl.ds(z_start, half_columns)
        ).astype(BF16)
        owner = chip ^ s
        for ref, slot, wanted in targets:

            @pl.when(owner == wanted)
            def store_block():
                ref[slot, out_base:small_base, 0:half_columns] = block[: shard // 2]
                ref[slot, out_base:small_base, half_columns:] = block[shard // 2 :]


def qkv_grad_kernel(
    where,
    normed_ref,
    p0,
    p1,
    p2,
    p3,
    wq_ref,
    wk_ref,
    wv_ref,
    small_ref,
    keep_ref,
    send_ref,
    total_ref,
):
    blocks, rows, features = normed_ref.shape
    width = wq_ref.shape[1]
    part, core, chip = where[0], where[1], where[2]
    near, across = 1 + core, 2 - core
    parts = 4
    shard = features // parts
    half = shard // 2
    column_sums = [jnp.zeros((1, width), FP32) for n in range(3)]
    for n in range(3):
        total = jnp.zeros((features, width), FP32)
        for b in range(blocks):
            grads = (p0, p1, p2, p3)[b][:, width * n : width * (n + 1)]
            total = total + contract_rows(normed_ref[chip ^ b], grads)
            column_sums[n] = column_sums[n] + jnp.sum(grads.astype(FP32), axis=0, keepdims=True)
        total_ref[:, width * n : width * (n + 1)] = total
    sums = jnp.concatenate(column_sums, axis=1)
    shift_grad = jnp.zeros((features, 1), FP32)
    gain_grad = jnp.zeros((features, 1), FP32)
    for n, ref in enumerate((wq_ref, wk_ref, wv_ref)):
        wide = ref[...].astype(FP32)
        shift_grad = shift_grad + jnp.sum(wide * column_sums[n], axis=1, keepdims=True)
        gain_grad = gain_grad + jnp.sum(
            wide * total_ref[:, width * n : width * (n + 1)], axis=1, keepdims=True
        )
    columns = jnp.concatenate(
        [gain_grad, shift_grad, jnp.zeros((features, 126), FP32)], axis=1
    )
    norm_rows = columns.T[0:8]
    gain, shift = whole_vector(small_ref, 4), whole_vector(small_ref, 5)
    gain_row = (norm_rows[0:1] - shift * norm_rows[1:2]) / gain
    norm_rows = jnp.concatenate([gain_row, norm_rows[1:]], axis=0)
    order = [part, part ^ across, part ^ near, part ^ 3]
    other_order = [part, part ^ near, part ^ across, part ^ 3]
    for ref, which, owners in ((keep_ref, core, order), (send_ref, 1 - core, other_order)):
        for slot in range(parts):
            owner = owners[slot]
            first = pl.multiple_of(owner * shard + which * half, 16)
            ref[slot, 0:half, :] = total_ref[pl.ds(first, half), :].astype(ref.dtype)
            picked = jnp.zeros((8, shard), FP32)
            for f in range(parts):
                picked = jnp.where(owner == f, norm_rows[:, shard * f : shard * (f + 1)], picked)
            row = lax.broadcasted_iota(jnp.int32, (8, 3 * width), 0)
            packed = jnp.concatenate([picked, jnp.zeros((8, 3 * width - shard), FP32)], axis=1)
            tail = jnp.where(row < 2, packed, jnp.where(row == 2, sums, 0.0))
            tail = jnp.concatenate([tail, jnp.zeros_like(tail)], axis=0)
            ref[slot, half : half + 16, :] = tail.astype(ref.dtype)


def relay_kernel(where, keep_ref, theirs_ref, relay_ref):
    relay_ref[...] = (keep_ref[1].astype(FP32) + theirs_ref[1].astype(FP32)).astype(BF16)


def block_kernel(where, keep_ref, theirs_ref, last_ref, out_ref):
    total = keep_ref[0].astype(FP32) + theirs_ref[0].astype(FP32)
    out_ref[...] = (total + last_ref[...].astype(FP32)).astype(BF16)


def input_grad_kernel(
    where, p0, p1, p2, p3, w_ref, tokens_ref, dx_ref, small_ref, out_ref, packed_ref
):
    chip = where[2]
    features = w_ref.shape[0]
    width = p0.shape[1] // 3
    for z in range(4):
        for s, piece in enumerate((p0, p1, p2, p3)):

            @pl.when(chip == z ^ s)
            def place_piece():
                for n in range(3):
                    first = features * n + width * z
                    packed_ref[:, first : first + width] = piece[:, width * n : width * (n + 1)]

    total = dot_nt(packed_ref[...], w_ref[...])
    unit, inverse = layer_norm(
        tokens_ref[...].astype(FP32), whole_vector(small_ref, 4), whole_vector(small_ref, 5)
    )[1:]
    out_ref[...] = dx_ref[...] + norm_back(total, unit, inverse, whole_vector(small_ref, 4))[0]


def output_kernel(
    where, mine_ref, other_ref, proj_ref, fc_ref, out_ref, sums_ref
):
    core = where[1]
    half_columns = proj_ref.shape[0] // 2
    shard, features = out_ref.shape
    out_rows = half_columns + 2 * shard
    small_at = out_rows + shard // 2
    sums_ref[...] = mine_ref[small_at : small_at + 16, :].astype(FP32) + other_ref[
        small_at : small_at + 16, :
    ].astype(FP32)

    def place(ref, which):
        proj_ref[which * half_columns : (which + 1) * half_columns, :] = ref[
            0:half_columns, :
        ].astype(FP32)
        for j in range(2):
            first = half_columns + shard * j
            column = features * (2 * which + j)
            fc_ref[:, column : column + features] = ref[first : first + shard, :].astype(FP32)
        span = slice(features // 2 * which, features // 2 * (which + 1))
        middle = out_rows + shard // 2
        out_ref[0 : shard // 2, span] = ref[out_rows:middle, 0 : features // 2].astype(FP32)
        out_ref[shard // 2 :, span] = ref[out_rows:middle, features // 2 :].astype(FP32)

    @pl.when(core == 0)
    def first_core():
        place(mine_ref, 0)
        place(other_ref, 1)

    @pl.when(core == 1)
    def second_core():
        place(mine_ref, 1)
        place(other_ref, 0)


def qkv_output_kernel(where, h0, h1, h2, h3, out_ref, extra_ref, zero_ref):
    zero_ref[...] = jnp.zeros_like(zero_ref)
    core, chip = where[1], where[2]
    shard, wide = out_ref.shape
    features = wide // 3
    half = shard // 2
    width = h0.shape[2] // 3
    for s, ref in enumerate((h0, h1, h2, h3)):
        extra_ref[chip ^ s] = jnp.where(
            core == 0, ref[0, half : half + 16, :], ref[1, half : half + 16, :]
        ).astype(FP32)
        for z in range(4):

            @pl.when(chip == z ^ s)
            def place_piece():
                for n in range(3):
                    first = features * n + width * z
                    for slot, which in ((0, core), (1, 1 - core)):
                        rows = pl.ds(pl.multiple_of(which * half, 8), half)
                        out_ref[rows, first : first + width] = ref[
                            slot, 0:half, width * n : width * (n + 1)
                        ].astype(FP32)


def fast_body(
    tokens,
    cotangent,
    w_qkv,
    b_query,
    b_value,
    w_out,
    b_out,
    w_fc,
    b_fc,
    w_proj,
    b_proj,
    gain1,
    shift1,
    gain2,
    shift2,
    counts,
    seq_lengths,
):
    rows, features = tokens.shape
    ctx = lax.axis_size("ctx")
    fsdp = lax.axis_size("fsdp")
    chips = ctx // 2
    group_heads = HEADS // chips
    width = features // chips
    shard = features // fsdp
    hidden_width = w_fc.shape[1]
    columns = hidden_width // fsdp
    place = lax.axis_index("ctx")
    chip = place // 2
    core = place % 2
    part = lax.axis_index("fsdp")
    near = 1 + core
    across = 2 - core
    same_core = [[2 * z + k for z in range(chips)] for k in range(2)]
    where = jnp.stack([part, core, chip]).astype(jnp.int32)

    def exchange(value, partner):
        pairs = [
            (f * ctx + c, g * ctx + d)
            for f in range(fsdp)
            for c in range(ctx)
            for g, d in [partner(f, c)]
        ]
        return lax.ppermute(value, ("fsdp", "ctx"), pairs)

    def to_near(value):
        return exchange(value, lambda f, c: (f ^ (1 + c % 2), c))

    def to_across(value):
        return exchange(value, lambda f, c: (f ^ (2 - c % 2), c))

    def to_core(value):
        return exchange(value, lambda f, c: (f, c ^ 1))

    def to_chip(value, step):
        return exchange(value, lambda f, c: (f, c ^ (2 * step)))

    def pick(array, index, axis=0):
        return lax.dynamic_index_in_dim(array, index, axis, keepdims=False)

    def place_all(shape, dtype, items):
        buffer = jnp.zeros(shape, dtype)
        for index, value in items:
            full = value.reshape((1,) * (len(shape) - value.ndim) + value.shape)
            starts = tuple(index) + (0,) * (len(shape) - len(index))
            buffer = lax.dynamic_update_slice(buffer, full.astype(dtype), starts)
        return buffer

    half = shard // 2
    fc_half = lax.dynamic_slice_in_dim(w_fc, core * half, half, 0)
    bundle = jnp.concatenate(
        [
            lax.dynamic_slice_in_dim(w_proj, core * (columns // 2), columns // 2, 0),
            lax.dynamic_slice_in_dim(w_out, core * half, half, 0),
        ]
        + [fc_half[:, columns * j : columns * (j + 1)] for j in range(fsdp)],
        axis=0,
    )

    blocks = [tokens] + [to_chip(tokens, s) for s in (1, 2, 3)]
    bundles = lax.all_gather(bundle, "fsdp", axis=0)

    count_row = counts[0]
    offsets = jnp.cumsum(count_row) - count_row
    seq_ends = jnp.cumsum(seq_lengths[0])
    within = jnp.arange(rows, dtype=jnp.int32)
    slot = jnp.arange(ctx, dtype=jnp.int32)[:, None] * rows + within[None, :]
    live = within[None, :] < count_row[:, None]
    places = offsets[:, None] + within[None, :]
    starts = jnp.max(
        jnp.where(places[:, :, None] >= seq_ends[None, None, :], seq_ends[None, None, :], 0), axis=2
    )
    dead_id = -1 - slot
    key_ids = jnp.where(live, places, dead_id)
    lows = jnp.where(live, starts, dead_id)
    fars = jnp.where(live, starts, NEVER)
    key_tile = jnp.broadcast_to(key_ids[:, :, None], (ctx, rows, 128))

    def own_parity(array):
        return pick(array.reshape((chips, 2) + array.shape[1:]), core, 1)

    low_rows = own_parity(lows)[:, None, :]
    high_rows = own_parity(key_ids)[:, None, :]
    far_rows = own_parity(fars)[:, None, :]
    live_rows = (within < pick(count_row, place)).astype(FP32)[:, None]

    vectors = [b_query, b_value, b_out, b_proj, gain1, shift1, gain2, shift2]
    vectors += [b_fc[shard * n : shard * (n + 1)] for n in range(fsdp)]
    row = lax.broadcasted_iota(jnp.int32, (16, shard), 0)
    smalls = jnp.zeros((16, shard), BF16)
    for n, vector in enumerate(vectors):
        smalls = jnp.where(row == n, vector[None, :], smalls)
    mine = jnp.concatenate(
        [
            lax.dynamic_slice_in_dim(w_qkv, core * half, half, 0),
            jnp.pad(smalls, ((0, 0), (0, 3 * features - shard))),
        ],
        axis=0,
    )
    gathered = lax.all_gather(mine, "fsdp", axis=0)
    gathered = (gathered, to_core(gathered))
    beside = [to_core(v) for v in blocks]
    order = [v for pair in zip(blocks, beside) for v in pair]
    (stats,) = kernel_call(
        stats_kernel,
        [jax.ShapeDtypeStruct((ctx, rows, 2), FP32)],
        [],
        (where, *order),
        40,
    )
    *half_stores, qkv_full, weight_q, weight_k, weight_v, small_all = kernel_call(
        project_kernel,
        [
            jax.ShapeDtypeStruct((chips // 2, rows, width), BF16),
            jax.ShapeDtypeStruct((chips, rows, width), BF16),
            jax.ShapeDtypeStruct((chips, width, rows), BF16),
            jax.ShapeDtypeStruct((chips, rows, width), BF16),
            jax.ShapeDtypeStruct((chips, width, rows), BF16),
            jax.ShapeDtypeStruct((chips // 2, rows, features), BF16),
            jax.ShapeDtypeStruct((features, 3 * features), BF16),
            jax.ShapeDtypeStruct((features, width), BF16),
            jax.ShapeDtypeStruct((features, width), BF16),
            jax.ShapeDtypeStruct((features, width), BF16),
            jax.ShapeDtypeStruct((fsdp, 16, width), FP32),
        ],
        [],
        (where, blocks[0], beside[0], blocks[1], beside[1], stats, w_qkv) + gathered,
        9,
    )
    queries, keys, keys_t, values, normed_mine, *rest = kernel_call(
        attend_kernel,
        [
            jax.ShapeDtypeStruct((chips, rows, width), BF16),
            jax.ShapeDtypeStruct((ctx, rows, width), BF16),
            jax.ShapeDtypeStruct((ctx, width, rows), BF16),
            jax.ShapeDtypeStruct((ctx, rows, width), BF16),
            jax.ShapeDtypeStruct((chips, rows, features), BF16),
        ]
        + [jax.ShapeDtypeStruct((rows, width), BF16)] * 4
        + [
            jax.ShapeDtypeStruct((chips, width, rows), FP32),
            jax.ShapeDtypeStruct((chips, 8, rows), FP32),
            jax.ShapeDtypeStruct((16, 128), BF16),
        ],
        [
            pltpu.VMEM((ctx, width, rows), BF16),
            pltpu.VMEM((width, rows), FP32),
            pltpu.VMEM((chips, rows, width), BF16),
        ],
        (where, blocks[2], beside[2], blocks[3], beside[3])
        + (stats, weight_q, weight_k, weight_v, small_all)
        + tuple(half_stores)
        + (key_tile, low_rows, high_rows, far_rows),
        30,
    )
    attended_t, logs, zeros = rest[4:]

    def swap_chips(pieces):
        return [pieces[0]] + [to_chip(pieces[s], s) for s in (1, 2, 3)]

    bundles = lax.dynamic_update_slice(bundles, (bundles[0, :16, :128] + zeros)[None], (0, 0, 0))
    bundles_other = to_core(bundles)
    attended = swap_chips(rest[:4])
    bundle_width = 2 * hidden_width // 2 + 3 * features + features // 2
    hbm = pl.BlockSpec(memory_space=pl.ANY)
    block_out, grad_middle, d0, d1, d2, d3, bundle_mine, bundle_send, small_rows = kernel_call(
        middle_kernel,
        [
            jax.ShapeDtypeStruct((rows, features), BF16),
            jax.ShapeDtypeStruct((rows, features), FP32),
        ]
        + [jax.ShapeDtypeStruct((rows, width), BF16)] * 4
        + [
            jax.ShapeDtypeStruct((rows, bundle_width), BF16),
            jax.ShapeDtypeStruct((rows, bundle_width), BF16),
            jax.ShapeDtypeStruct((fsdp, 16, features), FP32),
        ],
        [
            pltpu.VMEM((features, features), BF16),
            pltpu.VMEM((fsdp, features, columns), BF16),
            pltpu.VMEM((hidden_width, features), BF16),
            pltpu.VMEM((rows, columns), BF16),
            pltpu.VMEM((rows, features), BF16),
            pltpu.SemaphoreType.DMA((8 * 6,)),
        ],
        tuple([where] + attended)
        + (
            tokens,
            cotangent,
            live_rows,
            small_all,
            bundles,
            bundles_other,
        ),
        21,
        special={9: hbm, 10: hbm},
    )

    grad_blocks = swap_chips([d0, d1, d2, d3])

    bundle_other = to_core(bundle_send)
    out_rows = columns // 2 + 2 * shard
    small_at = out_rows + half
    block_rows = small_at + 32
    pair_shape = jax.ShapeDtypeStruct((2, block_rows, features), BF16)
    grads_keep, grads_send = kernel_call(
        weight_grad_kernel,
        [pair_shape, pair_shape],
        [pltpu.VMEM((2, features, features), BF16)],
        (where, bundle_mine, bundle_other, small_rows),
        14,
        after=(grad_blocks[1],),
    )

    grad_query, grad_keep, grad_send = kernel_call(
        attend_back_kernel,
        [
            jax.ShapeDtypeStruct((chips, rows, width), BF16),
            jax.ShapeDtypeStruct((chips, rows, 2 * width), FP32),
            jax.ShapeDtypeStruct((chips, rows, 2 * width), BF16),
        ],
        [
            pltpu.VMEM((width, rows), FP32),
            pltpu.VMEM((group_heads, ctx, rows, 64), FP32),
            pltpu.VMEM((group_heads, ctx, rows, 64), FP32),
            pltpu.VMEM((chips, rows, width), BF16),
        ],
        (
            where,
            queries,
            keys,
            keys_t,
            values,
            *grad_blocks,
            key_tile,
            low_rows,
            high_rows,
            far_rows,
            attended_t,
            logs,
        ),
        30,
    )
    packed = kernel_call(
        pack_kernel,
        [jax.ShapeDtypeStruct((rows, 3 * width), BF16)] * 4,
        [],
        (where, grad_query, grad_keep, to_core(grad_send)),
        2,
    )

    def add_up(left_side, right_side):
        return left_side.astype(FP32) + right_side.astype(FP32)

    arrived = swap_chips(packed)
    theirs = to_near(grads_send)
    block = jax.ShapeDtypeStruct((block_rows, features), BF16)

    (relay,) = kernel_call(
        relay_kernel, [block], [], (where, grads_keep, theirs), 1, after=(packed[0],)
    )
    (grads_block,) = kernel_call(
        block_kernel,
        [block],
        [],
        (where, grads_keep, theirs, to_across(relay)),
        2,
        after=(arrived[1],),
    )

    grads_half = lax.psum(grads_block, "ctx", axis_index_groups=same_core)
    block_shape = (fsdp, half + 16, 3 * width)
    qkv_keep, qkv_send = kernel_call(
        qkv_grad_kernel,
        [jax.ShapeDtypeStruct(block_shape, FP32), jax.ShapeDtypeStruct(block_shape, BF16)],
        [pltpu.VMEM((features, 3 * width), FP32)],
        (
            where,
            normed_mine,
            *packed,
            weight_q,
            weight_k,
            weight_v,
            small_all,
        ),
        8,
        after=tuple(arrived[1:]) + (grads_block,),
    )
    qkv_blocks = add_up(qkv_keep, to_core(qkv_send)).astype(BF16)
    theirs_qkv = to_near(qkv_blocks[2:])
    last_qkv = to_across(add_up(qkv_blocks[1], theirs_qkv[1]).astype(BF16))
    qkv_half = (add_up(qkv_blocks[0], theirs_qkv[0]) + last_qkv.astype(FP32)).astype(BF16)
    (grad_tokens,) = kernel_call(
        input_grad_kernel,
        [jax.ShapeDtypeStruct((rows, features), FP32)],
        [pltpu.VMEM((rows, 3 * features), BF16)],
        tuple([where] + arrived) + (qkv_full, tokens, grad_middle, small_all),
        5,
        after=(theirs_qkv,),
    )

    halves = swap_chips([jnp.stack([qkv_half, to_core(qkv_half)])] * 4)
    d_qkv, extra, zeros = kernel_call(
        qkv_output_kernel,
        [
            jax.ShapeDtypeStruct((shard, 3 * features), FP32),
            jax.ShapeDtypeStruct((chips, 16, 3 * width), FP32),
            jax.ShapeDtypeStruct((16, 128), BF16),
        ],
        [],
        tuple([where] + halves),
        2,
        after=(grad_tokens,),
    )
    grads_half = lax.dynamic_update_slice(grads_half, grads_half[:16, :128] + zeros, (0, 0))
    d_proj, d_fc, d_out, small_sums = kernel_call(
        output_kernel,
        [
            jax.ShapeDtypeStruct((columns, features), FP32),
            jax.ShapeDtypeStruct((shard, hidden_width), FP32),
            jax.ShapeDtypeStruct((shard, features), FP32),
            jax.ShapeDtypeStruct((16, features), FP32),
        ],
        [],
        (where, grads_half, to_core(grads_half)),
        2,
    )
    d_bias_out, d_bias_proj, d_gain_two, d_shift_two = (
        small_sums[0, n * shard : (n + 1) * shard] for n in range(4)
    )
    d_bias_fc = small_sums[1]

    owner_extra = pick(extra, part)
    d_bias_q = owner_extra[2, :width]
    d_bias_v = owner_extra[2, 2 * width :]
    norm_total = jnp.sum(extra[:, :2, :shard], axis=0)
    d_gain_one = norm_total[0]
    d_shift_one = norm_total[1]

    return (
        block_out,
        grad_tokens,
        d_qkv,
        d_bias_q,
        d_bias_v,
        d_out,
        d_bias_out,
        d_fc,
        d_bias_fc,
        d_proj,
        d_bias_proj,
        d_gain_one,
        d_shift_one,
        d_gain_two,
        d_shift_two,
    )


def solution(mesh):
    in_specs = (
        P(("fsdp", "ctx"), None),
        P(("fsdp", "ctx"), None),
        P("fsdp", None),
        P("fsdp"),
        P("fsdp"),
        P("fsdp", None),
        P("fsdp"),
        P("fsdp", None),
        P("fsdp"),
        P("fsdp", None),
        P("fsdp"),
        P("fsdp"),
        P("fsdp"),
        P("fsdp"),
        P("fsdp"),
        P("fsdp", None),
        P("fsdp", None),
    )
    out_specs = (
        P(("fsdp", "ctx"), None),
        P(("fsdp", "ctx"), None),
        P("fsdp", None),
        P("fsdp"),
        P("fsdp"),
        P("fsdp", None),
        P("fsdp"),
        P("fsdp", None),
        P("fsdp"),
        P("fsdp", None),
        P("fsdp"),
        P("fsdp"),
        P("fsdp"),
        P("fsdp"),
        P("fsdp"),
    )
    ctx = mesh.shape["ctx"]
    four_by_four = mesh.shape["fsdp"] == 4 and ctx == 8 and HEADS % (ctx // 2) == 0
    body = fast_body if four_by_four else general_body
    return jax.shard_map(body, mesh=mesh, in_specs=in_specs, out_specs=out_specs, check_vma=False)
```
